32 devices in a mesh: groups: 2 (over y), slab: 4 (over z), probe: 2 (over x), sub: 2 (over core).
Axes of the slice: x: 2, y: 2, z: 4, core: 2. Of those that a mesh axis runs over, the one named last changes fastest.
Arguments:
- probes: bfloat16 [64, 16, 48, 512], P(('groups', 'slab'), 'sub', None, 'probe'), parts along dimension 0, may hold values from -6 to 6
- courant: float32 [32, 16, 48], P('slab', 'sub'), may hold values from 0.05 to 0.19
- source: float32 [4, 64, 16, 48], P(None, ('groups', 'slab'), 'sub'), parts along dimension 1, may hold values from -48 to 48, as said below
Outputs:
- coupling: float32 [1024, 512], P(('groups', 'slab')), parts along dimension 0
- norms: float32 [1024], P(('groups', 'slab')), parts along dimension 0
The draws below stay inside these ranges and needn't reach their ends.
There are 2 independent parts, one for each index of `groups`. The reference program is written for one: setup_inputs(seed, part) draws one part's arguments, and reference() takes and returns one part's arrays. A program takes and returns all parts, laid end to end along the dimension named above; an argument that names none is the same for every part. Nothing has to cross between parts.
Inputs may be any that keep to these rules, and one draw needn't show every extreme that they name: A signed background source, of a scale that varies smoothly over the grid.
All inputs are finite; a program needn't handle non-finite values.
Results may differ from the reference program's by a relative error of at most 0.003.
Values may be sent and summed in bfloat16 or wider, within the bound.
No kernel may reach another device: no remote copies, remote signals or barrier semaphores. Data moves between devices by JAX's collectives and lax.ppermute only.
A program may use at most 128 MiB of HBM per device.

```python
import math
import jax
import jax.numpy as jnp
from jax import lax

P_SIZE = 512
ITERS = 4
NY = 48
NZ = 32
NX = 16


def draw_source(key, part):
    key = jax.random.fold_in(key, 5)
    full_shape = (ITERS, NZ, NX, NY)
    depth_axis = jnp.arange(NZ, dtype=jnp.float32) / NZ
    width_axis = jnp.arange(NX, dtype=jnp.float32) / NX
    length_axis = jnp.arange(NY, dtype=jnp.float32) / NY
    level_sum = depth_axis[:, None, None] + width_axis[None, :, None] + length_axis[None, None, :]
    base_values = jnp.clip(jax.random.normal(key, full_shape, jnp.float32), -4.0, 4.0)
    rise_factor = 3.0
    amplitude = jnp.exp(0.5 * level_sum * jnp.log(rise_factor))
    return (base_values * amplitude[None]).astype(jnp.float32)


def block_scale(rng, shape, shards, low, high):
    def one(position, parts):
        heights = jax.random.uniform(jax.random.fold_in(jax.random.fold_in(rng, 6), position), (parts,), jnp.float32, low / len(shards), high / len(shards))
        return jnp.repeat(jnp.exp(heights), shape[position] // parts).reshape((-1,) + (1,) * (len(shape) - position - 1))

    loudness = one(*shards[0])
    for cut in shards[1:]:
        loudness = loudness * one(*cut)
    return loudness


def bell_draw(stream_key, dims, deviation, reach, cuts=(), held_as=jnp.bfloat16):
    result = jax.random.normal(stream_key, dims, jnp.float32) * deviation
    if len(cuts) > 0:
        result = block_scale(stream_key, dims, cuts, -0.22, 0.18) * result
    return jnp.clip(result, min=-reach, max=reach).astype(held_as)


def setup_inputs(seed: int = 0, part: int = 0) -> dict:
    key_of = jax.random.split(jax.random.key(seed), 4)
    part_splits = jax.random.split(jax.random.fold_in(key_of[3], part), 4)
    probes = bell_draw(part_splits[0], (NZ, NX, NY, P_SIZE), 1.0, 6.0, ((0, 4), (1, 2), (3, 2)))
    courant = jnp.clip(0.05 + 0.14 * jax.random.uniform(key_of[1], (NZ, NX, NY), jnp.float32) ** block_scale(key_of[1], (NZ, NX, NY), ((0, 4), (1, 2)), -0.2, 0.2), 0.05, 0.19)
    source = draw_source(jax.random.fold_in(jax.random.fold_in(key_of[3], part), 71), part)
    return {"probes": probes, "courant": courant, "source": source}


COEFFICIENTS = (-205.0 / 72.0, 8.0 / 5.0, -1.0 / 5.0, 8.0 / 315.0, -1.0 / 560.0)
EPSILON = 1e-06

def laplace(current):
    padded = jnp.pad(current, ((4, 4), (4, 4), (4, 4), (0, 0)))
    depth_cells, across, along_cells = (current.shape[0], current.shape[1], current.shape[2])
    summed = 3.0 * COEFFICIENTS[0] * current
    for distance in range(1, 5):
        pair_deep = padded[4 + distance:4 + distance + depth_cells, 4:4 + across, 4:4 + along_cells] + padded[4 - distance:4 - distance + depth_cells, 4:4 + across, 4:4 + along_cells]
        pair_wide = padded[4:4 + depth_cells, 4 + distance:4 + distance + across, 4:4 + along_cells] + padded[4:4 + depth_cells, 4 - distance:4 - distance + across, 4:4 + along_cells]
        pair_long = padded[4:4 + depth_cells, 4:4 + across, 4 + distance:4 + distance + along_cells] + padded[4:4 + depth_cells, 4:4 + across, 4 - distance:4 - distance + along_cells]
        summed = summed + COEFFICIENTS[distance] * (pair_deep + pair_wide + pair_long)
    return summed

def propagate(probe_block, courant, source):
    previous = jnp.zeros(probe_block.shape, jnp.float32)
    current = source[0][..., None] * probe_block
    for moment in range(1, source.shape[0]):
        upcoming = 2.0 * current - previous + courant[..., None] * laplace(current) + source[moment][..., None] * probe_block
        previous, current = (current, upcoming)
    return current.astype(jnp.bfloat16)

def reference(probes, courant, source):
    block_width = min(P_SIZE, 128)
    cell_count = NZ * NX * NY
    pieces = []
    for index_block in range(P_SIZE // block_width):
        probe_block = probes[:, :, :, index_block * block_width:(index_block + 1) * block_width]
        fields = propagate(probe_block, courant, source)
        pieces.append(fields.reshape(cell_count, block_width))
    flattened = jnp.concatenate(pieces, axis=1)
    gram_matrix = jnp.dot(flattened.T, flattened, preferred_element_type=jnp.float32)
    column_norms = jnp.sqrt(jnp.diagonal(gram_matrix) / cell_count + EPSILON)
    coupling = gram_matrix / math.sqrt(cell_count) / (column_norms[:, None] * column_norms[None, :])
    row_ids = lax.broadcasted_iota(jnp.int32, coupling.shape, 0)
    col_ids = lax.broadcasted_iota(jnp.int32, coupling.shape, 1)
    coupling = jnp.where(row_ids == col_ids, 0.0, coupling)
    return (coupling, column_norms)
```

```python
import functools
import math

import jax
import jax.numpy as jnp
from jax import lax
from jax.experimental import pallas as pl
from jax.experimental.pallas import tpu as pltpu
from jax.sharding import PartitionSpec as P

COEFFICIENTS = (-205.0 / 72.0, 8.0 / 5.0, -1.0 / 5.0, 8.0 / 315.0, -1.0 / 560.0)
EPSILON = 1e-06
LANES = 128
RADIUS = 4
EDGE = 8
TILE = 16
F32 = jnp.float32
BF16 = jnp.bfloat16
VMEM_LIMIT = 32 * 1024 * 1024


def params(*semantics):
    return pltpu.CompilerParams(
        dimension_semantics=semantics or None, vmem_limit_bytes=VMEM_LIMIT
    )


def edge_store(i, across, edge_ref, value_of):
    core = lax.axis_index("sub")
    first = (across - RADIUS) * (1 - core)
    slot = i - first

    @pl.when((slot >= 0) & (slot < RADIUS))
    def _():
        edge_ref[:, pl.ds(jnp.clip(slot, 0, RADIUS - 1), 1)] = value_of().astype(BF16)


def first_body(p_ref, s_ref, u_ref, low_ref, high_ref, edge_ref):
    i = pl.program_id(0)
    depth = u_ref.shape[0]
    u = s_ref[...] * p_ref[...].astype(F32)
    u_ref[...] = u
    low_ref[...] = u[:RADIUS].astype(BF16)
    high_ref[...] = u[depth - RADIUS :].astype(BF16)
    edge_store(i, pl.num_programs(0), edge_ref, lambda: u_ref[...])


def first_field(probes, chunk, source0):
    depth, across, along, _ = probes.shape
    column = lambda n: pl.BlockSpec((n, 1, along, LANES), lambda i: (0, i, 0, 0))
    shape = lambda n, m, dtype: jax.ShapeDtypeStruct((n, m, along, LANES), dtype)
    return pl.pallas_call(
        first_body,
        grid=(across,),
        in_specs=[
            pl.BlockSpec((depth, 1, along, LANES), lambda i: (0, i, 0, chunk)),
            column(depth),
        ],
        out_specs=[
            column(depth),
            column(RADIUS),
            column(RADIUS),
            pl.BlockSpec((depth, RADIUS, along, LANES), lambda i: (0, 0, 0, 0)),
        ],
        out_shape=[
            shape(depth, across, F32),
            shape(RADIUS, across, BF16),
            shape(RADIUS, across, BF16),
            shape(depth, RADIUS, BF16),
        ],
        compiler_params=params("arbitrary"),
    )(probes, source0)


def fill(wide, u_ref, below_ref, above_ref, beside_ref):
    depth, across, along, _ = u_ref.shape
    core = lax.axis_index("sub")
    far = across + RADIUS
    inner = pl.ds(RADIUS, across)
    rows = pl.ds(EDGE, along)
    blank = jnp.zeros((across, EDGE, LANES), F32)

    def plane(z, _):
        wide[RADIUS + z, inner, rows] = u_ref[z]
        wide[RADIUS + z, inner, pl.ds(0, EDGE)] = blank
        wide[RADIUS + z, inner, pl.ds(EDGE + along, EDGE)] = blank
        wide[RADIUS + z, pl.ds(far * (1 - core), RADIUS), rows] = beside_ref[z].astype(F32)
        wide[RADIUS + z, pl.ds(far * core, RADIUS), rows] = jnp.zeros(
            (RADIUS, along, LANES), F32
        )
        return 0

    def outer(z, _):
        wide[z, inner, rows] = below_ref[z].astype(F32)
        wide[RADIUS + depth + z, inner, rows] = above_ref[z].astype(F32)
        return 0

    lax.fori_loop(0, depth, plane, 0)
    lax.fori_loop(0, RADIUS, outer, 0)


def step_body(has_previous, last, *refs):
    refs = list(refs)
    u_ref, below_ref, above_ref, beside_ref, p_ref, c_ref, s_ref = refs[:7]
    refs = refs[7:]
    prev_ref = refs.pop(0) if has_previous else None
    wide = refs.pop()
    i = pl.program_id(0)
    depth, across, along, _ = u_ref.shape

    @pl.when(i == 0)
    def _():
        fill(wide, u_ref, below_ref, above_ref, beside_ref)

    x = RADIUS + i

    def update(z, start, column):
        here = RADIUS + z
        rows = EDGE + start
        total = (3.0 * COEFFICIENTS[0]) * column[here]
        for r in range(1, RADIUS + 1):
            deep = column[here + r] + column[here - r]
            wide_pair = wide[here, x + r, pl.ds(rows, TILE)] + wide[here, x - r, pl.ds(rows, TILE)]
            long = wide[here, x, pl.ds(rows + r, TILE)] + wide[here, x, pl.ds(rows - r, TILE)]
            total = total + COEFFICIENTS[r] * (deep + wide_pair + long)
        span = pl.ds(start, TILE)
        new = 2.0 * column[here]
        if has_previous:
            new = new - prev_ref[z, 0, span]
        new = new + c_ref[z, 0, span] * total
        return new + s_ref[z, 0, span] * p_ref[z, 0, span].astype(F32)

    for start in range(0, along, TILE):
        span = pl.ds(start, TILE)
        column = [wide[z, x, pl.ds(EDGE + start, TILE)] for z in range(depth + 2 * RADIUS)]
        if last == "half":
            keep_ref, send_ref = refs
            lower = lax.axis_index("probe") == 0
            for z in range(depth // 2):
                one = update(z, start, column)
                two = update(z + depth // 2, start, column)
                keep_ref[z, 0, span] = jnp.where(lower, one, two).astype(BF16)
                send_ref[z, 0, span] = jnp.where(lower, two, one).astype(BF16)
        elif last:
            for z in range(depth):
                refs[0][z, 0, span] = update(z, start, column).astype(BF16)
        else:
            out_ref, low_ref, high_ref, edge_ref = refs
            for z in range(depth):
                new = update(z, start, column)
                out_ref[z, 0, span] = new
                if z < RADIUS:
                    low_ref[z, 0, span] = new.astype(BF16)
                if z >= depth - RADIUS:
                    high_ref[z - depth + RADIUS, 0, span] = new.astype(BF16)
    if not last:
        edge_store(i, across, refs[3], lambda: refs[0][...])


def step(u, halos, probes, chunk, courant, source, previous, last):
    depth, across, along, _ = u.shape
    below, above, beside = halos
    whole = lambda a: pl.BlockSpec(a.shape, lambda i: (0, 0, 0, 0))
    column = lambda n: pl.BlockSpec((n, 1, along, LANES), lambda i: (0, i, 0, 0))
    shape = lambda n, m, dtype: jax.ShapeDtypeStruct((n, m, along, LANES), dtype)
    operands = [u, below, above, beside, probes, courant, source]
    in_specs = [
        whole(u),
        whole(below),
        whole(above),
        whole(beside),
        pl.BlockSpec((depth, 1, along, LANES), lambda i: (0, i, 0, chunk)),
        column(depth),
        column(depth),
    ]
    if previous is not None:
        operands.append(previous)
        in_specs.append(column(depth))
    if last == "half":
        out_specs = [column(depth // 2)] * 2
        out_shape = [shape(depth // 2, across, BF16)] * 2
    elif last:
        out_specs = [column(depth)]
        out_shape = [shape(depth, across, BF16)]
    else:
        out_specs = [
            column(depth),
            column(RADIUS),
            column(RADIUS),
            pl.BlockSpec((depth, RADIUS, along, LANES), lambda i: (0, 0, 0, 0)),
        ]
        out_shape = [
            shape(depth, across, F32),
            shape(RADIUS, across, BF16),
            shape(RADIUS, across, BF16),
            shape(depth, RADIUS, BF16),
        ]
    return pl.pallas_call(
        functools.partial(step_body, previous is not None, last),
        grid=(across,),
        in_specs=in_specs,
        out_specs=out_specs,
        out_shape=out_shape,
        scratch_shapes=[
            pltpu.VMEM(
                (depth + 2 * RADIUS, across + 2 * RADIUS, along + 2 * EDGE, LANES), F32
            )
        ],
        compiler_params=params("arbitrary"),
    )(*operands)


def exchange(low, high, edge):
    slabs = lax.axis_size("slab")
    up = [(i, i + 1) for i in range(slabs - 1)]
    down = [(i + 1, i) for i in range(slabs - 1)]
    below = lax.ppermute(high, "slab", up)
    above = lax.ppermute(low, "slab", down)
    beside = lax.ppermute(edge, "sub", [(0, 1), (1, 0)])
    return below, above, beside


def gram_body(parts, *refs):
    ins, (keep_ref, send_ref), panel = refs[:parts], refs[parts : parts + 2], refs[-1]
    half = parts // 2
    chip = lax.axis_index("probe")
    core = lax.axis_index("sub")
    for n in range(half):
        mine = pl.multiple_of((chip * half + n) * LANES, LANES)
        other = pl.multiple_of(((1 - chip) * half + n) * LANES, LANES)
        panel[:, pl.ds(mine, LANES)] = ins[2 * n][...]
        panel[:, pl.ds(other, LANES)] = ins[2 * n + 1][...]
    size = parts * LANES
    everything = panel[...]

    def columns(which):
        one = panel[:, pl.ds(pl.multiple_of(which * LANES, LANES), LANES)]
        two = panel[:, pl.ds(pl.multiple_of((2 + which) * LANES, LANES), LANES)]
        return lax.dot_general(
            everything,
            jnp.concatenate([one, two], axis=1),
            (((0,), (0,)), ((), ())),
            preferred_element_type=F32,
        )

    rows = lax.broadcasted_iota(jnp.int32, (LANES, LANES), 0)
    cols = lax.broadcasted_iota(jnp.int32, (LANES, LANES), 1)
    eye = rows == cols
    keep = columns(core)
    send = columns(1 - core)
    keep_ref[:size] = keep
    send_ref[:size] = send

    def diagonal(which, first):
        side = which // 2
        a = keep_ref[which * LANES : (which + 1) * LANES, side * LANES : (side + 1) * LANES]
        b = send_ref[which * LANES : (which + 1) * LANES, side * LANES : (side + 1) * LANES]
        block = jnp.where(core == which % 2, a, b)
        return jnp.sum(jnp.where(eye, block, 0.0), axis=0, keepdims=True)

    diag = [diagonal(n, None) for n in range(parts)]
    row0 = jnp.concatenate(diag[:2], axis=1)
    row1 = jnp.concatenate(diag[2:], axis=1)
    tail = jnp.concatenate([row0, row1, jnp.zeros((6, 2 * LANES), F32)], axis=0)
    keep_ref[size:] = tail
    send_ref[size:] = tail


def gram(fields):
    parts = len(fields)
    size = parts * LANES
    shape = jax.ShapeDtypeStruct((size + 8, 2 * LANES), F32)
    return pl.pallas_call(
        functools.partial(gram_body, parts),
        out_shape=[shape, shape],
        scratch_shapes=[pltpu.VMEM((fields[0].shape[0], size), BF16)],
        compiler_params=params(),
    )(*fields)


def rows_body(slabs, count, keep_ref, got_ref, *outs):
    slab = lax.axis_index("slab")
    size = slabs * count
    tail = keep_ref[pl.ds(size, 8)] + got_ref[pl.ds(size, 8)]
    for d in range(slabs):
        owner = lax.rem(slab + d, slabs)
        span = pl.ds(pl.multiple_of(owner * count, count), count)
        outs[d][:count] = keep_ref[span] + got_ref[span]
        outs[d][count:] = tail


def split_rows(keep, got, slabs):
    count = (keep.shape[0] - 8) // slabs
    shape = jax.ShapeDtypeStruct((count + 8, keep.shape[1]), F32)
    return pl.pallas_call(
        functools.partial(rows_body, slabs, count),
        out_shape=[shape] * slabs,
        compiler_params=params(),
    )(keep, got)


def sum_body(*refs):
    total = refs[0][...]
    for ref in refs[1:-1]:
        total = total + ref[...]
    refs[-1][...] = total


def sum_all(pieces):
    return pl.pallas_call(
        sum_body,
        out_shape=jax.ShapeDtypeStruct(pieces[0].shape, F32),
        compiler_params=params(),
    )(*pieces)


def finish_body(cell_count, a_ref, b_ref, c_ref, d_ref, out_ref, norms_ref):
    slab = lax.axis_index("slab")
    core = lax.axis_index("sub")
    count = out_ref.shape[0]
    near = a_ref[...] + b_ref[...]
    far = c_ref[:count] + d_ref[:count]
    squares = near[count : count + 2]
    norms = jnp.sqrt(squares / cell_count + EPSILON)
    blocks = [norms[n // 2 : n // 2 + 1, (n % 2) * LANES : (n % 2 + 1) * LANES] for n in range(4)]
    own = blocks[0]
    for n in range(1, 4):
        own = jnp.where(slab == n, blocks[n], own)
    norms_ref[...] = own
    rows = lax.broadcasted_iota(jnp.int32, (LANES, LANES), 0)
    cols = lax.broadcasted_iota(jnp.int32, (LANES, LANES), 1)
    eye = rows == cols
    own_column = jnp.sum(
        jnp.where(eye, jnp.broadcast_to(own, (LANES, LANES)), 0.0), axis=1, keepdims=True
    )
    for side in range(2):
        for block, which in ((near, core), (far, 1 - core)):
            index = 2 * side + which
            others = jnp.where(which == 0, blocks[2 * side], blocks[2 * side + 1])
            value = block[:count, side * LANES : (side + 1) * LANES]
            value = value / math.sqrt(cell_count) / (own_column * others)
            value = jnp.where(eye & (index == slab), 0.0, value)
            out_ref[:, pl.ds(pl.multiple_of(index * LANES, LANES), LANES)] = value


def finish(pieces, cell_count):
    count = pieces[0].shape[0] - 8
    return pl.pallas_call(
        functools.partial(finish_body, cell_count),
        out_shape=[
            jax.ShapeDtypeStruct((count, 4 * LANES), F32),
            jax.ShapeDtypeStruct((1, LANES), F32),
        ],
        compiler_params=params(),
    )(*pieces)


def coupled(keeps, gots, cell_count):
    slabs = 4
    flat = lambda a: a.reshape(-1, LANES)
    fields = []
    for keep, got in zip(keeps, gots):
        fields += [flat(keep), flat(got)]
    keep, send = gram(fields)
    got = lax.ppermute(send, "sub", [(0, 1), (1, 0)])
    pieces = split_rows(keep, got, slabs)
    arrived = [pieces[0]]
    for d in range(1, slabs):
        arrived.append(
            lax.ppermute(pieces[d], "slab", [(i, (i + d) % slabs) for i in range(slabs)])
        )
    mine = sum_all(arrived)
    both = ("probe", "sub")
    others = [
        lax.ppermute(mine, both, [(i, i ^ flip) for i in range(4)]) for flip in (2, 1, 3)
    ]
    coupling, norms = finish([mine] + others, cell_count)
    return coupling, norms.reshape(-1)


def coupled_general(fields, cell_count):
    chips = lax.axis_size("probe")
    sketch = jnp.concatenate(fields, axis=-1)
    sketch = sketch.reshape(-1, sketch.shape[-1])
    if chips > 1:
        sketch = lax.all_to_all(sketch, "probe", split_axis=0, concat_axis=1, tiled=True)
    partial_gram = lax.dot_general(
        sketch, sketch, (((0,), (0,)), ((), ())), preferred_element_type=F32
    )
    rows = lax.psum_scatter(partial_gram, "slab", scatter_dimension=0, tiled=True)
    rows = lax.psum(rows, ("probe", "sub"))
    count = rows.shape[0]
    start = lax.axis_index("slab") * count
    own = jnp.diagonal(lax.dynamic_slice_in_dim(rows, start, count, 1))
    own_norms = jnp.sqrt(own / cell_count + EPSILON)
    norms = lax.all_gather(own_norms, "slab", axis=0, tiled=True)
    coupling = rows / math.sqrt(cell_count) / (own_norms[:, None] * norms[None, :])
    row_ids = start + lax.broadcasted_iota(jnp.int32, coupling.shape, 0)
    col_ids = lax.broadcasted_iota(jnp.int32, coupling.shape, 1)
    return jnp.where(row_ids == col_ids, 0.0, coupling), own_norms


def shards(probes, courant, source):
    depth, across, along, count = probes.shape
    chunks = count // LANES
    slabs, chips = lax.axis_size("slab"), lax.axis_size("probe")
    cell_count = depth * across * along * slabs * lax.axis_size("sub")
    paired = chips == 2 and slabs == 4 and chunks == 2
    spread = lambda a: jnp.broadcast_to(a[..., None], a.shape + (LANES,))
    steps = source.shape[0]
    wide_source = [spread(source[n]) for n in range(steps)]
    wide_courant = spread(courant)

    now, previous, halos = [], [None] * chunks, []
    for c in range(chunks):
        u, low, high, edge = first_field(probes, c, wide_source[0])
        now.append(u)
        halos.append(exchange(low, high, edge))
    done = []
    for n in range(1, steps):
        last = n == steps - 1
        for c in range(chunks):
            kind = "half" if last and paired else last
            out = step(
                now[c], halos[c], probes, c, wide_courant, wide_source[n], previous[c], kind
            )
            if last and paired:
                done.append((out[0], lax.ppermute(out[1], "probe", [(0, 1), (1, 0)])))
            elif last:
                done.append(out[0])
            else:
                previous[c], now[c] = now[c], out[0]
                halos[c] = exchange(*out[1:])
    if paired:
        return coupled([a for a, _ in done], [b for _, b in done], cell_count)
    return coupled_general(done, cell_count)


def solution(mesh):
    placed = (
        P(("groups", "slab"), "sub", None, "probe"),
        P("slab", "sub", None),
        P(None, ("groups", "slab"), "sub", None),
    )
    return jax.shard_map(
        shards,
        mesh=mesh,
        in_specs=placed,
        out_specs=(P(("groups", "slab"), None), P(("groups", "slab"))),
        check_vma=False,
    )
```

```python
import functools
import math

import jax
import jax.numpy as jnp
from jax import lax
from jax.experimental import pallas as pl
from jax.experimental.pallas import tpu as pltpu
from jax.sharding import PartitionSpec as P

COEFFICIENTS = (-205.0 / 72.0, 8.0 / 5.0, -1.0 / 5.0, 8.0 / 315.0, -1.0 / 560.0)
EPSILON = 1e-06
LANES = 128
RADIUS = 4
EDGE = 8
TILE = 16
F32 = jnp.float32
BF16 = jnp.bfloat16
VMEM_LIMIT = 32 * 1024 * 1024


def params(*semantics):
    return pltpu.CompilerParams(
        dimension_semantics=semantics or None, vmem_limit_bytes=VMEM_LIMIT
    )


def whole_vmem(count):
    return [pl.BlockSpec(memory_space=pltpu.VMEM)] * count


def shape_of(depth, across, along, dtype):
    return jax.ShapeDtypeStruct((depth, across, along, LANES), dtype)


def turned(field, scratch):
    rows, along = field.shape
    scratch[:rows, :along] = field
    return jnp.transpose(scratch[...])


def lane(values, n):
    return jnp.broadcast_to(values[:, n : n + 1], (values.shape[0], LANES))


def store_edges(z, x, span, new, depth, across, core, refs):
    low_refs, high_refs, edge_ref = refs
    value = new.astype(BF16)
    width = across // len(low_refs)
    if z < RADIUS:
        low_refs[x // width][z, x % width, span] = value
    if z >= depth - RADIUS:
        high_refs[x // width][z - depth + RADIUS, x % width, span] = value

    for mine, first in ((0, across - RADIUS), (1, 0)):
        if first <= x < first + RADIUS:

            @pl.when(core == mine)
            def _():
                edge_ref[z, x - first, span] = value


def clear_pads(u_ref):
    depth, across, padded, _ = u_ref.shape

    def plane(z, _):
        blank = jnp.zeros((across, EDGE, LANES), F32)
        u_ref[z, :, pl.ds(0, EDGE)] = blank
        u_ref[z, :, pl.ds(padded - EDGE, EDGE)] = blank
        return 0

    lax.fori_loop(0, depth, plane, 0)


def tiles(along, body):
    def one(t, _):
        body(pl.multiple_of(t * TILE, TILE))
        return 0

    lax.fori_loop(0, along // TILE, one, 0)


def first_body(chunk, p_ref, s_ref, u_ref, low_ref, high_ref, edge_ref, square, turned_s):
    depth, across, padded, _ = u_ref.shape
    along = padded - 2 * EDGE
    core = lax.axis_index("sub")
    turned_s[...] = turned(s_ref[0], square)
    clear_pads(u_ref)

    def tile(start):
        span = pl.ds(start, TILE)
        source = turned_s[span]
        for z in range(depth):
            for x in range(across):
                p = p_ref[z, x, span, chunk * LANES : (chunk + 1) * LANES].astype(F32)
                new = lane(source, z * across + x) * p
                u_ref[z, x, pl.ds(start + EDGE, TILE)] = new
                store_edges(
                    z, x, span, new, depth, across, core, ([low_ref], [high_ref], edge_ref)
                )

    tiles(along, tile)


def square_scratch():
    return [pltpu.VMEM((LANES, LANES), F32)] * 2


def first_field(probes, chunk, source):
    depth, across, along, _ = probes.shape
    return pl.pallas_call(
        functools.partial(first_body, chunk),
        in_specs=whole_vmem(2),
        out_specs=whole_vmem(4),
        out_shape=[
            shape_of(depth, across, along + 2 * EDGE, F32),
            shape_of(RADIUS, across, along, BF16),
            shape_of(RADIUS, across, along, BF16),
            shape_of(depth, RADIUS, along, BF16),
        ],
        scratch_shapes=square_scratch(),
        compiler_params=params(),
    )(probes, source)


def local_body(chunk, moment, has_previous, *refs):
    refs = list(refs)
    u_ref, beside_ref, p_ref, c_ref, s_ref = refs[:5]
    prev_ref = refs[5] if has_previous else None
    base_ref, square, turned_c, turned_s = refs[-4:]
    depth, across, along, _ = base_ref.shape
    core = lax.axis_index("sub")
    left_on = (core == 1).astype(F32)
    right_on = (core == 0).astype(F32)
    turned_c[...] = turned(c_ref[...], square)
    turned_s[...] = turned(s_ref[moment], square)

    def tile(start):
        span = pl.ds(start, TILE)
        rows = start + EDGE
        courant = turned_c[span]
        source = turned_s[span]
        for z in range(depth):
            beside = [beside_ref[z, j, span].astype(F32) for j in range(RADIUS)]
            row = [v * left_on for v in beside]
            row += [u_ref[z, x, pl.ds(rows, TILE)] for x in range(across)]
            row += [v * right_on for v in beside]
            for x in range(across):
                here = row[RADIUS + x]
                total = (3.0 * COEFFICIENTS[0]) * here
                for r in range(1, RADIUS + 1):
                    near = row[RADIUS + x + r] + row[RADIUS + x - r]
                    near = near + (
                        u_ref[z, x, pl.ds(rows + r, TILE)] + u_ref[z, x, pl.ds(rows - r, TILE)]
                    )
                    if z + r < depth:
                        near = near + u_ref[z + r, x, pl.ds(rows, TILE)]
                    if z - r >= 0:
                        near = near + u_ref[z - r, x, pl.ds(rows, TILE)]
                    total = total + COEFFICIENTS[r] * near
                cell = z * across + x
                p = p_ref[z, x, span, chunk * LANES : (chunk + 1) * LANES].astype(F32)
                new = 2.0 * here
                if has_previous:
                    new = new - prev_ref[z, x, pl.ds(rows, TILE)]
                new = new + lane(courant, cell) * total + lane(source, cell) * p
                base_ref[z, x, span] = new

    tiles(along, tile)


def local_step(u, beside, probes, chunk, courant, source, moment, previous):
    depth, across, along, _ = probes.shape
    operands = [u, beside, probes, courant, source]
    if previous is not None:
        operands.append(previous)
    return pl.pallas_call(
        functools.partial(local_body, chunk, moment, previous is not None),
        in_specs=whole_vmem(len(operands)),
        out_specs=whole_vmem(1)[0],
        out_shape=shape_of(depth, across, along, F32),
        scratch_shapes=square_scratch() + square_scratch()[:1],
        compiler_params=params(),
    )(*operands)


def rim_body(first, kind, parts, *refs):
    base_ref, below_ref, above_ref, c_ref = refs[:4]
    outs, (square, turned_c) = refs[4:-2], refs[-2:]
    depth, all_across, along, _ = base_ref.shape
    across = below_ref.shape[1]
    core = lax.axis_index("sub")
    turned_c[...] = turned(c_ref[...], square)
    if kind == "middle":
        clear_pads(outs[0])

    def tile(start):
        span = pl.ds(start, TILE)
        courant = turned_c[span]
        for x in range(across):
            place = first + x
            below = [below_ref[j, x, span].astype(F32) for j in range(RADIUS)]
            above = [above_ref[j, x, span].astype(F32) for j in range(RADIUS)]
            news = []
            for z in range(depth):
                added = None
                for r in range(1, RADIUS + 1):
                    if z - r < 0:
                        term = COEFFICIENTS[r] * below[RADIUS + z - r]
                        added = term if added is None else added + term
                    if z + r >= depth:
                        term = COEFFICIENTS[r] * above[z + r - depth]
                        added = term if added is None else added + term
                new = base_ref[z, place, span]
                if added is not None:
                    new = new + lane(courant, z * all_across + place) * added
                news.append(new)
            if kind == "middle":
                for z, new in enumerate(news):
                    outs[0][z, place, pl.ds(start + EDGE, TILE)] = new
                    edges = (outs[1 : 1 + parts], outs[1 + parts : 1 + 2 * parts], outs[-1])
                    store_edges(z, place, span, new, depth, all_across, core, edges)
            elif kind == "half":
                keep_ref, send_ref = outs
                lower = lax.axis_index("probe") == 0
                for z in range(depth // 2):
                    one, two = news[z], news[z + depth // 2]
                    keep_ref[z, x, span] = jnp.where(lower, one, two).astype(BF16)
                    send_ref[z, x, span] = jnp.where(lower, two, one).astype(BF16)
            else:
                for z, new in enumerate(news):
                    outs[0][z, x, span] = new.astype(BF16)

    tiles(along, tile)


def rim_step(base, below, above, courant, kind, first=0, parts=1):
    depth, all_across, along, _ = base.shape
    across = below.shape[1]
    if kind == "middle":
        edge = [shape_of(RADIUS, across // parts, along, BF16)] * parts
        out_shape = [shape_of(depth, across, along + 2 * EDGE, F32)]
        out_shape += edge + edge + [shape_of(depth, RADIUS, along, BF16)]
    elif kind == "half":
        out_shape = [shape_of(depth // 2, across, along, BF16)] * 2
    else:
        out_shape = [shape_of(depth, across, along, BF16)]
    return pl.pallas_call(
        functools.partial(rim_body, first, kind, parts),
        in_specs=whole_vmem(4),
        out_specs=whole_vmem(len(out_shape)),
        out_shape=out_shape,
        scratch_shapes=square_scratch(),
        compiler_params=params(),
    )(base, below, above, courant)


def exchange(lows, highs, edge):
    slabs = lax.axis_size("slab")
    up = [(i, i + 1) for i in range(slabs - 1)]
    down = [(i + 1, i) for i in range(slabs - 1)]
    pairs = []
    for low, high in zip(lows, highs):
        pairs.append((lax.ppermute(high, "slab", up), lax.ppermute(low, "slab", down)))
    return pairs, lax.ppermute(edge, "sub", [(0, 1), (1, 0)])


def gram_body(parts, pieces, *refs):
    ins, (keep_ref, send_ref), panel = refs[: 2 * len(pieces)], refs[-3:-1], refs[-1]
    half = parts // 2
    chip = lax.axis_index("probe")
    core = lax.axis_index("sub")
    depth, _, along, _ = ins[0].shape
    across = panel.shape[0] // (depth * along)
    for (chunk, first), keep, got in zip(pieces, ins[0::2], ins[1::2]):
        mine = pl.multiple_of((chip * half + chunk) * LANES, LANES)
        other = pl.multiple_of(((1 - chip) * half + chunk) * LANES, LANES)
        width = keep.shape[1]
        for z in range(depth):
            rows = pl.ds((z * across + first) * along, width * along)
            panel[rows, pl.ds(mine, LANES)] = keep[z].reshape(width * along, LANES)
            panel[rows, pl.ds(other, LANES)] = got[z].reshape(width * along, LANES)
    size = parts * LANES
    everything = panel[...]

    def columns(which):
        one = panel[:, pl.ds(pl.multiple_of(which * LANES, LANES), LANES)]
        two = panel[:, pl.ds(pl.multiple_of((2 + which) * LANES, LANES), LANES)]
        return lax.dot_general(
            everything,
            jnp.concatenate([one, two], axis=1),
            (((0,), (0,)), ((), ())),
            preferred_element_type=F32,
        )

    rows = lax.broadcasted_iota(jnp.int32, (LANES, LANES), 0)
    cols = lax.broadcasted_iota(jnp.int32, (LANES, LANES), 1)
    eye = rows == cols
    keep = columns(core)
    send = columns(1 - core)
    keep_ref[:size] = keep
    send_ref[:size] = send

    def diagonal(which, first):
        side = which // 2
        a = keep_ref[which * LANES : (which + 1) * LANES, side * LANES : (side + 1) * LANES]
        b = send_ref[which * LANES : (which + 1) * LANES, side * LANES : (side + 1) * LANES]
        block = jnp.where(core == which % 2, a, b)
        return jnp.sum(jnp.where(eye, block, 0.0), axis=0, keepdims=True)

    diag = [diagonal(n, None) for n in range(parts)]
    row0 = jnp.concatenate(diag[:2], axis=1)
    row1 = jnp.concatenate(diag[2:], axis=1)
    tail = jnp.concatenate([row0, row1, jnp.zeros((6, 2 * LANES), F32)], axis=0)
    keep_ref[size:] = tail
    send_ref[size:] = tail


def gram(parts, pieces, fields, cells):
    size = parts * LANES
    shape = jax.ShapeDtypeStruct((size + 8, 2 * LANES), F32)
    return pl.pallas_call(
        functools.partial(gram_body, parts, pieces),
        in_specs=whole_vmem(len(fields)),
        out_specs=whole_vmem(2),
        out_shape=[shape, shape],
        scratch_shapes=[pltpu.VMEM((cells, size), BF16)],
        compiler_params=params(),
    )(*fields)


def rounded(ref, block, tail):
    count = block.shape[0]
    high = tail.astype(BF16)
    low = tail - high.astype(F32)
    ref[:count] = block.astype(BF16)
    ref[count:] = jnp.concatenate([high.astype(F32), low], axis=0).astype(BF16)


def opened(ref):
    count = ref.shape[0] - 16
    tail = ref[count:].astype(F32)
    return ref[:count].astype(F32), tail[:8] + tail[8:]


def rows_body(slabs, count, keep_ref, got_ref, own_ref, *outs):
    slab = lax.axis_index("slab")
    size = slabs * count
    tail = keep_ref[pl.ds(size, 8)] + got_ref[pl.ds(size, 8)]
    for d in range(slabs):
        owner = lax.rem(slab + d, slabs)
        span = pl.ds(pl.multiple_of(owner * count, count), count)
        block = keep_ref[span] + got_ref[span]
        if d == 0:
            own_ref[:count] = block
            own_ref[count:] = tail
        else:
            rounded(outs[d - 1], block, tail)


def split_rows(keep, got, slabs):
    count = (keep.shape[0] - 8) // slabs
    own = jax.ShapeDtypeStruct((count + 8, keep.shape[1]), F32)
    sent = jax.ShapeDtypeStruct((count + 16, keep.shape[1]), BF16)
    return pl.pallas_call(
        functools.partial(rows_body, slabs, count),
        in_specs=whole_vmem(2),
        out_specs=whole_vmem(slabs),
        out_shape=[own] + [sent] * (slabs - 1),
        compiler_params=params(),
    )(keep, got)


def sum_body(own_ref, *refs):
    count = own_ref.shape[0] - 8
    block, tail = own_ref[:count], own_ref[count:]
    for ref in refs[:-1]:
        more, more_tail = opened(ref)
        block, tail = block + more, tail + more_tail
    rounded(refs[-1], block, tail)


def sum_all(own, others):
    return pl.pallas_call(
        sum_body,
        in_specs=whole_vmem(1 + len(others)),
        out_specs=whole_vmem(1)[0],
        out_shape=jax.ShapeDtypeStruct(others[0].shape, BF16),
        compiler_params=params(),
    )(own, *others)


def finish_body(cell_count, a_ref, b_ref, c_ref, d_ref, out_ref, norms_ref):
    slab = lax.axis_index("slab")
    core = lax.axis_index("sub")
    count = out_ref.shape[0]
    near, tail = opened(a_ref)
    far, _ = opened(c_ref)
    more, more_tail = opened(b_ref)
    near = near + more
    far = far + opened(d_ref)[0]
    norms = jnp.sqrt((tail + more_tail)[:2] / cell_count + EPSILON)
    blocks = [norms[n // 2 : n // 2 + 1, (n % 2) * LANES : (n % 2 + 1) * LANES] for n in range(4)]
    own = blocks[0]
    for n in range(1, 4):
        own = jnp.where(slab == n, blocks[n], own)
    norms_ref[...] = own
    rows = lax.broadcasted_iota(jnp.int32, (LANES, LANES), 0)
    cols = lax.broadcasted_iota(jnp.int32, (LANES, LANES), 1)
    eye = rows == cols
    own_column = jnp.sum(
        jnp.where(eye, jnp.broadcast_to(own, (LANES, LANES)), 0.0), axis=1, keepdims=True
    )
    for side in range(2):
        for block, which in ((near, core), (far, 1 - core)):
            index = 2 * side + which
            others = jnp.where(which == 0, blocks[2 * side], blocks[2 * side + 1])
            value = block[:count, side * LANES : (side + 1) * LANES]
            value = value / math.sqrt(cell_count) / (own_column * others)
            value = jnp.where(eye & (index == slab), 0.0, value)
            out_ref[:, pl.ds(pl.multiple_of(index * LANES, LANES), LANES)] = value


def finish(pieces, cell_count):
    count = pieces[0].shape[0] - 16
    return pl.pallas_call(
        functools.partial(finish_body, cell_count),
        in_specs=whole_vmem(4),
        out_specs=whole_vmem(2),
        out_shape=[
            jax.ShapeDtypeStruct((count, 4 * LANES), F32),
            jax.ShapeDtypeStruct((1, LANES), F32),
        ],
        compiler_params=params(),
    )(*pieces)


def coupled(pieces, fields, cells, cell_count):
    slabs = 4
    keep, send = gram(4, pieces, fields, cells)
    got = lax.ppermute(send, "sub", [(0, 1), (1, 0)])
    own, *sent = split_rows(keep, got, slabs)
    arrived = [
        lax.ppermute(block, "slab", [(i, (i + d) % slabs) for i in range(slabs)])
        for d, block in enumerate(sent, 1)
    ]
    mine = sum_all(own, arrived)
    both = ("probe", "sub")
    others = [
        lax.ppermute(mine, both, [(i, i ^ flip) for i in range(4)]) for flip in (2, 1, 3)
    ]
    coupling, norms = finish([mine] + others, cell_count)
    return coupling, norms.reshape(-1)


def coupled_general(fields, cell_count):
    chips = lax.axis_size("probe")
    sketch = jnp.concatenate(fields, axis=-1)
    sketch = sketch.reshape(-1, sketch.shape[-1])
    if chips > 1:
        sketch = lax.all_to_all(sketch, "probe", split_axis=0, concat_axis=1, tiled=True)
    partial_gram = lax.dot_general(
        sketch, sketch, (((0,), (0,)), ((), ())), preferred_element_type=F32
    )
    rows = lax.psum_scatter(partial_gram, "slab", scatter_dimension=0, tiled=True)
    rows = lax.psum(rows, ("probe", "sub"))
    count = rows.shape[0]
    start = lax.axis_index("slab") * count
    own = jnp.diagonal(lax.dynamic_slice_in_dim(rows, start, count, 1))
    own_norms = jnp.sqrt(own / cell_count + EPSILON)
    norms = lax.all_gather(own_norms, "slab", axis=0, tiled=True)
    coupling = rows / math.sqrt(cell_count) / (own_norms[:, None] * norms[None, :])
    row_ids = start + lax.broadcasted_iota(jnp.int32, coupling.shape, 0)
    col_ids = lax.broadcasted_iota(jnp.int32, coupling.shape, 1)
    return jnp.where(row_ids == col_ids, 0.0, coupling), own_norms


def shards(probes, courant, source):
    depth, across, along, count = probes.shape
    chunks = count // LANES
    slabs, chips = lax.axis_size("slab"), lax.axis_size("probe")
    cell_count = depth * across * along * slabs * lax.axis_size("sub")
    paired = chips == 2 and slabs == 4 and chunks == 2
    steps = source.shape[0]
    courant = courant.reshape(depth * across, along)
    source = source.reshape(steps, depth * across, along)

    now, previous, halos = [], [None] * chunks, []
    for c in range(chunks):
        u, low, high, edge = first_field(probes, c, source)
        now.append(u)
        halos.append(exchange([low], [high], edge))
    pieces, fields = [], []
    for n in range(1, steps):
        for c in range(chunks):
            pairs, beside = halos[c]
            base = local_step(now[c], beside, probes, c, courant, source, n, previous[c])
            if n == steps - 1:
                width = across // len(pairs)
                for h, (below, above) in enumerate(pairs):
                    kind = "half" if paired else "all"
                    out = rim_step(base, below, above, courant, kind, h * width)
                    if paired:
                        pieces.append((c, h * width))
                        fields += [out[0], lax.ppermute(out[1], "probe", [(0, 1), (1, 0)])]
                    else:
                        fields.append(out[0])
            else:
                parts = 2 if paired and n == steps - 2 and c == chunks - 1 else 1
                ((below, above),) = pairs
                out = rim_step(base, below, above, courant, "middle", parts=parts)
                previous[c], now[c] = now[c], out[0]
                halos[c] = exchange(out[1 : 1 + parts], out[1 + parts : 1 + 2 * parts], out[-1])
    if paired:
        cells = depth // 2 * across * along
        return coupled(tuple(pieces), fields, cells, cell_count)
    return coupled_general(fields, cell_count)


def solution(mesh):
    placed = (
        P(("groups", "slab"), "sub", None, "probe"),
        P("slab", "sub", None),
        P(None, ("groups", "slab"), "sub", None),
    )
    return jax.shard_map(
        shards,
        mesh=mesh,
        in_specs=placed,
        out_specs=(P(("groups", "slab"), None), P(("groups", "slab"))),
        check_vma=False,
    )
```

```python
import functools
import math

import jax
import jax.numpy as jnp
from jax import lax
from jax.experimental import pallas as pl
from jax.experimental.pallas import tpu as pltpu
from jax.sharding import PartitionSpec as P

COEFFICIENTS = (-205.0 / 72.0, 8.0 / 5.0, -1.0 / 5.0, 8.0 / 315.0, -1.0 / 560.0)
EPSILON = 1e-06
LANES = 128
RADIUS = 4
EDGE = 8
TILE = 16
F32 = jnp.float32
BF16 = jnp.bfloat16
VMEM_LIMIT = 32 * 1024 * 1024


def params(*semantics):
    return pltpu.CompilerParams(
        dimension_semantics=semantics or None, vmem_limit_bytes=VMEM_LIMIT
    )


def whole_vmem(count):
    return [pl.BlockSpec(memory_space=pltpu.VMEM)] * count


def shape_of(depth, across, along, dtype):
    return jax.ShapeDtypeStruct((depth, across, along, LANES), dtype)


def turned(field, scratch):
    rows, along = field.shape
    scratch[:rows, :along] = field
    return jnp.transpose(scratch[...])


def lane(values, n):
    return jnp.broadcast_to(values[:, n : n + 1], (values.shape[0], LANES))


def store_edges(x, span, news, even, refs):
    even_refs, odd_refs = refs
    width = even_refs[0].shape[1]
    part, x = x // width, x % width
    for j in range(RADIUS):
        low = news[j].astype(BF16)
        high = news[len(news) - RADIUS + j].astype(BF16)
        even_refs[part][j, x, span] = jnp.where(even, high, low)
        odd_refs[part][j, x, span] = jnp.where(even, low, high)


def store_beside(span, rows, core, u_ref, edge_ref):
    depth, across, _, _ = u_ref.shape
    first = (across - RADIUS) * (1 - core)
    for z in range(depth):
        for j in range(RADIUS):
            edge_ref[z, j, span] = u_ref[z, first + j, rows].astype(BF16)


def slab_is_even():
    return lax.rem(lax.axis_index("slab"), 2) == 0


def clear_pads(u_ref):
    depth, across, padded, _ = u_ref.shape

    def plane(z, _):
        blank = jnp.zeros((across, EDGE, LANES), F32)
        u_ref[z, :, pl.ds(0, EDGE)] = blank
        u_ref[z, :, pl.ds(padded - EDGE, EDGE)] = blank
        return 0

    lax.fori_loop(0, depth, plane, 0)


def tiles(along, body):
    def one(t, _):
        body(pl.multiple_of(t * TILE, TILE))
        return 0

    lax.fori_loop(0, along // TILE, one, 0)


def first_body(chunk, p_ref, s_ref, u_ref, even_ref, odd_ref, edge_ref, square, turned_s):
    depth, across, padded, _ = u_ref.shape
    along = padded - 2 * EDGE
    core = lax.axis_index("sub")
    even = slab_is_even()
    turned_s[...] = turned(s_ref[0], square)
    clear_pads(u_ref)

    def tile(start):
        span = pl.ds(start, TILE)
        rows = pl.ds(start + EDGE, TILE)
        source = turned_s[span]
        for x in range(across):
            news = []
            for z in range(depth):
                p = p_ref[z, x, span, chunk * LANES : (chunk + 1) * LANES].astype(F32)
                new = lane(source, z * across + x) * p
                u_ref[z, x, rows] = new
                news.append(new)
            store_edges(x, span, news, even, ([even_ref], [odd_ref]))
        store_beside(span, rows, core, u_ref, edge_ref)

    tiles(along, tile)


def square_scratch():
    return [pltpu.VMEM((LANES, LANES), F32)] * 2


def first_field(probes, chunk, source):
    depth, across, along, _ = probes.shape
    return pl.pallas_call(
        functools.partial(first_body, chunk),
        in_specs=whole_vmem(2),
        out_specs=whole_vmem(4),
        out_shape=[
            shape_of(depth, across, along + 2 * EDGE, F32),
            shape_of(RADIUS, across, along, BF16),
            shape_of(RADIUS, across, along, BF16),
            shape_of(depth, RADIUS, along, BF16),
        ],
        scratch_shapes=square_scratch(),
        compiler_params=params(),
    )(probes, source)


def local_body(chunk, moment, has_previous, *refs):
    refs = list(refs)
    u_ref, beside_ref, p_ref, c_ref, s_ref = refs[:5]
    prev_ref = refs[5] if has_previous else None
    base_ref, square, turned_c, turned_s = refs[-4:]
    depth, across, along, _ = base_ref.shape
    core = lax.axis_index("sub")
    left_on = (core == 1).astype(F32)
    right_on = (core == 0).astype(F32)
    turned_c[...] = turned(c_ref[...], square)
    turned_s[...] = turned(s_ref[moment], square)

    def tile(start):
        span = pl.ds(start, TILE)
        rows = start + EDGE
        courant = turned_c[span]
        source = turned_s[span]
        for z in range(depth):
            beside = [beside_ref[z, j, span].astype(F32) for j in range(RADIUS)]
            row = [v * left_on for v in beside]
            row += [u_ref[z, x, pl.ds(rows, TILE)] for x in range(across)]
            row += [v * right_on for v in beside]
            for x in range(across):
                here = row[RADIUS + x]
                total = (3.0 * COEFFICIENTS[0]) * here
                for r in range(1, RADIUS + 1):
                    near = row[RADIUS + x + r] + row[RADIUS + x - r]
                    near = near + (
                        u_ref[z, x, pl.ds(rows + r, TILE)] + u_ref[z, x, pl.ds(rows - r, TILE)]
                    )
                    if z + r < depth:
                        near = near + u_ref[z + r, x, pl.ds(rows, TILE)]
                    if z - r >= 0:
                        near = near + u_ref[z - r, x, pl.ds(rows, TILE)]
                    total = total + COEFFICIENTS[r] * near
                cell = z * across + x
                p = p_ref[z, x, span, chunk * LANES : (chunk + 1) * LANES].astype(F32)
                new = 2.0 * here
                if has_previous:
                    new = new - prev_ref[z, x, pl.ds(rows, TILE)]
                new = new + lane(courant, cell) * total + lane(source, cell) * p
                base_ref[z, x, span] = new

    tiles(along, tile)


def local_step(u, beside, probes, chunk, courant, source, moment, previous):
    depth, across, along, _ = probes.shape
    operands = [u, beside, probes, courant, source]
    if previous is not None:
        operands.append(previous)
    return pl.pallas_call(
        functools.partial(local_body, chunk, moment, previous is not None),
        in_specs=whole_vmem(len(operands)),
        out_specs=whole_vmem(1)[0],
        out_shape=shape_of(depth, across, along, F32),
        scratch_shapes=square_scratch() + square_scratch()[:1],
        compiler_params=params(),
    )(*operands)


def rim_body(first, kind, parts, *refs):
    base_ref, even_ref, odd_ref, c_ref = refs[:4]
    outs, (square, turned_c) = refs[4:-2], refs[-2:]
    depth, all_across, along, _ = base_ref.shape
    across = even_ref.shape[1]
    core = lax.axis_index("sub")
    even = slab_is_even()
    turned_c[...] = turned(c_ref[...], square)
    if kind == "middle":
        clear_pads(outs[0])

    def tile(start):
        span = pl.ds(start, TILE)
        rows = pl.ds(start + EDGE, TILE)
        courant = turned_c[span]
        for x in range(across):
            place = first + x
            below, above = [], []
            for j in range(RADIUS):
                one, two = even_ref[j, x, span], odd_ref[j, x, span]
                below.append(jnp.where(even, two, one).astype(F32))
                above.append(jnp.where(even, one, two).astype(F32))
            news = []
            for z in range(depth):
                added = None
                for r in range(1, RADIUS + 1):
                    if z - r < 0:
                        term = COEFFICIENTS[r] * below[RADIUS + z - r]
                        added = term if added is None else added + term
                    if z + r >= depth:
                        term = COEFFICIENTS[r] * above[z + r - depth]
                        added = term if added is None else added + term
                new = base_ref[z, place, span]
                if added is not None:
                    new = new + lane(courant, z * all_across + place) * added
                news.append(new)
            if kind == "middle":
                for z, new in enumerate(news):
                    outs[0][z, place, rows] = new
                edges = (outs[1 : 1 + parts], outs[1 + parts : 1 + 2 * parts])
                store_edges(place, span, news, even, edges)
            elif kind == "half":
                keep_ref, send_ref = outs
                lower = lax.axis_index("probe") == 0
                for z in range(depth // 2):
                    one, two = news[z].astype(BF16), news[z + depth // 2].astype(BF16)
                    keep_ref[z, x, span] = jnp.where(lower, one, two)
                    send_ref[z, x, span] = jnp.where(lower, two, one)
            else:
                for z, new in enumerate(news):
                    outs[0][z, x, span] = new.astype(BF16)
        if kind == "middle":
            store_beside(span, rows, core, outs[0], outs[-1])

    tiles(along, tile)


def rim_step(base, evens, odds, courant, kind, first=0, parts=1):
    depth, all_across, along, _ = base.shape
    across = evens.shape[1]
    if kind == "middle":
        edge = [shape_of(RADIUS, across // parts, along, BF16)] * parts
        out_shape = [shape_of(depth, across, along + 2 * EDGE, F32)]
        out_shape += edge + edge + [shape_of(depth, RADIUS, along, BF16)]
    elif kind == "half":
        out_shape = [shape_of(depth // 2, across, along, BF16)] * 2
    else:
        out_shape = [shape_of(depth, across, along, BF16)]
    return pl.pallas_call(
        functools.partial(rim_body, first, kind, parts),
        in_specs=whole_vmem(4),
        out_specs=whole_vmem(len(out_shape)),
        out_shape=out_shape,
        scratch_shapes=square_scratch(),
        compiler_params=params(),
    )(base, evens, odds, courant)


def swap(x, axis, pairs):
    return lax.ppermute(x, axis, [p for a, b in pairs for p in ((a, b), (b, a))])


def exchange(evens, odds, edge):
    slabs = lax.axis_size("slab")
    pairs = []
    for one, two in zip(evens, odds):
        pairs.append(
            (
                swap(one, "slab", [(i, i + 1) for i in range(0, slabs - 1, 2)]),
                swap(two, "slab", [(i, i + 1) for i in range(1, slabs - 1, 2)]),
            )
        )
    return pairs, swap(edge, "sub", [(0, 1)])


def gram_body(parts, pieces, *refs):
    ins, (keep_ref, send_ref), panel = refs[: 2 * len(pieces)], refs[-3:-1], refs[-1]
    half = parts // 2
    chip = lax.axis_index("probe")
    core = lax.axis_index("sub")
    depth, _, along, _ = ins[0].shape
    across = panel.shape[0] // (depth * along)
    for (chunk, first), keep, got in zip(pieces, ins[0::2], ins[1::2]):
        mine = pl.multiple_of((chip * half + chunk) * LANES, LANES)
        other = pl.multiple_of(((1 - chip) * half + chunk) * LANES, LANES)
        width = keep.shape[1]
        for z in range(depth):
            rows = pl.ds((z * across + first) * along, width * along)
            panel[rows, pl.ds(mine, LANES)] = keep[z].reshape(width * along, LANES)
            panel[rows, pl.ds(other, LANES)] = got[z].reshape(width * along, LANES)
    size = parts * LANES
    everything = panel[...]

    def columns(which):
        one = panel[:, pl.ds(pl.multiple_of(which * LANES, LANES), LANES)]
        two = panel[:, pl.ds(pl.multiple_of((2 + which) * LANES, LANES), LANES)]
        return lax.dot_general(
            everything,
            jnp.concatenate([one, two], axis=1),
            (((0,), (0,)), ((), ())),
            preferred_element_type=F32,
        )

    rows = lax.broadcasted_iota(jnp.int32, (LANES, LANES), 0)
    cols = lax.broadcasted_iota(jnp.int32, (LANES, LANES), 1)
    eye = rows == cols
    keep = columns(core)
    send = columns(1 - core)
    keep_ref[:size] = keep
    send_ref[:size] = send

    def diagonal(which, first):
        side = which // 2
        a = keep_ref[which * LANES : (which + 1) * LANES, side * LANES : (side + 1) * LANES]
        b = send_ref[which * LANES : (which + 1) * LANES, side * LANES : (side + 1) * LANES]
        block = jnp.where(core == which % 2, a, b)
        return jnp.sum(jnp.where(eye, block, 0.0), axis=0, keepdims=True)

    diag = [diagonal(n, None) for n in range(parts)]
    row0 = jnp.concatenate(diag[:2], axis=1)
    row1 = jnp.concatenate(diag[2:], axis=1)
    tail = jnp.concatenate([row0, row1, jnp.zeros((6, 2 * LANES), F32)], axis=0)
    keep_ref[size:] = tail
    send_ref[size:] = tail


def gram(parts, pieces, fields, cells):
    size = parts * LANES
    shape = jax.ShapeDtypeStruct((size + 8, 2 * LANES), F32)
    return pl.pallas_call(
        functools.partial(gram_body, parts, pieces),
        in_specs=whole_vmem(len(fields)),
        out_specs=whole_vmem(2),
        out_shape=[shape, shape],
        scratch_shapes=[pltpu.VMEM((cells, size), BF16)],
        compiler_params=params(),
    )(*fields)


def rounded(ref, block, tail):
    count = block.shape[0]
    high = tail.astype(BF16)
    low = tail - high.astype(F32)
    ref[:count] = block.astype(BF16)
    ref[count:] = jnp.concatenate([high.astype(F32), low], axis=0).astype(BF16)


def opened(ref):
    count = ref.shape[0] - 16
    tail = ref[count:].astype(F32)
    return ref[:count].astype(F32), tail[:8] + tail[8:]


def rows_body(slabs, count, keep_ref, got_ref, own_ref, *outs):
    slab = lax.axis_index("slab")
    size = slabs * count
    tail = keep_ref[pl.ds(size, 8)] + got_ref[pl.ds(size, 8)]
    for d in range(slabs):
        owner = slab ^ d
        span = pl.ds(pl.multiple_of(owner * count, count), count)
        block = keep_ref[span] + got_ref[span]
        if d == 0:
            own_ref[:count] = block
            own_ref[count:] = tail
        else:
            rounded(outs[d - 1], block, tail)


def split_rows(keep, got, slabs):
    count = (keep.shape[0] - 8) // slabs
    own = jax.ShapeDtypeStruct((count + 8, keep.shape[1]), F32)
    sent = jax.ShapeDtypeStruct((count + 16, keep.shape[1]), BF16)
    return pl.pallas_call(
        functools.partial(rows_body, slabs, count),
        in_specs=whole_vmem(2),
        out_specs=whole_vmem(slabs),
        out_shape=[own] + [sent] * (slabs - 1),
        compiler_params=params(),
    )(keep, got)


def sum_body(own_ref, *refs):
    count = own_ref.shape[0] - 8
    block, tail = own_ref[:count], own_ref[count:]
    for ref in refs[:-1]:
        more, more_tail = opened(ref)
        block, tail = block + more, tail + more_tail
    rounded(refs[-1], block, tail)


def sum_all(own, others):
    return pl.pallas_call(
        sum_body,
        in_specs=whole_vmem(1 + len(others)),
        out_specs=whole_vmem(1)[0],
        out_shape=jax.ShapeDtypeStruct(others[0].shape, BF16),
        compiler_params=params(),
    )(own, *others)


def finish_body(cell_count, a_ref, b_ref, c_ref, d_ref, out_ref, norms_ref):
    slab = lax.axis_index("slab")
    core = lax.axis_index("sub")
    count = out_ref.shape[0]
    near, tail = opened(a_ref)
    far, _ = opened(c_ref)
    more, more_tail = opened(b_ref)
    near = near + more
    far = far + opened(d_ref)[0]
    norms = jnp.sqrt((tail + more_tail)[:2] / cell_count + EPSILON)
    blocks = [norms[n // 2 : n // 2 + 1, (n % 2) * LANES : (n % 2 + 1) * LANES] for n in range(4)]
    own = blocks[0]
    for n in range(1, 4):
        own = jnp.where(slab == n, blocks[n], own)
    norms_ref[...] = own
    rows = lax.broadcasted_iota(jnp.int32, (LANES, LANES), 0)
    cols = lax.broadcasted_iota(jnp.int32, (LANES, LANES), 1)
    eye = rows == cols
    own_column = jnp.sum(
        jnp.where(eye, jnp.broadcast_to(own, (LANES, LANES)), 0.0), axis=1, keepdims=True
    )
    for side in range(2):
        for block, which in ((near, core), (far, 1 - core)):
            index = 2 * side + which
            others = jnp.where(which == 0, blocks[2 * side], blocks[2 * side + 1])
            value = block[:count, side * LANES : (side + 1) * LANES]
            value = value / math.sqrt(cell_count) / (own_column * others)
            value = jnp.where(eye & (index == slab), 0.0, value)
            out_ref[:, pl.ds(pl.multiple_of(index * LANES, LANES), LANES)] = value


def finish(pieces, cell_count):
    count = pieces[0].shape[0] - 16
    return pl.pallas_call(
        functools.partial(finish_body, cell_count),
        in_specs=whole_vmem(4),
        out_specs=whole_vmem(2),
        out_shape=[
            jax.ShapeDtypeStruct((count, 4 * LANES), F32),
            jax.ShapeDtypeStruct((1, LANES), F32),
        ],
        compiler_params=params(),
    )(*pieces)


def coupled(pieces, fields, cells, cell_count):
    slabs = 4
    keep, send = gram(4, pieces, fields, cells)
    got = swap(send, "sub", [(0, 1)])
    own, *sent = split_rows(keep, got, slabs)
    arrived = [
        lax.ppermute(block, "slab", [(i, i ^ d) for i in range(slabs)])
        for d, block in enumerate(sent, 1)
    ]
    mine = sum_all(own, arrived)
    both = ("probe", "sub")
    others = [
        lax.ppermute(mine, both, [(i, i ^ flip) for i in range(4)]) for flip in (2, 1, 3)
    ]
    coupling, norms = finish([mine] + others, cell_count)
    return coupling, norms.reshape(-1)


def coupled_general(fields, cell_count):
    chips = lax.axis_size("probe")
    sketch = jnp.concatenate(fields, axis=-1)
    sketch = sketch.reshape(-1, sketch.shape[-1])
    if chips > 1:
        sketch = lax.all_to_all(sketch, "probe", split_axis=0, concat_axis=1, tiled=True)
    partial_gram = lax.dot_general(
        sketch, sketch, (((0,), (0,)), ((), ())), preferred_element_type=F32
    )
    rows = lax.psum_scatter(partial_gram, "slab", scatter_dimension=0, tiled=True)
    rows = lax.psum(rows, ("probe", "sub"))
    count = rows.shape[0]
    start = lax.axis_index("slab") * count
    own = jnp.diagonal(lax.dynamic_slice_in_dim(rows, start, count, 1))
    own_norms = jnp.sqrt(own / cell_count + EPSILON)
    norms = lax.all_gather(own_norms, "slab", axis=0, tiled=True)
    coupling = rows / math.sqrt(cell_count) / (own_norms[:, None] * norms[None, :])
    row_ids = start + lax.broadcasted_iota(jnp.int32, coupling.shape, 0)
    col_ids = lax.broadcasted_iota(jnp.int32, coupling.shape, 1)
    return jnp.where(row_ids == col_ids, 0.0, coupling), own_norms


def shards(probes, courant, source):
    depth, across, along, count = probes.shape
    chunks = count // LANES
    slabs, chips = lax.axis_size("slab"), lax.axis_size("probe")
    cell_count = depth * across * along * slabs * lax.axis_size("sub")
    paired = chips == 2 and slabs == 4 and chunks == 2
    steps = source.shape[0]
    courant = courant.reshape(depth * across, along)
    source = source.reshape(steps, depth * across, along)

    now, previous, halos = [], [None] * chunks, []
    for c in range(chunks):
        u, one, two, edge = first_field(probes, c, source)
        now.append(u)
        halos.append(exchange([one], [two], edge))
    pieces, fields = [], []
    for n in range(1, steps):
        for c in range(chunks):
            pairs, beside = halos[c]
            base = local_step(now[c], beside, probes, c, courant, source, n, previous[c])
            if n == steps - 1:
                width = across // len(pairs)
                for h, (one, two) in enumerate(pairs):
                    kind = "half" if paired else "all"
                    out = rim_step(base, one, two, courant, kind, h * width)
                    if paired:
                        pieces.append((c, h * width))
                        fields += [out[0], swap(out[1], "probe", [(0, 1)])]
                    else:
                        fields.append(out[0])
            else:
                parts = 2 if paired and n == steps - 2 else 1
                ((one, two),) = pairs
                out = rim_step(base, one, two, courant, "middle", parts=parts)
                previous[c], now[c] = now[c], out[0]
                halos[c] = exchange(out[1 : 1 + parts], out[1 + parts : 1 + 2 * parts], out[-1])
    if paired:
        cells = depth // 2 * across * along
        return coupled(tuple(pieces), fields, cells, cell_count)
    return coupled_general(fields, cell_count)


def solution(mesh):
    placed = (
        P(("groups", "slab"), "sub", None, "probe"),
        P("slab", "sub", None),
        P(None, ("groups", "slab"), "sub", None),
    )
    return jax.shard_map(
        shards,
        mesh=mesh,
        in_specs=placed,
        out_specs=(P(("groups", "slab"), None), P(("groups", "slab"))),
        check_vma=False,
    )
```

```python
import functools
import math

import jax
import jax.numpy as jnp
from jax import lax
from jax.experimental import pallas as pl
from jax.experimental.pallas import tpu as pltpu
from jax.sharding import PartitionSpec as P

COEFFICIENTS = (-205.0 / 72.0, 8.0 / 5.0, -1.0 / 5.0, 8.0 / 315.0, -1.0 / 560.0)
EPSILON = 1e-06
LANES = 128
RADIUS = 4
EDGE = 8
TILE = 16
F32 = jnp.float32
BF16 = jnp.bfloat16
VMEM_LIMIT = 32 * 1024 * 1024


def params(*semantics):
    return pltpu.CompilerParams(
        dimension_semantics=semantics or None, vmem_limit_bytes=VMEM_LIMIT
    )


def whole_vmem(count):
    return [pl.BlockSpec(memory_space=pltpu.VMEM)] * count


def shape_of(depth, across, along, dtype):
    return jax.ShapeDtypeStruct((depth, across, along, LANES), dtype)


def turned(field, scratch):
    rows, along = field.shape
    scratch[:rows, :along] = field
    return jnp.transpose(scratch[...])


def lane(values, n):
    return jnp.broadcast_to(values[:, n : n + 1], (values.shape[0], LANES))


def store_edges(x, span, news, even, refs):
    even_refs, odd_refs = refs
    width = even_refs[0].shape[1]
    part, x = x // width, x % width
    for j in range(RADIUS):
        low = news[j].astype(BF16)
        high = news[len(news) - RADIUS + j].astype(BF16)
        even_refs[part][j, x, span] = jnp.where(even, high, low)
        odd_refs[part][j, x, span] = jnp.where(even, low, high)


def store_beside(span, rows, core, u_ref, edge_ref):
    depth, across, _, _ = u_ref.shape
    first = (across - RADIUS) * (1 - core)
    for z in range(depth):
        for j in range(RADIUS):
            edge_ref[z, j, span] = u_ref[z, first + j, rows].astype(BF16)


def slab_is_even():
    return lax.rem(lax.axis_index("slab"), 2) == 0


def clear_pads(u_ref):
    depth, across, padded, _ = u_ref.shape

    def plane(z, _):
        blank = jnp.zeros((across, EDGE, LANES), F32)
        u_ref[z, :, pl.ds(0, EDGE)] = blank
        u_ref[z, :, pl.ds(padded - EDGE, EDGE)] = blank
        return 0

    lax.fori_loop(0, depth, plane, 0)


def tiles(along, body):
    def one(t, _):
        body(pl.multiple_of(t * TILE, TILE))
        return 0

    lax.fori_loop(0, along // TILE, one, 0)


def first_body(chunk, p_ref, s_ref, u_ref, even_ref, odd_ref, edge_ref, square, turned_s):
    depth, across, padded, _ = u_ref.shape
    along = padded - 2 * EDGE
    core = lax.axis_index("sub")
    even = slab_is_even()
    turned_s[...] = turned(s_ref[0], square)
    clear_pads(u_ref)

    def tile(start):
        span = pl.ds(start, TILE)
        rows = pl.ds(start + EDGE, TILE)
        source = turned_s[span]
        for x in range(across):
            news = []
            for z in range(depth):
                p = p_ref[z, x, span, chunk * LANES : (chunk + 1) * LANES].astype(F32)
                new = lane(source, z * across + x) * p
                u_ref[z, x, rows] = new
                news.append(new)
            store_edges(x, span, news, even, ([even_ref], [odd_ref]))
        store_beside(span, rows, core, u_ref, edge_ref)

    tiles(along, tile)


def square_scratch():
    return [pltpu.VMEM((LANES, LANES), F32)] * 2


def first_field(probes, chunk, source):
    depth, across, along, _ = probes.shape
    return pl.pallas_call(
        functools.partial(first_body, chunk),
        in_specs=whole_vmem(2),
        out_specs=whole_vmem(4),
        out_shape=[
            shape_of(depth, across, along + 2 * EDGE, F32),
            shape_of(RADIUS, across, along, BF16),
            shape_of(RADIUS, across, along, BF16),
            shape_of(depth, RADIUS, along, BF16),
        ],
        scratch_shapes=square_scratch(),
        compiler_params=params(),
    )(probes, source)


def local_body(chunk, moment, has_previous, *refs):
    refs = list(refs)
    u_ref, beside_ref, p_ref, c_ref, s_ref = refs[:5]
    prev_ref = refs[5] if has_previous else None
    base_ref, square, turned_c, turned_s = refs[-4:]
    depth, across, along, _ = base_ref.shape
    core = lax.axis_index("sub")
    left_on = (core == 1).astype(F32)
    right_on = (core == 0).astype(F32)
    turned_c[...] = turned(c_ref[...], square)
    turned_s[...] = turned(s_ref[moment], square)

    def tile(start):
        span = pl.ds(start, TILE)
        rows = start + EDGE
        courant = turned_c[span]
        source = turned_s[span]
        for z in range(depth):
            beside = [beside_ref[z, j, span].astype(F32) for j in range(RADIUS)]
            row = [v * left_on for v in beside]
            row += [u_ref[z, x, pl.ds(rows, TILE)] for x in range(across)]
            row += [v * right_on for v in beside]
            for x in range(across):
                here = row[RADIUS + x]
                total = (3.0 * COEFFICIENTS[0]) * here
                for r in range(1, RADIUS + 1):
                    near = row[RADIUS + x + r] + row[RADIUS + x - r]
                    near = near + (
                        u_ref[z, x, pl.ds(rows + r, TILE)] + u_ref[z, x, pl.ds(rows - r, TILE)]
                    )
                    if z + r < depth:
                        near = near + u_ref[z + r, x, pl.ds(rows, TILE)]
                    if z - r >= 0:
                        near = near + u_ref[z - r, x, pl.ds(rows, TILE)]
                    total = total + COEFFICIENTS[r] * near
                cell = z * across + x
                p = p_ref[z, x, span, chunk * LANES : (chunk + 1) * LANES].astype(F32)
                new = 2.0 * here
                if has_previous:
                    new = new - prev_ref[z, x, pl.ds(rows, TILE)]
                new = new + lane(courant, cell) * total + lane(source, cell) * p
                base_ref[z, x, span] = new

    tiles(along, tile)


def local_step(u, beside, probes, chunk, courant, source, moment, previous):
    depth, across, along, _ = probes.shape
    operands = [u, beside, probes, courant, source]
    if previous is not None:
        operands.append(previous)
    return pl.pallas_call(
        functools.partial(local_body, chunk, moment, previous is not None),
        in_specs=whole_vmem(len(operands)),
        out_specs=whole_vmem(1)[0],
        out_shape=shape_of(depth, across, along, F32),
        scratch_shapes=square_scratch() + square_scratch()[:1],
        compiler_params=params(),
    )(*operands)


def rim_body(first, kind, parts, *refs):
    base_ref, even_ref, odd_ref, c_ref = refs[:4]
    outs, (square, turned_c) = refs[4:-2], refs[-2:]
    depth, all_across, along, _ = base_ref.shape
    across = even_ref.shape[1]
    core = lax.axis_index("sub")
    even = slab_is_even()
    turned_c[...] = turned(c_ref[...], square)
    if kind == "middle":
        clear_pads(outs[0])

    def tile(start):
        span = pl.ds(start, TILE)
        rows = pl.ds(start + EDGE, TILE)
        courant = turned_c[span]
        for x in range(across):
            place = first + x
            below, above = [], []
            for j in range(RADIUS):
                one, two = even_ref[j, x, span], odd_ref[j, x, span]
                below.append(jnp.where(even, two, one).astype(F32))
                above.append(jnp.where(even, one, two).astype(F32))
            news = []
            for z in range(depth):
                added = None
                for r in range(1, RADIUS + 1):
                    if z - r < 0:
                        term = COEFFICIENTS[r] * below[RADIUS + z - r]
                        added = term if added is None else added + term
                    if z + r >= depth:
                        term = COEFFICIENTS[r] * above[z + r - depth]
                        added = term if added is None else added + term
                new = base_ref[z, place, span]
                if added is not None:
                    new = new + lane(courant, z * all_across + place) * added
                news.append(new)
            if kind == "middle":
                for z, new in enumerate(news):
                    outs[0][z, place, rows] = new
                edges = (outs[1 : 1 + parts], outs[1 + parts : 1 + 2 * parts])
                store_edges(place, span, news, even, edges)
            elif kind == "half":
                keep_ref, send_ref = outs
                lower = lax.axis_index("probe") == 0
                for z in range(depth // 2):
                    one, two = news[z].astype(BF16), news[z + depth // 2].astype(BF16)
                    keep_ref[z, x, span] = jnp.where(lower, one, two)
                    send_ref[z, x, span] = jnp.where(lower, two, one)
            else:
                for z, new in enumerate(news):
                    outs[0][z, x, span] = new.astype(BF16)
        if kind == "middle":
            store_beside(span, rows, core, outs[0], outs[-1])

    tiles(along, tile)


def rim_step(base, evens, odds, courant, kind, first=0, parts=1):
    depth, all_across, along, _ = base.shape
    across = evens.shape[1]
    if kind == "middle":
        edge = [shape_of(RADIUS, across // parts, along, BF16)] * parts
        out_shape = [shape_of(depth, across, along + 2 * EDGE, F32)]
        out_shape += edge + edge + [shape_of(depth, RADIUS, along, BF16)]
    elif kind == "half":
        out_shape = [shape_of(depth // 2, across, along, BF16)] * 2
    else:
        out_shape = [shape_of(depth, across, along, BF16)]
    return pl.pallas_call(
        functools.partial(rim_body, first, kind, parts),
        in_specs=whole_vmem(4),
        out_specs=whole_vmem(len(out_shape)),
        out_shape=out_shape,
        scratch_shapes=square_scratch(),
        compiler_params=params(),
    )(base, evens, odds, courant)


def swap(x, axis, pairs):
    return lax.ppermute(x, axis, [p for a, b in pairs for p in ((a, b), (b, a))])


def exchange(evens, odds, edge):
    slabs = lax.axis_size("slab")
    pairs = []
    for one, two in zip(evens, odds):
        pairs.append(
            (
                swap(one, "slab", [(i, i + 1) for i in range(0, slabs - 1, 2)]),
                swap(two, "slab", [(i, i + 1) for i in range(1, slabs - 1, 2)]),
            )
        )
    return pairs, swap(edge, "sub", [(0, 1)])


def gram_body(parts, pieces, *refs):
    ins, (keep_ref, send_ref), panel = refs[: 2 * len(pieces)], refs[-3:-1], refs[-1]
    half = parts // 2
    chip = lax.axis_index("probe")
    core = lax.axis_index("sub")
    depth, _, along, _ = ins[0].shape
    across = panel.shape[0] // (depth * along)
    for (chunk, first), keep, got in zip(pieces, ins[0::2], ins[1::2]):
        mine = pl.multiple_of((chip * half + chunk) * LANES, LANES)
        other = pl.multiple_of(((1 - chip) * half + chunk) * LANES, LANES)
        width = keep.shape[1]
        for z in range(depth):
            rows = pl.ds((z * across + first) * along, width * along)
            panel[rows, pl.ds(mine, LANES)] = keep[z].reshape(width * along, LANES)
            panel[rows, pl.ds(other, LANES)] = got[z].reshape(width * along, LANES)
    size = parts * LANES
    everything = panel[...]

    def columns(which):
        one = panel[:, pl.ds(pl.multiple_of(which * LANES, LANES), LANES)]
        two = panel[:, pl.ds(pl.multiple_of((2 + which) * LANES, LANES), LANES)]
        return lax.dot_general(
            everything,
            jnp.concatenate([one, two], axis=1),
            (((0,), (0,)), ((), ())),
            preferred_element_type=F32,
        )

    rows = lax.broadcasted_iota(jnp.int32, (LANES, LANES), 0)
    cols = lax.broadcasted_iota(jnp.int32, (LANES, LANES), 1)
    eye = rows == cols
    keep = columns(core)
    send = columns(1 - core)
    keep_ref[:size] = keep
    send_ref[:size] = send

    def diagonal(which, first):
        side = which // 2
        a = keep_ref[which * LANES : (which + 1) * LANES, side * LANES : (side + 1) * LANES]
        b = send_ref[which * LANES : (which + 1) * LANES, side * LANES : (side + 1) * LANES]
        block = jnp.where(core == which % 2, a, b)
        return jnp.sum(jnp.where(eye, block, 0.0), axis=0, keepdims=True)

    diag = [diagonal(n, None) for n in range(parts)]
    row0 = jnp.concatenate(diag[:2], axis=1)
    row1 = jnp.concatenate(diag[2:], axis=1)
    tail = jnp.concatenate([row0, row1, jnp.zeros((6, 2 * LANES), F32)], axis=0)
    keep_ref[size:] = tail
    send_ref[size:] = tail


def gram(parts, pieces, fields, cells):
    size = parts * LANES
    shape = jax.ShapeDtypeStruct((size + 8, 2 * LANES), F32)
    return pl.pallas_call(
        functools.partial(gram_body, parts, pieces),
        in_specs=whole_vmem(len(fields)),
        out_specs=whole_vmem(2),
        out_shape=[shape, shape],
        scratch_shapes=[pltpu.VMEM((cells, size), BF16)],
        compiler_params=params(),
    )(*fields)


def rounded(ref, block, tail):
    count = block.shape[0]
    high = tail.astype(BF16)
    low = tail - high.astype(F32)
    ref[:count] = block.astype(BF16)
    ref[count:] = jnp.concatenate([high.astype(F32), low], axis=0).astype(BF16)


def opened(ref):
    count = ref.shape[0] - 16
    tail = ref[count:].astype(F32)
    return ref[:count].astype(F32), tail[:8] + tail[8:]


def rows_body(slabs, count, keep_ref, got_ref, own_ref, *outs):
    slab = lax.axis_index("slab")
    size = slabs * count
    tail = keep_ref[pl.ds(size, 8)] + got_ref[pl.ds(size, 8)]
    for d in range(slabs):
        owner = slab ^ d
        span = pl.ds(pl.multiple_of(owner * count, count), count)
        block = keep_ref[span] + got_ref[span]
        if d == 0:
            own_ref[:count] = block
            own_ref[count:] = tail
        else:
            rounded(outs[d - 1], block, tail)


def split_rows(keep, got, slabs):
    count = (keep.shape[0] - 8) // slabs
    own = jax.ShapeDtypeStruct((count + 8, keep.shape[1]), F32)
    sent = jax.ShapeDtypeStruct((count + 16, keep.shape[1]), BF16)
    return pl.pallas_call(
        functools.partial(rows_body, slabs, count),
        in_specs=whole_vmem(2),
        out_specs=whole_vmem(slabs),
        out_shape=[own] + [sent] * (slabs - 1),
        compiler_params=params(),
    )(keep, got)


def sum_body(own_ref, *refs):
    count = own_ref.shape[0] - 8
    block, tail = own_ref[:count], own_ref[count:]
    for ref in refs[:-1]:
        more, more_tail = opened(ref)
        block, tail = block + more, tail + more_tail
    rounded(refs[-1], block, tail)


def sum_all(own, others):
    return pl.pallas_call(
        sum_body,
        in_specs=whole_vmem(1 + len(others)),
        out_specs=whole_vmem(1)[0],
        out_shape=jax.ShapeDtypeStruct(others[0].shape, BF16),
        compiler_params=params(),
    )(own, *others)


def finish_body(cell_count, a_ref, b_ref, c_ref, d_ref, out_ref, norms_ref):
    slab = lax.axis_index("slab")
    core = lax.axis_index("sub")
    count = out_ref.shape[0]
    near, tail = opened(a_ref)
    far, _ = opened(c_ref)
    more, more_tail = opened(b_ref)
    near = near + more
    far = far + opened(d_ref)[0]
    norms = jnp.sqrt((tail + more_tail)[:2] / cell_count + EPSILON)
    blocks = [norms[n // 2 : n // 2 + 1, (n % 2) * LANES : (n % 2 + 1) * LANES] for n in range(4)]
    own = blocks[0]
    for n in range(1, 4):
        own = jnp.where(slab == n, blocks[n], own)
    norms_ref[...] = own
    rows = lax.broadcasted_iota(jnp.int32, (LANES, LANES), 0)
    cols = lax.broadcasted_iota(jnp.int32, (LANES, LANES), 1)
    eye = rows == cols
    own_column = jnp.sum(
        jnp.where(eye, jnp.broadcast_to(own, (LANES, LANES)), 0.0), axis=1, keepdims=True
    )
    for side in range(2):
        for block, which in ((near, core), (far, 1 - core)):
            index = 2 * side + which
            others = jnp.where(which == 0, blocks[2 * side], blocks[2 * side + 1])
            value = block[:count, side * LANES : (side + 1) * LANES]
            value = value / math.sqrt(cell_count) / (own_column * others)
            value = jnp.where(eye & (index == slab), 0.0, value)
            out_ref[:, pl.ds(pl.multiple_of(index * LANES, LANES), LANES)] = value


def finish(pieces, cell_count):
    count = pieces[0].shape[0] - 16
    return pl.pallas_call(
        functools.partial(finish_body, cell_count),
        in_specs=whole_vmem(4),
        out_specs=whole_vmem(2),
        out_shape=[
            jax.ShapeDtypeStruct((count, 4 * LANES), F32),
            jax.ShapeDtypeStruct((1, LANES), F32),
        ],
        compiler_params=params(),
    )(*pieces)


def coupled(pieces, fields, cells, cell_count):
    slabs = 4
    keep, send = gram(4, pieces, fields, cells)
    got = swap(send, "sub", [(0, 1)])
    own, *sent = split_rows(keep, got, slabs)
    arrived = [
        lax.ppermute(block, "slab", [(i, i ^ d) for i in range(slabs)])
        for d, block in enumerate(sent, 1)
    ]
    mine = sum_all(own, arrived)
    both = ("probe", "sub")
    others = [
        lax.ppermute(mine, both, [(i, i ^ flip) for i in range(4)]) for flip in (2, 1, 3)
    ]
    coupling, norms = finish([mine] + others, cell_count)
    return coupling, norms.reshape(-1)


def coupled_general(fields, cell_count):
    chips = lax.axis_size("probe")
    sketch = jnp.concatenate(fields, axis=-1)
    sketch = sketch.reshape(-1, sketch.shape[-1])
    if chips > 1:
        sketch = lax.all_to_all(sketch, "probe", split_axis=0, concat_axis=1, tiled=True)
    partial_gram = lax.dot_general(
        sketch, sketch, (((0,), (0,)), ((), ())), preferred_element_type=F32
    )
    rows = lax.psum_scatter(partial_gram, "slab", scatter_dimension=0, tiled=True)
    rows = lax.psum(rows, ("probe", "sub"))
    count = rows.shape[0]
    start = lax.axis_index("slab") * count
    own = jnp.diagonal(lax.dynamic_slice_in_dim(rows, start, count, 1))
    own_norms = jnp.sqrt(own / cell_count + EPSILON)
    norms = lax.all_gather(own_norms, "slab", axis=0, tiled=True)
    coupling = rows / math.sqrt(cell_count) / (own_norms[:, None] * norms[None, :])
    row_ids = start + lax.broadcasted_iota(jnp.int32, coupling.shape, 0)
    col_ids = lax.broadcasted_iota(jnp.int32, coupling.shape, 1)
    return jnp.where(row_ids == col_ids, 0.0, coupling), own_norms


def shards(probes, courant, source):
    depth, across, along, count = probes.shape
    chunks = count // LANES
    slabs, chips = lax.axis_size("slab"), lax.axis_size("probe")
    cell_count = depth * across * along * slabs * lax.axis_size("sub")
    paired = chips == 2 and slabs == 4 and chunks == 2
    steps = source.shape[0]
    courant = courant.reshape(depth * across, along)
    source = source.reshape(steps, depth * across, along)

    now, previous, halos = [], [None] * chunks, []
    for c in range(chunks):
        u, one, two, edge = first_field(probes, c, source)
        now.append(u)
        halos.append(exchange([one], [two], edge))
    pieces, fields = [], []
    for n in range(1, steps):
        for c in range(chunks):
            pairs, beside = halos[c]
            base = local_step(now[c], beside, probes, c, courant, source, n, previous[c])
            if n == steps - 1:
                width = across // len(pairs)
                for h, (one, two) in enumerate(pairs):
                    kind = "half" if paired else "all"
                    out = rim_step(base, one, two, courant, kind, h * width)
                    if paired:
                        pieces.append((c, h * width))
                        fields += [out[0], swap(out[1], "probe", [(0, 1)])]
                    else:
                        fields.append(out[0])
            else:
                ((one, two),) = pairs
                out = rim_step(base, one, two, courant, "middle")
                previous[c], now[c] = now[c], out[0]
                halos[c] = exchange([out[1]], [out[2]], out[3])
    if paired:
        cells = depth // 2 * across * along
        return coupled(tuple(pieces), fields, cells, cell_count)
    return coupled_general(fields, cell_count)


def solution(mesh):
    placed = (
        P(("groups", "slab"), "sub", None, "probe"),
        P("slab", "sub", None),
        P(None, ("groups", "slab"), "sub", None),
    )
    return jax.shard_map(
        shards,
        mesh=mesh,
        in_specs=placed,
        out_specs=(P(("groups", "slab"), None), P(("groups", "slab"))),
        check_vma=False,
    )
```

```python
import functools
import math

import jax
import jax.numpy as jnp
from jax import lax
from jax.experimental import pallas as pl
from jax.experimental.pallas import tpu as pltpu
from jax.sharding import PartitionSpec as P

COEFFICIENTS = (-205.0 / 72.0, 8.0 / 5.0, -1.0 / 5.0, 8.0 / 315.0, -1.0 / 560.0)
EPSILON = 1e-06
LANES = 128
RADIUS = 4
EDGE = 8
TILE = 16
F32 = jnp.float32
BF16 = jnp.bfloat16
VMEM_LIMIT = 32 * 1024 * 1024


def params(*semantics):
    return pltpu.CompilerParams(
        dimension_semantics=semantics or None, vmem_limit_bytes=VMEM_LIMIT
    )


def whole_vmem(count):
    return [pl.BlockSpec(memory_space=pltpu.VMEM)] * count


def shape_of(depth, across, along, dtype):
    return jax.ShapeDtypeStruct((depth, across, along, LANES), dtype)


def turned(field, scratch):
    rows, along = field.shape
    scratch[:rows, :along] = field
    return jnp.transpose(scratch[...])


def lane(values, n):
    return jnp.broadcast_to(values[:, n : n + 1], (values.shape[0], LANES))


def store_edges(x, span, news, even, refs):
    even_refs, odd_refs = refs
    width = even_refs[0].shape[1]
    part, x = x // width, x % width
    for j in range(RADIUS):
        low = news[j].astype(BF16)
        high = news[len(news) - RADIUS + j].astype(BF16)
        even_refs[part][j, x, span] = jnp.where(even, high, low)
        odd_refs[part][j, x, span] = jnp.where(even, low, high)


def store_beside(span, rows, core, u_ref, edge_ref):
    depth, across, _, _ = u_ref.shape
    first = (across - RADIUS) * (1 - core)
    for z in range(depth):
        for j in range(RADIUS):
            edge_ref[z, j, span] = u_ref[z, first + j, rows].astype(BF16)


def slab_is_even():
    return lax.rem(lax.axis_index("slab"), 2) == 0


def clear_pads(u_ref):
    depth, across, padded, _ = u_ref.shape

    def plane(z, _):
        blank = jnp.zeros((across, EDGE, LANES), F32)
        u_ref[z, :, pl.ds(0, EDGE)] = blank
        u_ref[z, :, pl.ds(padded - EDGE, EDGE)] = blank
        return 0

    lax.fori_loop(0, depth, plane, 0)


def tiles(along, body):
    def one(t, _):
        body(pl.multiple_of(t * TILE, TILE))
        return 0

    lax.fori_loop(0, along // TILE, one, 0)


def first_body(chunk, p_ref, s_ref, u_ref, even_ref, odd_ref, edge_ref, square, turned_s):
    depth, across, padded, _ = u_ref.shape
    along = padded - 2 * EDGE
    core = lax.axis_index("sub")
    even = slab_is_even()
    turned_s[...] = turned(s_ref[0], square)
    clear_pads(u_ref)

    def tile(start):
        span = pl.ds(start, TILE)
        rows = pl.ds(start + EDGE, TILE)
        source = turned_s[span]
        for x in range(across):
            news = []
            for z in range(depth):
                p = p_ref[z, x, span, chunk * LANES : (chunk + 1) * LANES].astype(F32)
                new = lane(source, z * across + x) * p
                u_ref[z, x, rows] = new
                news.append(new)
            store_edges(x, span, news, even, ([even_ref], [odd_ref]))
        store_beside(span, rows, core, u_ref, edge_ref)

    tiles(along, tile)


def square_scratch():
    return [pltpu.VMEM((LANES, LANES), F32)] * 2


def first_field(probes, chunk, source):
    depth, across, along, _ = probes.shape
    return pl.pallas_call(
        functools.partial(first_body, chunk),
        in_specs=whole_vmem(2),
        out_specs=whole_vmem(4),
        out_shape=[
            shape_of(depth, across, along + 2 * EDGE, F32),
            shape_of(RADIUS, across, along, BF16),
            shape_of(RADIUS, across, along, BF16),
            shape_of(depth, RADIUS, along, BF16),
        ],
        scratch_shapes=square_scratch(),
        compiler_params=params(),
    )(probes, source)


def local_body(chunk, moment, has_previous, *refs):
    refs = list(refs)
    u_ref, beside_ref, p_ref, c_ref, s_ref = refs[:5]
    prev_ref = refs[5] if has_previous else None
    base_ref, square, turned_c, turned_s = refs[-4:]
    depth, across, along, _ = base_ref.shape
    core = lax.axis_index("sub")
    left_on = (core == 1).astype(F32)
    right_on = (core == 0).astype(F32)
    turned_c[...] = turned(c_ref[...], square)
    turned_s[...] = turned(s_ref[moment], square)

    def tile(start):
        span = pl.ds(start, TILE)
        rows = start + EDGE
        courant = turned_c[span]
        source = turned_s[span]
        for z in range(depth):
            beside = [beside_ref[z, j, span].astype(F32) for j in range(RADIUS)]
            row = [v * left_on for v in beside]
            row += [u_ref[z, x, pl.ds(rows, TILE)] for x in range(across)]
            row += [v * right_on for v in beside]
            for x in range(across):
                here = row[RADIUS + x]
                total = (3.0 * COEFFICIENTS[0]) * here
                for r in range(1, RADIUS + 1):
                    near = row[RADIUS + x + r] + row[RADIUS + x - r]
                    near = near + (
                        u_ref[z, x, pl.ds(rows + r, TILE)] + u_ref[z, x, pl.ds(rows - r, TILE)]
                    )
                    if z + r < depth:
                        near = near + u_ref[z + r, x, pl.ds(rows, TILE)]
                    if z - r >= 0:
                        near = near + u_ref[z - r, x, pl.ds(rows, TILE)]
                    total = total + COEFFICIENTS[r] * near
                cell = z * across + x
                p = p_ref[z, x, span, chunk * LANES : (chunk + 1) * LANES].astype(F32)
                new = 2.0 * here
                if has_previous:
                    new = new - prev_ref[z, x, pl.ds(rows, TILE)]
                new = new + lane(courant, cell) * total + lane(source, cell) * p
                base_ref[z, x, span] = new

    tiles(along, tile)


def local_step(u, beside, probes, chunk, courant, source, moment, previous):
    depth, across, along, _ = probes.shape
    operands = [u, beside, probes, courant, source]
    if previous is not None:
        operands.append(previous)
    return pl.pallas_call(
        functools.partial(local_body, chunk, moment, previous is not None),
        in_specs=whole_vmem(len(operands)),
        out_specs=whole_vmem(1)[0],
        out_shape=shape_of(depth, across, along, F32),
        scratch_shapes=square_scratch() + square_scratch()[:1],
        compiler_params=params(),
    )(*operands)


def rim_body(first, kind, parts, *refs):
    base_ref, even_ref, odd_ref, c_ref = refs[:4]
    outs, (square, turned_c) = refs[4:-2], refs[-2:]
    depth, all_across, along, _ = base_ref.shape
    across = even_ref.shape[1]
    core = lax.axis_index("sub")
    even = slab_is_even()
    turned_c[...] = turned(c_ref[...], square)
    if kind == "middle":
        clear_pads(outs[0])

    def tile(start):
        span = pl.ds(start, TILE)
        rows = pl.ds(start + EDGE, TILE)
        courant = turned_c[span]
        for x in range(across):
            place = first + x
            below, above = [], []
            for j in range(RADIUS):
                one, two = even_ref[j, x, span], odd_ref[j, x, span]
                below.append(jnp.where(even, two, one).astype(F32))
                above.append(jnp.where(even, one, two).astype(F32))
            news = []
            for z in range(depth):
                added = None
                for r in range(1, RADIUS + 1):
                    if z - r < 0:
                        term = COEFFICIENTS[r] * below[RADIUS + z - r]
                        added = term if added is None else added + term
                    if z + r >= depth:
                        term = COEFFICIENTS[r] * above[z + r - depth]
                        added = term if added is None else added + term
                new = base_ref[z, place, span]
                if added is not None:
                    new = new + lane(courant, z * all_across + place) * added
                news.append(new)
            if kind == "middle":
                for z, new in enumerate(news):
                    outs[0][z, place, rows] = new
                edges = (outs[1 : 1 + parts], outs[1 + parts : 1 + 2 * parts])
                store_edges(place, span, news, even, edges)
            elif kind == "half":
                keep_ref, send_ref = outs
                lower = lax.axis_index("probe") == 0
                for z in range(depth // 2):
                    one, two = news[z].astype(BF16), news[z + depth // 2].astype(BF16)
                    keep_ref[z, x, span] = jnp.where(lower, one, two)
                    send_ref[z, x, span] = jnp.where(lower, two, one)
            else:
                for z, new in enumerate(news):
                    outs[0][z, x, span] = new.astype(BF16)
        if kind == "middle":
            store_beside(span, rows, core, outs[0], outs[-1])

    tiles(along, tile)


def rim_step(base, evens, odds, courant, kind, first=0, parts=1):
    depth, all_across, along, _ = base.shape
    across = evens.shape[1]
    if kind == "middle":
        edge = [shape_of(RADIUS, across // parts, along, BF16)] * parts
        out_shape = [shape_of(depth, across, along + 2 * EDGE, F32)]
        out_shape += edge + edge + [shape_of(depth, RADIUS, along, BF16)]
    elif kind == "half":
        out_shape = [shape_of(depth // 2, across, along, BF16)] * 2
    else:
        out_shape = [shape_of(depth, across, along, BF16)]
    return pl.pallas_call(
        functools.partial(rim_body, first, kind, parts),
        in_specs=whole_vmem(4),
        out_specs=whole_vmem(len(out_shape)),
        out_shape=out_shape,
        scratch_shapes=square_scratch(),
        compiler_params=params(),
    )(base, evens, odds, courant)


def swap(x, axis, pairs):
    return lax.ppermute(x, axis, [p for a, b in pairs for p in ((a, b), (b, a))])


def exchange(evens, odds, edge):
    slabs = lax.axis_size("slab")
    pairs = []
    for one, two in zip(evens, odds):
        pairs.append(
            (
                swap(one, "slab", [(i, i + 1) for i in range(0, slabs - 1, 2)]),
                swap(two, "slab", [(i, i + 1) for i in range(1, slabs - 1, 2)]),
            )
        )
    return pairs, swap(edge, "sub", [(0, 1)])


def gram_body(parts, pieces, *refs):
    ins, (keep_ref, send_ref), panel = refs[: 2 * len(pieces)], refs[-3:-1], refs[-1]
    half = parts // 2
    chip = lax.axis_index("probe")
    core = lax.axis_index("sub")
    depth, _, along, _ = ins[0].shape
    across = panel.shape[0] // (depth * along)
    for (chunk, first), keep, got in zip(pieces, ins[0::2], ins[1::2]):
        mine = pl.multiple_of((chip * half + chunk) * LANES, LANES)
        other = pl.multiple_of(((1 - chip) * half + chunk) * LANES, LANES)
        width = keep.shape[1]
        for z in range(depth):
            rows = pl.ds((z * across + first) * along, width * along)
            panel[rows, pl.ds(mine, LANES)] = keep[z].reshape(width * along, LANES)
            panel[rows, pl.ds(other, LANES)] = got[z].reshape(width * along, LANES)
    size = parts * LANES
    everything = panel[...]

    def columns(which):
        one = panel[:, pl.ds(pl.multiple_of(which * LANES, LANES), LANES)]
        two = panel[:, pl.ds(pl.multiple_of((2 + which) * LANES, LANES), LANES)]
        return lax.dot_general(
            everything,
            jnp.concatenate([one, two], axis=1),
            (((0,), (0,)), ((), ())),
            preferred_element_type=F32,
        )

    rows = lax.broadcasted_iota(jnp.int32, (LANES, LANES), 0)
    cols = lax.broadcasted_iota(jnp.int32, (LANES, LANES), 1)
    eye = rows == cols
    keep = columns(core)
    send = columns(1 - core)
    keep_ref[:size] = keep
    send_ref[:size] = send

    def diagonal(which, first):
        side = which // 2
        a = keep_ref[which * LANES : (which + 1) * LANES, side * LANES : (side + 1) * LANES]
        b = send_ref[which * LANES : (which + 1) * LANES, side * LANES : (side + 1) * LANES]
        block = jnp.where(core == which % 2, a, b)
        return jnp.sum(jnp.where(eye, block, 0.0), axis=0, keepdims=True)

    diag = [diagonal(n, None) for n in range(parts)]
    row0 = jnp.concatenate(diag[:2], axis=1)
    row1 = jnp.concatenate(diag[2:], axis=1)
    tail = jnp.concatenate([row0, row1, jnp.zeros((6, 2 * LANES), F32)], axis=0)
    keep_ref[size:] = tail
    send_ref[size:] = tail


def gram(parts, pieces, fields, cells):
    size = parts * LANES
    shape = jax.ShapeDtypeStruct((size + 8, 2 * LANES), F32)
    return pl.pallas_call(
        functools.partial(gram_body, parts, pieces),
        in_specs=whole_vmem(len(fields)),
        out_specs=whole_vmem(2),
        out_shape=[shape, shape],
        scratch_shapes=[pltpu.VMEM((cells, size), BF16)],
        compiler_params=params(),
    )(*fields)


def rounded(ref, block, tail):
    count = block.shape[0]
    high = tail.astype(BF16)
    low = tail - high.astype(F32)
    ref[:count] = block.astype(BF16)
    ref[count:] = jnp.concatenate([high.astype(F32), low], axis=0).astype(BF16)


def opened(ref):
    count = ref.shape[0] - 16
    tail = ref[count:].astype(F32)
    return ref[:count].astype(F32), tail[:8] + tail[8:]


def rows_body(slabs, count, keep_ref, got_ref, own_ref, *outs):
    slab = lax.axis_index("slab")
    size = slabs * count
    tail = keep_ref[pl.ds(size, 8)] + got_ref[pl.ds(size, 8)]
    for d in range(slabs):
        owner = slab ^ d
        span = pl.ds(pl.multiple_of(owner * count, count), count)
        block = keep_ref[span] + got_ref[span]
        if d == 0:
            own_ref[:count] = block
            own_ref[count:] = tail
        else:
            rounded(outs[d - 1], block, tail)


def split_rows(keep, got, slabs):
    count = (keep.shape[0] - 8) // slabs
    own = jax.ShapeDtypeStruct((count + 8, keep.shape[1]), F32)
    sent = jax.ShapeDtypeStruct((count + 16, keep.shape[1]), BF16)
    return pl.pallas_call(
        functools.partial(rows_body, slabs, count),
        in_specs=whole_vmem(2),
        out_specs=whole_vmem(slabs),
        out_shape=[own] + [sent] * (slabs - 1),
        compiler_params=params(),
    )(keep, got)


def sum_body(own_ref, *refs):
    count = own_ref.shape[0] - 8
    block, tail = own_ref[:count], own_ref[count:]
    for ref in refs[:-1]:
        more, more_tail = opened(ref)
        block, tail = block + more, tail + more_tail
    rounded(refs[-1], block, tail)


def sum_all(own, others):
    return pl.pallas_call(
        sum_body,
        in_specs=whole_vmem(1 + len(others)),
        out_specs=whole_vmem(1)[0],
        out_shape=jax.ShapeDtypeStruct(others[0].shape, BF16),
        compiler_params=params(),
    )(own, *others)


def normalise_body(cell_count, mine_ref, other_ref, out_ref, norms_ref):
    slab = lax.axis_index("slab")
    core = lax.axis_index("sub")
    one, one_tail = opened(mine_ref)
    two, two_tail = opened(other_ref)
    total = one + two
    norms = jnp.sqrt((one_tail + two_tail)[:2] / cell_count + EPSILON)
    blocks = [norms[n // 2 : n // 2 + 1, (n % 2) * LANES : (n % 2 + 1) * LANES] for n in range(4)]
    own = blocks[0]
    for n in range(1, 4):
        own = jnp.where(slab == n, blocks[n], own)
    norms_ref[...] = own
    rows = lax.broadcasted_iota(jnp.int32, (LANES, LANES), 0)
    cols = lax.broadcasted_iota(jnp.int32, (LANES, LANES), 1)
    eye = rows == cols
    own_column = jnp.sum(
        jnp.where(eye, jnp.broadcast_to(own, (LANES, LANES)), 0.0), axis=1, keepdims=True
    )
    for side in range(2):
        columns = slice(side * LANES, (side + 1) * LANES)
        others = jnp.where(core == 0, blocks[2 * side], blocks[2 * side + 1])
        value = total[:, columns] / math.sqrt(cell_count) / (own_column * others)
        out_ref[:, columns] = jnp.where(eye & (2 * side + core == slab), 0.0, value)


def normalise(mine, other, cell_count):
    count = mine.shape[0] - 16
    return pl.pallas_call(
        functools.partial(normalise_body, cell_count),
        in_specs=whole_vmem(2),
        out_specs=whole_vmem(2),
        out_shape=[
            jax.ShapeDtypeStruct((count, 2 * LANES), F32),
            jax.ShapeDtypeStruct((1, LANES), F32),
        ],
        compiler_params=params(),
    )(mine, other)


def assemble_body(near_ref, far_ref, out_ref):
    core = lax.axis_index("sub")
    for side in range(2):
        columns = slice(side * LANES, (side + 1) * LANES)
        for ref, which in ((near_ref, core), (far_ref, 1 - core)):
            start = pl.multiple_of((2 * side + which) * LANES, LANES)
            out_ref[:, pl.ds(start, LANES)] = ref[:, columns]


def assemble(near, far):
    return pl.pallas_call(
        assemble_body,
        in_specs=whole_vmem(2),
        out_specs=whole_vmem(1)[0],
        out_shape=jax.ShapeDtypeStruct((near.shape[0], 4 * LANES), F32),
        compiler_params=params(),
    )(near, far)


def coupled(pieces, fields, cells, cell_count):
    slabs = 4
    keep, send = gram(4, pieces, fields, cells)
    got = swap(send, "sub", [(0, 1)])
    own, *sent = split_rows(keep, got, slabs)
    arrived = [
        lax.ppermute(sent[d - 1], "slab", [(i, i ^ d) for i in range(slabs)]) for d in (2, 3, 1)
    ]
    mine = sum_all(own, arrived)
    other = swap(mine, "probe", [(0, 1)])
    near, norms = normalise(mine, other, cell_count)
    far = swap(near, "sub", [(0, 1)])
    return assemble(near, far), norms.reshape(-1)


def coupled_general(fields, cell_count):
    chips = lax.axis_size("probe")
    sketch = jnp.concatenate(fields, axis=-1)
    sketch = sketch.reshape(-1, sketch.shape[-1])
    if chips > 1:
        sketch = lax.all_to_all(sketch, "probe", split_axis=0, concat_axis=1, tiled=True)
    partial_gram = lax.dot_general(
        sketch, sketch, (((0,), (0,)), ((), ())), preferred_element_type=F32
    )
    rows = lax.psum_scatter(partial_gram, "slab", scatter_dimension=0, tiled=True)
    rows = lax.psum(rows, ("probe", "sub"))
    count = rows.shape[0]
    start = lax.axis_index("slab") * count
    own = jnp.diagonal(lax.dynamic_slice_in_dim(rows, start, count, 1))
    own_norms = jnp.sqrt(own / cell_count + EPSILON)
    norms = lax.all_gather(own_norms, "slab", axis=0, tiled=True)
    coupling = rows / math.sqrt(cell_count) / (own_norms[:, None] * norms[None, :])
    row_ids = start + lax.broadcasted_iota(jnp.int32, coupling.shape, 0)
    col_ids = lax.broadcasted_iota(jnp.int32, coupling.shape, 1)
    return jnp.where(row_ids == col_ids, 0.0, coupling), own_norms


def shards(probes, courant, source):
    depth, across, along, count = probes.shape
    chunks = count // LANES
    slabs, chips = lax.axis_size("slab"), lax.axis_size("probe")
    cell_count = depth * across * along * slabs * lax.axis_size("sub")
    paired = chips == 2 and slabs == 4 and chunks == 2
    steps = source.shape[0]
    courant = courant.reshape(depth * across, along)
    source = source.reshape(steps, depth * across, along)

    now, previous, halos = [], [None] * chunks, []
    for c in range(chunks):
        u, one, two, edge = first_field(probes, c, source)
        now.append(u)
        halos.append(exchange([one], [two], edge))
    pieces, fields = [], []
    for n in range(1, steps):
        for c in range(chunks):
            pairs, beside = halos[c]
            base = local_step(now[c], beside, probes, c, courant, source, n, previous[c])
            if n == steps - 1:
                width = across // len(pairs)
                for h, (one, two) in enumerate(pairs):
                    kind = "half" if paired else "all"
                    out = rim_step(base, one, two, courant, kind, h * width)
                    if paired:
                        pieces.append((c, h * width))
                        fields += [out[0], swap(out[1], "probe", [(0, 1)])]
                    else:
                        fields.append(out[0])
            else:
                ((one, two),) = pairs
                out = rim_step(base, one, two, courant, "middle")
                previous[c], now[c] = now[c], out[0]
                halos[c] = exchange([out[1]], [out[2]], out[3])
    if paired:
        cells = depth // 2 * across * along
        return coupled(tuple(pieces), fields, cells, cell_count)
    return coupled_general(fields, cell_count)


def solution(mesh):
    placed = (
        P(("groups", "slab"), "sub", None, "probe"),
        P("slab", "sub", None),
        P(None, ("groups", "slab"), "sub", None),
    )
    return jax.shard_map(
        shards,
        mesh=mesh,
        in_specs=placed,
        out_specs=(P(("groups", "slab"), None), P(("groups", "slab"))),
        check_vma=False,
    )
```

```python
import functools
import math

import jax
import jax.numpy as jnp
from jax import lax
from jax.experimental import pallas as pl
from jax.experimental.pallas import tpu as pltpu
from jax.sharding import PartitionSpec as P

COEFFICIENTS = (-205.0 / 72.0, 8.0 / 5.0, -1.0 / 5.0, 8.0 / 315.0, -1.0 / 560.0)
EPSILON = 1e-06
LANES = 128
RADIUS = 4
EDGE = 8
TILE = 16
F32 = jnp.float32
BF16 = jnp.bfloat16
VMEM_LIMIT = 32 * 1024 * 1024


def params(*semantics):
    return pltpu.CompilerParams(
        dimension_semantics=semantics or None, vmem_limit_bytes=VMEM_LIMIT
    )


def carried(operands, in_specs, out_specs, out_shape, carry):
    aliases = {}
    for array in carry:
        aliases[len(operands)] = len(out_shape)
        operands.append(array)
        in_specs.append(pl.BlockSpec(memory_space=pl.ANY))
        out_specs.append(pl.BlockSpec(memory_space=pl.ANY))
        out_shape.append(jax.ShapeDtypeStruct(array.shape, array.dtype))
    return aliases


def whole_vmem(count):
    return [pl.BlockSpec(memory_space=pltpu.VMEM)] * count


def shape_of(depth, across, along, dtype):
    return jax.ShapeDtypeStruct((depth, across, along, LANES), dtype)


def turned(field, scratch):
    rows, along = field.shape
    scratch[:rows, :along] = field
    return jnp.transpose(scratch[...])


def lane(values, n):
    return jnp.broadcast_to(values[:, n : n + 1], (values.shape[0], LANES))


def store_edges(x, span, news, even, refs):
    even_refs, odd_refs = refs
    width = even_refs[0].shape[1]
    part, x = x // width, x % width
    for j in range(RADIUS):
        low = news[j].astype(BF16)
        high = news[len(news) - RADIUS + j].astype(BF16)
        even_refs[part][j, x, span] = jnp.where(even, high, low)
        odd_refs[part][j, x, span] = jnp.where(even, low, high)


def store_beside(span, rows, core, u_ref, edge_ref):
    depth, across, _, _ = u_ref.shape
    first = (across - RADIUS) * (1 - core)
    for z in range(depth):
        for j in range(RADIUS):
            edge_ref[z, j, span] = u_ref[z, first + j, rows].astype(BF16)


def slab_is_even():
    return lax.rem(lax.axis_index("slab"), 2) == 0


def clear_pads(u_ref):
    depth, across, padded, _ = u_ref.shape

    def plane(z, _):
        blank = jnp.zeros((across, EDGE, LANES), F32)
        u_ref[z, :, pl.ds(0, EDGE)] = blank
        u_ref[z, :, pl.ds(padded - EDGE, EDGE)] = blank
        return 0

    lax.fori_loop(0, depth, plane, 0)


def tiles(along, body):
    def one(t, _):
        body(pl.multiple_of(t * TILE, TILE))
        return 0

    lax.fori_loop(0, along // TILE, one, 0)


def first_body(chunk, p_ref, s_ref, u_ref, even_ref, odd_ref, edge_ref, square, turned_s):
    depth, across, padded, _ = u_ref.shape
    along = padded - 2 * EDGE
    core = lax.axis_index("sub")
    even = slab_is_even()
    turned_s[...] = turned(s_ref[0], square)
    clear_pads(u_ref)

    def tile(start):
        span = pl.ds(start, TILE)
        rows = pl.ds(start + EDGE, TILE)
        source = turned_s[span]
        for x in range(across):
            news = []
            for z in range(depth):
                p = p_ref[z, x, span, chunk * LANES : (chunk + 1) * LANES].astype(F32)
                new = lane(source, z * across + x) * p
                u_ref[z, x, rows] = new
                news.append(new)
            store_edges(x, span, news, even, ([even_ref], [odd_ref]))
        store_beside(span, rows, core, u_ref, edge_ref)

    tiles(along, tile)


def square_scratch():
    return [pltpu.VMEM((LANES, LANES), F32)] * 2


def first_field(probes, chunk, source):
    depth, across, along, _ = probes.shape
    return pl.pallas_call(
        functools.partial(first_body, chunk),
        in_specs=whole_vmem(2),
        out_specs=whole_vmem(4),
        out_shape=[
            shape_of(depth, across, along + 2 * EDGE, F32),
            shape_of(RADIUS, across, along, BF16),
            shape_of(RADIUS, across, along, BF16),
            shape_of(depth, RADIUS, along, BF16),
        ],
        scratch_shapes=square_scratch(),
        compiler_params=params(),
    )(probes, source)


def local_body(chunk, moment, has_previous, carries, *refs):
    refs = list(refs)
    u_ref, beside_ref, p_ref, c_ref, s_ref = refs[:5]
    prev_ref = refs[5] if has_previous else None
    base_ref = refs[5 + has_previous + carries]
    square, turned_c, turned_s = refs[-3:]
    depth, across, along, _ = base_ref.shape
    core = lax.axis_index("sub")
    left_on = (core == 1).astype(F32)
    right_on = (core == 0).astype(F32)
    turned_c[...] = turned(c_ref[...], square)
    turned_s[...] = turned(s_ref[moment], square)

    def tile(start):
        span = pl.ds(start, TILE)
        rows = start + EDGE
        courant = turned_c[span]
        source = turned_s[span]
        for z in range(depth):
            beside = [beside_ref[z, j, span].astype(F32) for j in range(RADIUS)]
            row = [v * left_on for v in beside]
            row += [u_ref[z, x, pl.ds(rows, TILE)] for x in range(across)]
            row += [v * right_on for v in beside]
            for x in range(across):
                here = row[RADIUS + x]
                total = (3.0 * COEFFICIENTS[0]) * here
                for r in range(1, RADIUS + 1):
                    near = row[RADIUS + x + r] + row[RADIUS + x - r]
                    near = near + (
                        u_ref[z, x, pl.ds(rows + r, TILE)] + u_ref[z, x, pl.ds(rows - r, TILE)]
                    )
                    if z + r < depth:
                        near = near + u_ref[z + r, x, pl.ds(rows, TILE)]
                    if z - r >= 0:
                        near = near + u_ref[z - r, x, pl.ds(rows, TILE)]
                    total = total + COEFFICIENTS[r] * near
                cell = z * across + x
                p = p_ref[z, x, span, chunk * LANES : (chunk + 1) * LANES].astype(F32)
                new = 2.0 * here
                if has_previous:
                    new = new - prev_ref[z, x, pl.ds(rows, TILE)]
                new = new + lane(courant, cell) * total + lane(source, cell) * p
                base_ref[z, x, span] = new

    tiles(along, tile)


def local_step(u, beside, probes, chunk, courant, source, moment, previous, carry=()):
    depth, across, along, _ = probes.shape
    operands = [u, beside, probes, courant, source]
    if previous is not None:
        operands.append(previous)
    in_specs, out_specs = whole_vmem(len(operands)), whole_vmem(1)
    out_shape = [shape_of(depth, across, along, F32)]
    aliases = carried(operands, in_specs, out_specs, out_shape, carry)
    return pl.pallas_call(
        functools.partial(local_body, chunk, moment, previous is not None, len(carry)),
        in_specs=in_specs,
        out_specs=out_specs,
        out_shape=out_shape,
        input_output_aliases=aliases,
        scratch_shapes=square_scratch() + square_scratch()[:1],
        compiler_params=params(),
    )(*operands)


def rim_body(first, kind, parts, after, *refs):
    base_ref, even_ref, odd_ref, c_ref = refs[:4]
    outs, (square, turned_c) = refs[4 + after : -2], refs[-2:]
    depth, all_across, along, _ = base_ref.shape
    across = even_ref.shape[1]
    core = lax.axis_index("sub")
    even = slab_is_even()
    turned_c[...] = turned(c_ref[...], square)
    if kind == "middle":
        clear_pads(outs[0])

    def tile(start):
        span = pl.ds(start, TILE)
        rows = pl.ds(start + EDGE, TILE)
        courant = turned_c[span]
        for x in range(across):
            place = first + x
            below, above = [], []
            for j in range(RADIUS):
                one, two = even_ref[j, x, span], odd_ref[j, x, span]
                below.append(jnp.where(even, two, one).astype(F32))
                above.append(jnp.where(even, one, two).astype(F32))
            news = []
            for z in range(depth):
                added = None
                for r in range(1, RADIUS + 1):
                    if z - r < 0:
                        term = COEFFICIENTS[r] * below[RADIUS + z - r]
                        added = term if added is None else added + term
                    if z + r >= depth:
                        term = COEFFICIENTS[r] * above[z + r - depth]
                        added = term if added is None else added + term
                new = base_ref[z, place, span]
                if added is not None:
                    new = new + lane(courant, z * all_across + place) * added
                news.append(new)
            if kind == "middle":
                for z, new in enumerate(news):
                    outs[0][z, place, rows] = new
                edges = (outs[1 : 1 + parts], outs[1 + parts : 1 + 2 * parts])
                store_edges(place, span, news, even, edges)
            else:
                for z, new in enumerate(news):
                    outs[0][z, x, span] = new.astype(BF16)
        if kind == "middle":
            store_beside(span, rows, core, outs[0], outs[-1])

    tiles(along, tile)


def rim_step(base, evens, odds, courant, kind, first=0, parts=1, after=()):
    depth, all_across, along, _ = base.shape
    across = evens.shape[1]
    if kind == "middle":
        edge = [shape_of(RADIUS, across // parts, along, BF16)] * parts
        out_shape = [shape_of(depth, across, along + 2 * EDGE, F32)]
        out_shape += edge + edge + [shape_of(depth, RADIUS, along, BF16)]
    else:
        out_shape = [shape_of(depth, across, along, BF16)]
    return pl.pallas_call(
        functools.partial(rim_body, first, kind, parts, len(after)),
        in_specs=whole_vmem(4) + [pl.BlockSpec(memory_space=pl.ANY)] * len(after),
        out_specs=whole_vmem(len(out_shape)),
        out_shape=out_shape,
        scratch_shapes=square_scratch(),
        compiler_params=params(),
    )(base, evens, odds, courant, *after)


def last_body(first, sent, carries, *refs):
    base_ref, even_ref, odd_ref, c_ref = refs[:4]
    out_ref = refs[4 + carries]
    square, turned_c = refs[-2:]
    depth, all_across, along, _ = base_ref.shape
    across = even_ref.shape[1]
    chip = lax.axis_index("probe")
    low = (chip == 1) if sent else (chip == 0)
    from_odd = low == slab_is_even()
    turned_c[...] = turned(c_ref[...], square)

    def tile(start):
        span = pl.ds(start, TILE)
        courant = turned_c[span]
        for x in range(across):
            place = first + x
            near = []
            for j in range(RADIUS):
                at = jnp.where(low, RADIUS - 1 - j, j)
                near.append(
                    jnp.where(from_odd, odd_ref[at, x, span], even_ref[at, x, span]).astype(F32)
                )
            for m in range(RADIUS):
                mirror = depth - 1 - m
                added = COEFFICIENTS[m + 1] * near[0]
                for r in range(m + 2, RADIUS + 1):
                    added = added + COEFFICIENTS[r] * near[r - m - 1]
                scale = jnp.where(
                    low,
                    lane(courant, m * all_across + place),
                    lane(courant, mirror * all_across + place),
                )
                new = base_ref[jnp.where(low, m, mirror), place, span] + scale * added
                out_ref[m, x, span] = new.astype(BF16)

    tiles(along, tile)


def last_step(base, evens, odds, courant, first, sent, carry=()):
    _, _, along, _ = base.shape
    across = evens.shape[1]
    operands = [base, evens, odds, courant]
    in_specs, out_specs = whole_vmem(4), whole_vmem(1)
    out_shape = [shape_of(RADIUS, across, along, BF16)]
    aliases = carried(operands, in_specs, out_specs, out_shape, carry)
    return pl.pallas_call(
        functools.partial(last_body, first, sent, len(carry)),
        in_specs=in_specs,
        out_specs=out_specs,
        out_shape=out_shape,
        input_output_aliases=aliases,
        scratch_shapes=square_scratch(),
        compiler_params=params(),
    )(*operands)


def swap(x, axis, pairs):
    return lax.ppermute(x, axis, [p for a, b in pairs for p in ((a, b), (b, a))])


def even_swap(x):
    return swap(x, "slab", [(i, i + 1) for i in range(0, lax.axis_size("slab") - 1, 2)])


def odd_swap(x):
    return swap(x, "slab", [(i, i + 1) for i in range(1, lax.axis_size("slab") - 1, 2)])


def core_swap(x):
    return swap(x, "sub", [(0, 1)])


def chip_swap(x):
    return swap(x, "probe", [(0, 1)])


def gram_body(parts, first, last, *refs):
    half = parts // 2
    ins, (keep_ref, send_ref), panel = refs[:parts], refs[-3:-1], refs[-1]
    chip = lax.axis_index("probe")
    core = lax.axis_index("sub")
    cells = panel.shape[0]
    for n in range(half):
        mine = pl.multiple_of((chip * half + n) * LANES, LANES)
        other = pl.multiple_of(((1 - chip) * half + n) * LANES, LANES)
        panel[:, pl.ds(mine, LANES)] = ins[2 * n][...].reshape(cells, LANES)
        panel[:, pl.ds(other, LANES)] = ins[2 * n + 1][...].reshape(cells, LANES)
    size = parts * LANES
    everything = panel[...]

    def columns(which):
        one = panel[:, pl.ds(pl.multiple_of(which * LANES, LANES), LANES)]
        two = panel[:, pl.ds(pl.multiple_of((2 + which) * LANES, LANES), LANES)]
        return lax.dot_general(
            everything,
            jnp.concatenate([one, two], axis=1),
            (((0,), (0,)), ((), ())),
            preferred_element_type=F32,
        )

    keep = columns(core)
    send = columns(1 - core)
    if not first:
        keep = keep + refs[parts][...]
        send = send + refs[parts + 1][...]
    keep_ref[:size] = keep
    send_ref[:size] = send
    if not last:
        return

    rows = lax.broadcasted_iota(jnp.int32, (LANES, LANES), 0)
    cols = lax.broadcasted_iota(jnp.int32, (LANES, LANES), 1)
    eye = rows == cols

    def diagonal(which):
        side = which // 2
        a = keep_ref[which * LANES : (which + 1) * LANES, side * LANES : (side + 1) * LANES]
        b = send_ref[which * LANES : (which + 1) * LANES, side * LANES : (side + 1) * LANES]
        block = jnp.where(core == which % 2, a, b)
        return jnp.sum(jnp.where(eye, block, 0.0), axis=0, keepdims=True)

    diag = [diagonal(n) for n in range(parts)]
    row0 = jnp.concatenate(diag[:2], axis=1)
    row1 = jnp.concatenate(diag[2:], axis=1)
    tail = jnp.concatenate([row0, row1, jnp.zeros((6, 2 * LANES), F32)], axis=0)
    keep_ref[size:] = tail
    send_ref[size:] = tail


def gram(parts, fields, before, last):
    size = parts * LANES
    depth, across, along, _ = fields[0].shape
    shape = jax.ShapeDtypeStruct((size + 8 * last, 2 * LANES), F32)
    operands = list(fields) + list(before)
    return pl.pallas_call(
        functools.partial(gram_body, parts, not before, last),
        in_specs=whole_vmem(len(operands)),
        out_specs=whole_vmem(2),
        out_shape=[shape, shape],
        scratch_shapes=[pltpu.VMEM((depth * across * along, size), BF16)],
        compiler_params=params(),
    )(*operands)


def rounded(ref, block, tail):
    count = block.shape[0]
    high = tail.astype(BF16)
    low = tail - high.astype(F32)
    ref[:count] = block.astype(BF16)
    ref[count:] = jnp.concatenate([high.astype(F32), low], axis=0).astype(BF16)


def opened(ref):
    count = ref.shape[0] - 16
    tail = ref[count:].astype(F32)
    return ref[:count].astype(F32), tail[:8] + tail[8:]


def rows_body(slabs, count, keep_ref, got_ref, own_ref, *outs):
    slab = lax.axis_index("slab")
    size = slabs * count
    tail = keep_ref[pl.ds(size, 8)] + got_ref[pl.ds(size, 8)]
    for d in range(slabs):
        owner = slab ^ d
        span = pl.ds(pl.multiple_of(owner * count, count), count)
        block = keep_ref[span] + got_ref[span]
        if d == 0:
            own_ref[:count] = block
            own_ref[count:] = tail
        else:
            rounded(outs[d - 1], block, tail)


def split_rows(keep, got, slabs):
    count = (keep.shape[0] - 8) // slabs
    own = jax.ShapeDtypeStruct((count + 8, keep.shape[1]), F32)
    sent = jax.ShapeDtypeStruct((count + 16, keep.shape[1]), BF16)
    return pl.pallas_call(
        functools.partial(rows_body, slabs, count),
        in_specs=whole_vmem(2),
        out_specs=whole_vmem(slabs),
        out_shape=[own] + [sent] * (slabs - 1),
        compiler_params=params(),
    )(keep, got)


def sum_body(own_ref, *refs):
    count = own_ref.shape[0] - 8
    block, tail = own_ref[:count], own_ref[count:]
    for ref in refs[:-1]:
        more, more_tail = opened(ref)
        block, tail = block + more, tail + more_tail
    rounded(refs[-1], block, tail)


def sum_all(own, others):
    return pl.pallas_call(
        sum_body,
        in_specs=whole_vmem(1 + len(others)),
        out_specs=whole_vmem(1)[0],
        out_shape=jax.ShapeDtypeStruct(others[0].shape, BF16),
        compiler_params=params(),
    )(own, *others)


def normalise_body(cell_count, mine_ref, other_ref, out_ref, norms_ref):
    slab = lax.axis_index("slab")
    core = lax.axis_index("sub")
    one, one_tail = opened(mine_ref)
    two, two_tail = opened(other_ref)
    total = one + two
    norms = jnp.sqrt((one_tail + two_tail)[:2] / cell_count + EPSILON)
    blocks = [norms[n // 2 : n // 2 + 1, (n % 2) * LANES : (n % 2 + 1) * LANES] for n in range(4)]
    own = blocks[0]
    for n in range(1, 4):
        own = jnp.where(slab == n, blocks[n], own)
    norms_ref[...] = own
    rows = lax.broadcasted_iota(jnp.int32, (LANES, LANES), 0)
    cols = lax.broadcasted_iota(jnp.int32, (LANES, LANES), 1)
    eye = rows == cols
    own_column = jnp.sum(
        jnp.where(eye, jnp.broadcast_to(own, (LANES, LANES)), 0.0), axis=1, keepdims=True
    )
    for side in range(2):
        columns = slice(side * LANES, (side + 1) * LANES)
        others = jnp.where(core == 0, blocks[2 * side], blocks[2 * side + 1])
        value = total[:, columns] / math.sqrt(cell_count) / (own_column * others)
        out_ref[:, columns] = jnp.where(eye & (2 * side + core == slab), 0.0, value)


def normalise(mine, other, cell_count):
    count = mine.shape[0] - 16
    return pl.pallas_call(
        functools.partial(normalise_body, cell_count),
        in_specs=whole_vmem(2),
        out_specs=whole_vmem(2),
        out_shape=[
            jax.ShapeDtypeStruct((count, 2 * LANES), F32),
            jax.ShapeDtypeStruct((1, LANES), F32),
        ],
        compiler_params=params(),
    )(mine, other)


def assemble_body(near_ref, far_ref, out_ref):
    core = lax.axis_index("sub")
    for side in range(2):
        columns = slice(side * LANES, (side + 1) * LANES)
        for ref, which in ((near_ref, core), (far_ref, 1 - core)):
            start = pl.multiple_of((2 * side + which) * LANES, LANES)
            out_ref[:, pl.ds(start, LANES)] = ref[:, columns]


def assemble(near, far):
    return pl.pallas_call(
        assemble_body,
        in_specs=whole_vmem(2),
        out_specs=whole_vmem(1)[0],
        out_shape=jax.ShapeDtypeStruct((near.shape[0], 4 * LANES), F32),
        compiler_params=params(),
    )(near, far)


def coupled(groups, cell_count):
    slabs = 4
    sums = ()
    for n, fields in enumerate(groups):
        sums = gram(4, fields, sums, n == len(groups) - 1)
    keep, send = sums
    got = core_swap(send)
    own, *sent = split_rows(keep, got, slabs)
    arrived = [
        lax.ppermute(sent[d - 1], "slab", [(i, i ^ d) for i in range(slabs)]) for d in (2, 3, 1)
    ]
    mine = sum_all(own, arrived)
    other = chip_swap(mine)
    near, norms = normalise(mine, other, cell_count)
    far = core_swap(near)
    return assemble(near, far), norms.reshape(-1)


def coupled_general(fields, cell_count):
    chips = lax.axis_size("probe")
    sketch = jnp.concatenate(fields, axis=-1)
    sketch = sketch.reshape(-1, sketch.shape[-1])
    if chips > 1:
        sketch = lax.all_to_all(sketch, "probe", split_axis=0, concat_axis=1, tiled=True)
    partial_gram = lax.dot_general(
        sketch, sketch, (((0,), (0,)), ((), ())), preferred_element_type=F32
    )
    rows = lax.psum_scatter(partial_gram, "slab", scatter_dimension=0, tiled=True)
    rows = lax.psum(rows, ("probe", "sub"))
    count = rows.shape[0]
    start = lax.axis_index("slab") * count
    own = jnp.diagonal(lax.dynamic_slice_in_dim(rows, start, count, 1))
    own_norms = jnp.sqrt(own / cell_count + EPSILON)
    norms = lax.all_gather(own_norms, "slab", axis=0, tiled=True)
    coupling = rows / math.sqrt(cell_count) / (own_norms[:, None] * norms[None, :])
    row_ids = start + lax.broadcasted_iota(jnp.int32, coupling.shape, 0)
    col_ids = lax.broadcasted_iota(jnp.int32, coupling.shape, 1)
    return jnp.where(row_ids == col_ids, 0.0, coupling), own_norms


def shards(probes, courant, source):
    depth, across, along, count = probes.shape
    chunks = count // LANES
    slabs, chips = lax.axis_size("slab"), lax.axis_size("probe")
    cell_count = depth * across * along * slabs * lax.axis_size("sub")
    paired = chips == 2 and slabs == 4 and chunks == 2 and depth == 2 * RADIUS
    steps = source.shape[0]
    courant = courant.reshape(depth * across, along)
    source = source.reshape(steps, depth * across, along)

    now, previous, halos = [], [None] * chunks, []
    for c in range(chunks):
        u, even, odd, edge = first_field(probes, c, source)
        now.append(u)
        halos.append((even_swap(even), odd_swap(odd), core_swap(edge)))
    parts = 2 if paired else 1
    finals, order = [], ()
    for n in range(1, steps):
        for c in range(chunks):
            even, odd, beside = halos[c]
            if n == 1:
                (base,) = local_step(
                    now[c], beside, probes, c, courant, source, n, previous[c]
                )
            else:
                base = beside
            if n == steps - 1:
                finals.append((base, even, odd))
                continue
            ahead = n == steps - 2
            pieces = parts if ahead else 1
            out = rim_step(base, even, odd, courant, "middle", parts=pieces, after=order)
            previous[c], now[c] = now[c], out[0]
            evens, odds, edge = out[1 : 1 + pieces], out[1 + pieces : 1 + 2 * pieces], out[-1]
            odd = odd_swap(odds[0])
            base, *rest = local_step(
                now[c],
                core_swap(edge),
                probes,
                c,
                courant,
                source,
                n + 1,
                previous[c],
                carry=list(evens) + list(odds[1:]),
            )
            order = (base,)
            halos[c] = ([rest[:pieces], [odd], rest[pieces:]], None, base) if ahead else (
                even_swap(rest[0]),
                odd,
                base,
            )
    if not paired:
        fields = []
        for base, ((even,), (odd,), _), _ in finals:
            fields += rim_step(base, even_swap(even), odd, courant, "all")
        return coupled_general(fields, cell_count)

    width = across // parts
    groups = [[] for _ in range(parts)]
    waiting = None
    for c, (base, (evens, (odd,), odds), _) in enumerate(finals):
        if c == 0:
            waiting = finals[1][1]
        halves_even = [even_swap(evens[0])]
        halves_odd = [odd]
        for h in range(1, parts):
            halves_even.append(even_swap(evens[h]))
            halves_odd.append(odd_swap(odds[h - 1]))
        for h in range(parts):
            carry = ()
            if c == 0 and h == 0:
                carry = (waiting[0][1], waiting[2][0])
            sent, *rest = last_step(
                base, halves_even[h], halves_odd[h], courant, h * width, True, carry
            )
            if rest:
                waiting[0][1], waiting[2][0] = rest
            (kept,) = last_step(base, halves_even[h], halves_odd[h], courant, h * width, False)
            groups[h] += [kept, chip_swap(sent)]
    return coupled(groups, cell_count)


def solution(mesh):
    placed = (
        P(("groups", "slab"), "sub", None, "probe"),
        P("slab", "sub", None),
        P(None, ("groups", "slab"), "sub", None),
    )
    return jax.shard_map(
        shards,
        mesh=mesh,
        in_specs=placed,
        out_specs=(P(("groups", "slab"), None), P(("groups", "slab"))),
        check_vma=False,
    )
```

```python
import functools
import math

import jax
import jax.numpy as jnp
from jax import lax
from jax.experimental import pallas as pl
from jax.experimental.pallas import tpu as pltpu
from jax.sharding import PartitionSpec as P

COEFFICIENTS = (-205.0 / 72.0, 8.0 / 5.0, -1.0 / 5.0, 8.0 / 315.0, -1.0 / 560.0)
EPSILON = 1e-06
LANES = 128
RADIUS = 4
EDGE = 8
TILE = 16
F32 = jnp.float32
BF16 = jnp.bfloat16
VMEM_LIMIT = 32 * 1024 * 1024


def params(*semantics):
    return pltpu.CompilerParams(
        dimension_semantics=semantics or None, vmem_limit_bytes=VMEM_LIMIT
    )


def whole_vmem(count):
    return [pl.BlockSpec(memory_space=pltpu.VMEM)] * count


def shape_of(depth, across, along, dtype):
    return jax.ShapeDtypeStruct((depth, across, along, LANES), dtype)


def turned(field, scratch):
    rows, along = field.shape
    scratch[:rows, :along] = field
    return jnp.transpose(scratch[...])


def lane(values, n):
    return jnp.broadcast_to(values[:, n : n + 1], (values.shape[0], LANES))


def store_edges(x, span, news, even, even_ref, odd_ref):
    for j in range(RADIUS):
        low = news[j].astype(BF16)
        high = news[len(news) - RADIUS + j].astype(BF16)
        even_ref[j, x, span] = jnp.where(even, high, low)
        odd_ref[j, x, span] = jnp.where(even, low, high)


def store_beside(span, rows, core, u_ref, edge_ref):
    depth, across, _, _ = u_ref.shape
    first = (across - RADIUS) * (1 - core)
    for z in range(depth):
        for j in range(RADIUS):
            edge_ref[z, j, span] = u_ref[z, first + j, rows].astype(BF16)


def slab_is_even():
    return lax.rem(lax.axis_index("slab"), 2) == 0


def clear_pads(u_ref):
    depth, across, padded, _ = u_ref.shape

    def plane(z, _):
        blank = jnp.zeros((across, EDGE, LANES), F32)
        u_ref[z, :, pl.ds(0, EDGE)] = blank
        u_ref[z, :, pl.ds(padded - EDGE, EDGE)] = blank
        return 0

    lax.fori_loop(0, depth, plane, 0)


def tiles(along, body):
    def one(t, _):
        body(pl.multiple_of(t * TILE, TILE))
        return 0

    lax.fori_loop(0, along // TILE, one, 0)


def first_body(chunk, p_ref, s_ref, u_ref, even_ref, odd_ref, edge_ref, square, turned_s):
    depth, across, padded, _ = u_ref.shape
    along = padded - 2 * EDGE
    core = lax.axis_index("sub")
    even = slab_is_even()
    turned_s[...] = turned(s_ref[0], square)
    clear_pads(u_ref)

    def tile(start):
        span = pl.ds(start, TILE)
        rows = pl.ds(start + EDGE, TILE)
        source = turned_s[span]
        for x in range(across):
            news = []
            for z in range(depth):
                p = p_ref[z, x, span, chunk * LANES : (chunk + 1) * LANES].astype(F32)
                new = lane(source, z * across + x) * p
                u_ref[z, x, rows] = new
                news.append(new)
            store_edges(x, span, news, even, even_ref, odd_ref)
        store_beside(span, rows, core, u_ref, edge_ref)

    tiles(along, tile)


def square_scratch():
    return [pltpu.VMEM((LANES, LANES), F32)] * 2


def first_field(probes, chunk, source):
    depth, across, along, _ = probes.shape
    return pl.pallas_call(
        functools.partial(first_body, chunk),
        in_specs=whole_vmem(2),
        out_specs=whole_vmem(4),
        out_shape=[
            shape_of(depth, across, along + 2 * EDGE, F32),
            shape_of(RADIUS, across, along, BF16),
            shape_of(RADIUS, across, along, BF16),
            shape_of(depth, RADIUS, along, BF16),
        ],
        scratch_shapes=square_scratch(),
        compiler_params=params(),
    )(probes, source)


def local_body(chunk, moment, has_previous, *refs):
    refs = list(refs)
    u_ref, beside_ref, p_ref, c_ref, s_ref = refs[:5]
    prev_ref = refs[5] if has_previous else None
    base_ref, square, turned_c, turned_s = refs[-4:]
    depth, across, along, _ = base_ref.shape
    core = lax.axis_index("sub")
    left_on = (core == 1).astype(F32)
    right_on = (core == 0).astype(F32)
    turned_c[...] = turned(c_ref[...], square)
    turned_s[...] = turned(s_ref[moment], square)

    def tile(start):
        span = pl.ds(start, TILE)
        rows = start + EDGE
        courant = turned_c[span]
        source = turned_s[span]
        for z in range(depth):
            beside = [beside_ref[z, j, span].astype(F32) for j in range(RADIUS)]
            row = [v * left_on for v in beside]
            row += [u_ref[z, x, pl.ds(rows, TILE)] for x in range(across)]
            row += [v * right_on for v in beside]
            for x in range(across):
                here = row[RADIUS + x]
                total = (3.0 * COEFFICIENTS[0]) * here
                for r in range(1, RADIUS + 1):
                    near = row[RADIUS + x + r] + row[RADIUS + x - r]
                    near = near + (
                        u_ref[z, x, pl.ds(rows + r, TILE)] + u_ref[z, x, pl.ds(rows - r, TILE)]
                    )
                    if z + r < depth:
                        near = near + u_ref[z + r, x, pl.ds(rows, TILE)]
                    if z - r >= 0:
                        near = near + u_ref[z - r, x, pl.ds(rows, TILE)]
                    total = total + COEFFICIENTS[r] * near
                cell = z * across + x
                p = p_ref[z, x, span, chunk * LANES : (chunk + 1) * LANES].astype(F32)
                new = 2.0 * here
                if has_previous:
                    new = new - prev_ref[z, x, pl.ds(rows, TILE)]
                new = new + lane(courant, cell) * total + lane(source, cell) * p
                base_ref[z, x, span] = new

    tiles(along, tile)


def local_step(u, beside, probes, chunk, courant, source, moment, previous):
    depth, across, along, _ = probes.shape
    operands = [u, beside, probes, courant, source]
    if previous is not None:
        operands.append(previous)
    return pl.pallas_call(
        functools.partial(local_body, chunk, moment, previous is not None),
        in_specs=whole_vmem(len(operands)),
        out_specs=whole_vmem(1)[0],
        out_shape=shape_of(depth, across, along, F32),
        scratch_shapes=square_scratch() + square_scratch()[:1],
        compiler_params=params(),
    )(*operands)


def rim_body(middle, *refs):
    base_ref, even_ref, odd_ref, c_ref = refs[:4]
    outs, (square, turned_c) = refs[4:-2], refs[-2:]
    depth, across, along, _ = base_ref.shape
    core = lax.axis_index("sub")
    even = slab_is_even()
    turned_c[...] = turned(c_ref[...], square)
    if middle:
        clear_pads(outs[0])

    def tile(start):
        span = pl.ds(start, TILE)
        rows = pl.ds(start + EDGE, TILE)
        courant = turned_c[span]
        for x in range(across):
            below, above = [], []
            for j in range(RADIUS):
                one, two = even_ref[j, x, span], odd_ref[j, x, span]
                below.append(jnp.where(even, two, one).astype(F32))
                above.append(jnp.where(even, one, two).astype(F32))
            news = []
            for z in range(depth):
                added = None
                for r in range(1, RADIUS + 1):
                    if z - r < 0:
                        term = COEFFICIENTS[r] * below[RADIUS + z - r]
                        added = term if added is None else added + term
                    if z + r >= depth:
                        term = COEFFICIENTS[r] * above[z + r - depth]
                        added = term if added is None else added + term
                new = base_ref[z, x, span]
                if added is not None:
                    new = new + lane(courant, z * across + x) * added
                news.append(new)
            if middle:
                for z, new in enumerate(news):
                    outs[0][z, x, rows] = new
                store_edges(x, span, news, even, outs[1], outs[2])
            else:
                for z, new in enumerate(news):
                    outs[0][z, x, span] = new.astype(BF16)
        if middle:
            store_beside(span, rows, core, outs[0], outs[3])

    tiles(along, tile)


def rim_step(base, evens, odds, courant, middle):
    depth, across, along, _ = base.shape
    if middle:
        out_shape = [
            shape_of(depth, across, along + 2 * EDGE, F32),
            shape_of(RADIUS, across, along, BF16),
            shape_of(RADIUS, across, along, BF16),
            shape_of(depth, RADIUS, along, BF16),
        ]
    else:
        out_shape = [shape_of(depth, across, along, BF16)]
    return pl.pallas_call(
        functools.partial(rim_body, middle),
        in_specs=whole_vmem(4),
        out_specs=whole_vmem(len(out_shape)),
        out_shape=out_shape,
        scratch_shapes=square_scratch(),
        compiler_params=params(),
    )(base, evens, odds, courant)


def last_body(sent, base_ref, even_ref, odd_ref, c_ref, out_ref, square, turned_c):
    depth, across, along, _ = base_ref.shape
    chip = lax.axis_index("probe")
    low = (chip == 1) if sent else (chip == 0)
    from_odd = low == slab_is_even()
    turned_c[...] = turned(c_ref[...], square)

    def tile(start):
        span = pl.ds(start, TILE)
        courant = turned_c[span]
        for x in range(across):
            near = []
            for j in range(RADIUS):
                at = jnp.where(low, RADIUS - 1 - j, j)
                near.append(
                    jnp.where(from_odd, odd_ref[at, x, span], even_ref[at, x, span]).astype(F32)
                )
            for m in range(RADIUS):
                mirror = depth - 1 - m
                added = COEFFICIENTS[m + 1] * near[0]
                for r in range(m + 2, RADIUS + 1):
                    added = added + COEFFICIENTS[r] * near[r - m - 1]
                scale = jnp.where(
                    low, lane(courant, m * across + x), lane(courant, mirror * across + x)
                )
                new = base_ref[jnp.where(low, m, mirror), x, span] + scale * added
                out_ref[m, x, span] = new.astype(BF16)

    tiles(along, tile)


def last_step(base, evens, odds, courant, sent):
    _, across, along, _ = base.shape
    return pl.pallas_call(
        functools.partial(last_body, sent),
        in_specs=whole_vmem(4),
        out_specs=whole_vmem(1)[0],
        out_shape=shape_of(RADIUS, across, along, BF16),
        scratch_shapes=square_scratch(),
        compiler_params=params(),
    )(base, evens, odds, courant)


def swap(x, axis, pairs):
    return lax.ppermute(x, axis, [p for a, b in pairs for p in ((a, b), (b, a))])


def even_swap(x):
    return swap(x, "slab", [(i, i + 1) for i in range(0, lax.axis_size("slab") - 1, 2)])


def odd_swap(x):
    return swap(x, "slab", [(i, i + 1) for i in range(1, lax.axis_size("slab") - 1, 2)])


def core_swap(x):
    return swap(x, "sub", [(0, 1)])


def chip_swap(x):
    return swap(x, "probe", [(0, 1)])


def product(a, b):
    return lax.dot_general(a, b, (((0,), (0,)), ((), ())), preferred_element_type=F32)


def block_of(array, i, j):
    return array[i * LANES : (i + 1) * LANES, j * LANES : (j + 1) * LANES]


def eye():
    rows = lax.broadcasted_iota(jnp.int32, (LANES, LANES), 0)
    cols = lax.broadcasted_iota(jnp.int32, (LANES, LANES), 1)
    return rows == cols


def inner_body(kept0, sent0, kept1, sent1, keep_ref, send_ref, diag_ref, panel):
    half = panel.shape[0] // 2
    for n, (kept, sent) in enumerate(((kept0, sent0), (kept1, sent1))):
        columns = slice(n * LANES, (n + 1) * LANES)
        panel[:half, columns] = kept[...].reshape(half, LANES)
        panel[half:, columns] = sent[...].reshape(half, LANES)
    core = lax.axis_index("sub")
    whole = product(panel[...], panel[...])
    first, second = whole[:, :LANES], whole[:, LANES:]
    keep_ref[...] = jnp.where(core == 0, first, second)
    send_ref[...] = jnp.where(core == 0, second, first)
    diag = [
        jnp.sum(jnp.where(eye(), block_of(whole, n, n), 0.0), axis=0, keepdims=True)
        for n in range(2)
    ]
    none = jnp.zeros_like(diag[0])
    chip = lax.axis_index("probe")
    rows = [jnp.where(chip == n // 2, diag[n % 2], none) for n in range(4)]
    diag_ref[...] = jnp.concatenate(rows + [none] * 4, axis=0)


def inner_gram(fields):
    size = 2 * LANES
    cells = 2 * math.prod(fields[0].shape[:3])
    half = jax.ShapeDtypeStruct((size, LANES), F32)
    return pl.pallas_call(
        inner_body,
        in_specs=whole_vmem(4),
        out_specs=whole_vmem(3),
        out_shape=[half, half, jax.ShapeDtypeStruct((8, LANES), F32)],
        scratch_shapes=[pltpu.VMEM((cells, size), BF16)],
        compiler_params=params(),
    )(*fields)


def inner_rows_body(keep_ref, got_ref, *outs):
    slab = lax.axis_index("slab")
    chip = lax.axis_index("probe")
    for d, out in enumerate(outs):
        row = jnp.clip((slab ^ d) - 2 * chip, 0, 1)
        span = pl.ds(pl.multiple_of(row * LANES, LANES), LANES)
        out[...] = keep_ref[span] + got_ref[span]


def inner_rows(keep, got, slabs):
    block = jax.ShapeDtypeStruct((LANES, LANES), F32)
    return pl.pallas_call(
        inner_rows_body,
        in_specs=whole_vmem(2),
        out_specs=whole_vmem(slabs),
        out_shape=[block] * slabs,
        compiler_params=params(),
    )(keep, got)


def cross_body(kept0, got0, kept1, got1, keep_ref, send_ref, panel):
    chip = lax.axis_index("probe")
    core = lax.axis_index("sub")
    cells = panel.shape[0]
    for n, (kept, got) in enumerate(((kept0, got0), (kept1, got1))):
        mine = pl.multiple_of((chip * 2 + n) * LANES, LANES)
        other = pl.multiple_of(((1 - chip) * 2 + n) * LANES, LANES)
        panel[:, pl.ds(mine, LANES)] = kept[...].reshape(cells, LANES)
        panel[:, pl.ds(other, LANES)] = got[...].reshape(cells, LANES)
    whole = product(panel[:, : 2 * LANES], panel[:, 2 * LANES :])
    for ref, which in ((keep_ref, core), (send_ref, 1 - core)):
        here = which == 0
        ref[:LANES] = jnp.where(here, block_of(whole, 0, 0), block_of(whole, 0, 1))
        ref[LANES : 2 * LANES] = jnp.where(here, block_of(whole, 1, 0), block_of(whole, 1, 1))
        mixed = jnp.where(here, block_of(whole, 0, 1), block_of(whole, 1, 0))
        ref[2 * LANES :] = mixed


def cross_gram(fields):
    cells = math.prod(fields[0].shape[:3])
    three = jax.ShapeDtypeStruct((3 * LANES, LANES), F32)
    return pl.pallas_call(
        cross_body,
        in_specs=whole_vmem(4),
        out_specs=whole_vmem(2),
        out_shape=[three, three],
        scratch_shapes=[pltpu.VMEM((cells, 4 * LANES), BF16)],
        compiler_params=params(),
    )(*fields)


def rounded(ref, block, tail):
    count = block.shape[0]
    high = tail.astype(BF16)
    low = tail - high.astype(F32)
    ref[:count] = block.astype(BF16)
    ref[count : count + 16] = jnp.concatenate([high.astype(F32), low], axis=0).astype(BF16)


def opened(ref, count):
    tail = ref[count : count + 16].astype(F32)
    return ref[:count].astype(F32), tail[:8] + tail[8:]


def cross_rows_body(keep_ref, got_ref, diag_ref, other_diag_ref, own_ref, *outs):
    slab = lax.axis_index("slab")
    core = lax.axis_index("sub")
    tail = diag_ref[...] + other_diag_ref[...]
    for d in range(len(outs) + 1):
        owner = slab ^ d
        late = jnp.where(core == 0, jnp.where(owner == 2, 0, 2), jnp.where(owner == 2, 2, 1))
        at = jnp.where(owner < 2, owner, late)
        span = pl.ds(pl.multiple_of(at * LANES, LANES), LANES)
        block = keep_ref[span] + got_ref[span]
        if d == 0:
            own_ref[:LANES] = block
            own_ref[LANES:] = tail
        else:
            rounded(outs[d - 1], block, tail)


def cross_rows(keep, got, diag, other_diag, slabs):
    own = jax.ShapeDtypeStruct((LANES + 8, LANES), F32)
    sent = jax.ShapeDtypeStruct((LANES + 16, LANES), BF16)
    return pl.pallas_call(
        cross_rows_body,
        in_specs=whole_vmem(4),
        out_specs=whole_vmem(slabs),
        out_shape=[own] + [sent] * (slabs - 1),
        compiler_params=params(),
    )(keep, got, diag, other_diag)


def sum_body(slabs, own_ref, *refs):
    block, tail = own_ref[:LANES], own_ref[LANES:]
    for ref in refs[: slabs - 1]:
        more, more_tail = opened(ref, LANES)
        block, tail = block + more, tail + more_tail
    inner = refs[slabs - 1][...]
    for ref in refs[slabs : 2 * slabs - 1]:
        inner = inner + ref[...]
    out_ref = refs[-1]
    rounded(out_ref, block, tail)
    out_ref[LANES + 16 :] = inner.astype(BF16)


def sum_all(own, others, inner, inner_others):
    slabs = 1 + len(others)
    return pl.pallas_call(
        functools.partial(sum_body, slabs),
        in_specs=whole_vmem(2 * slabs),
        out_specs=whole_vmem(1)[0],
        out_shape=jax.ShapeDtypeStruct((2 * LANES + 16, LANES), BF16),
        compiler_params=params(),
    )(own, *others, inner, *inner_others)


def normalise_body(cell_count, mine_ref, other_ref, out_ref, norms_ref):
    slab = lax.axis_index("slab")
    core = lax.axis_index("sub")
    chip = lax.axis_index("probe")
    one, one_tail = opened(mine_ref, LANES)
    two, two_tail = opened(other_ref, LANES)
    cross = one + two
    inner_span = pl.ds(LANES + 16, LANES)
    inner = jnp.where(slab // 2 == chip, mine_ref[inner_span], other_ref[inner_span]).astype(F32)
    upper = slab < 2
    values = [jnp.where(upper, inner, cross.T), jnp.where(upper, cross, inner)]
    norms = jnp.sqrt((one_tail + two_tail) / cell_count + EPSILON)
    blocks = [norms[n : n + 1] for n in range(4)]
    own = blocks[0]
    for n in range(1, 4):
        own = jnp.where(slab == n, blocks[n], own)
    norms_ref[...] = own
    own_column = jnp.sum(
        jnp.where(eye(), jnp.broadcast_to(own, (LANES, LANES)), 0.0), axis=1, keepdims=True
    )
    for side in range(2):
        others = jnp.where(core == 0, blocks[2 * side], blocks[2 * side + 1])
        value = values[side] / math.sqrt(cell_count) / (own_column * others)
        value = jnp.where(eye() & (2 * side + core == slab), 0.0, value)
        out_ref[:, side * LANES : (side + 1) * LANES] = value


def normalise(mine, other, cell_count):
    return pl.pallas_call(
        functools.partial(normalise_body, cell_count),
        in_specs=whole_vmem(2),
        out_specs=whole_vmem(2),
        out_shape=[
            jax.ShapeDtypeStruct((LANES, 2 * LANES), F32),
            jax.ShapeDtypeStruct((1, LANES), F32),
        ],
        compiler_params=params(),
    )(mine, other)


def assemble_body(near_ref, far_ref, out_ref):
    core = lax.axis_index("sub")
    for side in range(2):
        columns = slice(side * LANES, (side + 1) * LANES)
        for ref, which in ((near_ref, core), (far_ref, 1 - core)):
            start = pl.multiple_of((2 * side + which) * LANES, LANES)
            out_ref[:, pl.ds(start, LANES)] = ref[:, columns]


def assemble(near, far):
    return pl.pallas_call(
        assemble_body,
        in_specs=whole_vmem(2),
        out_specs=whole_vmem(1)[0],
        out_shape=jax.ShapeDtypeStruct((near.shape[0], 4 * LANES), F32),
        compiler_params=params(),
    )(near, far)


def coupled(finals, cell_count):
    slabs = 4
    own = [field for kept, sent, _ in finals for field in (kept, sent)]
    keep, send, diag = inner_gram(own)
    inner = inner_rows(keep, core_swap(send), slabs)
    other_diag = core_swap(diag)
    inner_arrived = []
    for d in (2, 3, 1):
        pairs = [
            (2 * (k ^ d) + chip, 2 * k + chip)
            for chip in range(2)
            for k in (2 * chip, 2 * chip + 1)
        ]
        inner_arrived.append(lax.ppermute(inner[d], ("slab", "probe"), pairs))

    keep, send = cross_gram([field for kept, _, got in finals for field in (kept, got)])
    mine, *blocks = cross_rows(keep, core_swap(send), diag, other_diag, slabs)
    arrived = [
        lax.ppermute(blocks[d - 1], "slab", [(i, i ^ d) for i in range(slabs)])
        for d in (2, 3, 1)
    ]
    total = sum_all(mine, arrived, inner[0], inner_arrived)
    near, norms = normalise(total, chip_swap(total), cell_count)
    return assemble(near, core_swap(near)), norms.reshape(-1)


def coupled_general(fields, cell_count):
    chips = lax.axis_size("probe")
    sketch = jnp.concatenate(fields, axis=-1)
    sketch = sketch.reshape(-1, sketch.shape[-1])
    if chips > 1:
        sketch = lax.all_to_all(sketch, "probe", split_axis=0, concat_axis=1, tiled=True)
    partial_gram = lax.dot_general(
        sketch, sketch, (((0,), (0,)), ((), ())), preferred_element_type=F32
    )
    rows = lax.psum_scatter(partial_gram, "slab", scatter_dimension=0, tiled=True)
    rows = lax.psum(rows, ("probe", "sub"))
    count = rows.shape[0]
    start = lax.axis_index("slab") * count
    own = jnp.diagonal(lax.dynamic_slice_in_dim(rows, start, count, 1))
    own_norms = jnp.sqrt(own / cell_count + EPSILON)
    norms = lax.all_gather(own_norms, "slab", axis=0, tiled=True)
    coupling = rows / math.sqrt(cell_count) / (own_norms[:, None] * norms[None, :])
    row_ids = start + lax.broadcasted_iota(jnp.int32, coupling.shape, 0)
    col_ids = lax.broadcasted_iota(jnp.int32, coupling.shape, 1)
    return jnp.where(row_ids == col_ids, 0.0, coupling), own_norms


def shards(probes, courant, source):
    depth, across, along, count = probes.shape
    chunks = count // LANES
    slabs, chips = lax.axis_size("slab"), lax.axis_size("probe")
    cell_count = depth * across * along * slabs * lax.axis_size("sub")
    paired = chips == 2 and slabs == 4 and chunks == 2 and depth == 2 * RADIUS
    steps = source.shape[0]
    courant = courant.reshape(depth * across, along)
    source = source.reshape(steps, depth * across, along)

    exchange = lambda even, odd, edge: (even_swap(even), odd_swap(odd), core_swap(edge))
    now, previous, halos = [], [None] * chunks, []
    for c in range(chunks):
        u, *edges = first_field(probes, c, source)
        now.append(u)
        halos.append(exchange(*edges))
    finals = []
    for n in range(1, steps):
        for c in range(chunks):
            even, odd, beside = halos[c]
            base = local_step(now[c], beside, probes, c, courant, source, n, previous[c])
            if n < steps - 1:
                u, *edges = rim_step(base, even, odd, courant, True)
                previous[c], now[c] = now[c], u
                halos[c] = exchange(*edges)
            elif paired:
                sent = last_step(base, even, odd, courant, True)
                kept = last_step(base, even, odd, courant, False)
                finals.append((kept, sent, chip_swap(sent)))
            else:
                finals += rim_step(base, even, odd, courant, False)
    return (coupled if paired else coupled_general)(finals, cell_count)


def solution(mesh):
    placed = (
        P(("groups", "slab"), "sub", None, "probe"),
        P("slab", "sub", None),
        P(None, ("groups", "slab"), "sub", None),
    )
    return jax.shard_map(
        shards,
        mesh=mesh,
        in_specs=placed,
        out_specs=(P(("groups", "slab"), None), P(("groups", "slab"))),
        check_vma=False,
    )
```

```python
import functools
import math

import jax
import jax.numpy as jnp
from jax import lax
from jax.experimental import pallas as pl
from jax.experimental.pallas import tpu as pltpu
from jax.sharding import PartitionSpec as P

COEFFICIENTS = (-205.0 / 72.0, 8.0 / 5.0, -1.0 / 5.0, 8.0 / 315.0, -1.0 / 560.0)
EPSILON = 1e-06
LANES = 128
RADIUS = 4
EDGE = 8
TILE = 16
F32 = jnp.float32
BF16 = jnp.bfloat16
VMEM_LIMIT = 32 * 1024 * 1024


def params(*semantics):
    return pltpu.CompilerParams(
        dimension_semantics=semantics or None, vmem_limit_bytes=VMEM_LIMIT
    )


def whole_vmem(count):
    return [pl.BlockSpec(memory_space=pltpu.VMEM)] * count


def shape_of(depth, across, along, dtype):
    return jax.ShapeDtypeStruct((depth, across, along, LANES), dtype)


def turned(field, scratch):
    rows, along = field.shape
    scratch[:rows, :along] = field
    return jnp.transpose(scratch[...])


def lane(values, n):
    return jnp.broadcast_to(values[:, n : n + 1], (values.shape[0], LANES))


def store_edges(x, span, news, even, even_ref, odd_ref):
    for j in range(RADIUS):
        low = news[j].astype(BF16)
        high = news[len(news) - RADIUS + j].astype(BF16)
        even_ref[j, x, span] = jnp.where(even, high, low)
        odd_ref[j, x, span] = jnp.where(even, low, high)


def store_beside(span, rows, core, u_ref, edge_ref):
    depth, across, _, _ = u_ref.shape
    first = (across - RADIUS) * (1 - core)
    for z in range(depth):
        for j in range(RADIUS):
            edge_ref[z, j, span] = u_ref[z, first + j, rows].astype(BF16)


def slab_is_even():
    return lax.rem(lax.axis_index("slab"), 2) == 0


def clear_pads(u_ref):
    depth, across, padded, _ = u_ref.shape

    def plane(z, _):
        blank = jnp.zeros((across, EDGE, LANES), F32)
        u_ref[z, :, pl.ds(0, EDGE)] = blank
        u_ref[z, :, pl.ds(padded - EDGE, EDGE)] = blank
        return 0

    lax.fori_loop(0, depth, plane, 0)


def tiles(along, body):
    def one(t, _):
        body(pl.multiple_of(t * TILE, TILE))
        return 0

    lax.fori_loop(0, along // TILE, one, 0)


def first_body(chunk, p_ref, s_ref, u_ref, even_ref, odd_ref, edge_ref, square, turned_s):
    depth, across, padded, _ = u_ref.shape
    along = padded - 2 * EDGE
    core = lax.axis_index("sub")
    even = slab_is_even()
    turned_s[...] = turned(s_ref[0], square)
    clear_pads(u_ref)

    def tile(start):
        span = pl.ds(start, TILE)
        rows = pl.ds(start + EDGE, TILE)
        source = turned_s[span]
        for x in range(across):
            news = []
            for z in range(depth):
                p = p_ref[z, x, span, chunk * LANES : (chunk + 1) * LANES].astype(F32)
                new = lane(source, z * across + x) * p
                u_ref[z, x, rows] = new
                news.append(new)
            store_edges(x, span, news, even, even_ref, odd_ref)
        store_beside(span, rows, core, u_ref, edge_ref)

    tiles(along, tile)


def square_scratch():
    return [pltpu.VMEM((LANES, LANES), F32)] * 2


def first_field(probes, chunk, source):
    depth, across, along, _ = probes.shape
    return pl.pallas_call(
        functools.partial(first_body, chunk),
        in_specs=whole_vmem(2),
        out_specs=whole_vmem(4),
        out_shape=[
            shape_of(depth, across, along + 2 * EDGE, F32),
            shape_of(RADIUS, across, along, BF16),
            shape_of(RADIUS, across, along, BF16),
            shape_of(depth, RADIUS, along, BF16),
        ],
        scratch_shapes=square_scratch(),
        compiler_params=params(),
    )(probes, source)


def local_body(chunk, moment, has_previous, *refs):
    refs = list(refs)
    u_ref, beside_ref, p_ref, c_ref, s_ref = refs[:5]
    prev_ref = refs[5] if has_previous else None
    base_ref, square, turned_c, turned_s = refs[-4:]
    depth, across, along, _ = base_ref.shape
    core = lax.axis_index("sub")
    left_on = (core == 1).astype(F32)
    right_on = (core == 0).astype(F32)
    turned_c[...] = turned(c_ref[...], square)
    turned_s[...] = turned(s_ref[moment], square)

    def tile(start):
        span = pl.ds(start, TILE)
        rows = start + EDGE
        courant = turned_c[span]
        source = turned_s[span]
        for z in range(depth):
            beside = [beside_ref[z, j, span].astype(F32) for j in range(RADIUS)]
            row = [v * left_on for v in beside]
            row += [u_ref[z, x, pl.ds(rows, TILE)] for x in range(across)]
            row += [v * right_on for v in beside]
            for x in range(across):
                here = row[RADIUS + x]
                total = (3.0 * COEFFICIENTS[0]) * here
                for r in range(1, RADIUS + 1):
                    near = row[RADIUS + x + r] + row[RADIUS + x - r]
                    near = near + (
                        u_ref[z, x, pl.ds(rows + r, TILE)] + u_ref[z, x, pl.ds(rows - r, TILE)]
                    )
                    if z + r < depth:
                        near = near + u_ref[z + r, x, pl.ds(rows, TILE)]
                    if z - r >= 0:
                        near = near + u_ref[z - r, x, pl.ds(rows, TILE)]
                    total = total + COEFFICIENTS[r] * near
                cell = z * across + x
                p = p_ref[z, x, span, chunk * LANES : (chunk + 1) * LANES].astype(F32)
                new = 2.0 * here
                if has_previous:
                    new = new - prev_ref[z, x, pl.ds(rows, TILE)]
                new = new + lane(courant, cell) * total + lane(source, cell) * p
                base_ref[z, x, span] = new

    tiles(along, tile)


def local_step(u, beside, probes, chunk, courant, source, moment, previous):
    depth, across, along, _ = probes.shape
    operands = [u, beside, probes, courant, source]
    if previous is not None:
        operands.append(previous)
    return pl.pallas_call(
        functools.partial(local_body, chunk, moment, previous is not None),
        in_specs=whole_vmem(len(operands)),
        out_specs=whole_vmem(1)[0],
        out_shape=shape_of(depth, across, along, F32),
        scratch_shapes=square_scratch() + square_scratch()[:1],
        compiler_params=params(),
    )(*operands)


def rim_body(kind, *refs):
    base_ref, even_ref, odd_ref, c_ref = refs[:4]
    outs, (square, turned_c) = refs[4:-2], refs[-2:]
    depth, across, along, _ = base_ref.shape
    core = lax.axis_index("sub")
    even = slab_is_even()
    lower = lax.axis_index("probe") == 0
    turned_c[...] = turned(c_ref[...], square)
    if kind == "middle":
        clear_pads(outs[0])

    def tile(start):
        span = pl.ds(start, TILE)
        rows = pl.ds(start + EDGE, TILE)
        courant = turned_c[span]
        for x in range(across):
            below, above = [], []
            for j in range(RADIUS):
                one, two = even_ref[j, x, span], odd_ref[j, x, span]
                below.append(jnp.where(even, two, one).astype(F32))
                above.append(jnp.where(even, one, two).astype(F32))
            news = []
            for z in range(depth):
                added = None
                for r in range(1, RADIUS + 1):
                    if z - r < 0:
                        term = COEFFICIENTS[r] * below[RADIUS + z - r]
                        added = term if added is None else added + term
                    if z + r >= depth:
                        term = COEFFICIENTS[r] * above[z + r - depth]
                        added = term if added is None else added + term
                new = base_ref[z, x, span]
                if added is not None:
                    new = new + lane(courant, z * across + x) * added
                news.append(new)
            if kind == "middle":
                for z, new in enumerate(news):
                    outs[0][z, x, rows] = new
                store_edges(x, span, news, even, outs[1], outs[2])
            elif kind == "half":
                for z in range(depth // 2):
                    one, two = news[z].astype(BF16), news[z + depth // 2].astype(BF16)
                    outs[0][z, x, span] = jnp.where(lower, one, two)
                    outs[1][z, x, span] = jnp.where(lower, two, one)
            else:
                for z, new in enumerate(news):
                    outs[0][z, x, span] = new.astype(BF16)
        if kind == "middle":
            store_beside(span, rows, core, outs[0], outs[3])

    tiles(along, tile)


def rim_step(base, evens, odds, courant, kind):
    depth, across, along, _ = base.shape
    if kind == "middle":
        out_shape = [
            shape_of(depth, across, along + 2 * EDGE, F32),
            shape_of(RADIUS, across, along, BF16),
            shape_of(RADIUS, across, along, BF16),
            shape_of(depth, RADIUS, along, BF16),
        ]
    elif kind == "half":
        out_shape = [shape_of(depth // 2, across, along, BF16)] * 2
    else:
        out_shape = [shape_of(depth, across, along, BF16)]
    return pl.pallas_call(
        functools.partial(rim_body, kind),
        in_specs=whole_vmem(4),
        out_specs=whole_vmem(len(out_shape)),
        out_shape=out_shape,
        scratch_shapes=square_scratch(),
        compiler_params=params(),
    )(base, evens, odds, courant)


def swap(x, axis, pairs):
    return lax.ppermute(x, axis, [p for a, b in pairs for p in ((a, b), (b, a))])


def even_swap(x):
    return swap(x, "slab", [(i, i + 1) for i in range(0, lax.axis_size("slab") - 1, 2)])


def odd_swap(x):
    return swap(x, "slab", [(i, i + 1) for i in range(1, lax.axis_size("slab") - 1, 2)])


def core_swap(x):
    return swap(x, "sub", [(0, 1)])


def chip_swap(x):
    return swap(x, "probe", [(0, 1)])


def product(a, b):
    return lax.dot_general(a, b, (((0,), (0,)), ((), ())), preferred_element_type=F32)


def block_of(array, i, j):
    return array[i * LANES : (i + 1) * LANES, j * LANES : (j + 1) * LANES]


def eye():
    rows = lax.broadcasted_iota(jnp.int32, (LANES, LANES), 0)
    cols = lax.broadcasted_iota(jnp.int32, (LANES, LANES), 1)
    return rows == cols


def inner_body(kept0, sent0, kept1, sent1, keep_ref, send_ref, panel):
    half = panel.shape[0] // 2
    for n, (kept, sent) in enumerate(((kept0, sent0), (kept1, sent1))):
        columns = slice(n * LANES, (n + 1) * LANES)
        panel[:half, columns] = kept[...].reshape(half, LANES)
        panel[half:, columns] = sent[...].reshape(half, LANES)
    core = lax.axis_index("sub")
    whole = product(panel[...], panel[...])
    first, second = whole[:, :LANES], whole[:, LANES:]
    size = 2 * LANES
    keep_ref[:size] = jnp.where(core == 0, first, second)
    send_ref[:size] = jnp.where(core == 0, second, first)
    diag = [
        jnp.sum(jnp.where(eye(), block_of(whole, n, n), 0.0), axis=0, keepdims=True)
        for n in range(2)
    ]
    none = jnp.zeros_like(diag[0])
    chip = lax.axis_index("probe")
    rows = [jnp.where(chip == n // 2, diag[n % 2], none) for n in range(4)]
    tail = jnp.concatenate(rows + [none] * 4, axis=0)
    keep_ref[size:] = tail
    send_ref[size:] = tail


def inner_gram(fields):
    size = 2 * LANES
    cells = 2 * math.prod(fields[0].shape[:3])
    half = jax.ShapeDtypeStruct((size + 8, LANES), F32)
    return pl.pallas_call(
        inner_body,
        in_specs=whole_vmem(4),
        out_specs=whole_vmem(2),
        out_shape=[half, half],
        scratch_shapes=[pltpu.VMEM((cells, size), BF16)],
        compiler_params=params(),
    )(*fields)


def inner_rows_body(keep_ref, got_ref, tail_ref, *outs):
    slab = lax.axis_index("slab")
    chip = lax.axis_index("probe")
    tail_ref[...] = keep_ref[2 * LANES :] + got_ref[2 * LANES :]
    for d, out in enumerate(outs):
        row = jnp.clip((slab ^ d) - 2 * chip, 0, 1)
        span = pl.ds(pl.multiple_of(row * LANES, LANES), LANES)
        out[...] = (keep_ref[span] + got_ref[span]).astype(out.dtype)


def inner_rows(keep, got, slabs):
    own = jax.ShapeDtypeStruct((LANES, LANES), F32)
    sent = jax.ShapeDtypeStruct((LANES, LANES), BF16)
    return pl.pallas_call(
        inner_rows_body,
        in_specs=whole_vmem(2),
        out_specs=whole_vmem(1 + slabs),
        out_shape=[jax.ShapeDtypeStruct((8, LANES), F32), own] + [sent] * (slabs - 1),
        compiler_params=params(),
    )(keep, got)


def cross_body(kept0, got0, kept1, got1, *refs):
    keep_ref, send_ref, panel = refs[-3:]
    chip = lax.axis_index("probe")
    core = lax.axis_index("sub")
    cells = panel.shape[0]
    for n, (kept, got) in enumerate(((kept0, got0), (kept1, got1))):
        mine = pl.multiple_of((chip * 2 + n) * LANES, LANES)
        other = pl.multiple_of(((1 - chip) * 2 + n) * LANES, LANES)
        panel[:, pl.ds(mine, LANES)] = kept[...].reshape(cells, LANES)
        panel[:, pl.ds(other, LANES)] = got[...].reshape(cells, LANES)
    whole = product(panel[:, : 2 * LANES], panel[:, 2 * LANES :])
    for ref, which in ((keep_ref, core), (send_ref, 1 - core)):
        here = which == 0
        ref[:LANES] = jnp.where(here, block_of(whole, 0, 0), block_of(whole, 0, 1))
        ref[LANES : 2 * LANES] = jnp.where(here, block_of(whole, 1, 0), block_of(whole, 1, 1))
        mixed = jnp.where(here, block_of(whole, 0, 1), block_of(whole, 1, 0))
        ref[2 * LANES :] = mixed


def cross_gram(fields, after):
    cells = math.prod(fields[0].shape[:3])
    three = jax.ShapeDtypeStruct((3 * LANES, LANES), F32)
    return pl.pallas_call(
        cross_body,
        in_specs=whole_vmem(4) + [pl.BlockSpec(memory_space=pl.ANY)] * len(after),
        out_specs=whole_vmem(2),
        out_shape=[three, three],
        scratch_shapes=[pltpu.VMEM((cells, 4 * LANES), BF16)],
        compiler_params=params(),
    )(*fields, *after)


def rounded(ref, block, tail):
    count = block.shape[0]
    high = tail.astype(BF16)
    low = tail - high.astype(F32)
    ref[:count] = block.astype(BF16)
    ref[count : count + 16] = jnp.concatenate([high.astype(F32), low], axis=0).astype(BF16)


def opened(ref, count):
    tail = ref[count : count + 16].astype(F32)
    return ref[:count].astype(F32), tail[:8] + tail[8:]


def cross_rows_body(keep_ref, got_ref, tail_ref, own_ref, *outs):
    slab = lax.axis_index("slab")
    core = lax.axis_index("sub")
    tail = tail_ref[...]
    for d in range(len(outs) + 1):
        owner = slab ^ d
        late = jnp.where(core == 0, jnp.where(owner == 2, 0, 2), jnp.where(owner == 2, 2, 1))
        at = jnp.where(owner < 2, owner, late)
        span = pl.ds(pl.multiple_of(at * LANES, LANES), LANES)
        block = keep_ref[span] + got_ref[span]
        if d == 0:
            own_ref[:LANES] = block
            own_ref[LANES:] = tail
        else:
            rounded(outs[d - 1], block, tail)


def cross_rows(keep, got, tail, slabs):
    own = jax.ShapeDtypeStruct((LANES + 8, LANES), F32)
    sent = jax.ShapeDtypeStruct((LANES + 16, LANES), BF16)
    return pl.pallas_call(
        cross_rows_body,
        in_specs=whole_vmem(3),
        out_specs=whole_vmem(slabs),
        out_shape=[own] + [sent] * (slabs - 1),
        compiler_params=params(),
    )(keep, got, tail)


def sum_body(slabs, own_ref, *refs):
    block, tail = own_ref[:LANES], own_ref[LANES:]
    for ref in refs[: slabs - 1]:
        more, more_tail = opened(ref, LANES)
        block, tail = block + more, tail + more_tail
    inner = refs[slabs - 1][...]
    for ref in refs[slabs : 2 * slabs - 1]:
        inner = inner + ref[...].astype(F32)
    out_ref = refs[-1]
    rounded(out_ref, block, tail)
    out_ref[LANES + 16 :] = inner.astype(BF16)


def sum_all(own, others, inner, inner_others):
    slabs = 1 + len(others)
    return pl.pallas_call(
        functools.partial(sum_body, slabs),
        in_specs=whole_vmem(2 * slabs),
        out_specs=whole_vmem(1)[0],
        out_shape=jax.ShapeDtypeStruct((2 * LANES + 16, LANES), BF16),
        compiler_params=params(),
    )(own, *others, inner, *inner_others)


def normalise_body(cell_count, mine_ref, other_ref, out_ref, norms_ref):
    slab = lax.axis_index("slab")
    core = lax.axis_index("sub")
    chip = lax.axis_index("probe")
    one, one_tail = opened(mine_ref, LANES)
    two, two_tail = opened(other_ref, LANES)
    cross = one + two
    inner_span = pl.ds(LANES + 16, LANES)
    inner = jnp.where(slab // 2 == chip, mine_ref[inner_span], other_ref[inner_span]).astype(F32)
    upper = slab < 2
    values = [jnp.where(upper, inner, cross.T), jnp.where(upper, cross, inner)]
    norms = jnp.sqrt((one_tail + two_tail) / cell_count + EPSILON)
    blocks = [norms[n : n + 1] for n in range(4)]
    own = blocks[0]
    for n in range(1, 4):
        own = jnp.where(slab == n, blocks[n], own)
    norms_ref[...] = own
    own_column = jnp.sum(
        jnp.where(eye(), jnp.broadcast_to(own, (LANES, LANES)), 0.0), axis=1, keepdims=True
    )
    for side in range(2):
        others = jnp.where(core == 0, blocks[2 * side], blocks[2 * side + 1])
        value = values[side] / math.sqrt(cell_count) / (own_column * others)
        value = jnp.where(eye() & (2 * side + core == slab), 0.0, value)
        out_ref[:, side * LANES : (side + 1) * LANES] = value


def normalise(mine, other, cell_count):
    return pl.pallas_call(
        functools.partial(normalise_body, cell_count),
        in_specs=whole_vmem(2),
        out_specs=whole_vmem(2),
        out_shape=[
            jax.ShapeDtypeStruct((LANES, 2 * LANES), F32),
            jax.ShapeDtypeStruct((1, LANES), F32),
        ],
        compiler_params=params(),
    )(mine, other)


def assemble_body(near_ref, far_ref, out_ref):
    core = lax.axis_index("sub")
    for side in range(2):
        columns = slice(side * LANES, (side + 1) * LANES)
        for ref, which in ((near_ref, core), (far_ref, 1 - core)):
            start = pl.multiple_of((2 * side + which) * LANES, LANES)
            out_ref[:, pl.ds(start, LANES)] = ref[:, columns]


def assemble(near, far):
    return pl.pallas_call(
        assemble_body,
        in_specs=whole_vmem(2),
        out_specs=whole_vmem(1)[0],
        out_shape=jax.ShapeDtypeStruct((near.shape[0], 4 * LANES), F32),
        compiler_params=params(),
    )(near, far)


def coupled(finals, cell_count):
    slabs = 4
    own = [field for kept, sent, _ in finals for field in (kept, sent)]
    keep, send = inner_gram(own)
    tail, *inner = inner_rows(keep, core_swap(send), slabs)
    inner_arrived = []
    for d in (2, 3, 1):
        pairs = [
            (2 * (k ^ d) + chip, 2 * k + chip)
            for chip in range(2)
            for k in (2 * chip, 2 * chip + 1)
        ]
        inner_arrived.append(lax.ppermute(inner[d], ("slab", "probe"), pairs))

    pairs = [field for kept, _, got in finals for field in (kept, got)]
    keep, send = cross_gram(pairs, inner_arrived)
    mine, *blocks = cross_rows(keep, core_swap(send), tail, slabs)
    arrived = [
        lax.ppermute(blocks[d - 1], "slab", [(i, i ^ d) for i in range(slabs)])
        for d in (2, 3, 1)
    ]
    total = sum_all(mine, arrived, inner[0], inner_arrived)
    near, norms = normalise(total, chip_swap(total), cell_count)
    return assemble(near, core_swap(near)), norms.reshape(-1)


def coupled_general(fields, cell_count):
    chips = lax.axis_size("probe")
    sketch = jnp.concatenate(fields, axis=-1)
    sketch = sketch.reshape(-1, sketch.shape[-1])
    if chips > 1:
        sketch = lax.all_to_all(sketch, "probe", split_axis=0, concat_axis=1, tiled=True)
    partial_gram = lax.dot_general(
        sketch, sketch, (((0,), (0,)), ((), ())), preferred_element_type=F32
    )
    rows = lax.psum_scatter(partial_gram, "slab", scatter_dimension=0, tiled=True)
    rows = lax.psum(rows, ("probe", "sub"))
    count = rows.shape[0]
    start = lax.axis_index("slab") * count
    own = jnp.diagonal(lax.dynamic_slice_in_dim(rows, start, count, 1))
    own_norms = jnp.sqrt(own / cell_count + EPSILON)
    norms = lax.all_gather(own_norms, "slab", axis=0, tiled=True)
    coupling = rows / math.sqrt(cell_count) / (own_norms[:, None] * norms[None, :])
    row_ids = start + lax.broadcasted_iota(jnp.int32, coupling.shape, 0)
    col_ids = lax.broadcasted_iota(jnp.int32, coupling.shape, 1)
    return jnp.where(row_ids == col_ids, 0.0, coupling), own_norms


def shards(probes, courant, source):
    depth, across, along, count = probes.shape
    chunks = count // LANES
    slabs, chips = lax.axis_size("slab"), lax.axis_size("probe")
    cell_count = depth * across * along * slabs * lax.axis_size("sub")
    paired = chips == 2 and slabs == 4 and chunks == 2 and depth == 2 * RADIUS
    steps = source.shape[0]
    courant = courant.reshape(depth * across, along)
    source = source.reshape(steps, depth * across, along)

    exchange = lambda even, odd, edge: (even_swap(even), odd_swap(odd), core_swap(edge))
    now, previous, halos = [], [None] * chunks, []
    for c in range(chunks):
        u, *edges = first_field(probes, c, source)
        now.append(u)
        halos.append(exchange(*edges))
    finals = []
    for n in range(1, steps):
        for c in range(chunks):
            even, odd, beside = halos[c]
            base = local_step(now[c], beside, probes, c, courant, source, n, previous[c])
            if n < steps - 1:
                u, *edges = rim_step(base, even, odd, courant, "middle")
                previous[c], now[c] = now[c], u
                halos[c] = exchange(*edges)
            elif paired:
                kept, sent = rim_step(base, even, odd, courant, "half")
                finals.append((kept, sent, chip_swap(sent)))
            else:
                finals += rim_step(base, even, odd, courant, "all")
    return (coupled if paired else coupled_general)(finals, cell_count)


def solution(mesh):
    placed = (
        P(("groups", "slab"), "sub", None, "probe"),
        P("slab", "sub", None),
        P(None, ("groups", "slab"), "sub", None),
    )
    return jax.shard_map(
        shards,
        mesh=mesh,
        in_specs=placed,
        out_specs=(P(("groups", "slab"), None), P(("groups", "slab"))),
        check_vma=False,
    )
```

```python
import functools
import math

import jax
import jax.numpy as jnp
from jax import lax
from jax.experimental import pallas as pl
from jax.experimental.pallas import tpu as pltpu
from jax.sharding import PartitionSpec as P

COEFFICIENTS = (-205.0 / 72.0, 8.0 / 5.0, -1.0 / 5.0, 8.0 / 315.0, -1.0 / 560.0)
EPSILON = 1e-06
LANES = 128
RADIUS = 4
EDGE = 8
TILE = 16
F32 = jnp.float32
BF16 = jnp.bfloat16
VMEM_LIMIT = 32 * 1024 * 1024


def call(body, **options):
    return pl.pallas_call(
        body,
        compiler_params=pltpu.CompilerParams(vmem_limit_bytes=VMEM_LIMIT),
        cost_estimate=pl.CostEstimate(flops=1, bytes_accessed=1, transcendentals=0),
        **options,
    )


def whole_vmem(count):
    return [pl.BlockSpec(memory_space=pltpu.VMEM)] * count


def shape_of(depth, across, along, dtype):
    return jax.ShapeDtypeStruct((depth, across, along, LANES), dtype)


def turned(field, scratch):
    rows, along = field.shape
    scratch[:rows, :along] = field
    return jnp.transpose(scratch[...])


def lane(values, n):
    return jnp.broadcast_to(values[:, n : n + 1], (values.shape[0], LANES))


def store_edges(x, span, news, even, even_ref, odd_ref):
    for j in range(RADIUS):
        low = news[j].astype(BF16)
        high = news[len(news) - RADIUS + j].astype(BF16)
        even_ref[j, x, span] = jnp.where(even, high, low)
        odd_ref[j, x, span] = jnp.where(even, low, high)


def store_beside(span, rows, core, u_ref, edge_ref):
    depth, across, _, _ = u_ref.shape
    first = (across - RADIUS) * (1 - core)
    for z in range(depth):
        for j in range(RADIUS):
            edge_ref[z, j, span] = u_ref[z, first + j, rows].astype(BF16)


def slab_is_even():
    return lax.rem(lax.axis_index("slab"), 2) == 0


def clear_pads(u_ref):
    depth, across, padded, _ = u_ref.shape

    def plane(z, _):
        blank = jnp.zeros((across, EDGE, LANES), F32)
        u_ref[z, :, pl.ds(0, EDGE)] = blank
        u_ref[z, :, pl.ds(padded - EDGE, EDGE)] = blank
        return 0

    lax.fori_loop(0, depth, plane, 0)


def tiles(along, body):
    def one(t, _):
        body(pl.multiple_of(t * TILE, TILE))
        return 0

    lax.fori_loop(0, along // TILE, one, 0)


def first_body(chunk, p_ref, s_ref, u_ref, odd_ref, even_ref, edge_ref, square, turned_s):
    depth, across, padded, _ = u_ref.shape
    along = padded - 2 * EDGE
    core = lax.axis_index("sub")
    even = slab_is_even()
    turned_s[...] = turned(s_ref[0], square)
    clear_pads(u_ref)

    def tile(start):
        span = pl.ds(start, TILE)
        rows = pl.ds(start + EDGE, TILE)
        source = turned_s[span]
        for x in range(across):
            news = []
            for z in range(depth):
                p = p_ref[z, x, span, chunk * LANES : (chunk + 1) * LANES].astype(F32)
                new = lane(source, z * across + x) * p
                u_ref[z, x, rows] = new
                news.append(new)
            store_edges(x, span, news, even, even_ref, odd_ref)
        store_beside(span, rows, core, u_ref, edge_ref)

    tiles(along, tile)


def square_scratch():
    return [pltpu.VMEM((LANES, LANES), F32)] * 2


def first_field(probes, chunk, source):
    depth, across, along, _ = probes.shape
    return call(
        functools.partial(first_body, chunk),
        in_specs=whole_vmem(2),
        out_specs=whole_vmem(4),
        out_shape=[
            shape_of(depth, across, along + 2 * EDGE, F32),
            shape_of(RADIUS, across, along, BF16),
            shape_of(RADIUS, across, along, BF16),
            shape_of(depth, RADIUS, along, BF16),
        ],
        scratch_shapes=square_scratch(),
    )(probes, source)


def local_body(chunk, moment, has_previous, *refs):
    refs = list(refs)
    u_ref, beside_ref, p_ref, c_ref, s_ref = refs[:5]
    prev_ref = refs[5] if has_previous else None
    base_ref, square, turned_c, turned_s = refs[-4:]
    depth, across, along, _ = base_ref.shape
    core = lax.axis_index("sub")
    left_on = (core == 1).astype(F32)
    right_on = (core == 0).astype(F32)
    turned_c[...] = turned(c_ref[...], square)
    turned_s[...] = turned(s_ref[moment], square)

    def tile(start):
        span = pl.ds(start, TILE)
        rows = start + EDGE
        courant = turned_c[span]
        source = turned_s[span]
        for z in range(depth):
            beside = [beside_ref[z, j, span].astype(F32) for j in range(RADIUS)]
            row = [v * left_on for v in beside]
            row += [u_ref[z, x, pl.ds(rows, TILE)] for x in range(across)]
            row += [v * right_on for v in beside]
            for x in range(across):
                here = row[RADIUS + x]
                total = (3.0 * COEFFICIENTS[0]) * here
                for r in range(1, RADIUS + 1):
                    near = row[RADIUS + x + r] + row[RADIUS + x - r]
                    near = near + (
                        u_ref[z, x, pl.ds(rows + r, TILE)] + u_ref[z, x, pl.ds(rows - r, TILE)]
                    )
                    if z + r < depth:
                        near = near + u_ref[z + r, x, pl.ds(rows, TILE)]
                    if z - r >= 0:
                        near = near + u_ref[z - r, x, pl.ds(rows, TILE)]
                    total = total + COEFFICIENTS[r] * near
                cell = z * across + x
                p = p_ref[z, x, span, chunk * LANES : (chunk + 1) * LANES].astype(F32)
                new = 2.0 * here
                if has_previous:
                    new = new - prev_ref[z, x, pl.ds(rows, TILE)]
                new = new + lane(courant, cell) * total + lane(source, cell) * p
                base_ref[z, x, span] = new

    tiles(along, tile)


def local_step(u, beside, probes, chunk, courant, source, moment, previous):
    depth, across, along, _ = probes.shape
    operands = [u, beside, probes, courant, source]
    if previous is not None:
        operands.append(previous)
    return call(
        functools.partial(local_body, chunk, moment, previous is not None),
        in_specs=whole_vmem(len(operands)),
        out_specs=whole_vmem(1)[0],
        out_shape=shape_of(depth, across, along, F32),
        scratch_shapes=square_scratch() + square_scratch()[:1],
    )(*operands)


def rim_body(kind, *refs):
    base_ref, even_ref, odd_ref, c_ref = refs[:4]
    outs, (square, turned_c) = refs[4:-2], refs[-2:]
    depth, across, along, _ = base_ref.shape
    core = lax.axis_index("sub")
    even = slab_is_even()
    lower = lax.axis_index("probe") == 0
    turned_c[...] = turned(c_ref[...], square)
    if kind == "middle":
        clear_pads(outs[0])

    def tile(start):
        span = pl.ds(start, TILE)
        rows = pl.ds(start + EDGE, TILE)
        courant = turned_c[span]
        for x in range(across):
            below, above = [], []
            for j in range(RADIUS):
                one, two = even_ref[j, x, span], odd_ref[j, x, span]
                below.append(jnp.where(even, two, one).astype(F32))
                above.append(jnp.where(even, one, two).astype(F32))
            news = []
            for z in range(depth):
                added = None
                for r in range(1, RADIUS + 1):
                    if z - r < 0:
                        term = COEFFICIENTS[r] * below[RADIUS + z - r]
                        added = term if added is None else added + term
                    if z + r >= depth:
                        term = COEFFICIENTS[r] * above[z + r - depth]
                        added = term if added is None else added + term
                new = base_ref[z, x, span]
                if added is not None:
                    new = new + lane(courant, z * across + x) * added
                news.append(new)
            if kind == "middle":
                for z, new in enumerate(news):
                    outs[0][z, x, rows] = new
                store_edges(x, span, news, even, outs[2], outs[1])
            elif kind == "half":
                for z in range(depth // 2):
                    one, two = news[z].astype(BF16), news[z + depth // 2].astype(BF16)
                    outs[0][z, x, span] = jnp.where(lower, one, two)
                    outs[1][z, x, span] = jnp.where(lower, two, one)
            else:
                for z, new in enumerate(news):
                    outs[0][z, x, span] = new.astype(BF16)
        if kind == "middle":
            store_beside(span, rows, core, outs[0], outs[3])

    tiles(along, tile)


def rim_step(base, evens, odds, courant, kind):
    depth, across, along, _ = base.shape
    if kind == "middle":
        out_shape = [
            shape_of(depth, across, along + 2 * EDGE, F32),
            shape_of(RADIUS, across, along, BF16),
            shape_of(RADIUS, across, along, BF16),
            shape_of(depth, RADIUS, along, BF16),
        ]
    elif kind == "half":
        out_shape = [shape_of(depth // 2, across, along, BF16)] * 2
    else:
        out_shape = [shape_of(depth, across, along, BF16)]
    return call(
        functools.partial(rim_body, kind),
        in_specs=whole_vmem(4),
        out_specs=whole_vmem(len(out_shape)),
        out_shape=out_shape,
        scratch_shapes=square_scratch(),
    )(base, evens, odds, courant)


def swap(x, axis, pairs):
    return lax.ppermute(x, axis, [p for a, b in pairs for p in ((a, b), (b, a))])


def even_swap(x):
    return swap(x, "slab", [(i, i + 1) for i in range(0, lax.axis_size("slab") - 1, 2)])


def odd_swap(x):
    return swap(x, "slab", [(i, i + 1) for i in range(1, lax.axis_size("slab") - 1, 2)])


def core_swap(x):
    return swap(x, "sub", [(0, 1)])


def chip_swap(x):
    return swap(x, "probe", [(0, 1)])


def product(a, b):
    return lax.dot_general(a, b, (((0,), (0,)), ((), ())), preferred_element_type=F32)


def block_of(array, i, j):
    return array[i * LANES : (i + 1) * LANES, j * LANES : (j + 1) * LANES]


def eye():
    rows = lax.broadcasted_iota(jnp.int32, (LANES, LANES), 0)
    cols = lax.broadcasted_iota(jnp.int32, (LANES, LANES), 1)
    return rows == cols


def inner_body(kept0, sent0, kept1, sent1, keep_ref, send_ref, panel):
    half = panel.shape[0] // 2
    for n, (kept, sent) in enumerate(((kept0, sent0), (kept1, sent1))):
        columns = slice(n * LANES, (n + 1) * LANES)
        panel[:half, columns] = kept[...].reshape(half, LANES)
        panel[half:, columns] = sent[...].reshape(half, LANES)
    core = lax.axis_index("sub")
    whole = product(panel[...], panel[...])
    first, second = whole[:, :LANES], whole[:, LANES:]
    size = 2 * LANES
    keep_ref[:size] = jnp.where(core == 0, first, second)
    send_ref[:size] = jnp.where(core == 0, second, first)
    diag = [
        jnp.sum(jnp.where(eye(), block_of(whole, n, n), 0.0), axis=0, keepdims=True)
        for n in range(2)
    ]
    none = jnp.zeros_like(diag[0])
    chip = lax.axis_index("probe")
    rows = [jnp.where(chip == n // 2, diag[n % 2], none) for n in range(4)]
    tail = jnp.concatenate(rows + [none] * 4, axis=0)
    keep_ref[size:] = tail
    send_ref[size:] = tail


def inner_gram(fields):
    size = 2 * LANES
    cells = 2 * math.prod(fields[0].shape[:3])
    half = jax.ShapeDtypeStruct((size + 8, LANES), F32)
    return call(
        inner_body,
        in_specs=whole_vmem(4),
        out_specs=whole_vmem(2),
        out_shape=[half, half],
        scratch_shapes=[pltpu.VMEM((cells, size), BF16)],
    )(*fields)


def inner_rows_body(keep_ref, got_ref, tail_ref, *outs):
    slab = lax.axis_index("slab")
    chip = lax.axis_index("probe")
    tail_ref[...] = keep_ref[2 * LANES :] + got_ref[2 * LANES :]
    for d, out in enumerate(outs):
        row = jnp.clip((slab ^ d) - 2 * chip, 0, 1)
        span = pl.ds(pl.multiple_of(row * LANES, LANES), LANES)
        out[...] = (keep_ref[span] + got_ref[span]).astype(out.dtype)


def inner_rows(keep, got, slabs):
    own = jax.ShapeDtypeStruct((LANES, LANES), F32)
    sent = jax.ShapeDtypeStruct((LANES, LANES), BF16)
    return call(
        inner_rows_body,
        in_specs=whole_vmem(2),
        out_specs=whole_vmem(1 + slabs),
        out_shape=[jax.ShapeDtypeStruct((8, LANES), F32), own] + [sent] * (slabs - 1),
    )(keep, got)


def cross_body(kept0, got0, kept1, got1, *refs):
    keep_ref, send_ref, panel = refs[-3:]
    chip = lax.axis_index("probe")
    core = lax.axis_index("sub")
    cells = panel.shape[0]
    for n, (kept, got) in enumerate(((kept0, got0), (kept1, got1))):
        mine = pl.multiple_of((chip * 2 + n) * LANES, LANES)
        other = pl.multiple_of(((1 - chip) * 2 + n) * LANES, LANES)
        panel[:, pl.ds(mine, LANES)] = kept[...].reshape(cells, LANES)
        panel[:, pl.ds(other, LANES)] = got[...].reshape(cells, LANES)
    whole = product(panel[:, : 2 * LANES], panel[:, 2 * LANES :])
    for ref, which in ((keep_ref, core), (send_ref, 1 - core)):
        here = which == 0
        ref[:LANES] = jnp.where(here, block_of(whole, 0, 0), block_of(whole, 0, 1))
        ref[LANES : 2 * LANES] = jnp.where(here, block_of(whole, 1, 0), block_of(whole, 1, 1))
        mixed = jnp.where(here, block_of(whole, 0, 1), block_of(whole, 1, 0))
        ref[2 * LANES :] = mixed


def cross_gram(fields, after):
    cells = math.prod(fields[0].shape[:3])
    three = jax.ShapeDtypeStruct((3 * LANES, LANES), F32)
    return call(
        cross_body,
        in_specs=whole_vmem(4) + [pl.BlockSpec(memory_space=pl.ANY)] * len(after),
        out_specs=whole_vmem(2),
        out_shape=[three, three],
        scratch_shapes=[pltpu.VMEM((cells, 4 * LANES), BF16)],
    )(*fields, *after)


def rounded(ref, block, tail):
    count = block.shape[0]
    high = tail.astype(BF16)
    low = tail - high.astype(F32)
    ref[:count] = block.astype(BF16)
    ref[count : count + 16] = jnp.concatenate([high.astype(F32), low], axis=0).astype(BF16)


def opened(ref, count):
    tail = ref[count : count + 16].astype(F32)
    return ref[:count].astype(F32), tail[:8] + tail[8:]


def cross_rows_body(keep_ref, got_ref, tail_ref, own_ref, *outs):
    slab = lax.axis_index("slab")
    core = lax.axis_index("sub")
    tail = tail_ref[...]
    for d in range(len(outs) + 1):
        owner = slab ^ d
        late = jnp.where(core == 0, jnp.where(owner == 2, 0, 2), jnp.where(owner == 2, 2, 1))
        at = jnp.where(owner < 2, owner, late)
        span = pl.ds(pl.multiple_of(at * LANES, LANES), LANES)
        block = keep_ref[span] + got_ref[span]
        if d == 0:
            own_ref[:LANES] = block
            own_ref[LANES:] = tail
        else:
            rounded(outs[d - 1], block, tail)


def cross_rows(keep, got, tail, slabs):
    own = jax.ShapeDtypeStruct((LANES + 8, LANES), F32)
    sent = jax.ShapeDtypeStruct((LANES + 16, LANES), BF16)
    return call(
        cross_rows_body,
        in_specs=whole_vmem(3),
        out_specs=whole_vmem(slabs),
        out_shape=[own] + [sent] * (slabs - 1),
    )(keep, got, tail)


def sum_body(slabs, own_ref, *refs):
    block, tail = own_ref[:LANES], own_ref[LANES:]
    for ref in refs[: slabs - 1]:
        more, more_tail = opened(ref, LANES)
        block, tail = block + more, tail + more_tail
    inner = refs[slabs - 1][...]
    for ref in refs[slabs : 2 * slabs - 1]:
        inner = inner + ref[...].astype(F32)
    out_ref = refs[-1]
    rounded(out_ref, block, tail)
    out_ref[LANES + 16 :] = inner.astype(BF16)


def sum_all(own, others, inner, inner_others):
    slabs = 1 + len(others)
    return call(
        functools.partial(sum_body, slabs),
        in_specs=whole_vmem(2 * slabs),
        out_specs=whole_vmem(1)[0],
        out_shape=jax.ShapeDtypeStruct((2 * LANES + 16, LANES), BF16),
    )(own, *others, inner, *inner_others)


def normalise_body(cell_count, mine_ref, other_ref, out_ref, norms_ref):
    slab = lax.axis_index("slab")
    core = lax.axis_index("sub")
    chip = lax.axis_index("probe")
    one, one_tail = opened(mine_ref, LANES)
    two, two_tail = opened(other_ref, LANES)
    cross = one + two
    inner_span = pl.ds(LANES + 16, LANES)
    inner = jnp.where(slab // 2 == chip, mine_ref[inner_span], other_ref[inner_span]).astype(F32)
    upper = slab < 2
    values = [jnp.where(upper, inner, cross.T), jnp.where(upper, cross, inner)]
    norms = jnp.sqrt((one_tail + two_tail) / cell_count + EPSILON)
    blocks = [norms[n : n + 1] for n in range(4)]
    own = blocks[0]
    for n in range(1, 4):
        own = jnp.where(slab == n, blocks[n], own)
    norms_ref[...] = own
    own_column = jnp.sum(
        jnp.where(eye(), jnp.broadcast_to(own, (LANES, LANES)), 0.0), axis=1, keepdims=True
    )
    for side in range(2):
        others = jnp.where(core == 0, blocks[2 * side], blocks[2 * side + 1])
        value = values[side] / math.sqrt(cell_count) / (own_column * others)
        value = jnp.where(eye() & (2 * side + core == slab), 0.0, value)
        out_ref[:, side * LANES : (side + 1) * LANES] = value


def normalise(mine, other, cell_count):
    return call(
        functools.partial(normalise_body, cell_count),
        in_specs=whole_vmem(2),
        out_specs=whole_vmem(2),
        out_shape=[
            jax.ShapeDtypeStruct((LANES, 2 * LANES), F32),
            jax.ShapeDtypeStruct((1, LANES), F32),
        ],
    )(mine, other)


def assemble_body(near_ref, far_ref, out_ref):
    core = lax.axis_index("sub")
    for side in range(2):
        columns = slice(side * LANES, (side + 1) * LANES)
        for ref, which in ((near_ref, core), (far_ref, 1 - core)):
            start = pl.multiple_of((2 * side + which) * LANES, LANES)
            out_ref[:, pl.ds(start, LANES)] = ref[:, columns]


def assemble(near, far):
    return call(
        assemble_body,
        in_specs=whole_vmem(2),
        out_specs=whole_vmem(1)[0],
        out_shape=jax.ShapeDtypeStruct((near.shape[0], 4 * LANES), F32),
    )(near, far)


def coupled(finals, cell_count):
    slabs = 4
    own = [field for kept, sent, _ in finals for field in (kept, sent)]
    keep, send = inner_gram(own)
    tail, *inner = inner_rows(keep, core_swap(send), slabs)
    inner_arrived = []
    for d in (2, 3, 1):
        pairs = [
            (2 * (k ^ d) + chip, 2 * k + chip)
            for chip in range(2)
            for k in (2 * chip, 2 * chip + 1)
        ]
        inner_arrived.append(lax.ppermute(inner[d], ("slab", "probe"), pairs))

    pairs = [field for kept, _, got in finals for field in (kept, got)]
    keep, send = cross_gram(pairs, inner_arrived)
    mine, *blocks = cross_rows(keep, core_swap(send), tail, slabs)
    arrived = [
        lax.ppermute(blocks[d - 1], "slab", [(i, i ^ d) for i in range(slabs)])
        for d in (2, 3, 1)
    ]
    total = sum_all(mine, arrived, inner[0], inner_arrived)
    near, norms = normalise(total, chip_swap(total), cell_count)
    return assemble(near, core_swap(near)), norms.reshape(-1)


def coupled_general(fields, cell_count):
    chips = lax.axis_size("probe")
    sketch = jnp.concatenate(fields, axis=-1)
    sketch = sketch.reshape(-1, sketch.shape[-1])
    if chips > 1:
        sketch = lax.all_to_all(sketch, "probe", split_axis=0, concat_axis=1, tiled=True)
    partial_gram = lax.dot_general(
        sketch, sketch, (((0,), (0,)), ((), ())), preferred_element_type=F32
    )
    rows = lax.psum_scatter(partial_gram, "slab", scatter_dimension=0, tiled=True)
    rows = lax.psum(rows, ("probe", "sub"))
    count = rows.shape[0]
    start = lax.axis_index("slab") * count
    own = jnp.diagonal(lax.dynamic_slice_in_dim(rows, start, count, 1))
    own_norms = jnp.sqrt(own / cell_count + EPSILON)
    norms = lax.all_gather(own_norms, "slab", axis=0, tiled=True)
    coupling = rows / math.sqrt(cell_count) / (own_norms[:, None] * norms[None, :])
    row_ids = start + lax.broadcasted_iota(jnp.int32, coupling.shape, 0)
    col_ids = lax.broadcasted_iota(jnp.int32, coupling.shape, 1)
    return jnp.where(row_ids == col_ids, 0.0, coupling), own_norms


def shards(probes, courant, source):
    depth, across, along, count = probes.shape
    chunks = count // LANES
    slabs, chips = lax.axis_size("slab"), lax.axis_size("probe")
    cell_count = depth * across * along * slabs * lax.axis_size("sub")
    paired = chips == 2 and slabs == 4 and chunks == 2 and depth == 2 * RADIUS
    steps = source.shape[0]
    courant = courant.reshape(depth * across, along)
    source = source.reshape(steps, depth * across, along)

    exchange = lambda odd, even, edge: (odd_swap(odd), even_swap(even), core_swap(edge))
    now, previous, halos = [], [None] * chunks, []
    for c in range(chunks):
        u, *edges = first_field(probes, c, source)
        now.append(u)
        halos.append(exchange(*edges))
    finals = []
    for n in range(1, steps):
        for c in range(chunks):
            odd, even, beside = halos[c]
            base = local_step(now[c], beside, probes, c, courant, source, n, previous[c])
            if n < steps - 1:
                u, *edges = rim_step(base, even, odd, courant, "middle")
                previous[c], now[c] = now[c], u
                halos[c] = exchange(*edges)
            elif paired:
                kept, sent = rim_step(base, even, odd, courant, "half")
                finals.append((kept, sent, chip_swap(sent)))
            else:
                finals += rim_step(base, even, odd, courant, "all")
    return (coupled if paired else coupled_general)(finals, cell_count)


def solution(mesh):
    placed = (
        P(("groups", "slab"), "sub", None, "probe"),
        P("slab", "sub", None),
        P(None, ("groups", "slab"), "sub", None),
    )
    return jax.shard_map(
        shards,
        mesh=mesh,
        in_specs=placed,
        out_specs=(P(("groups", "slab"), None), P(("groups", "slab"))),
        check_vma=False,
    )
```

```python
import functools
import math

import jax
import jax.numpy as jnp
from jax import lax
from jax.experimental import pallas as pl
from jax.experimental.pallas import tpu as pltpu
from jax.sharding import PartitionSpec as P

COEFFICIENTS = (-205.0 / 72.0, 8.0 / 5.0, -1.0 / 5.0, 8.0 / 315.0, -1.0 / 560.0)
EPSILON = 1e-06
LANES = 128
RADIUS = 4
EDGE = 8
TILE = 16
F32 = jnp.float32
BF16 = jnp.bfloat16
VMEM_LIMIT = 32 * 1024 * 1024


def call(body, **options):
    return pl.pallas_call(
        body,
        compiler_params=pltpu.CompilerParams(vmem_limit_bytes=VMEM_LIMIT),
        cost_estimate=pl.CostEstimate(flops=1, bytes_accessed=1, transcendentals=0),
        **options,
    )


def whole_vmem(count):
    return [pl.BlockSpec(memory_space=pltpu.VMEM)] * count


def shape_of(depth, across, along, dtype):
    return jax.ShapeDtypeStruct((depth, across, along, LANES), dtype)


def turned(field, scratch):
    rows, along = field.shape
    scratch[:rows, :along] = field
    return jnp.transpose(scratch[...])


def lane(values, n):
    return jnp.broadcast_to(values[:, n : n + 1], (values.shape[0], LANES))


def store_edges(x, span, news, even, even_ref, odd_ref):
    for j in range(RADIUS):
        low = news[j].astype(BF16)
        high = news[len(news) - RADIUS + j].astype(BF16)
        even_ref[j, x, span] = jnp.where(even, high, low)
        odd_ref[j, x, span] = jnp.where(even, low, high)


def store_beside(span, rows, core, u_ref, edge_ref):
    depth, across, _, _ = u_ref.shape
    first = (across - RADIUS) * (1 - core)
    for z in range(depth):
        for j in range(RADIUS):
            edge_ref[z, j, span] = u_ref[z, first + j, rows].astype(BF16)


def slab_is_even():
    return lax.rem(lax.axis_index("slab"), 2) == 0


def clear_pads(u_ref):
    depth, across, padded, _ = u_ref.shape

    def plane(z, _):
        blank = jnp.zeros((across, EDGE, LANES), F32)
        u_ref[z, :, pl.ds(0, EDGE)] = blank
        u_ref[z, :, pl.ds(padded - EDGE, EDGE)] = blank
        return 0

    lax.fori_loop(0, depth, plane, 0)


def tiles(along, body):
    def one(t, _):
        body(pl.multiple_of(t * TILE, TILE))
        return 0

    lax.fori_loop(0, along // TILE, one, 0)


def first_body(
    chunk, p_hbm, s_hbm, u_ref, odd_ref, even_ref, edge_ref, p_ref, s_ref, square, turned_s, sems
):
    depth, across, padded, _ = u_ref.shape
    along = padded - 2 * EDGE
    core = lax.axis_index("sub")
    even = slab_is_even()
    lanes = pl.ds(chunk * LANES, LANES)
    pairs = [(j, depth - RADIUS + j) for j in range(RADIUS)]
    order = [z for pair in pairs for z in pair] + list(range(RADIUS, depth - RADIUS))
    source_copy = pltpu.make_async_copy(s_hbm.at[0], s_ref, sems.at[depth])
    source_copy.start()
    copies = {}
    for z in order:
        copies[z] = pltpu.make_async_copy(p_hbm.at[z, :, :, lanes], p_ref.at[z], sems.at[z])
        copies[z].start()
    clear_pads(u_ref)
    source_copy.wait()
    turned_s[...] = turned(s_ref[...], square)

    def planes(zs):
        for z in zs:
            copies[z].wait()

        def tile(start):
            span = pl.ds(start, TILE)
            source = turned_s[span]
            for x in range(across):
                news = []
                for z in zs:
                    new = lane(source, z * across + x) * p_ref[z, x, span].astype(F32)
                    u_ref[z, x, pl.ds(start + EDGE, TILE)] = new
                    news.append(new.astype(BF16))
                if len(zs) == 2:
                    low, high = news
                    even_ref[zs[0], x, span] = jnp.where(even, high, low)
                    odd_ref[zs[0], x, span] = jnp.where(even, low, high)

        tiles(along, tile)

    for pair in pairs:
        planes(pair)
    for z in range(RADIUS, depth - RADIUS):
        planes((z,))

    def beside(start):
        store_beside(pl.ds(start, TILE), pl.ds(start + EDGE, TILE), core, u_ref, edge_ref)

    tiles(along, beside)


def square_scratch():
    return [pltpu.VMEM((LANES, LANES), F32)] * 2


def first_field(probes, chunk, source):
    depth, across, along, _ = probes.shape
    return call(
        functools.partial(first_body, chunk),
        in_specs=[pl.BlockSpec(memory_space=pltpu.HBM)] * 2,
        out_specs=whole_vmem(4),
        out_shape=[
            shape_of(depth, across, along + 2 * EDGE, F32),
            shape_of(RADIUS, across, along, BF16),
            shape_of(RADIUS, across, along, BF16),
            shape_of(depth, RADIUS, along, BF16),
        ],
        scratch_shapes=[
            pltpu.VMEM((depth, across, along, LANES), BF16),
            pltpu.VMEM(source.shape[1:], F32),
        ]
        + square_scratch()
        + [pltpu.SemaphoreType.DMA((depth + 1,))],
    )(probes, source)


def local_body(chunk, moment, has_previous, *refs):
    refs = list(refs)
    u_ref, beside_ref, p_ref, c_ref, s_ref = refs[:5]
    prev_ref = refs[5] if has_previous else None
    base_ref, square, turned_c, turned_s = refs[-4:]
    depth, across, along, _ = base_ref.shape
    core = lax.axis_index("sub")
    left_on = (core == 1).astype(F32)
    right_on = (core == 0).astype(F32)
    turned_c[...] = turned(c_ref[...], square)
    turned_s[...] = turned(s_ref[moment], square)

    def tile(start):
        span = pl.ds(start, TILE)
        rows = start + EDGE
        courant = turned_c[span]
        source = turned_s[span]
        for z in range(depth):
            beside = [beside_ref[z, j, span].astype(F32) for j in range(RADIUS)]
            row = [v * left_on for v in beside]
            row += [u_ref[z, x, pl.ds(rows, TILE)] for x in range(across)]
            row += [v * right_on for v in beside]
            for x in range(across):
                here = row[RADIUS + x]
                total = (3.0 * COEFFICIENTS[0]) * here
                for r in range(1, RADIUS + 1):
                    near = row[RADIUS + x + r] + row[RADIUS + x - r]
                    near = near + (
                        u_ref[z, x, pl.ds(rows + r, TILE)] + u_ref[z, x, pl.ds(rows - r, TILE)]
                    )
                    if z + r < depth:
                        near = near + u_ref[z + r, x, pl.ds(rows, TILE)]
                    if z - r >= 0:
                        near = near + u_ref[z - r, x, pl.ds(rows, TILE)]
                    total = total + COEFFICIENTS[r] * near
                cell = z * across + x
                p = p_ref[z, x, span, chunk * LANES : (chunk + 1) * LANES].astype(F32)
                new = 2.0 * here
                if has_previous:
                    new = new - prev_ref[z, x, pl.ds(rows, TILE)]
                new = new + lane(courant, cell) * total + lane(source, cell) * p
                base_ref[z, x, span] = new

    tiles(along, tile)


def local_step(u, beside, probes, chunk, courant, source, moment, previous):
    depth, across, along, _ = probes.shape
    operands = [u, beside, probes, courant, source]
    if previous is not None:
        operands.append(previous)
    return call(
        functools.partial(local_body, chunk, moment, previous is not None),
        in_specs=whole_vmem(len(operands)),
        out_specs=whole_vmem(1)[0],
        out_shape=shape_of(depth, across, along, F32),
        scratch_shapes=square_scratch() + square_scratch()[:1],
    )(*operands)


def rim_body(kind, *refs):
    base_ref, odd_ref, even_ref, c_ref = refs[:4]
    outs, (square, turned_c) = refs[4:-2], refs[-2:]
    depth, across, along, _ = base_ref.shape
    core = lax.axis_index("sub")
    even = slab_is_even()
    lower = lax.axis_index("probe") == 0
    turned_c[...] = turned(c_ref[...], square)
    if kind == "middle":
        clear_pads(outs[0])

    def tile(start):
        span = pl.ds(start, TILE)
        rows = pl.ds(start + EDGE, TILE)
        courant = turned_c[span]
        for x in range(across):
            below, above = [], []
            for j in range(RADIUS):
                one, two = even_ref[j, x, span], odd_ref[j, x, span]
                below.append(jnp.where(even, two, one).astype(F32))
                above.append(jnp.where(even, one, two).astype(F32))
            news = []
            for z in range(depth):
                added = None
                for r in range(1, RADIUS + 1):
                    if z - r < 0:
                        term = COEFFICIENTS[r] * below[RADIUS + z - r]
                        added = term if added is None else added + term
                    if z + r >= depth:
                        term = COEFFICIENTS[r] * above[z + r - depth]
                        added = term if added is None else added + term
                new = base_ref[z, x, span]
                if added is not None:
                    new = new + lane(courant, z * across + x) * added
                news.append(new)
            if kind == "middle":
                for z, new in enumerate(news):
                    outs[0][z, x, rows] = new
                store_edges(x, span, news, even, outs[2], outs[1])
            elif kind == "half":
                for z in range(depth // 2):
                    one, two = news[z].astype(BF16), news[z + depth // 2].astype(BF16)
                    outs[0][z, x, span] = jnp.where(lower, one, two)
                    outs[1][z, x, span] = jnp.where(lower, two, one)
            else:
                for z, new in enumerate(news):
                    outs[0][z, x, span] = new.astype(BF16)
        if kind == "middle":
            store_beside(span, rows, core, outs[0], outs[3])

    tiles(along, tile)


def rim_step(base, odds, evens, courant, kind):
    depth, across, along, _ = base.shape
    if kind == "middle":
        out_shape = [
            shape_of(depth, across, along + 2 * EDGE, F32),
            shape_of(RADIUS, across, along, BF16),
            shape_of(RADIUS, across, along, BF16),
            shape_of(depth, RADIUS, along, BF16),
        ]
    elif kind == "half":
        out_shape = [shape_of(depth // 2, across, along, BF16)] * 2
    else:
        out_shape = [shape_of(depth, across, along, BF16)]
    return call(
        functools.partial(rim_body, kind),
        in_specs=whole_vmem(4),
        out_specs=whole_vmem(len(out_shape)),
        out_shape=out_shape,
        scratch_shapes=square_scratch(),
    )(base, odds, evens, courant)


def swap(x, axis, pairs):
    return lax.ppermute(x, axis, [p for a, b in pairs for p in ((a, b), (b, a))])


def even_swap(x):
    return swap(x, "slab", [(i, i + 1) for i in range(0, lax.axis_size("slab") - 1, 2)])


def odd_swap(x):
    return swap(x, "slab", [(i, i + 1) for i in range(1, lax.axis_size("slab") - 1, 2)])


def core_swap(x):
    return swap(x, "sub", [(0, 1)])


def chip_swap(x):
    return swap(x, "probe", [(0, 1)])


def product(a, b):
    return lax.dot_general(a, b, (((0,), (0,)), ((), ())), preferred_element_type=F32)


def block_of(array, i, j):
    return array[i * LANES : (i + 1) * LANES, j * LANES : (j + 1) * LANES]


def eye():
    rows = lax.broadcasted_iota(jnp.int32, (LANES, LANES), 0)
    cols = lax.broadcasted_iota(jnp.int32, (LANES, LANES), 1)
    return rows == cols


def inner_body(kept0, sent0, kept1, sent1, keep_ref, send_ref, panel):
    half = panel.shape[0] // 2
    for n, (kept, sent) in enumerate(((kept0, sent0), (kept1, sent1))):
        columns = slice(n * LANES, (n + 1) * LANES)
        panel[:half, columns] = kept[...].reshape(half, LANES)
        panel[half:, columns] = sent[...].reshape(half, LANES)
    core = lax.axis_index("sub")
    whole = product(panel[...], panel[...])
    first, second = whole[:, :LANES], whole[:, LANES:]
    size = 2 * LANES
    keep_ref[:size] = jnp.where(core == 0, first, second)
    send_ref[:size] = jnp.where(core == 0, second, first)
    diag = [
        jnp.sum(jnp.where(eye(), block_of(whole, n, n), 0.0), axis=0, keepdims=True)
        for n in range(2)
    ]
    none = jnp.zeros_like(diag[0])
    chip = lax.axis_index("probe")
    rows = [jnp.where(chip == n // 2, diag[n % 2], none) for n in range(4)]
    tail = jnp.concatenate(rows + [none] * 4, axis=0)
    keep_ref[size:] = tail
    send_ref[size:] = tail


def inner_gram(fields):
    size = 2 * LANES
    cells = 2 * math.prod(fields[0].shape[:3])
    half = jax.ShapeDtypeStruct((size + 8, LANES), F32)
    return call(
        inner_body,
        in_specs=whole_vmem(4),
        out_specs=whole_vmem(2),
        out_shape=[half, half],
        scratch_shapes=[pltpu.VMEM((cells, size), BF16)],
    )(*fields)


def inner_rows_body(keep_ref, got_ref, tail_ref, *outs):
    slab = lax.axis_index("slab")
    chip = lax.axis_index("probe")
    tail_ref[...] = keep_ref[2 * LANES :] + got_ref[2 * LANES :]
    for d, out in enumerate(outs):
        row = jnp.clip((slab ^ d) - 2 * chip, 0, 1)
        span = pl.ds(pl.multiple_of(row * LANES, LANES), LANES)
        out[...] = (keep_ref[span] + got_ref[span]).astype(out.dtype)


def inner_rows(keep, got, slabs):
    own = jax.ShapeDtypeStruct((LANES, LANES), F32)
    sent = jax.ShapeDtypeStruct((LANES, LANES), BF16)
    return call(
        inner_rows_body,
        in_specs=whole_vmem(2),
        out_specs=whole_vmem(1 + slabs),
        out_shape=[jax.ShapeDtypeStruct((8, LANES), F32), own] + [sent] * (slabs - 1),
    )(keep, got)


def cross_body(kept0, got0, kept1, got1, *refs):
    keep_ref, send_ref, panel = refs[-3:]
    chip = lax.axis_index("probe")
    core = lax.axis_index("sub")
    cells = panel.shape[0]
    for n, (kept, got) in enumerate(((kept0, got0), (kept1, got1))):
        mine = pl.multiple_of((chip * 2 + n) * LANES, LANES)
        other = pl.multiple_of(((1 - chip) * 2 + n) * LANES, LANES)
        panel[:, pl.ds(mine, LANES)] = kept[...].reshape(cells, LANES)
        panel[:, pl.ds(other, LANES)] = got[...].reshape(cells, LANES)
    whole = product(panel[:, : 2 * LANES], panel[:, 2 * LANES :])
    for ref, which in ((keep_ref, core), (send_ref, 1 - core)):
        here = which == 0
        ref[:LANES] = jnp.where(here, block_of(whole, 0, 0), block_of(whole, 0, 1))
        ref[LANES : 2 * LANES] = jnp.where(here, block_of(whole, 1, 0), block_of(whole, 1, 1))
        mixed = jnp.where(here, block_of(whole, 0, 1), block_of(whole, 1, 0))
        ref[2 * LANES :] = mixed


def cross_gram(fields, after):
    cells = math.prod(fields[0].shape[:3])
    three = jax.ShapeDtypeStruct((3 * LANES, LANES), F32)
    return call(
        cross_body,
        in_specs=whole_vmem(4) + [pl.BlockSpec(memory_space=pl.ANY)] * len(after),
        out_specs=whole_vmem(2),
        out_shape=[three, three],
        scratch_shapes=[pltpu.VMEM((cells, 4 * LANES), BF16)],
    )(*fields, *after)


def rounded(ref, block, tail):
    count = block.shape[0]
    high = tail.astype(BF16)
    low = tail - high.astype(F32)
    ref[:count] = block.astype(BF16)
    ref[count : count + 16] = jnp.concatenate([high.astype(F32), low], axis=0).astype(BF16)


def opened(ref, count):
    tail = ref[count : count + 16].astype(F32)
    return ref[:count].astype(F32), tail[:8] + tail[8:]


def cross_rows_body(keep_ref, got_ref, tail_ref, own_ref, *outs):
    slab = lax.axis_index("slab")
    core = lax.axis_index("sub")
    tail = tail_ref[...]
    for d in range(len(outs) + 1):
        owner = slab ^ d
        late = jnp.where(core == 0, jnp.where(owner == 2, 0, 2), jnp.where(owner == 2, 2, 1))
        at = jnp.where(owner < 2, owner, late)
        span = pl.ds(pl.multiple_of(at * LANES, LANES), LANES)
        block = keep_ref[span] + got_ref[span]
        if d == 0:
            own_ref[:LANES] = block
            own_ref[LANES:] = tail
        else:
            rounded(outs[d - 1], block, tail)


def cross_rows(keep, got, tail, slabs):
    own = jax.ShapeDtypeStruct((LANES + 8, LANES), F32)
    sent = jax.ShapeDtypeStruct((LANES + 16, LANES), BF16)
    return call(
        cross_rows_body,
        in_specs=whole_vmem(3),
        out_specs=whole_vmem(slabs),
        out_shape=[own] + [sent] * (slabs - 1),
    )(keep, got, tail)


def sum_body(slabs, own_ref, *refs):
    block, tail = own_ref[:LANES], own_ref[LANES:]
    for ref in refs[: slabs - 1]:
        more, more_tail = opened(ref, LANES)
        block, tail = block + more, tail + more_tail
    inner = refs[slabs - 1][...]
    for ref in refs[slabs : 2 * slabs - 1]:
        inner = inner + ref[...].astype(F32)
    out_ref = refs[-1]
    rounded(out_ref, block, tail)
    out_ref[LANES + 16 :] = inner.astype(BF16)


def sum_all(own, others, inner, inner_others):
    slabs = 1 + len(others)
    return call(
        functools.partial(sum_body, slabs),
        in_specs=whole_vmem(2 * slabs),
        out_specs=whole_vmem(1)[0],
        out_shape=jax.ShapeDtypeStruct((2 * LANES + 16, LANES), BF16),
    )(own, *others, inner, *inner_others)


def normalise_body(cell_count, mine_ref, other_ref, out_ref, norms_ref):
    slab = lax.axis_index("slab")
    core = lax.axis_index("sub")
    chip = lax.axis_index("probe")
    one, one_tail = opened(mine_ref, LANES)
    two, two_tail = opened(other_ref, LANES)
    cross = one + two
    inner_span = pl.ds(LANES + 16, LANES)
    inner = jnp.where(slab // 2 == chip, mine_ref[inner_span], other_ref[inner_span]).astype(F32)
    upper = slab < 2
    values = [jnp.where(upper, inner, cross.T), jnp.where(upper, cross, inner)]
    norms = jnp.sqrt((one_tail + two_tail) / cell_count + EPSILON)
    blocks = [norms[n : n + 1] for n in range(4)]
    own = blocks[0]
    for n in range(1, 4):
        own = jnp.where(slab == n, blocks[n], own)
    norms_ref[...] = own
    own_column = jnp.sum(
        jnp.where(eye(), jnp.broadcast_to(own, (LANES, LANES)), 0.0), axis=1, keepdims=True
    )
    for side in range(2):
        others = jnp.where(core == 0, blocks[2 * side], blocks[2 * side + 1])
        value = values[side] / math.sqrt(cell_count) / (own_column * others)
        value = jnp.where(eye() & (2 * side + core == slab), 0.0, value)
        out_ref[:, side * LANES : (side + 1) * LANES] = value


def normalise(mine, other, cell_count):
    return call(
        functools.partial(normalise_body, cell_count),
        in_specs=whole_vmem(2),
        out_specs=whole_vmem(2),
        out_shape=[
            jax.ShapeDtypeStruct((LANES, 2 * LANES), F32),
            jax.ShapeDtypeStruct((1, LANES), F32),
        ],
    )(mine, other)


def assemble_body(near_ref, far_ref, out_ref):
    core = lax.axis_index("sub")
    for side in range(2):
        columns = slice(side * LANES, (side + 1) * LANES)
        for ref, which in ((near_ref, core), (far_ref, 1 - core)):
            start = pl.multiple_of((2 * side + which) * LANES, LANES)
            out_ref[:, pl.ds(start, LANES)] = ref[:, columns]


def assemble(near, far):
    return call(
        assemble_body,
        in_specs=whole_vmem(2),
        out_specs=whole_vmem(1)[0],
        out_shape=jax.ShapeDtypeStruct((near.shape[0], 4 * LANES), F32),
    )(near, far)


def coupled(finals, cell_count):
    slabs = 4
    own = [field for kept, sent, _ in finals for field in (kept, sent)]
    keep, send = inner_gram(own)
    tail, *inner = inner_rows(keep, core_swap(send), slabs)
    inner_arrived = []
    for d in (2, 3, 1):
        pairs = [
            (2 * (k ^ d) + chip, 2 * k + chip)
            for chip in range(2)
            for k in (2 * chip, 2 * chip + 1)
        ]
        inner_arrived.append(lax.ppermute(inner[d], ("slab", "probe"), pairs))

    pairs = [field for kept, _, got in finals for field in (kept, got)]
    keep, send = cross_gram(pairs, inner_arrived)
    mine, *blocks = cross_rows(keep, core_swap(send), tail, slabs)
    arrived = [
        lax.ppermute(blocks[d - 1], "slab", [(i, i ^ d) for i in range(slabs)])
        for d in (2, 3, 1)
    ]
    total = sum_all(mine, arrived, inner[0], inner_arrived)
    near, norms = normalise(total, chip_swap(total), cell_count)
    return assemble(near, core_swap(near)), norms.reshape(-1)


def coupled_general(fields, cell_count):
    chips = lax.axis_size("probe")
    sketch = jnp.concatenate(fields, axis=-1)
    sketch = sketch.reshape(-1, sketch.shape[-1])
    if chips > 1:
        sketch = lax.all_to_all(sketch, "probe", split_axis=0, concat_axis=1, tiled=True)
    partial_gram = lax.dot_general(
        sketch, sketch, (((0,), (0,)), ((), ())), preferred_element_type=F32
    )
    rows = lax.psum_scatter(partial_gram, "slab", scatter_dimension=0, tiled=True)
    rows = lax.psum(rows, ("probe", "sub"))
    count = rows.shape[0]
    start = lax.axis_index("slab") * count
    own = jnp.diagonal(lax.dynamic_slice_in_dim(rows, start, count, 1))
    own_norms = jnp.sqrt(own / cell_count + EPSILON)
    norms = lax.all_gather(own_norms, "slab", axis=0, tiled=True)
    coupling = rows / math.sqrt(cell_count) / (own_norms[:, None] * norms[None, :])
    row_ids = start + lax.broadcasted_iota(jnp.int32, coupling.shape, 0)
    col_ids = lax.broadcasted_iota(jnp.int32, coupling.shape, 1)
    return jnp.where(row_ids == col_ids, 0.0, coupling), own_norms


def shards(probes, courant, source):
    depth, across, along, count = probes.shape
    chunks = count // LANES
    slabs, chips = lax.axis_size("slab"), lax.axis_size("probe")
    cell_count = depth * across * along * slabs * lax.axis_size("sub")
    paired = chips == 2 and slabs == 4 and chunks == 2 and depth == 2 * RADIUS
    steps = source.shape[0]
    courant = courant.reshape(depth * across, along)
    source = source.reshape(steps, depth * across, along)

    exchange = lambda odd, even, edge: (odd_swap(odd), even_swap(even), core_swap(edge))
    now, previous, halos = [], [None] * chunks, []
    for c in range(chunks):
        u, *edges = first_field(probes, c, source)
        now.append(u)
        halos.append(exchange(*edges))
    finals = []
    for n in range(1, steps):
        for c in range(chunks):
            odd, even, beside = halos[c]
            base = local_step(now[c], beside, probes, c, courant, source, n, previous[c])
            if n < steps - 1:
                u, *edges = rim_step(base, odd, even, courant, "middle")
                previous[c], now[c] = now[c], u
                halos[c] = exchange(*edges)
            elif paired:
                kept, sent = rim_step(base, odd, even, courant, "half")
                finals.append((kept, sent, chip_swap(sent)))
            else:
                finals += rim_step(base, odd, even, courant, "all")
    return (coupled if paired else coupled_general)(finals, cell_count)


def solution(mesh):
    placed = (
        P(("groups", "slab"), "sub", None, "probe"),
        P("slab", "sub", None),
        P(None, ("groups", "slab"), "sub", None),
    )
    return jax.shard_map(
        shards,
        mesh=mesh,
        in_specs=placed,
        out_specs=(P(("groups", "slab"), None), P(("groups", "slab"))),
        check_vma=False,
    )
```

```python
import functools
import math

import jax
import jax.numpy as jnp
from jax import lax
from jax.experimental import pallas as pl
from jax.experimental.pallas import tpu as pltpu
from jax.sharding import PartitionSpec as P

COEFFICIENTS = (-205.0 / 72.0, 8.0 / 5.0, -1.0 / 5.0, 8.0 / 315.0, -1.0 / 560.0)
EPSILON = 1e-06
LANES = 128
RADIUS = 4
EDGE = 8
TILE = 16
F32 = jnp.float32
BF16 = jnp.bfloat16
VMEM_LIMIT = 32 * 1024 * 1024


def call(body, **options):
    return pl.pallas_call(
        body,
        compiler_params=pltpu.CompilerParams(vmem_limit_bytes=VMEM_LIMIT),
        cost_estimate=pl.CostEstimate(flops=1, bytes_accessed=1, transcendentals=0),
        **options,
    )


def whole_vmem(count):
    return [pl.BlockSpec(memory_space=pltpu.VMEM)] * count


def shape_of(depth, across, along, dtype):
    return jax.ShapeDtypeStruct((depth, across, along, LANES), dtype)


def turned(field, scratch):
    rows, along = field.shape
    scratch[:rows, :along] = field
    return jnp.transpose(scratch[...])


def lane(values, n):
    return jnp.broadcast_to(values[:, n : n + 1], (values.shape[0], LANES))


def store_edges(x, span, news, even, even_ref, odd_ref):
    for j in range(RADIUS):
        low = news[j].astype(BF16)
        high = news[len(news) - RADIUS + j].astype(BF16)
        even_ref[j, x, span] = jnp.where(even, high, low)
        odd_ref[j, x, span] = jnp.where(even, low, high)


def store_beside(span, rows, core, u_ref, edge_ref):
    depth, across, _, _ = u_ref.shape
    first = (across - RADIUS) * (1 - core)
    for z in range(depth):
        for j in range(RADIUS):
            edge_ref[z, j, span] = u_ref[z, first + j, rows].astype(BF16)


def slab_is_even():
    return lax.rem(lax.axis_index("slab"), 2) == 0


def clear_pads(u_ref):
    depth, across, padded, _ = u_ref.shape

    def plane(z, _):
        blank = jnp.zeros((across, EDGE, LANES), F32)
        u_ref[z, :, pl.ds(0, EDGE)] = blank
        u_ref[z, :, pl.ds(padded - EDGE, EDGE)] = blank
        return 0

    lax.fori_loop(0, depth, plane, 0)


def tiles(along, body):
    def one(t, _):
        body(pl.multiple_of(t * TILE, TILE))
        return 0

    lax.fori_loop(0, along // TILE, one, 0)


def first_body(chunk, p_ref, s_ref, u_ref, odd_ref, even_ref, edge_ref, square, turned_s):
    depth, across, padded, _ = u_ref.shape
    along = padded - 2 * EDGE
    core = lax.axis_index("sub")
    even = slab_is_even()
    turned_s[...] = turned(s_ref[0], square)
    clear_pads(u_ref)

    def tile(start):
        span = pl.ds(start, TILE)
        rows = pl.ds(start + EDGE, TILE)
        source = turned_s[span]
        for x in range(across):
            news = []
            for z in range(depth):
                p = p_ref[z, x, span, chunk * LANES : (chunk + 1) * LANES].astype(F32)
                new = lane(source, z * across + x) * p
                u_ref[z, x, rows] = new
                news.append(new)
            store_edges(x, span, news, even, even_ref, odd_ref)
        store_beside(span, rows, core, u_ref, edge_ref)

    tiles(along, tile)


def square_scratch():
    return [pltpu.VMEM((LANES, LANES), F32)] * 2


def first_field(probes, chunk, source):
    depth, across, along, _ = probes.shape
    return call(
        functools.partial(first_body, chunk),
        in_specs=whole_vmem(2),
        out_specs=whole_vmem(4),
        out_shape=[
            shape_of(depth, across, along + 2 * EDGE, F32),
            shape_of(RADIUS, across, along, BF16),
            shape_of(RADIUS, across, along, BF16),
            shape_of(depth, RADIUS, along, BF16),
        ],
        scratch_shapes=square_scratch(),
    )(probes, source)


def local_body(chunk, moment, has_previous, *refs):
    refs = list(refs)
    u_ref, beside_ref, p_ref, c_ref, s_ref = refs[:5]
    prev_ref = refs[5] if has_previous else None
    base_ref, square, turned_c, turned_s = refs[-4:]
    depth, across, along, _ = base_ref.shape
    core = lax.axis_index("sub")
    left_on = (core == 1).astype(F32)
    right_on = (core == 0).astype(F32)
    turned_c[...] = turned(c_ref[...], square)
    turned_s[...] = turned(s_ref[moment], square)

    def tile(start):
        span = pl.ds(start, TILE)
        rows = start + EDGE
        courant = turned_c[span]
        source = turned_s[span]
        for z in range(depth):
            beside = [beside_ref[z, j, span].astype(F32) for j in range(RADIUS)]
            row = [v * left_on for v in beside]
            row += [u_ref[z, x, pl.ds(rows, TILE)] for x in range(across)]
            row += [v * right_on for v in beside]
            for x in range(across):
                here = row[RADIUS + x]
                total = (3.0 * COEFFICIENTS[0]) * here
                for r in range(1, RADIUS + 1):
                    near = row[RADIUS + x + r] + row[RADIUS + x - r]
                    near = near + (
                        u_ref[z, x, pl.ds(rows + r, TILE)] + u_ref[z, x, pl.ds(rows - r, TILE)]
                    )
                    if z + r < depth:
                        near = near + u_ref[z + r, x, pl.ds(rows, TILE)]
                    if z - r >= 0:
                        near = near + u_ref[z - r, x, pl.ds(rows, TILE)]
                    total = total + COEFFICIENTS[r] * near
                cell = z * across + x
                p = p_ref[z, x, span, chunk * LANES : (chunk + 1) * LANES].astype(F32)
                new = 2.0 * here
                if has_previous:
                    new = new - prev_ref[z, x, pl.ds(rows, TILE)]
                new = new + lane(courant, cell) * total + lane(source, cell) * p
                base_ref[z, x, span] = new

    tiles(along, tile)


def local_step(u, beside, probes, chunk, courant, source, moment, previous):
    depth, across, along, _ = probes.shape
    operands = [u, beside, probes, courant, source]
    if previous is not None:
        operands.append(previous)
    return call(
        functools.partial(local_body, chunk, moment, previous is not None),
        in_specs=whole_vmem(len(operands)),
        out_specs=whole_vmem(1)[0],
        out_shape=shape_of(depth, across, along, F32),
        scratch_shapes=square_scratch() + square_scratch()[:1],
    )(*operands)


def rim_body(kind, *refs):
    base_ref, odd_ref, even_ref, c_ref = refs[:4]
    outs, (square, turned_c) = refs[4:-2], refs[-2:]
    depth, across, along, _ = base_ref.shape
    core = lax.axis_index("sub")
    even = slab_is_even()
    lower = lax.axis_index("probe") == 0
    turned_c[...] = turned(c_ref[...], square)
    if kind == "middle":
        clear_pads(outs[0])

    def tile(start):
        span = pl.ds(start, TILE)
        rows = pl.ds(start + EDGE, TILE)
        courant = turned_c[span]
        for x in range(across):
            below, above = [], []
            for j in range(RADIUS):
                one, two = even_ref[j, x, span], odd_ref[j, x, span]
                below.append(jnp.where(even, two, one).astype(F32))
                above.append(jnp.where(even, one, two).astype(F32))
            news = []
            for z in range(depth):
                added = None
                for r in range(1, RADIUS + 1):
                    if z - r < 0:
                        term = COEFFICIENTS[r] * below[RADIUS + z - r]
                        added = term if added is None else added + term
                    if z + r >= depth:
                        term = COEFFICIENTS[r] * above[z + r - depth]
                        added = term if added is None else added + term
                new = base_ref[z, x, span]
                if added is not None:
                    new = new + lane(courant, z * across + x) * added
                news.append(new)
            if kind == "middle":
                for z, new in enumerate(news):
                    outs[0][z, x, rows] = new
                store_edges(x, span, news, even, outs[2], outs[1])
            elif kind == "half":
                for z in range(depth // 2):
                    one, two = news[z].astype(BF16), news[z + depth // 2].astype(BF16)
                    outs[0][z, x, span] = jnp.where(lower, one, two)
                    outs[1][z, x, span] = jnp.where(lower, two, one)
            else:
                for z, new in enumerate(news):
                    outs[0][z, x, span] = new.astype(BF16)
        if kind == "middle":
            store_beside(span, rows, core, outs[0], outs[3])

    tiles(along, tile)


def rim_step(base, odds, evens, courant, kind):
    depth, across, along, _ = base.shape
    if kind == "middle":
        out_shape = [
            shape_of(depth, across, along + 2 * EDGE, F32),
            shape_of(RADIUS, across, along, BF16),
            shape_of(RADIUS, across, along, BF16),
            shape_of(depth, RADIUS, along, BF16),
        ]
    elif kind == "half":
        out_shape = [shape_of(depth // 2, across, along, BF16)] * 2
    else:
        out_shape = [shape_of(depth, across, along, BF16)]
    return call(
        functools.partial(rim_body, kind),
        in_specs=whole_vmem(4),
        out_specs=whole_vmem(len(out_shape)),
        out_shape=out_shape,
        scratch_shapes=square_scratch(),
    )(base, odds, evens, courant)


def swap(x, axis, pairs):
    return lax.ppermute(x, axis, [p for a, b in pairs for p in ((a, b), (b, a))])


def even_swap(x):
    return swap(x, "slab", [(i, i + 1) for i in range(0, lax.axis_size("slab") - 1, 2)])


def odd_swap(x):
    return swap(x, "slab", [(i, i + 1) for i in range(1, lax.axis_size("slab") - 1, 2)])


def core_swap(x):
    return swap(x, "sub", [(0, 1)])


def chip_swap(x):
    return swap(x, "probe", [(0, 1)])


def product(a, b):
    return lax.dot_general(a, b, (((0,), (0,)), ((), ())), preferred_element_type=F32)


def block_of(array, i, j):
    return array[i * LANES : (i + 1) * LANES, j * LANES : (j + 1) * LANES]


def eye():
    rows = lax.broadcasted_iota(jnp.int32, (LANES, LANES), 0)
    cols = lax.broadcasted_iota(jnp.int32, (LANES, LANES), 1)
    return rows == cols


def inner_body(kept0, sent0, kept1, sent1, keep_ref, send_ref, panel):
    half = panel.shape[0] // 2
    for n, (kept, sent) in enumerate(((kept0, sent0), (kept1, sent1))):
        columns = slice(n * LANES, (n + 1) * LANES)
        panel[:half, columns] = kept[...].reshape(half, LANES)
        panel[half:, columns] = sent[...].reshape(half, LANES)
    core = lax.axis_index("sub")
    whole = product(panel[...], panel[...])
    first, second = whole[:, :LANES], whole[:, LANES:]
    size = 2 * LANES
    keep_ref[:size] = jnp.where(core == 0, first, second)
    send_ref[:size] = jnp.where(core == 0, second, first)
    diag = [
        jnp.sum(jnp.where(eye(), block_of(whole, n, n), 0.0), axis=0, keepdims=True)
        for n in range(2)
    ]
    none = jnp.zeros_like(diag[0])
    chip = lax.axis_index("probe")
    rows = [jnp.where(chip == n // 2, diag[n % 2], none) for n in range(4)]
    tail = jnp.concatenate(rows + [none] * 4, axis=0)
    keep_ref[size:] = tail
    send_ref[size:] = tail


def inner_gram(fields):
    size = 2 * LANES
    cells = 2 * math.prod(fields[0].shape[:3])
    half = jax.ShapeDtypeStruct((size + 8, LANES), F32)
    return call(
        inner_body,
        in_specs=whole_vmem(4),
        out_specs=whole_vmem(2),
        out_shape=[half, half],
        scratch_shapes=[pltpu.VMEM((cells, size), BF16)],
    )(*fields)


def inner_rows_body(keep_ref, got_ref, tail_ref, *outs):
    slab = lax.axis_index("slab")
    chip = lax.axis_index("probe")
    tail_ref[...] = keep_ref[2 * LANES :] + got_ref[2 * LANES :]
    for d, out in enumerate(outs):
        row = jnp.clip((slab ^ d) - 2 * chip, 0, 1)
        span = pl.ds(pl.multiple_of(row * LANES, LANES), LANES)
        out[...] = (keep_ref[span] + got_ref[span]).astype(out.dtype)


def inner_rows(keep, got, slabs):
    own = jax.ShapeDtypeStruct((LANES, LANES), F32)
    sent = jax.ShapeDtypeStruct((LANES, LANES), BF16)
    return call(
        inner_rows_body,
        in_specs=whole_vmem(2),
        out_specs=whole_vmem(1 + slabs),
        out_shape=[jax.ShapeDtypeStruct((8, LANES), F32), own] + [sent] * (slabs - 1),
    )(keep, got)


def cross_body(kept0, got0, kept1, got1, keep_ref, send_ref, panel):
    chip = lax.axis_index("probe")
    core = lax.axis_index("sub")
    cells = panel.shape[0]
    for n, (kept, got) in enumerate(((kept0, got0), (kept1, got1))):
        mine = pl.multiple_of((chip * 2 + n) * LANES, LANES)
        other = pl.multiple_of(((1 - chip) * 2 + n) * LANES, LANES)
        panel[:, pl.ds(mine, LANES)] = kept[...].reshape(cells, LANES)
        panel[:, pl.ds(other, LANES)] = got[...].reshape(cells, LANES)
    whole = product(panel[:, : 2 * LANES], panel[:, 2 * LANES :])
    for ref, which in ((keep_ref, core), (send_ref, 1 - core)):
        here = which == 0
        ref[:LANES] = jnp.where(here, block_of(whole, 0, 0), block_of(whole, 0, 1))
        ref[LANES : 2 * LANES] = jnp.where(here, block_of(whole, 1, 0), block_of(whole, 1, 1))
        mixed = jnp.where(here, block_of(whole, 0, 1), block_of(whole, 1, 0))
        ref[2 * LANES :] = mixed


def cross_gram(fields):
    cells = math.prod(fields[0].shape[:3])
    three = jax.ShapeDtypeStruct((3 * LANES, LANES), F32)
    return call(
        cross_body,
        in_specs=whole_vmem(4),
        out_specs=whole_vmem(2),
        out_shape=[three, three],
        scratch_shapes=[pltpu.VMEM((cells, 4 * LANES), BF16)],
    )(*fields)


def rounded(ref, block, tail):
    count = block.shape[0]
    high = tail.astype(BF16)
    low = tail - high.astype(F32)
    ref[:count] = block.astype(BF16)
    ref[count : count + 16] = jnp.concatenate([high.astype(F32), low], axis=0).astype(BF16)


def opened(ref, count):
    tail = ref[count : count + 16].astype(F32)
    return ref[:count].astype(F32), tail[:8] + tail[8:]


def cross_rows_body(after, keep_ref, got_ref, tail_ref, *refs):
    own_ref, *outs = refs[after:]
    slab = lax.axis_index("slab")
    core = lax.axis_index("sub")
    tail = tail_ref[...]
    for d in range(len(outs) + 1):
        owner = slab ^ d
        late = jnp.where(core == 0, jnp.where(owner == 2, 0, 2), jnp.where(owner == 2, 2, 1))
        at = jnp.where(owner < 2, owner, late)
        span = pl.ds(pl.multiple_of(at * LANES, LANES), LANES)
        block = keep_ref[span] + got_ref[span]
        if d == 0:
            own_ref[:LANES] = block
            own_ref[LANES:] = tail
        else:
            rounded(outs[d - 1], block, tail)


def cross_rows(keep, got, tail, slabs, after):
    own = jax.ShapeDtypeStruct((LANES + 8, LANES), F32)
    sent = jax.ShapeDtypeStruct((LANES + 16, LANES), BF16)
    return call(
        functools.partial(cross_rows_body, len(after)),
        in_specs=whole_vmem(3) + [pl.BlockSpec(memory_space=pl.ANY)] * len(after),
        out_specs=whole_vmem(slabs),
        out_shape=[own] + [sent] * (slabs - 1),
    )(keep, got, tail, *after)


def sum_body(slabs, own_ref, *refs):
    block, tail = own_ref[:LANES], own_ref[LANES:]
    for ref in refs[: slabs - 1]:
        more, more_tail = opened(ref, LANES)
        block, tail = block + more, tail + more_tail
    inner = refs[slabs - 1][...]
    for ref in refs[slabs : 2 * slabs - 1]:
        inner = inner + ref[...].astype(F32)
    out_ref = refs[-1]
    rounded(out_ref, block, tail)
    out_ref[LANES + 16 :] = inner.astype(BF16)


def sum_all(own, others, inner, inner_others):
    slabs = 1 + len(others)
    return call(
        functools.partial(sum_body, slabs),
        in_specs=whole_vmem(2 * slabs),
        out_specs=whole_vmem(1)[0],
        out_shape=jax.ShapeDtypeStruct((2 * LANES + 16, LANES), BF16),
    )(own, *others, inner, *inner_others)


def normalise_body(cell_count, mine_ref, other_ref, out_ref, norms_ref):
    slab = lax.axis_index("slab")
    core = lax.axis_index("sub")
    chip = lax.axis_index("probe")
    one, one_tail = opened(mine_ref, LANES)
    two, two_tail = opened(other_ref, LANES)
    cross = one + two
    inner_span = pl.ds(LANES + 16, LANES)
    inner = jnp.where(slab // 2 == chip, mine_ref[inner_span], other_ref[inner_span]).astype(F32)
    upper = slab < 2
    values = [jnp.where(upper, inner, cross.T), jnp.where(upper, cross, inner)]
    norms = jnp.sqrt((one_tail + two_tail) / cell_count + EPSILON)
    blocks = [norms[n : n + 1] for n in range(4)]
    own = blocks[0]
    for n in range(1, 4):
        own = jnp.where(slab == n, blocks[n], own)
    norms_ref[...] = own
    own_column = jnp.sum(
        jnp.where(eye(), jnp.broadcast_to(own, (LANES, LANES)), 0.0), axis=1, keepdims=True
    )
    for side in range(2):
        others = jnp.where(core == 0, blocks[2 * side], blocks[2 * side + 1])
        value = values[side] / math.sqrt(cell_count) / (own_column * others)
        value = jnp.where(eye() & (2 * side + core == slab), 0.0, value)
        out_ref[:, side * LANES : (side + 1) * LANES] = value


def normalise(mine, other, cell_count):
    return call(
        functools.partial(normalise_body, cell_count),
        in_specs=whole_vmem(2),
        out_specs=whole_vmem(2),
        out_shape=[
            jax.ShapeDtypeStruct((LANES, 2 * LANES), F32),
            jax.ShapeDtypeStruct((1, LANES), F32),
        ],
    )(mine, other)


def assemble_body(near_ref, far_ref, out_ref):
    core = lax.axis_index("sub")
    for side in range(2):
        columns = slice(side * LANES, (side + 1) * LANES)
        for ref, which in ((near_ref, core), (far_ref, 1 - core)):
            start = pl.multiple_of((2 * side + which) * LANES, LANES)
            out_ref[:, pl.ds(start, LANES)] = ref[:, columns]


def assemble(near, far):
    return call(
        assemble_body,
        in_specs=whole_vmem(2),
        out_specs=whole_vmem(1)[0],
        out_shape=jax.ShapeDtypeStruct((near.shape[0], 4 * LANES), F32),
    )(near, far)


def coupled(finals, cell_count):
    slabs = 4
    own = [field for kept, sent, _ in finals for field in (kept, sent)]
    keep, send = inner_gram(own)
    tail, *inner = inner_rows(keep, core_swap(send), slabs)
    inner_arrived = []
    for d in (2, 3, 1):
        pairs = [
            (2 * (k ^ d) + chip, 2 * k + chip)
            for chip in range(2)
            for k in (2 * chip, 2 * chip + 1)
        ]
        inner_arrived.append(lax.ppermute(inner[d], ("slab", "probe"), pairs))

    pairs = [field for kept, _, got in finals for field in (kept, got)]
    keep, send = cross_gram(pairs)
    mine, *blocks = cross_rows(keep, core_swap(send), tail, slabs, inner_arrived)
    arrived = [
        lax.ppermute(blocks[d - 1], "slab", [(i, i ^ d) for i in range(slabs)])
        for d in (2, 3, 1)
    ]
    total = sum_all(mine, arrived, inner[0], inner_arrived)
    near, norms = normalise(total, chip_swap(total), cell_count)
    return assemble(near, core_swap(near)), norms.reshape(-1)


def coupled_general(fields, cell_count):
    chips = lax.axis_size("probe")
    sketch = jnp.concatenate(fields, axis=-1)
    sketch = sketch.reshape(-1, sketch.shape[-1])
    if chips > 1:
        sketch = lax.all_to_all(sketch, "probe", split_axis=0, concat_axis=1, tiled=True)
    partial_gram = lax.dot_general(
        sketch, sketch, (((0,), (0,)), ((), ())), preferred_element_type=F32
    )
    rows = lax.psum_scatter(partial_gram, "slab", scatter_dimension=0, tiled=True)
    rows = lax.psum(rows, ("probe", "sub"))
    count = rows.shape[0]
    start = lax.axis_index("slab") * count
    own = jnp.diagonal(lax.dynamic_slice_in_dim(rows, start, count, 1))
    own_norms = jnp.sqrt(own / cell_count + EPSILON)
    norms = lax.all_gather(own_norms, "slab", axis=0, tiled=True)
    coupling = rows / math.sqrt(cell_count) / (own_norms[:, None] * norms[None, :])
    row_ids = start + lax.broadcasted_iota(jnp.int32, coupling.shape, 0)
    col_ids = lax.broadcasted_iota(jnp.int32, coupling.shape, 1)
    return jnp.where(row_ids == col_ids, 0.0, coupling), own_norms


def shards(probes, courant, source):
    depth, across, along, count = probes.shape
    chunks = count // LANES
    slabs, chips = lax.axis_size("slab"), lax.axis_size("probe")
    cell_count = depth * across * along * slabs * lax.axis_size("sub")
    paired = chips == 2 and slabs == 4 and chunks == 2 and depth == 2 * RADIUS
    steps = source.shape[0]
    courant = courant.reshape(depth * across, along)
    source = source.reshape(steps, depth * across, along)

    exchange = lambda odd, even, edge: (odd_swap(odd), even_swap(even), core_swap(edge))
    now, previous, halos = [], [None] * chunks, []
    for c in range(chunks):
        u, *edges = first_field(probes, c, source[:1])
        now.append(u)
        halos.append(exchange(*edges))
    finals = []
    for n in range(1, steps):
        for c in range(chunks):
            odd, even, beside = halos[c]
            base = local_step(now[c], beside, probes, c, courant, source, n, previous[c])
            if n < steps - 1:
                u, *edges = rim_step(base, odd, even, courant, "middle")
                previous[c], now[c] = now[c], u
                halos[c] = exchange(*edges)
            elif paired:
                kept, sent = rim_step(base, odd, even, courant, "half")
                finals.append((kept, sent, chip_swap(sent)))
            else:
                finals += rim_step(base, odd, even, courant, "all")
    return (coupled if paired else coupled_general)(finals, cell_count)


def solution(mesh):
    placed = (
        P(("groups", "slab"), "sub", None, "probe"),
        P("slab", "sub", None),
        P(None, ("groups", "slab"), "sub", None),
    )
    return jax.shard_map(
        shards,
        mesh=mesh,
        in_specs=placed,
        out_specs=(P(("groups", "slab"), None), P(("groups", "slab"))),
        check_vma=False,
    )
```

```python
import functools
import math

import jax
import jax.numpy as jnp
from jax import lax
from jax.experimental import pallas as pl
from jax.experimental.pallas import tpu as pltpu
from jax.sharding import PartitionSpec as P

COEFFICIENTS = (-205.0 / 72.0, 8.0 / 5.0, -1.0 / 5.0, 8.0 / 315.0, -1.0 / 560.0)
EPSILON = 1e-06
LANES = 128
RADIUS = 4
EDGE = 8
TILE = 16
F32 = jnp.float32
BF16 = jnp.bfloat16
VMEM_LIMIT = 32 * 1024 * 1024


def call(body, **options):
    return pl.pallas_call(
        body,
        compiler_params=pltpu.CompilerParams(vmem_limit_bytes=VMEM_LIMIT),
        cost_estimate=pl.CostEstimate(flops=1, bytes_accessed=1, transcendentals=0),
        **options,
    )


def whole_vmem(count):
    return [pl.BlockSpec(memory_space=pltpu.VMEM)] * count


def shape_of(depth, across, along, dtype):
    return jax.ShapeDtypeStruct((depth, across, along, LANES), dtype)


def turned(field, scratch):
    rows, along = field.shape
    scratch[:rows, :along] = field
    return jnp.transpose(scratch[...])


def lane(values, n):
    return jnp.broadcast_to(values[:, n : n + 1], (values.shape[0], LANES))


def store_edges(x, span, news, even, even_ref, odd_ref):
    for j in range(RADIUS):
        low = news[j].astype(BF16)
        high = news[len(news) - RADIUS + j].astype(BF16)
        even_ref[j, x, span] = jnp.where(even, high, low)
        odd_ref[j, x, span] = jnp.where(even, low, high)


def store_beside(span, rows, core, u_ref, edge_ref):
    depth, across, _, _ = u_ref.shape
    first = (across - RADIUS) * (1 - core)
    for z in range(depth):
        for j in range(RADIUS):
            edge_ref[z, j, span] = u_ref[z, first + j, rows].astype(BF16)


def slab_is_even():
    return lax.rem(lax.axis_index("slab"), 2) == 0


def clear_pads(u_ref):
    depth, across, padded, _ = u_ref.shape

    def plane(z, _):
        blank = jnp.zeros((across, EDGE, LANES), F32)
        u_ref[z, :, pl.ds(0, EDGE)] = blank
        u_ref[z, :, pl.ds(padded - EDGE, EDGE)] = blank
        return 0

    lax.fori_loop(0, depth, plane, 0)


def tiles(along, body):
    def one(t, _):
        body(pl.multiple_of(t * TILE, TILE))
        return 0

    lax.fori_loop(0, along // TILE, one, 0)


def first_body(chunk, p_ref, s_ref, u_ref, odd_ref, even_ref, edge_ref, square, turned_s):
    depth, across, padded, _ = u_ref.shape
    along = padded - 2 * EDGE
    core = lax.axis_index("sub")
    even = slab_is_even()
    turned_s[...] = turned(s_ref[0], square)
    clear_pads(u_ref)

    def tile(start):
        span = pl.ds(start, TILE)
        rows = pl.ds(start + EDGE, TILE)
        source = turned_s[span]
        for x in range(across):
            news = []
            for z in range(depth):
                p = p_ref[z, x, span, chunk * LANES : (chunk + 1) * LANES].astype(F32)
                new = lane(source, z * across + x) * p
                u_ref[z, x, rows] = new
                news.append(new)
            store_edges(x, span, news, even, even_ref, odd_ref)
        store_beside(span, rows, core, u_ref, edge_ref)

    tiles(along, tile)


def square_scratch():
    return [pltpu.VMEM((LANES, LANES), F32)] * 2


def first_field(probes, chunk, source):
    depth, across, along, _ = probes.shape
    return call(
        functools.partial(first_body, chunk),
        in_specs=whole_vmem(2),
        out_specs=whole_vmem(4),
        out_shape=[
            shape_of(depth, across, along + 2 * EDGE, F32),
            shape_of(RADIUS, across, along, BF16),
            shape_of(RADIUS, across, along, BF16),
            shape_of(depth, RADIUS, along, BF16),
        ],
        scratch_shapes=square_scratch(),
    )(probes, source)


def local_body(chunk, moment, has_previous, *refs):
    refs = list(refs)
    u_ref, beside_ref, p_ref, c_ref, s_ref = refs[:5]
    prev_ref = refs[5] if has_previous else None
    base_ref, square, turned_c, turned_s = refs[-4:]
    depth, across, along, _ = base_ref.shape
    core = lax.axis_index("sub")
    left_on = (core == 1).astype(F32)
    right_on = (core == 0).astype(F32)
    turned_c[...] = turned(c_ref[...], square)
    turned_s[...] = turned(s_ref[moment], square)

    def tile(start):
        span = pl.ds(start, TILE)
        rows = start + EDGE
        courant = turned_c[span]
        source = turned_s[span]
        for z in range(depth):
            beside = [beside_ref[z, j, span].astype(F32) for j in range(RADIUS)]
            row = [v * left_on for v in beside]
            row += [u_ref[z, x, pl.ds(rows, TILE)] for x in range(across)]
            row += [v * right_on for v in beside]
            for x in range(across):
                here = row[RADIUS + x]
                total = (3.0 * COEFFICIENTS[0]) * here
                for r in range(1, RADIUS + 1):
                    near = row[RADIUS + x + r] + row[RADIUS + x - r]
                    near = near + (
                        u_ref[z, x, pl.ds(rows + r, TILE)] + u_ref[z, x, pl.ds(rows - r, TILE)]
                    )
                    if z + r < depth:
                        near = near + u_ref[z + r, x, pl.ds(rows, TILE)]
                    if z - r >= 0:
                        near = near + u_ref[z - r, x, pl.ds(rows, TILE)]
                    total = total + COEFFICIENTS[r] * near
                cell = z * across + x
                p = p_ref[z, x, span, chunk * LANES : (chunk + 1) * LANES].astype(F32)
                new = 2.0 * here
                if has_previous:
                    new = new - prev_ref[z, x, pl.ds(rows, TILE)]
                new = new + lane(courant, cell) * total + lane(source, cell) * p
                base_ref[z, x, span] = new

    tiles(along, tile)


def local_step(u, beside, probes, chunk, courant, source, moment, previous):
    depth, across, along, _ = probes.shape
    operands = [u, beside, probes, courant, source]
    if previous is not None:
        operands.append(previous)
    return call(
        functools.partial(local_body, chunk, moment, previous is not None),
        in_specs=whole_vmem(len(operands)),
        out_specs=whole_vmem(1)[0],
        out_shape=shape_of(depth, across, along, F32),
        scratch_shapes=square_scratch() + square_scratch()[:1],
    )(*operands)


def rim_body(kind, *refs):
    base_ref, odd_ref, even_ref, c_ref = refs[:4]
    outs, (square, turned_c) = refs[4:-2], refs[-2:]
    depth, across, along, _ = base_ref.shape
    core = lax.axis_index("sub")
    even = slab_is_even()
    lower = lax.axis_index("probe") == 0
    turned_c[...] = turned(c_ref[...], square)
    if kind == "middle":
        clear_pads(outs[0])

    def tile(start):
        span = pl.ds(start, TILE)
        rows = pl.ds(start + EDGE, TILE)
        courant = turned_c[span]
        for x in range(across):
            below, above = [], []
            for j in range(RADIUS):
                one, two = even_ref[j, x, span], odd_ref[j, x, span]
                below.append(jnp.where(even, two, one).astype(F32))
                above.append(jnp.where(even, one, two).astype(F32))
            news = []
            for z in range(depth):
                added = None
                for r in range(1, RADIUS + 1):
                    if z - r < 0:
                        term = COEFFICIENTS[r] * below[RADIUS + z - r]
                        added = term if added is None else added + term
                    if z + r >= depth:
                        term = COEFFICIENTS[r] * above[z + r - depth]
                        added = term if added is None else added + term
                new = base_ref[z, x, span]
                if added is not None:
                    new = new + lane(courant, z * across + x) * added
                news.append(new)
            if kind == "middle":
                for z, new in enumerate(news):
                    outs[0][z, x, rows] = new
                store_edges(x, span, news, even, outs[2], outs[1])
            elif kind == "half":
                for z in range(depth // 2):
                    one, two = news[z].astype(BF16), news[z + depth // 2].astype(BF16)
                    outs[0][z, x, span] = jnp.where(lower, one, two)
                    outs[1][z, x, span] = jnp.where(lower, two, one)
            else:
                for z, new in enumerate(news):
                    outs[0][z, x, span] = new.astype(BF16)
        if kind == "middle":
            store_beside(span, rows, core, outs[0], outs[3])

    tiles(along, tile)


def rim_step(base, odds, evens, courant, kind):
    depth, across, along, _ = base.shape
    if kind == "middle":
        out_shape = [
            shape_of(depth, across, along + 2 * EDGE, F32),
            shape_of(RADIUS, across, along, BF16),
            shape_of(RADIUS, across, along, BF16),
            shape_of(depth, RADIUS, along, BF16),
        ]
    elif kind == "half":
        out_shape = [shape_of(depth // 2, across, along, BF16)] * 2
    else:
        out_shape = [shape_of(depth, across, along, BF16)]
    return call(
        functools.partial(rim_body, kind),
        in_specs=whole_vmem(4),
        out_specs=whole_vmem(len(out_shape)),
        out_shape=out_shape,
        scratch_shapes=square_scratch(),
    )(base, odds, evens, courant)


def swap(x, axis, pairs):
    return lax.ppermute(x, axis, [p for a, b in pairs for p in ((a, b), (b, a))])


def even_swap(x):
    return swap(x, "slab", [(i, i + 1) for i in range(0, lax.axis_size("slab") - 1, 2)])


def odd_swap(x):
    return swap(x, "slab", [(i, i + 1) for i in range(1, lax.axis_size("slab") - 1, 2)])


def core_swap(x):
    return swap(x, "sub", [(0, 1)])


def chip_swap(x):
    return swap(x, "probe", [(0, 1)])


def product(a, b):
    return lax.dot_general(a, b, (((0,), (0,)), ((), ())), preferred_element_type=F32)


def block_of(array, i, j):
    return array[i * LANES : (i + 1) * LANES, j * LANES : (j + 1) * LANES]


def eye():
    rows = lax.broadcasted_iota(jnp.int32, (LANES, LANES), 0)
    cols = lax.broadcasted_iota(jnp.int32, (LANES, LANES), 1)
    return rows == cols


def inner_body(kept0, sent0, kept1, sent1, keep_ref, send_ref, panel):
    half = panel.shape[0] // 2
    for n, (kept, sent) in enumerate(((kept0, sent0), (kept1, sent1))):
        columns = slice(n * LANES, (n + 1) * LANES)
        panel[:half, columns] = kept[...].reshape(half, LANES)
        panel[half:, columns] = sent[...].reshape(half, LANES)
    core = lax.axis_index("sub")
    whole = product(panel[...], panel[...])
    first, second = whole[:, :LANES], whole[:, LANES:]
    size = 2 * LANES
    keep_ref[:size] = jnp.where(core == 0, first, second)
    send_ref[:size] = jnp.where(core == 0, second, first)
    diag = [
        jnp.sum(jnp.where(eye(), block_of(whole, n, n), 0.0), axis=0, keepdims=True)
        for n in range(2)
    ]
    none = jnp.zeros_like(diag[0])
    chip = lax.axis_index("probe")
    rows = [jnp.where(chip == n // 2, diag[n % 2], none) for n in range(4)]
    tail = jnp.concatenate(rows + [none] * 4, axis=0)
    keep_ref[size:] = tail
    send_ref[size:] = tail


def inner_gram(fields):
    size = 2 * LANES
    cells = 2 * math.prod(fields[0].shape[:3])
    half = jax.ShapeDtypeStruct((size + 8, LANES), F32)
    return call(
        inner_body,
        in_specs=whole_vmem(4),
        out_specs=whole_vmem(2),
        out_shape=[half, half],
        scratch_shapes=[pltpu.VMEM((cells, size), BF16)],
    )(*fields)


def inner_sum_body(keep_ref, got_ref, tail_ref, own_ref, sent_ref):
    size = sent_ref.shape[0]
    total = keep_ref[:size] + got_ref[:size]
    own_ref[...] = total
    sent_ref[...] = total.astype(BF16)
    tail_ref[...] = keep_ref[size:] + got_ref[size:]


def inner_sum(keep, got):
    size = keep.shape[0] - 8
    return call(
        inner_sum_body,
        in_specs=whole_vmem(2),
        out_specs=whole_vmem(3),
        out_shape=[
            jax.ShapeDtypeStruct((8, LANES), F32),
            jax.ShapeDtypeStruct((size, LANES), F32),
            jax.ShapeDtypeStruct((size, LANES), BF16),
        ],
    )(keep, got)


def cross_body(kept0, got0, kept1, got1, _, keep_ref, send_ref, panel):
    chip = lax.axis_index("probe")
    core = lax.axis_index("sub")
    cells = panel.shape[0]
    for n, (kept, got) in enumerate(((kept0, got0), (kept1, got1))):
        mine = pl.multiple_of((chip * 2 + n) * LANES, LANES)
        other = pl.multiple_of(((1 - chip) * 2 + n) * LANES, LANES)
        panel[:, pl.ds(mine, LANES)] = kept[...].reshape(cells, LANES)
        panel[:, pl.ds(other, LANES)] = got[...].reshape(cells, LANES)
    whole = product(panel[:, : 2 * LANES], panel[:, 2 * LANES :])
    for ref, which in ((keep_ref, core), (send_ref, 1 - core)):
        here = which == 0
        ref[:LANES] = jnp.where(here, block_of(whole, 0, 0), block_of(whole, 0, 1))
        ref[LANES : 2 * LANES] = jnp.where(here, block_of(whole, 1, 0), block_of(whole, 1, 1))
        mixed = jnp.where(here, block_of(whole, 0, 1), block_of(whole, 1, 0))
        ref[2 * LANES :] = mixed


def cross_gram(fields, after):
    cells = math.prod(fields[0].shape[:3])
    three = jax.ShapeDtypeStruct((3 * LANES, LANES), F32)
    return call(
        cross_body,
        in_specs=whole_vmem(4) + [pl.BlockSpec(memory_space=pl.ANY)],
        out_specs=whole_vmem(2),
        out_shape=[three, three],
        scratch_shapes=[pltpu.VMEM((cells, 4 * LANES), BF16)],
    )(*fields, after)


def rounded(ref, block, tail):
    count = block.shape[0]
    high = tail.astype(BF16)
    low = tail - high.astype(F32)
    ref[:count] = block.astype(BF16)
    ref[count : count + 16] = jnp.concatenate([high.astype(F32), low], axis=0).astype(BF16)


def opened(ref, count):
    tail = ref[count : count + 16].astype(F32)
    return ref[:count].astype(F32), tail[:8] + tail[8:]


def cross_rows_body(keep_ref, got_ref, tail_ref, inner_ref, inner_got_ref, own_ref, *outs):
    slab = lax.axis_index("slab")
    core = lax.axis_index("sub")
    chip = lax.axis_index("probe")
    tail = tail_ref[...]
    for d in range(len(outs) + 1):
        owner = slab ^ d
        late = jnp.where(core == 0, jnp.where(owner == 2, 0, 2), jnp.where(owner == 2, 2, 1))
        at = jnp.where(owner < 2, owner, late)
        span = pl.ds(pl.multiple_of(at * LANES, LANES), LANES)
        block = keep_ref[span] + got_ref[span]
        row = pl.multiple_of(jnp.clip(owner - 2 * chip, 0, 1) * LANES, LANES)
        inner = inner_ref[pl.ds(row, LANES)] + inner_got_ref[pl.ds(row, LANES)].astype(F32)
        if d == 0:
            own_ref[:LANES] = block
            own_ref[LANES : LANES + 8] = tail
            own_ref[LANES + 8 :] = inner
        else:
            rounded(outs[d - 1], block, tail)
            if d == 1:
                outs[0][LANES + 16 :] = inner.astype(BF16)


def cross_rows(keep, got, tail, inner, inner_got, slabs):
    own = jax.ShapeDtypeStruct((2 * LANES + 8, LANES), F32)
    near = jax.ShapeDtypeStruct((2 * LANES + 16, LANES), BF16)
    far = jax.ShapeDtypeStruct((LANES + 16, LANES), BF16)
    return call(
        cross_rows_body,
        in_specs=whole_vmem(5),
        out_specs=whole_vmem(slabs),
        out_shape=[own, near] + [far] * (slabs - 2),
    )(keep, got, tail, inner, inner_got)


def sum_body(own_ref, *refs):
    block, tail = own_ref[:LANES], own_ref[LANES : LANES + 8]
    *others, out_ref = refs
    for ref in others:
        more, more_tail = opened(ref, LANES)
        block, tail = block + more, tail + more_tail
    inner = own_ref[LANES + 8 :] + others[-1][LANES + 16 :].astype(F32)
    rounded(out_ref, block, tail)
    out_ref[LANES + 16 :] = inner.astype(BF16)


def sum_all(own, others):
    return call(
        sum_body,
        in_specs=whole_vmem(1 + len(others)),
        out_specs=whole_vmem(1)[0],
        out_shape=jax.ShapeDtypeStruct(others[-1].shape, BF16),
    )(own, *others)


def normalise_body(cell_count, mine_ref, other_ref, out_ref, norms_ref):
    slab = lax.axis_index("slab")
    core = lax.axis_index("sub")
    chip = lax.axis_index("probe")
    one, one_tail = opened(mine_ref, LANES)
    two, two_tail = opened(other_ref, LANES)
    cross = one + two
    inner_span = pl.ds(LANES + 16, LANES)
    inner = jnp.where(slab // 2 == chip, mine_ref[inner_span], other_ref[inner_span]).astype(F32)
    upper = slab < 2
    values = [jnp.where(upper, inner, cross.T), jnp.where(upper, cross, inner)]
    norms = jnp.sqrt((one_tail + two_tail) / cell_count + EPSILON)
    blocks = [norms[n : n + 1] for n in range(4)]
    own = blocks[0]
    for n in range(1, 4):
        own = jnp.where(slab == n, blocks[n], own)
    norms_ref[...] = own
    own_column = jnp.sum(
        jnp.where(eye(), jnp.broadcast_to(own, (LANES, LANES)), 0.0), axis=1, keepdims=True
    )
    for side in range(2):
        others = jnp.where(core == 0, blocks[2 * side], blocks[2 * side + 1])
        value = values[side] / math.sqrt(cell_count) / (own_column * others)
        value = jnp.where(eye() & (2 * side + core == slab), 0.0, value)
        out_ref[:, side * LANES : (side + 1) * LANES] = value


def normalise(mine, other, cell_count):
    return call(
        functools.partial(normalise_body, cell_count),
        in_specs=whole_vmem(2),
        out_specs=whole_vmem(2),
        out_shape=[
            jax.ShapeDtypeStruct((LANES, 2 * LANES), F32),
            jax.ShapeDtypeStruct((1, LANES), F32),
        ],
    )(mine, other)


def assemble_body(near_ref, far_ref, out_ref):
    core = lax.axis_index("sub")
    for side in range(2):
        columns = slice(side * LANES, (side + 1) * LANES)
        for ref, which in ((near_ref, core), (far_ref, 1 - core)):
            start = pl.multiple_of((2 * side + which) * LANES, LANES)
            out_ref[:, pl.ds(start, LANES)] = ref[:, columns]


def assemble(near, far):
    return call(
        assemble_body,
        in_specs=whole_vmem(2),
        out_specs=whole_vmem(1)[0],
        out_shape=jax.ShapeDtypeStruct((near.shape[0], 4 * LANES), F32),
    )(near, far)


def coupled(finals, cell_count):
    slabs = 4
    own = [field for kept, sent, _ in finals for field in (kept, sent)]
    keep, send = inner_gram(own)
    tail, inner, sent = inner_sum(keep, core_swap(send))
    pairs = [
        (2 * (k ^ 2) + chip, 2 * k + chip) for chip in range(2) for k in (2 * chip, 2 * chip + 1)
    ]
    inner_got = lax.ppermute(sent, ("slab", "probe"), pairs)

    pairs = [field for kept, _, got in finals for field in (kept, got)]
    keep, send = cross_gram(pairs, inner_got)
    mine, *blocks = cross_rows(keep, core_swap(send), tail, inner, inner_got, slabs)
    arrived = [
        lax.ppermute(blocks[d - 1], "slab", [(i, i ^ d) for i in range(slabs)])
        for d in (2, 3, 1)
    ]
    total = sum_all(mine, arrived)
    near, norms = normalise(total, chip_swap(total), cell_count)
    return assemble(near, core_swap(near)), norms.reshape(-1)


def coupled_general(fields, cell_count):
    chips = lax.axis_size("probe")
    sketch = jnp.concatenate(fields, axis=-1)
    sketch = sketch.reshape(-1, sketch.shape[-1])
    if chips > 1:
        sketch = lax.all_to_all(sketch, "probe", split_axis=0, concat_axis=1, tiled=True)
    partial_gram = lax.dot_general(
        sketch, sketch, (((0,), (0,)), ((), ())), preferred_element_type=F32
    )
    rows = lax.psum_scatter(partial_gram, "slab", scatter_dimension=0, tiled=True)
    rows = lax.psum(rows, ("probe", "sub"))
    count = rows.shape[0]
    start = lax.axis_index("slab") * count
    own = jnp.diagonal(lax.dynamic_slice_in_dim(rows, start, count, 1))
    own_norms = jnp.sqrt(own / cell_count + EPSILON)
    norms = lax.all_gather(own_norms, "slab", axis=0, tiled=True)
    coupling = rows / math.sqrt(cell_count) / (own_norms[:, None] * norms[None, :])
    row_ids = start + lax.broadcasted_iota(jnp.int32, coupling.shape, 0)
    col_ids = lax.broadcasted_iota(jnp.int32, coupling.shape, 1)
    return jnp.where(row_ids == col_ids, 0.0, coupling), own_norms


def shards(probes, courant, source):
    depth, across, along, count = probes.shape
    chunks = count // LANES
    slabs, chips = lax.axis_size("slab"), lax.axis_size("probe")
    cell_count = depth * across * along * slabs * lax.axis_size("sub")
    paired = chips == 2 and slabs == 4 and chunks == 2 and depth == 2 * RADIUS
    steps = source.shape[0]
    courant = courant.reshape(depth * across, along)
    source = source.reshape(steps, depth * across, along)

    exchange = lambda odd, even, edge: (odd_swap(odd), even_swap(even), core_swap(edge))
    now, previous, halos = [], [None] * chunks, []
    for c in range(chunks):
        u, *edges = first_field(probes, c, source[:1])
        now.append(u)
        halos.append(exchange(*edges))
    finals = []
    for n in range(1, steps):
        for c in range(chunks):
            odd, even, beside = halos[c]
            base = local_step(now[c], beside, probes, c, courant, source, n, previous[c])
            if n < steps - 1:
                u, *edges = rim_step(base, odd, even, courant, "middle")
                previous[c], now[c] = now[c], u
                halos[c] = exchange(*edges)
            elif paired:
                kept, sent = rim_step(base, odd, even, courant, "half")
                finals.append((kept, sent, chip_swap(sent)))
            else:
                finals += rim_step(base, odd, even, courant, "all")
    return (coupled if paired else coupled_general)(finals, cell_count)


def solution(mesh):
    placed = (
        P(("groups", "slab"), "sub", None, "probe"),
        P("slab", "sub", None),
        P(None, ("groups", "slab"), "sub", None),
    )
    return jax.shard_map(
        shards,
        mesh=mesh,
        in_specs=placed,
        out_specs=(P(("groups", "slab"), None), P(("groups", "slab"))),
        check_vma=False,
    )
```

```python
import functools
import math

import jax
import jax.numpy as jnp
from jax import lax
from jax.experimental import pallas as pl
from jax.experimental.pallas import tpu as pltpu
from jax.sharding import PartitionSpec as P

COEFFICIENTS = (-205.0 / 72.0, 8.0 / 5.0, -1.0 / 5.0, 8.0 / 315.0, -1.0 / 560.0)
EPSILON = 1e-06
LANES = 128
RADIUS = 4
EDGE = 8
TILE = 16
F32 = jnp.float32
BF16 = jnp.bfloat16
VMEM_LIMIT = 32 * 1024 * 1024


def call(body, **options):
    return pl.pallas_call(
        body,
        compiler_params=pltpu.CompilerParams(vmem_limit_bytes=VMEM_LIMIT),
        cost_estimate=pl.CostEstimate(flops=1, bytes_accessed=1, transcendentals=0),
        **options,
    )


def whole_vmem(count):
    return [pl.BlockSpec(memory_space=pltpu.VMEM)] * count


def shape_of(depth, across, along, dtype):
    return jax.ShapeDtypeStruct((depth, across, along, LANES), dtype)


def turned(field, scratch):
    rows, along = field.shape
    scratch[:rows, :along] = field
    return jnp.transpose(scratch[...])


def lane(values, n):
    return jnp.broadcast_to(values[:, n : n + 1], (values.shape[0], LANES))


def store_edges(x, span, news, even, even_ref, odd_ref):
    for j in range(RADIUS):
        low = news[j].astype(BF16)
        high = news[len(news) - RADIUS + j].astype(BF16)
        even_ref[j, x, span] = jnp.where(even, high, low)
        odd_ref[j, x, span] = jnp.where(even, low, high)


def store_beside(span, rows, core, u_ref, edge_ref):
    depth, across, _, _ = u_ref.shape
    first = (across - RADIUS) * (1 - core)
    for z in range(depth):
        for j in range(RADIUS):
            edge_ref[z, j, span] = u_ref[z, first + j, rows].astype(BF16)


def slab_is_even():
    return lax.rem(lax.axis_index("slab"), 2) == 0


def clear_pads(u_ref):
    depth, across, padded, _ = u_ref.shape

    def plane(z, _):
        blank = jnp.zeros((across, EDGE, LANES), F32)
        u_ref[z, :, pl.ds(0, EDGE)] = blank
        u_ref[z, :, pl.ds(padded - EDGE, EDGE)] = blank
        return 0

    lax.fori_loop(0, depth, plane, 0)


def tiles(along, body):
    def one(t, _):
        body(pl.multiple_of(t * TILE, TILE))
        return 0

    lax.fori_loop(0, along // TILE, one, 0)


def first_body(chunk, p_ref, s_ref, u_ref, odd_ref, even_ref, edge_ref, square, turned_s):
    depth, across, padded, _ = u_ref.shape
    along = padded - 2 * EDGE
    core = lax.axis_index("sub")
    even = slab_is_even()
    turned_s[...] = turned(s_ref[0], square)
    clear_pads(u_ref)

    def tile(start):
        span = pl.ds(start, TILE)
        rows = pl.ds(start + EDGE, TILE)
        source = turned_s[span]
        for x in range(across):
            news = []
            for z in range(depth):
                p = p_ref[z, x, span, chunk * LANES : (chunk + 1) * LANES].astype(F32)
                new = lane(source, z * across + x) * p
                u_ref[z, x, rows] = new
                news.append(new)
            store_edges(x, span, news, even, even_ref, odd_ref)
        store_beside(span, rows, core, u_ref, edge_ref)

    tiles(along, tile)


def square_scratch():
    return [pltpu.VMEM((LANES, LANES), F32)] * 2


def first_field(probes, chunk, source):
    depth, across, along, _ = probes.shape
    return call(
        functools.partial(first_body, chunk),
        in_specs=whole_vmem(2),
        out_specs=whole_vmem(4),
        out_shape=[
            shape_of(depth, across, along + 2 * EDGE, F32),
            shape_of(RADIUS, across, along, BF16),
            shape_of(RADIUS, across, along, BF16),
            shape_of(depth, RADIUS, along, BF16),
        ],
        scratch_shapes=square_scratch(),
    )(probes, source)


def local_body(chunk, moment, has_previous, *refs):
    refs = list(refs)
    u_ref, beside_ref, p_ref, c_ref, s_ref = refs[:5]
    prev_ref = refs[5] if has_previous else None
    base_ref, square, turned_c, turned_s = refs[-4:]
    depth, across, along, _ = base_ref.shape
    core = lax.axis_index("sub")
    left_on = (core == 1).astype(F32)
    right_on = (core == 0).astype(F32)
    turned_c[...] = turned(c_ref[...], square)
    turned_s[...] = turned(s_ref[moment], square)

    def tile(start):
        span = pl.ds(start, TILE)
        rows = start + EDGE
        courant = turned_c[span]
        source = turned_s[span]
        for z in range(depth):
            beside = [beside_ref[z, j, span].astype(F32) for j in range(RADIUS)]
            row = [v * left_on for v in beside]
            row += [u_ref[z, x, pl.ds(rows, TILE)] for x in range(across)]
            row += [v * right_on for v in beside]
            for x in range(across):
                here = row[RADIUS + x]
                total = (3.0 * COEFFICIENTS[0]) * here
                for r in range(1, RADIUS + 1):
                    near = row[RADIUS + x + r] + row[RADIUS + x - r]
                    near = near + (
                        u_ref[z, x, pl.ds(rows + r, TILE)] + u_ref[z, x, pl.ds(rows - r, TILE)]
                    )
                    if z + r < depth:
                        near = near + u_ref[z + r, x, pl.ds(rows, TILE)]
                    if z - r >= 0:
                        near = near + u_ref[z - r, x, pl.ds(rows, TILE)]
                    total = total + COEFFICIENTS[r] * near
                cell = z * across + x
                p = p_ref[z, x, span, chunk * LANES : (chunk + 1) * LANES].astype(F32)
                new = 2.0 * here
                if has_previous:
                    new = new - prev_ref[z, x, pl.ds(rows, TILE)]
                new = new + lane(courant, cell) * total + lane(source, cell) * p
                base_ref[z, x, span] = new

    tiles(along, tile)


def local_step(u, beside, probes, chunk, courant, source, moment, previous):
    depth, across, along, _ = probes.shape
    operands = [u, beside, probes, courant, source]
    if previous is not None:
        operands.append(previous)
    return call(
        functools.partial(local_body, chunk, moment, previous is not None),
        in_specs=whole_vmem(len(operands)),
        out_specs=whole_vmem(1)[0],
        out_shape=shape_of(depth, across, along, F32),
        scratch_shapes=square_scratch() + square_scratch()[:1],
    )(*operands)


def rim_body(kind, *refs):
    base_ref, odd_ref, even_ref, c_ref = refs[:4]
    outs, (square, turned_c) = refs[4:-2], refs[-2:]
    depth, across, along, _ = base_ref.shape
    core = lax.axis_index("sub")
    even = slab_is_even()
    lower = lax.axis_index("probe") == 0
    turned_c[...] = turned(c_ref[...], square)
    if kind == "middle":
        clear_pads(outs[0])

    def tile(start):
        span = pl.ds(start, TILE)
        rows = pl.ds(start + EDGE, TILE)
        courant = turned_c[span]
        for x in range(across):
            below, above = [], []
            for j in range(RADIUS):
                one, two = even_ref[j, x, span], odd_ref[j, x, span]
                below.append(jnp.where(even, two, one).astype(F32))
                above.append(jnp.where(even, one, two).astype(F32))
            news = []
            for z in range(depth):
                added = None
                for r in range(1, RADIUS + 1):
                    if z - r < 0:
                        term = COEFFICIENTS[r] * below[RADIUS + z - r]
                        added = term if added is None else added + term
                    if z + r >= depth:
                        term = COEFFICIENTS[r] * above[z + r - depth]
                        added = term if added is None else added + term
                new = base_ref[z, x, span]
                if added is not None:
                    new = new + lane(courant, z * across + x) * added
                news.append(new)
            if kind == "middle":
                for z, new in enumerate(news):
                    outs[0][z, x, rows] = new
                store_edges(x, span, news, even, outs[2], outs[1])
            elif kind == "half":
                for z in range(depth // 2):
                    one, two = news[z].astype(BF16), news[z + depth // 2].astype(BF16)
                    outs[0][z, x, span] = jnp.where(lower, one, two)
                    outs[1][z, x, span] = jnp.where(lower, two, one)
            else:
                for z, new in enumerate(news):
                    outs[0][z, x, span] = new.astype(BF16)
        if kind == "middle":
            store_beside(span, rows, core, outs[0], outs[3])

    tiles(along, tile)


def rim_step(base, odds, evens, courant, kind):
    depth, across, along, _ = base.shape
    if kind == "middle":
        out_shape = [
            shape_of(depth, across, along + 2 * EDGE, F32),
            shape_of(RADIUS, across, along, BF16),
            shape_of(RADIUS, across, along, BF16),
            shape_of(depth, RADIUS, along, BF16),
        ]
    elif kind == "half":
        out_shape = [shape_of(depth // 2, across, along, BF16)] * 2
    else:
        out_shape = [shape_of(depth, across, along, BF16)]
    return call(
        functools.partial(rim_body, kind),
        in_specs=whole_vmem(4),
        out_specs=whole_vmem(len(out_shape)),
        out_shape=out_shape,
        scratch_shapes=square_scratch(),
    )(base, odds, evens, courant)


def swap(x, axis, pairs):
    return lax.ppermute(x, axis, [p for a, b in pairs for p in ((a, b), (b, a))])


def even_swap(x):
    return swap(x, "slab", [(i, i + 1) for i in range(0, lax.axis_size("slab") - 1, 2)])


def odd_swap(x):
    return swap(x, "slab", [(i, i + 1) for i in range(1, lax.axis_size("slab") - 1, 2)])


def core_swap(x):
    return swap(x, "sub", [(0, 1)])


def chip_swap(x):
    return swap(x, "probe", [(0, 1)])


def half_rows(square, field, half, chip):
    square[...] = turned(field, square)
    rows = square[pl.ds(pl.multiple_of(chip * half, 8), half)]
    return jnp.concatenate([rows, rows], axis=0)


def own_half(window, half, chip):
    return jnp.where(chip == 0, window[:half], window[window.shape[0] - half :])


def prepare_body(p_ref, s_ref, window_ref, odd_ref, even_ref, square):
    depth, across, rows, _ = window_ref.shape
    half = rows - EDGE
    along = 2 * half
    chip = lax.axis_index("probe")
    even = slab_is_even()
    lanes = slice(LANES, 2 * LANES)
    skip = along - rows

    def plane(z, _):
        start = pl.multiple_of((1 - chip) * skip, TILE)
        window_ref[z] = p_ref[z, :, pl.ds(start, rows), lanes]
        return 0

    lax.fori_loop(0, depth, plane, 0)
    source = half_rows(square, s_ref[0], half, chip)[:half]
    start = pl.multiple_of(chip * skip, TILE)

    def value(z, x):
        window = p_ref[z, x, pl.ds(start, rows), lanes].astype(F32)
        return lane(source, z * across + x) * own_half(window, half, chip)

    for j in range(RADIUS):
        for i in range(across // 2):
            low, high = [
                jnp.concatenate([value(z, 2 * i), value(z, 2 * i + 1)], axis=0).astype(BF16)
                for z in (j, depth - RADIUS + j)
            ]
            even_ref[j, i] = jnp.where(even, high, low)
            odd_ref[j, i] = jnp.where(even, low, high)


def prepare(probes, source):
    depth, across, along, _ = probes.shape
    edge = shape_of(RADIUS, across // 2, along, BF16)
    return call(
        prepare_body,
        in_specs=whole_vmem(2),
        out_specs=whole_vmem(3),
        out_shape=[shape_of(depth, across, along // 2 + EDGE, BF16), edge, edge],
        scratch_shapes=square_scratch()[:1],
    )(probes, source)


def store_sides(core, chip, u_ref, edge_ref, rows_ref):
    depth, across, padded, _ = u_ref.shape
    segment = padded // 2
    half = segment - 2 * EDGE
    first = (across - RADIUS) * (1 - core)
    near = pl.multiple_of(jnp.where(chip == 0, half, EDGE), 8)

    def plane(z, _):
        for j in range(RADIUS):
            parts = [
                u_ref[z, first + j, g * segment + EDGE : g * segment + EDGE + half]
                for g in range(2)
            ]
            edge_ref[z, j] = jnp.concatenate(parts, axis=0).astype(BF16)
        if rows_ref is not None:
            for x in range(across):
                parts = [u_ref[z, x, pl.ds(near + g * segment, EDGE)] for g in range(2)]
                rows_ref[z, x] = jnp.concatenate(parts, axis=0).astype(BF16)
        return 0

    lax.fori_loop(0, depth, plane, 0)


def shared_first_body(
    p_ref, got_ref, s_ref, u_ref, odd_ref, even_ref, edge_ref, both_ref, square
):
    depth, across, rows, _ = got_ref.shape
    half = rows - EDGE
    segment = half + 2 * EDGE
    along = 2 * half
    chip = lax.axis_index("probe")
    core = lax.axis_index("sub")
    even = slab_is_even()
    lanes = slice(LANES, 2 * LANES)
    square[...] = turned(s_ref[0], square)
    start = pl.multiple_of(chip * (along - rows), TILE)
    source = square[pl.ds(start, rows)]
    blank = jnp.zeros((EDGE, LANES), F32)
    for i in range(across // 2):
        theirs = []
        for z in range(depth):
            pair = []
            for x in (2 * i, 2 * i + 1):
                mine = p_ref[z, x, pl.ds(start, rows), lanes].astype(F32)
                got = got_ref[z, x].astype(F32)
                scale = lane(source, z * across + x)
                windows = [jnp.where(chip == 0, mine, got), jnp.where(chip == 0, got, mine)]
                for g, window in enumerate(windows):
                    at = pl.multiple_of(g * segment + EDGE * (1 - chip), 8)
                    u_ref[z, x, pl.ds(at, rows)] = scale * window
                    out = pl.multiple_of(g * segment + chip * (half + EDGE), 8)
                    u_ref[z, x, pl.ds(out, EDGE)] = blank
                both = [own_half(window, half, chip) for window in windows]
                both_ref[z, x] = jnp.concatenate(both, axis=0).astype(BF16)
                pair.append(own_half(scale * got, half, chip))
            theirs.append(jnp.concatenate(pair, axis=0))
        store_edges(i, pl.ds(0, along), theirs, even, even_ref, odd_ref)
    store_sides(core, chip, u_ref, edge_ref, None)


def shared_first(probes, got, source):
    depth, across, along, _ = probes.shape
    edge = shape_of(RADIUS, across // 2, along, BF16)
    return call(
        shared_first_body,
        in_specs=whole_vmem(3),
        out_specs=whole_vmem(5),
        out_shape=[
            shape_of(depth, across, along + 4 * EDGE, F32),
            edge,
            edge,
            shape_of(depth, RADIUS, along, BF16),
            shape_of(depth, across, along, BF16),
        ],
        scratch_shapes=square_scratch()[:1],
    )(probes, got, source)


def fill_rows(u_ref, rows_ref, chip):
    depth, across, padded, _ = u_ref.shape
    segment = padded // 2

    def plane(z, _):
        for x in range(across):
            got = rows_ref[z, x].astype(F32)
            for g in range(2):
                part = got[g * EDGE : (g + 1) * EDGE]
                blank = jnp.zeros_like(part)
                before, after = g * segment, (g + 1) * segment - EDGE
                u_ref[z, x, before : before + EDGE] = jnp.where(chip == 0, blank, part)
                u_ref[z, x, after : after + EDGE] = jnp.where(chip == 0, part, blank)
        return 0

    lax.fori_loop(0, depth, plane, 0)


def shared_local_body(moment, has_rows, has_previous, *refs):
    refs = list(refs)
    u_ref, beside_ref, p_ref, c_ref, s_ref = refs[:5]
    rest = refs[5:]
    rows_ref = rest.pop(0) if has_rows else None
    prev_ref = rest.pop(0) if has_previous else None
    base_ref = rest.pop(0)
    if has_rows:
        u_ref = rest.pop(0)
    square, turned_c, turned_s = rest
    depth, across, along, _ = base_ref.shape
    half = along // 2
    core = lax.axis_index("sub")
    chip = lax.axis_index("probe")
    left_on = (core == 1).astype(F32)
    right_on = (core == 0).astype(F32)
    turned_c[:along] = half_rows(square, c_ref[...], half, chip)
    turned_s[:along] = half_rows(square, s_ref[moment], half, chip)
    if has_rows:
        fill_rows(u_ref, rows_ref, chip)

    def tile(start):
        span = pl.ds(start, TILE)
        courant = turned_c[span]
        source = turned_s[span]
        firsts = []
        for k in range(TILE // 8):
            row = start + 8 * k
            firsts.append(pl.multiple_of(row + EDGE + jnp.where(row >= half, 2 * EDGE, 0), 8))

        def load(ref, z, x, shift=0):
            parts = [ref[z, x, pl.ds(first + shift, 8)] for first in firsts]
            return jnp.concatenate(parts, axis=0)

        for z in range(depth):
            beside = [beside_ref[z, j, span].astype(F32) for j in range(RADIUS)]
            row = [v * left_on for v in beside]
            row += [load(u_ref, z, x) for x in range(across)]
            row += [v * right_on for v in beside]
            for x in range(across):
                here = row[RADIUS + x]
                total = (3.0 * COEFFICIENTS[0]) * here
                for r in range(1, RADIUS + 1):
                    near = row[RADIUS + x + r] + row[RADIUS + x - r]
                    near = near + (load(u_ref, z, x, r) + load(u_ref, z, x, -r))
                    if z + r < depth:
                        near = near + load(u_ref, z + r, x)
                    if z - r >= 0:
                        near = near + load(u_ref, z - r, x)
                    total = total + COEFFICIENTS[r] * near
                cell = z * across + x
                new = 2.0 * here
                if has_previous:
                    new = new - load(prev_ref, z, x)
                p = p_ref[z, x, span].astype(F32)
                base_ref[z, x, span] = new + lane(courant, cell) * total + lane(source, cell) * p

    tiles(along, tile)


def shared_local(u, beside, both, courant, source, moment, rows, previous):
    depth, across, along, _ = both.shape
    operands = [u, beside, both, courant, source]
    operands += [a for a in (rows, previous) if a is not None]
    out_shape = [shape_of(depth, across, along, F32)]
    aliases = {}
    if rows is not None:
        aliases = {0: 1}
        out_shape.append(jax.ShapeDtypeStruct(u.shape, F32))
    out = call(
        functools.partial(shared_local_body, moment, rows is not None, previous is not None),
        in_specs=whole_vmem(len(operands)),
        out_specs=whole_vmem(len(out_shape)),
        out_shape=out_shape,
        input_output_aliases=aliases,
        scratch_shapes=square_scratch() + square_scratch()[:1],
    )(*operands)
    return out[0], (u if rows is None else out[1])


def planes_of(refs, x, half, chip):
    if len(refs) == 1:
        return [refs[0][j, x].astype(F32) for j in range(RADIUS)]
    planes = []
    for j in range(RADIUS):
        at = (x % 2) * half
        own, other = [ref[j, x // 2].astype(F32)[at : at + half] for ref in refs]
        parts = [jnp.where(chip == 0, own, other), jnp.where(chip == 0, other, own)]
        planes.append(jnp.concatenate(parts, axis=0))
    return planes


def wide_rim_body(kind, count, *refs):
    base_ref, c_ref = refs[:2]
    odd_refs, even_refs = refs[2 : 2 + count], refs[2 + count : 2 + 2 * count]
    outs, square = refs[2 + 2 * count : -1], refs[-1]
    depth, across, along, _ = base_ref.shape
    half = along // 2
    segment = half + 2 * EDGE
    core = lax.axis_index("sub")
    chip = lax.axis_index("probe")
    even = slab_is_even()
    if kind == "own":
        courant = turned(c_ref[...], square)[:along]
    else:
        courant = half_rows(square, c_ref[...], half, chip)

    def values(x):
        ones, twos = planes_of(even_refs, x, half, chip), planes_of(odd_refs, x, half, chip)
        below = [jnp.where(even, two, one) for one, two in zip(ones, twos)]
        above = [jnp.where(even, one, two) for one, two in zip(ones, twos)]
        news = []
        for z in range(depth):
            added = None
            for r in range(1, RADIUS + 1):
                if z - r < 0:
                    term = COEFFICIENTS[r] * below[RADIUS + z - r]
                    added = term if added is None else added + term
                if z + r >= depth:
                    term = COEFFICIENTS[r] * above[z + r - depth]
                    added = term if added is None else added + term
            new = base_ref[z, x]
            if added is not None:
                new = new + lane(courant, z * across + x) * added
            news.append(new)
        return news

    if kind == "middle":
        u_ref, odd_ref, even_ref, edge_ref, rows_ref = outs
        for x in range(across):
            news = values(x)
            for z, new in enumerate(news):
                for g in range(2):
                    at = g * segment + EDGE
                    u_ref[z, x, at : at + half] = new[g * half : (g + 1) * half]
            store_edges(x, pl.ds(0, along), news, even, even_ref, odd_ref)
        store_sides(core, chip, u_ref, edge_ref, rows_ref)
        return
    for i in range(across // 2):
        for z, (one, two) in enumerate(zip(values(2 * i), values(2 * i + 1))):
            first = jnp.concatenate([one[:half], two[:half]], axis=0).astype(BF16)
            second = jnp.concatenate([one[half:], two[half:]], axis=0).astype(BF16)
            if kind == "own":
                first, second = (
                    jnp.where(chip == 0, first, second),
                    jnp.where(chip == 0, second, first),
                )
            outs[0][z, i] = first
            outs[1][z, i] = second


def wide_rim(base, courant, odds, evens, kind):
    depth, across, along, _ = base.shape
    if kind == "middle":
        edge = shape_of(RADIUS, across, along, BF16)
        out_shape = [
            shape_of(depth, across, along + 4 * EDGE, F32),
            edge,
            edge,
            shape_of(depth, RADIUS, along, BF16),
            shape_of(depth, across, 2 * EDGE, BF16),
        ]
    else:
        out_shape = [shape_of(depth, across // 2, along, BF16)] * 2
    return call(
        functools.partial(wide_rim_body, kind, len(odds)),
        in_specs=whole_vmem(2 + 2 * len(odds)),
        out_specs=whole_vmem(len(out_shape)),
        out_shape=out_shape,
        scratch_shapes=square_scratch()[:1],
    )(base, courant, *odds, *evens)


def gram_body(kept_ref, got_ref, one_ref, two_ref, keep_ref, send_ref, panel):
    chip = lax.axis_index("probe")
    core = lax.axis_index("sub")
    cells, size = panel.shape
    places = (2 * chip, 2 * (1 - chip), 1, 3)
    for place, ref in zip(places, (kept_ref, got_ref, one_ref, two_ref)):
        at = place * LANES if isinstance(place, int) else pl.multiple_of(place * LANES, LANES)
        panel[:, pl.ds(at, LANES)] = ref[...].reshape(cells, LANES)
    everything = panel[...]

    def columns(which):
        one = panel[:, pl.ds(pl.multiple_of(which * LANES, LANES), LANES)]
        two = panel[:, pl.ds(pl.multiple_of((2 + which) * LANES, LANES), LANES)]
        return lax.dot_general(
            everything,
            jnp.concatenate([one, two], axis=1),
            (((0,), (0,)), ((), ())),
            preferred_element_type=F32,
        )

    keep_ref[:size] = columns(core)
    send_ref[:size] = columns(1 - core)
    rows = lax.broadcasted_iota(jnp.int32, (LANES, LANES), 0)
    cols = lax.broadcasted_iota(jnp.int32, (LANES, LANES), 1)
    eye = rows == cols

    def diagonal(which):
        block = slice(which * LANES, (which + 1) * LANES)
        lanes = slice(which // 2 * LANES, (which // 2 + 1) * LANES)
        block = jnp.where(core == which % 2, keep_ref[block, lanes], send_ref[block, lanes])
        return jnp.sum(jnp.where(eye, block, 0.0), axis=0, keepdims=True)

    diag = [diagonal(n) for n in range(4)]
    row0 = jnp.concatenate(diag[:2], axis=1)
    row1 = jnp.concatenate(diag[2:], axis=1)
    tail = jnp.concatenate([row0, row1, jnp.zeros((6, 2 * LANES), F32)], axis=0)
    keep_ref[size:] = tail
    send_ref[size:] = tail


def gram(fields):
    cells = math.prod(fields[0].shape[:3])
    size = 4 * LANES
    shape = jax.ShapeDtypeStruct((size + 8, 2 * LANES), F32)
    return call(
        gram_body,
        in_specs=whole_vmem(4),
        out_specs=whole_vmem(2),
        out_shape=[shape, shape],
        scratch_shapes=[pltpu.VMEM((cells, size), BF16)],
    )(*fields)


def rounded(ref, block, tail):
    count = block.shape[0]
    high = tail.astype(BF16)
    low = tail - high.astype(F32)
    ref[:count] = block.astype(BF16)
    ref[count:] = jnp.concatenate([high.astype(F32), low], axis=0).astype(BF16)


def opened(ref):
    count = ref.shape[0] - 16
    tail = ref[count:].astype(F32)
    return ref[:count].astype(F32), tail[:8] + tail[8:]


def rows_body(slabs, count, keep_ref, got_ref, own_ref, *outs):
    slab = lax.axis_index("slab")
    size = slabs * count
    tail = keep_ref[pl.ds(size, 8)] + got_ref[pl.ds(size, 8)]
    for d in range(slabs):
        owner = slab ^ d
        span = pl.ds(pl.multiple_of(owner * count, count), count)
        block = keep_ref[span] + got_ref[span]
        if d == 0:
            own_ref[:count] = block
            own_ref[count:] = tail
        else:
            rounded(outs[d - 1], block, tail)


def split_rows(keep, got, slabs):
    count = (keep.shape[0] - 8) // slabs
    own = jax.ShapeDtypeStruct((count + 8, keep.shape[1]), F32)
    sent = jax.ShapeDtypeStruct((count + 16, keep.shape[1]), BF16)
    return call(
        functools.partial(rows_body, slabs, count),
        in_specs=whole_vmem(2),
        out_specs=whole_vmem(slabs),
        out_shape=[own] + [sent] * (slabs - 1),
    )(keep, got)


def sum_body(own_ref, *refs):
    count = own_ref.shape[0] - 8
    block, tail = own_ref[:count], own_ref[count:]
    for ref in refs[:-1]:
        more, more_tail = opened(ref)
        block, tail = block + more, tail + more_tail
    rounded(refs[-1], block, tail)


def sum_all(own, others):
    return call(
        sum_body,
        in_specs=whole_vmem(1 + len(others)),
        out_specs=whole_vmem(1)[0],
        out_shape=jax.ShapeDtypeStruct(others[0].shape, BF16),
    )(own, *others)


def normalise_body(cell_count, mine_ref, other_ref, out_ref, norms_ref):
    slab = lax.axis_index("slab")
    core = lax.axis_index("sub")
    one, one_tail = opened(mine_ref)
    two, two_tail = opened(other_ref)
    total = one + two
    norms = jnp.sqrt((one_tail + two_tail)[:2] / cell_count + EPSILON)
    blocks = [norms[n // 2 : n // 2 + 1, (n % 2) * LANES : (n % 2 + 1) * LANES] for n in range(4)]
    own = blocks[0]
    for n in range(1, 4):
        own = jnp.where(slab == n, blocks[n], own)
    norms_ref[...] = own
    rows = lax.broadcasted_iota(jnp.int32, (LANES, LANES), 0)
    cols = lax.broadcasted_iota(jnp.int32, (LANES, LANES), 1)
    eye = rows == cols
    own_column = jnp.sum(
        jnp.where(eye, jnp.broadcast_to(own, (LANES, LANES)), 0.0), axis=1, keepdims=True
    )
    for side in range(2):
        columns = slice(side * LANES, (side + 1) * LANES)
        others = jnp.where(core == 0, blocks[2 * side], blocks[2 * side + 1])
        value = total[:, columns] / math.sqrt(cell_count) / (own_column * others)
        out_ref[:, columns] = jnp.where(eye & (2 * side + core == slab), 0.0, value)


def normalise(mine, other, cell_count):
    count = mine.shape[0] - 16
    return call(
        functools.partial(normalise_body, cell_count),
        in_specs=whole_vmem(2),
        out_specs=whole_vmem(2),
        out_shape=[
            jax.ShapeDtypeStruct((count, 2 * LANES), F32),
            jax.ShapeDtypeStruct((1, LANES), F32),
        ],
    )(mine, other)


def assemble_body(near_ref, far_ref, out_ref):
    core = lax.axis_index("sub")
    for side in range(2):
        columns = slice(side * LANES, (side + 1) * LANES)
        for ref, which in ((near_ref, core), (far_ref, 1 - core)):
            start = pl.multiple_of((2 * side + which) * LANES, LANES)
            out_ref[:, pl.ds(start, LANES)] = ref[:, columns]


def assemble(near, far):
    return call(
        assemble_body,
        in_specs=whole_vmem(2),
        out_specs=whole_vmem(1)[0],
        out_shape=jax.ShapeDtypeStruct((near.shape[0], 4 * LANES), F32),
    )(near, far)


def coupled(fields, cell_count):
    slabs = 4
    keep, send = gram(fields)
    own, *blocks = split_rows(keep, core_swap(send), slabs)
    arrived = [
        lax.ppermute(blocks[d - 1], "slab", [(i, i ^ d) for i in range(slabs)])
        for d in (2, 3, 1)
    ]
    mine = sum_all(own, arrived)
    near, norms = normalise(mine, chip_swap(mine), cell_count)
    return assemble(near, core_swap(near)), norms.reshape(-1)


def coupled_general(fields, cell_count):
    chips = lax.axis_size("probe")
    sketch = jnp.concatenate(fields, axis=-1)
    sketch = sketch.reshape(-1, sketch.shape[-1])
    if chips > 1:
        sketch = lax.all_to_all(sketch, "probe", split_axis=0, concat_axis=1, tiled=True)
    partial_gram = lax.dot_general(
        sketch, sketch, (((0,), (0,)), ((), ())), preferred_element_type=F32
    )
    rows = lax.psum_scatter(partial_gram, "slab", scatter_dimension=0, tiled=True)
    rows = lax.psum(rows, ("probe", "sub"))
    count = rows.shape[0]
    start = lax.axis_index("slab") * count
    own = jnp.diagonal(lax.dynamic_slice_in_dim(rows, start, count, 1))
    own_norms = jnp.sqrt(own / cell_count + EPSILON)
    norms = lax.all_gather(own_norms, "slab", axis=0, tiled=True)
    coupling = rows / math.sqrt(cell_count) / (own_norms[:, None] * norms[None, :])
    row_ids = start + lax.broadcasted_iota(jnp.int32, coupling.shape, 0)
    col_ids = lax.broadcasted_iota(jnp.int32, coupling.shape, 1)
    return jnp.where(row_ids == col_ids, 0.0, coupling), own_norms


def shards(probes, courant, source):
    depth, across, along, count = probes.shape
    chunks = count // LANES
    slabs, chips = lax.axis_size("slab"), lax.axis_size("probe")
    cell_count = depth * across * along * slabs * lax.axis_size("sub")
    half = along // 2
    paired = chips == 2 and slabs == 4 and chunks == 2 and depth == 2 * RADIUS
    paired = paired and half % 8 == 0 and (half - EDGE) % TILE == 0 and along % TILE == 0
    steps = source.shape[0]
    courant = courant.reshape(depth * across, along)
    source = source.reshape(steps, depth * across, along)
    exchange = lambda odd, even, edge: (odd_swap(odd), even_swap(even), core_swap(edge))
    if paired and across % 2 == 0:
        return shared_shards(probes, courant, source, exchange, cell_count)

    now, previous, halos = [], [None] * chunks, []
    for c in range(chunks):
        u, *edges = first_field(probes, c, source[:1])
        now.append(u)
        halos.append(exchange(*edges))
    fields = []
    for n in range(1, steps):
        for c in range(chunks):
            odd, even, beside = halos[c]
            base = local_step(now[c], beside, probes, c, courant, source, n, previous[c])
            if n == steps - 1:
                fields += rim_step(base, odd, even, courant, "all")
            else:
                u, *edges = rim_step(base, odd, even, courant, "middle")
                previous[c], now[c] = now[c], u
                halos[c] = exchange(*edges)
    return coupled_general(fields, cell_count)


def shared_shards(probes, courant, source, exchange, cell_count):
    steps = source.shape[0]
    first_source = source[:1]
    u, *edges = first_field(probes, 0, first_source)
    odd, even, beside = exchange(*edges)
    window, one, two = prepare(probes, first_source)
    got = chip_swap(window)
    odds, evens = [odd_swap(one)], [even_swap(two)]
    shared_u, one, two, edge, both = shared_first(probes, got, first_source)
    odds.append(odd_swap(one))
    evens.append(even_swap(two))
    shared_beside, rows = core_swap(edge), None

    previous = shared_previous = None
    for n in range(1, steps):
        last = n == steps - 1
        base = local_step(u, beside, probes, 0, courant, source, n, previous)
        if last:
            kept, sent = wide_rim(base, courant, [odd], [even], "own")
            fields = [kept, chip_swap(sent)]
        else:
            previous = u
            u, *edges = rim_step(base, odd, even, courant, "middle")
            odd, even, beside = exchange(*edges)
        base, shared_u = shared_local(
            shared_u, shared_beside, both, courant, source, n, rows, shared_previous
        )
        if last:
            fields += wide_rim(base, courant, odds, evens, "both")
        else:
            shared_previous = shared_u
            shared_u, one, two, edge, rows = wide_rim(base, courant, odds, evens, "middle")
            odds, evens = [odd_swap(one)], [even_swap(two)]
            shared_beside, rows = core_swap(edge), chip_swap(rows)
    return coupled(fields, cell_count)


def solution(mesh):
    placed = (
        P(("groups", "slab"), "sub", None, "probe"),
        P("slab", "sub", None),
        P(None, ("groups", "slab"), "sub", None),
    )
    return jax.shard_map(
        shards,
        mesh=mesh,
        in_specs=placed,
        out_specs=(P(("groups", "slab"), None), P(("groups", "slab"))),
        check_vma=False,
    )
```

```python
import functools
import math

import jax
import jax.numpy as jnp
from jax import lax
from jax.experimental import pallas as pl
from jax.experimental.pallas import tpu as pltpu
from jax.sharding import PartitionSpec as P

COEFFICIENTS = (-205.0 / 72.0, 8.0 / 5.0, -1.0 / 5.0, 8.0 / 315.0, -1.0 / 560.0)
EPSILON = 1e-06
LANES = 128
RADIUS = 4
EDGE = 8
TILE = 16
F32 = jnp.float32
BF16 = jnp.bfloat16
VMEM_LIMIT = 32 * 1024 * 1024


def call(body, **options):
    return pl.pallas_call(
        body,
        compiler_params=pltpu.CompilerParams(vmem_limit_bytes=VMEM_LIMIT),
        cost_estimate=pl.CostEstimate(flops=1, bytes_accessed=1, transcendentals=0),
        **options,
    )


def whole_vmem(count):
    return [pl.BlockSpec(memory_space=pltpu.VMEM)] * count


def shape_of(depth, across, along, dtype):
    return jax.ShapeDtypeStruct((depth, across, along, LANES), dtype)


def turned(field, scratch):
    rows, along = field.shape
    scratch[:rows, :along] = field
    return jnp.transpose(scratch[...])


def lane(values, n):
    return jnp.broadcast_to(values[:, n : n + 1], (values.shape[0], LANES))


def store_edges(x, span, news, even, even_ref, odd_ref):
    for j in range(RADIUS):
        low = news[j].astype(BF16)
        high = news[len(news) - RADIUS + j].astype(BF16)
        even_ref[j, x, span] = jnp.where(even, high, low)
        odd_ref[j, x, span] = jnp.where(even, low, high)


def store_beside(span, rows, core, u_ref, edge_ref):
    depth, across, _, _ = u_ref.shape
    first = (across - RADIUS) * (1 - core)
    for z in range(depth):
        for j in range(RADIUS):
            edge_ref[z, j, span] = u_ref[z, first + j, rows].astype(BF16)


def slab_is_even():
    return lax.rem(lax.axis_index("slab"), 2) == 0


def clear_pads(u_ref):
    depth, across, padded, _ = u_ref.shape

    def plane(z, _):
        blank = jnp.zeros((across, EDGE, LANES), F32)
        u_ref[z, :, pl.ds(0, EDGE)] = blank
        u_ref[z, :, pl.ds(padded - EDGE, EDGE)] = blank
        return 0

    lax.fori_loop(0, depth, plane, 0)


def tiles(along, body):
    def one(t, _):
        body(pl.multiple_of(t * TILE, TILE))
        return 0

    lax.fori_loop(0, along // TILE, one, 0)


def first_body(chunk, p_ref, s_ref, u_ref, odd_ref, even_ref, edge_ref, square, turned_s):
    depth, across, padded, _ = u_ref.shape
    along = padded - 2 * EDGE
    core = lax.axis_index("sub")
    even = slab_is_even()
    turned_s[...] = turned(s_ref[0], square)
    clear_pads(u_ref)

    def tile(start):
        span = pl.ds(start, TILE)
        rows = pl.ds(start + EDGE, TILE)
        source = turned_s[span]
        for x in range(across):
            news = []
            for z in range(depth):
                p = p_ref[z, x, span, chunk * LANES : (chunk + 1) * LANES].astype(F32)
                new = lane(source, z * across + x) * p
                u_ref[z, x, rows] = new
                news.append(new)
            store_edges(x, span, news, even, even_ref, odd_ref)
        store_beside(span, rows, core, u_ref, edge_ref)

    tiles(along, tile)


def square_scratch():
    return [pltpu.VMEM((LANES, LANES), F32)] * 2


def first_field(probes, chunk, source):
    depth, across, along, _ = probes.shape
    return call(
        functools.partial(first_body, chunk),
        in_specs=whole_vmem(2),
        out_specs=whole_vmem(4),
        out_shape=[
            shape_of(depth, across, along + 2 * EDGE, F32),
            shape_of(RADIUS, across, along, BF16),
            shape_of(RADIUS, across, along, BF16),
            shape_of(depth, RADIUS, along, BF16),
        ],
        scratch_shapes=square_scratch(),
    )(probes, source)


def local_body(chunk, moment, has_previous, *refs):
    refs = list(refs)
    u_ref, beside_ref, p_ref, c_ref, s_ref = refs[:5]
    prev_ref = refs[5] if has_previous else None
    base_ref, square, turned_c, turned_s = refs[-4:]
    depth, across, along, _ = base_ref.shape
    core = lax.axis_index("sub")
    left_on = (core == 1).astype(F32)
    right_on = (core == 0).astype(F32)
    turned_c[...] = turned(c_ref[...], square)
    turned_s[...] = turned(s_ref[moment], square)

    def tile(start):
        span = pl.ds(start, TILE)
        rows = start + EDGE
        courant = turned_c[span]
        source = turned_s[span]
        for z in range(depth):
            beside = [beside_ref[z, j, span].astype(F32) for j in range(RADIUS)]
            row = [v * left_on for v in beside]
            row += [u_ref[z, x, pl.ds(rows, TILE)] for x in range(across)]
            row += [v * right_on for v in beside]
            for x in range(across):
                here = row[RADIUS + x]
                total = (3.0 * COEFFICIENTS[0]) * here
                for r in range(1, RADIUS + 1):
                    near = row[RADIUS + x + r] + row[RADIUS + x - r]
                    near = near + (
                        u_ref[z, x, pl.ds(rows + r, TILE)] + u_ref[z, x, pl.ds(rows - r, TILE)]
                    )
                    if z + r < depth:
                        near = near + u_ref[z + r, x, pl.ds(rows, TILE)]
                    if z - r >= 0:
                        near = near + u_ref[z - r, x, pl.ds(rows, TILE)]
                    total = total + COEFFICIENTS[r] * near
                cell = z * across + x
                p = p_ref[z, x, span, chunk * LANES : (chunk + 1) * LANES].astype(F32)
                new = 2.0 * here
                if has_previous:
                    new = new - prev_ref[z, x, pl.ds(rows, TILE)]
                new = new + lane(courant, cell) * total + lane(source, cell) * p
                base_ref[z, x, span] = new

    tiles(along, tile)


def local_step(u, beside, probes, chunk, courant, source, moment, previous):
    depth, across, along, _ = probes.shape
    operands = [u, beside, probes, courant, source]
    if previous is not None:
        operands.append(previous)
    return call(
        functools.partial(local_body, chunk, moment, previous is not None),
        in_specs=whole_vmem(len(operands)),
        out_specs=whole_vmem(1)[0],
        out_shape=shape_of(depth, across, along, F32),
        scratch_shapes=square_scratch() + square_scratch()[:1],
    )(*operands)


def rim_body(kind, *refs):
    base_ref, odd_ref, even_ref, c_ref = refs[:4]
    outs, (square, turned_c) = refs[4:-2], refs[-2:]
    depth, across, along, _ = base_ref.shape
    core = lax.axis_index("sub")
    even = slab_is_even()
    lower = lax.axis_index("probe") == 0
    turned_c[...] = turned(c_ref[...], square)
    if kind == "middle":
        clear_pads(outs[0])

    def tile(start):
        span = pl.ds(start, TILE)
        rows = pl.ds(start + EDGE, TILE)
        courant = turned_c[span]
        for x in range(across):
            below, above = [], []
            for j in range(RADIUS):
                one, two = even_ref[j, x, span], odd_ref[j, x, span]
                below.append(jnp.where(even, two, one).astype(F32))
                above.append(jnp.where(even, one, two).astype(F32))
            news = []
            for z in range(depth):
                added = None
                for r in range(1, RADIUS + 1):
                    if z - r < 0:
                        term = COEFFICIENTS[r] * below[RADIUS + z - r]
                        added = term if added is None else added + term
                    if z + r >= depth:
                        term = COEFFICIENTS[r] * above[z + r - depth]
                        added = term if added is None else added + term
                new = base_ref[z, x, span]
                if added is not None:
                    new = new + lane(courant, z * across + x) * added
                news.append(new)
            if kind == "middle":
                for z, new in enumerate(news):
                    outs[0][z, x, rows] = new
                store_edges(x, span, news, even, outs[2], outs[1])
            elif kind == "half":
                for z in range(depth // 2):
                    one, two = news[z].astype(BF16), news[z + depth // 2].astype(BF16)
                    outs[0][z, x, span] = jnp.where(lower, one, two)
                    outs[1][z, x, span] = jnp.where(lower, two, one)
            else:
                for z, new in enumerate(news):
                    outs[0][z, x, span] = new.astype(BF16)
        if kind == "middle":
            store_beside(span, rows, core, outs[0], outs[3])

    tiles(along, tile)


def rim_step(base, odds, evens, courant, kind):
    depth, across, along, _ = base.shape
    if kind == "middle":
        out_shape = [
            shape_of(depth, across, along + 2 * EDGE, F32),
            shape_of(RADIUS, across, along, BF16),
            shape_of(RADIUS, across, along, BF16),
            shape_of(depth, RADIUS, along, BF16),
        ]
    elif kind == "half":
        out_shape = [shape_of(depth // 2, across, along, BF16)] * 2
    else:
        out_shape = [shape_of(depth, across, along, BF16)]
    return call(
        functools.partial(rim_body, kind),
        in_specs=whole_vmem(4),
        out_specs=whole_vmem(len(out_shape)),
        out_shape=out_shape,
        scratch_shapes=square_scratch(),
    )(base, odds, evens, courant)


def swap(x, axis, pairs):
    return lax.ppermute(x, axis, [p for a, b in pairs for p in ((a, b), (b, a))])


def even_swap(x):
    return swap(x, "slab", [(i, i + 1) for i in range(0, lax.axis_size("slab") - 1, 2)])


def odd_swap(x):
    return swap(x, "slab", [(i, i + 1) for i in range(1, lax.axis_size("slab") - 1, 2)])


def core_swap(x):
    return swap(x, "sub", [(0, 1)])


def chip_swap(x):
    return swap(x, "probe", [(0, 1)])


def half_rows(square, field, half, chip):
    square[...] = turned(field, square)
    rows = square[pl.ds(pl.multiple_of(chip * half, 8), half)]
    return jnp.concatenate([rows, rows], axis=0)


def own_half(window, half, chip):
    return jnp.where(chip == 0, window[:half], window[window.shape[0] - half :])


def window_body(p_ref, window_ref):
    depth, _, rows, _ = window_ref.shape
    skip = p_ref.shape[2] - rows
    start = pl.multiple_of((1 - lax.axis_index("probe")) * skip, TILE)

    def plane(z, _):
        window_ref[z] = p_ref[z, :, pl.ds(start, rows), LANES : 2 * LANES]
        return 0

    lax.fori_loop(0, depth, plane, 0)


def window_of(probes):
    depth, across, along, _ = probes.shape
    return call(
        window_body,
        in_specs=whole_vmem(1),
        out_specs=whole_vmem(1)[0],
        out_shape=shape_of(depth, across, along // 2 + EDGE, BF16),
    )(probes)


def store_sides(core, chip, u_ref, edge_ref, rows_ref):
    depth, across, padded, _ = u_ref.shape
    segment = padded // 2
    half = segment - 2 * EDGE
    first = (across - RADIUS) * (1 - core)
    near = pl.multiple_of(jnp.where(chip == 0, half, EDGE), 8)

    def plane(z, _):
        for j in range(RADIUS):
            parts = [
                u_ref[z, first + j, g * segment + EDGE : g * segment + EDGE + half]
                for g in range(2)
            ]
            edge_ref[z, j] = jnp.concatenate(parts, axis=0).astype(BF16)
        if rows_ref is not None:
            for x in range(across):
                parts = [u_ref[z, x, pl.ds(near + g * segment, EDGE)] for g in range(2)]
                rows_ref[z, x] = jnp.concatenate(parts, axis=0).astype(BF16)
        return 0

    lax.fori_loop(0, depth, plane, 0)


def shared_first_body(
    p_ref, got_ref, s_ref, u_ref, odd_ref, even_ref, edge_ref, both_ref, square
):
    depth, across, rows, _ = got_ref.shape
    half = rows - EDGE
    segment = half + 2 * EDGE
    along = 2 * half
    chip = lax.axis_index("probe")
    core = lax.axis_index("sub")
    even = slab_is_even()
    lanes = slice(LANES, 2 * LANES)
    square[...] = turned(s_ref[0], square)
    start = pl.multiple_of(chip * (along - rows), TILE)
    source = square[pl.ds(start, rows)]
    blank = jnp.zeros((EDGE, LANES), F32)
    for x in range(across):
        news = []
        for z in range(depth):
            mine = p_ref[z, x, pl.ds(start, rows), lanes].astype(F32)
            got = got_ref[z, x].astype(F32)
            scale = lane(source, z * across + x)
            windows = [jnp.where(chip == 0, mine, got), jnp.where(chip == 0, got, mine)]
            for g, window in enumerate(windows):
                at = pl.multiple_of(g * segment + EDGE * (1 - chip), 8)
                u_ref[z, x, pl.ds(at, rows)] = scale * window
                out = pl.multiple_of(g * segment + chip * (half + EDGE), 8)
                u_ref[z, x, pl.ds(out, EDGE)] = blank
            both = [own_half(window, half, chip) for window in windows]
            both_ref[z, x] = jnp.concatenate(both, axis=0).astype(BF16)
            u = [own_half(scale * window, half, chip) for window in windows]
            news.append(jnp.concatenate(u, axis=0))
        store_edges(x, pl.ds(0, along), news, even, even_ref, odd_ref)
    store_sides(core, chip, u_ref, edge_ref, None)


def shared_first(probes, got, source):
    depth, across, along, _ = probes.shape
    edge = shape_of(RADIUS, across, along, BF16)
    return call(
        shared_first_body,
        in_specs=whole_vmem(3),
        out_specs=whole_vmem(5),
        out_shape=[
            shape_of(depth, across, along + 4 * EDGE, F32),
            edge,
            edge,
            shape_of(depth, RADIUS, along, BF16),
            shape_of(depth, across, along, BF16),
        ],
        scratch_shapes=square_scratch()[:1],
    )(probes, got, source)


def shared_local_body(moment, has_previous, *refs):
    refs = list(refs)
    u_ref, beside_ref, p_ref, c_ref, s_ref = refs[:5]
    prev_ref = refs[5] if has_previous else None
    base_ref, square, turned_c, turned_s = refs[-4:]
    depth, across, along, _ = base_ref.shape
    half = along // 2
    core = lax.axis_index("sub")
    chip = lax.axis_index("probe")
    left_on = (core == 1).astype(F32)
    right_on = (core == 0).astype(F32)
    turned_c[:along] = half_rows(square, c_ref[...], half, chip)
    turned_s[:along] = half_rows(square, s_ref[moment], half, chip)

    def tile(start):
        span = pl.ds(start, TILE)
        courant = turned_c[span]
        source = turned_s[span]
        firsts = []
        for k in range(TILE // 8):
            row = start + 8 * k
            firsts.append(pl.multiple_of(row + EDGE + jnp.where(row >= half, 2 * EDGE, 0), 8))

        def load(ref, z, x, shift=0):
            parts = [ref[z, x, pl.ds(first + shift, 8)] for first in firsts]
            return jnp.concatenate(parts, axis=0)

        for z in range(depth):
            beside = [beside_ref[z, j, span].astype(F32) for j in range(RADIUS)]
            row = [v * left_on for v in beside]
            row += [load(u_ref, z, x) for x in range(across)]
            row += [v * right_on for v in beside]
            for x in range(across):
                here = row[RADIUS + x]
                total = (3.0 * COEFFICIENTS[0]) * here
                for r in range(1, RADIUS + 1):
                    near = row[RADIUS + x + r] + row[RADIUS + x - r]
                    near = near + (load(u_ref, z, x, r) + load(u_ref, z, x, -r))
                    if z + r < depth:
                        near = near + load(u_ref, z + r, x)
                    if z - r >= 0:
                        near = near + load(u_ref, z - r, x)
                    total = total + COEFFICIENTS[r] * near
                cell = z * across + x
                new = 2.0 * here
                if has_previous:
                    new = new - load(prev_ref, z, x)
                p = p_ref[z, x, span].astype(F32)
                base_ref[z, x, span] = new + lane(courant, cell) * total + lane(source, cell) * p

    tiles(along, tile)


def shared_local(u, beside, both, courant, source, moment, previous):
    depth, across, along, _ = both.shape
    operands = [u, beside, both, courant, source]
    if previous is not None:
        operands.append(previous)
    return call(
        functools.partial(shared_local_body, moment, previous is not None),
        in_specs=whole_vmem(len(operands)),
        out_specs=whole_vmem(1)[0],
        out_shape=shape_of(depth, across, along, F32),
        scratch_shapes=square_scratch() + square_scratch()[:1],
    )(*operands)


def wide_rim_body(kind, has_rows, *refs):
    base_ref, c_ref, odd_ref, even_ref = refs[:4]
    rows_ref = refs[4] if has_rows else None
    outs = refs[4 + has_rows : -2]
    square, shifted = refs[-2:]
    depth, across, along, _ = base_ref.shape
    half = along // 2
    segment = half + 2 * EDGE
    core = lax.axis_index("sub")
    chip = lax.axis_index("probe")
    even = slab_is_even()
    blank = jnp.zeros((EDGE, LANES), F32)
    if kind == "own":
        courant = turned(c_ref[...], square)[:along]
    else:
        courant = half_rows(square, c_ref[...], half, chip)

    if has_rows:

        def place(z, _):
            for x in range(across):
                got = rows_ref[z, x].astype(F32)
                for g in range(2):
                    shifted[z, x, g, :EDGE] = blank
                    shifted[z, x, g, EDGE : 2 * EDGE] = got[g * EDGE : (g + 1) * EDGE]
                    shifted[z, x, g, 2 * EDGE :] = blank
            return 0

        lax.fori_loop(0, depth, place, 0)

    def rows_beyond(z, x):
        parts = []
        for g in range(2):
            total = None
            for r in range(1, RADIUS + 1):
                after = shifted[z, x, g, r : r + EDGE]
                before = shifted[z, x, g, 2 * EDGE - r : 3 * EDGE - r]
                term = COEFFICIENTS[r] * jnp.where(chip == 0, after, before)
                total = term if total is None else total + term
            first = jnp.where(chip == 0, blank, total)
            last = jnp.where(chip == 0, total, blank)
            parts += [first] + [blank] * (half // EDGE - 2) + [last]
        return jnp.concatenate(parts, axis=0)

    def values(x):
        ones = [even_ref[j, x].astype(F32) for j in range(RADIUS)]
        twos = [odd_ref[j, x].astype(F32) for j in range(RADIUS)]
        below = [jnp.where(even, two, one) for one, two in zip(ones, twos)]
        above = [jnp.where(even, one, two) for one, two in zip(ones, twos)]
        news = []
        for z in range(depth):
            added = rows_beyond(z, x) if has_rows else None
            for r in range(1, RADIUS + 1):
                if z - r < 0:
                    term = COEFFICIENTS[r] * below[RADIUS + z - r]
                    added = term if added is None else added + term
                if z + r >= depth:
                    term = COEFFICIENTS[r] * above[z + r - depth]
                    added = term if added is None else added + term
            new = base_ref[z, x]
            if added is not None:
                new = new + lane(courant, z * across + x) * added
            news.append(new)
        return news

    if kind == "middle":
        u_ref, odd_out, even_out, edge_ref, rows_out = outs
        for x in range(across):
            news = values(x)
            for z, new in enumerate(news):
                for g in range(2):
                    at = g * segment + EDGE
                    u_ref[z, x, at - EDGE : at] = blank
                    u_ref[z, x, at : at + half] = new[g * half : (g + 1) * half]
                    u_ref[z, x, at + half : at + half + EDGE] = blank
            store_edges(x, pl.ds(0, along), news, even, even_out, odd_out)
        store_sides(core, chip, u_ref, edge_ref, rows_out)
        return
    for i in range(across // 2):
        for z, (one, two) in enumerate(zip(values(2 * i), values(2 * i + 1))):
            first = jnp.concatenate([one[:half], two[:half]], axis=0).astype(BF16)
            second = jnp.concatenate([one[half:], two[half:]], axis=0).astype(BF16)
            if kind == "own":
                first, second = (
                    jnp.where(chip == 0, first, second),
                    jnp.where(chip == 0, second, first),
                )
            outs[0][z, i] = first
            outs[1][z, i] = second


def wide_rim(base, courant, odd, even, kind, rows=None):
    depth, across, along, _ = base.shape
    if kind == "middle":
        edge = shape_of(RADIUS, across, along, BF16)
        out_shape = [
            shape_of(depth, across, along + 4 * EDGE, F32),
            edge,
            edge,
            shape_of(depth, RADIUS, along, BF16),
            shape_of(depth, across, 2 * EDGE, BF16),
        ]
    else:
        out_shape = [shape_of(depth, across // 2, along, BF16)] * 2
    operands = [base, courant, odd, even]
    if rows is not None:
        operands.append(rows)
    return call(
        functools.partial(wide_rim_body, kind, rows is not None),
        in_specs=whole_vmem(len(operands)),
        out_specs=whole_vmem(len(out_shape)),
        out_shape=out_shape,
        scratch_shapes=square_scratch()[:1]
        + [pltpu.VMEM((depth, across, 2, 3 * EDGE, LANES), F32)],
    )(*operands)


def gram_body(kept_ref, got_ref, one_ref, two_ref, keep_ref, send_ref, panel):
    chip = lax.axis_index("probe")
    core = lax.axis_index("sub")
    cells, size = panel.shape
    places = (2 * chip, 2 * (1 - chip), 1, 3)
    for place, ref in zip(places, (kept_ref, got_ref, one_ref, two_ref)):
        at = place * LANES if isinstance(place, int) else pl.multiple_of(place * LANES, LANES)
        panel[:, pl.ds(at, LANES)] = ref[...].reshape(cells, LANES)
    everything = panel[...]

    def columns(which):
        one = panel[:, pl.ds(pl.multiple_of(which * LANES, LANES), LANES)]
        two = panel[:, pl.ds(pl.multiple_of((2 + which) * LANES, LANES), LANES)]
        return lax.dot_general(
            everything,
            jnp.concatenate([one, two], axis=1),
            (((0,), (0,)), ((), ())),
            preferred_element_type=F32,
        )

    keep_ref[:size] = columns(core)
    send_ref[:size] = columns(1 - core)
    rows = lax.broadcasted_iota(jnp.int32, (LANES, LANES), 0)
    cols = lax.broadcasted_iota(jnp.int32, (LANES, LANES), 1)
    eye = rows == cols

    def diagonal(which):
        block = slice(which * LANES, (which + 1) * LANES)
        lanes = slice(which // 2 * LANES, (which // 2 + 1) * LANES)
        block = jnp.where(core == which % 2, keep_ref[block, lanes], send_ref[block, lanes])
        return jnp.sum(jnp.where(eye, block, 0.0), axis=0, keepdims=True)

    diag = [diagonal(n) for n in range(4)]
    row0 = jnp.concatenate(diag[:2], axis=1)
    row1 = jnp.concatenate(diag[2:], axis=1)
    tail = jnp.concatenate([row0, row1, jnp.zeros((6, 2 * LANES), F32)], axis=0)
    keep_ref[size:] = tail
    send_ref[size:] = tail


def gram(fields):
    cells = math.prod(fields[0].shape[:3])
    size = 4 * LANES
    shape = jax.ShapeDtypeStruct((size + 8, 2 * LANES), F32)
    return call(
        gram_body,
        in_specs=whole_vmem(4),
        out_specs=whole_vmem(2),
        out_shape=[shape, shape],
        scratch_shapes=[pltpu.VMEM((cells, size), BF16)],
    )(*fields)


def rounded(ref, block, tail):
    count = block.shape[0]
    high = tail.astype(BF16)
    low = tail - high.astype(F32)
    ref[:count] = block.astype(BF16)
    ref[count:] = jnp.concatenate([high.astype(F32), low], axis=0).astype(BF16)


def opened(ref):
    count = ref.shape[0] - 16
    tail = ref[count:].astype(F32)
    return ref[:count].astype(F32), tail[:8] + tail[8:]


def rows_body(slabs, count, keep_ref, got_ref, own_ref, *outs):
    slab = lax.axis_index("slab")
    size = slabs * count
    tail = keep_ref[pl.ds(size, 8)] + got_ref[pl.ds(size, 8)]
    for d in range(slabs):
        owner = slab ^ d
        span = pl.ds(pl.multiple_of(owner * count, count), count)
        block = keep_ref[span] + got_ref[span]
        if d == 0:
            own_ref[:count] = block
            own_ref[count:] = tail
        else:
            rounded(outs[d - 1], block, tail)


def split_rows(keep, got, slabs):
    count = (keep.shape[0] - 8) // slabs
    own = jax.ShapeDtypeStruct((count + 8, keep.shape[1]), F32)
    sent = jax.ShapeDtypeStruct((count + 16, keep.shape[1]), BF16)
    return call(
        functools.partial(rows_body, slabs, count),
        in_specs=whole_vmem(2),
        out_specs=whole_vmem(slabs),
        out_shape=[own] + [sent] * (slabs - 1),
    )(keep, got)


def sum_body(own_ref, *refs):
    count = own_ref.shape[0] - 8
    block, tail = own_ref[:count], own_ref[count:]
    for ref in refs[:-1]:
        more, more_tail = opened(ref)
        block, tail = block + more, tail + more_tail
    rounded(refs[-1], block, tail)


def sum_all(own, others):
    return call(
        sum_body,
        in_specs=whole_vmem(1 + len(others)),
        out_specs=whole_vmem(1)[0],
        out_shape=jax.ShapeDtypeStruct(others[0].shape, BF16),
    )(own, *others)


def normalise_body(cell_count, mine_ref, other_ref, out_ref, norms_ref):
    slab = lax.axis_index("slab")
    core = lax.axis_index("sub")
    one, one_tail = opened(mine_ref)
    two, two_tail = opened(other_ref)
    total = one + two
    norms = jnp.sqrt((one_tail + two_tail)[:2] / cell_count + EPSILON)
    blocks = [norms[n // 2 : n // 2 + 1, (n % 2) * LANES : (n % 2 + 1) * LANES] for n in range(4)]
    own = blocks[0]
    for n in range(1, 4):
        own = jnp.where(slab == n, blocks[n], own)
    norms_ref[...] = own
    rows = lax.broadcasted_iota(jnp.int32, (LANES, LANES), 0)
    cols = lax.broadcasted_iota(jnp.int32, (LANES, LANES), 1)
    eye = rows == cols
    own_column = jnp.sum(
        jnp.where(eye, jnp.broadcast_to(own, (LANES, LANES)), 0.0), axis=1, keepdims=True
    )
    for side in range(2):
        columns = slice(side * LANES, (side + 1) * LANES)
        others = jnp.where(core == 0, blocks[2 * side], blocks[2 * side + 1])
        value = total[:, columns] / math.sqrt(cell_count) / (own_column * others)
        out_ref[:, columns] = jnp.where(eye & (2 * side + core == slab), 0.0, value)


def normalise(mine, other, cell_count):
    count = mine.shape[0] - 16
    return call(
        functools.partial(normalise_body, cell_count),
        in_specs=whole_vmem(2),
        out_specs=whole_vmem(2),
        out_shape=[
            jax.ShapeDtypeStruct((count, 2 * LANES), F32),
            jax.ShapeDtypeStruct((1, LANES), F32),
        ],
    )(mine, other)


def assemble_body(near_ref, far_ref, out_ref):
    core = lax.axis_index("sub")
    for side in range(2):
        columns = slice(side * LANES, (side + 1) * LANES)
        for ref, which in ((near_ref, core), (far_ref, 1 - core)):
            start = pl.multiple_of((2 * side + which) * LANES, LANES)
            out_ref[:, pl.ds(start, LANES)] = ref[:, columns]


def assemble(near, far):
    return call(
        assemble_body,
        in_specs=whole_vmem(2),
        out_specs=whole_vmem(1)[0],
        out_shape=jax.ShapeDtypeStruct((near.shape[0], 4 * LANES), F32),
    )(near, far)


def coupled(fields, cell_count):
    slabs = 4
    keep, send = gram(fields)
    own, *blocks = split_rows(keep, core_swap(send), slabs)
    arrived = [
        lax.ppermute(blocks[d - 1], "slab", [(i, i ^ d) for i in range(slabs)])
        for d in (2, 3, 1)
    ]
    mine = sum_all(own, arrived)
    near, norms = normalise(mine, chip_swap(mine), cell_count)
    return assemble(near, core_swap(near)), norms.reshape(-1)


def coupled_general(fields, cell_count):
    chips = lax.axis_size("probe")
    sketch = jnp.concatenate(fields, axis=-1)
    sketch = sketch.reshape(-1, sketch.shape[-1])
    if chips > 1:
        sketch = lax.all_to_all(sketch, "probe", split_axis=0, concat_axis=1, tiled=True)
    partial_gram = lax.dot_general(
        sketch, sketch, (((0,), (0,)), ((), ())), preferred_element_type=F32
    )
    rows = lax.psum_scatter(partial_gram, "slab", scatter_dimension=0, tiled=True)
    rows = lax.psum(rows, ("probe", "sub"))
    count = rows.shape[0]
    start = lax.axis_index("slab") * count
    own = jnp.diagonal(lax.dynamic_slice_in_dim(rows, start, count, 1))
    own_norms = jnp.sqrt(own / cell_count + EPSILON)
    norms = lax.all_gather(own_norms, "slab", axis=0, tiled=True)
    coupling = rows / math.sqrt(cell_count) / (own_norms[:, None] * norms[None, :])
    row_ids = start + lax.broadcasted_iota(jnp.int32, coupling.shape, 0)
    col_ids = lax.broadcasted_iota(jnp.int32, coupling.shape, 1)
    return jnp.where(row_ids == col_ids, 0.0, coupling), own_norms


def shards(probes, courant, source):
    depth, across, along, count = probes.shape
    chunks = count // LANES
    slabs, chips = lax.axis_size("slab"), lax.axis_size("probe")
    cell_count = depth * across * along * slabs * lax.axis_size("sub")
    half = along // 2
    paired = chips == 2 and slabs == 4 and chunks == 2 and depth == 2 * RADIUS
    paired = paired and half % 8 == 0 and (half - EDGE) % TILE == 0 and along % TILE == 0
    steps = source.shape[0]
    courant = courant.reshape(depth * across, along)
    source = source.reshape(steps, depth * across, along)
    exchange = lambda odd, even, edge: (odd_swap(odd), even_swap(even), core_swap(edge))
    if paired and across % 2 == 0:
        return shared_shards(probes, courant, source, exchange, cell_count)

    now, previous, halos = [], [None] * chunks, []
    for c in range(chunks):
        u, *edges = first_field(probes, c, source[:1])
        now.append(u)
        halos.append(exchange(*edges))
    fields = []
    for n in range(1, steps):
        for c in range(chunks):
            odd, even, beside = halos[c]
            base = local_step(now[c], beside, probes, c, courant, source, n, previous[c])
            if n == steps - 1:
                fields += rim_step(base, odd, even, courant, "all")
            else:
                u, *edges = rim_step(base, odd, even, courant, "middle")
                previous[c], now[c] = now[c], u
                halos[c] = exchange(*edges)
    return coupled_general(fields, cell_count)


def shared_shards(probes, courant, source, exchange, cell_count):
    steps = source.shape[0]
    first_source = source[:1]
    got = chip_swap(window_of(probes))
    u, *edges = first_field(probes, 0, first_source)
    odd, even, beside = exchange(*edges)
    shared_u, *edges, both = shared_first(probes, got, first_source)
    shared_odd, shared_even, shared_beside = exchange(*edges)

    previous = shared_previous = rows = None
    for n in range(1, steps):
        last = n == steps - 1
        base = local_step(u, beside, probes, 0, courant, source, n, previous)
        if last:
            kept, sent = wide_rim(base, courant, odd, even, "own")
            fields = [kept, chip_swap(sent)]
        else:
            previous = u
            u, *edges = rim_step(base, odd, even, courant, "middle")
            odd, even, beside = exchange(*edges)
        base = shared_local(
            shared_u, shared_beside, both, courant, source, n, shared_previous
        )
        if last:
            fields += wide_rim(base, courant, shared_odd, shared_even, "both", rows)
        else:
            shared_previous = shared_u
            shared_u, *edges, rows = wide_rim(
                base, courant, shared_odd, shared_even, "middle", rows
            )
            shared_odd, shared_even, shared_beside = exchange(*edges)
            rows = chip_swap(rows)
    return coupled(fields, cell_count)


def solution(mesh):
    placed = (
        P(("groups", "slab"), "sub", None, "probe"),
        P("slab", "sub", None),
        P(None, ("groups", "slab"), "sub", None),
    )
    return jax.shard_map(
        shards,
        mesh=mesh,
        in_specs=placed,
        out_specs=(P(("groups", "slab"), None), P(("groups", "slab"))),
        check_vma=False,
    )
```

```python
import functools
import math

import jax
import jax.numpy as jnp
from jax import lax
from jax.experimental import pallas as pl
from jax.experimental.pallas import tpu as pltpu
from jax.sharding import PartitionSpec as P

COEFFICIENTS = (-205.0 / 72.0, 8.0 / 5.0, -1.0 / 5.0, 8.0 / 315.0, -1.0 / 560.0)
EPSILON = 1e-06
LANES = 128
RADIUS = 4
EDGE = 8
TILE = 16
F32 = jnp.float32
BF16 = jnp.bfloat16
VMEM_LIMIT = 32 * 1024 * 1024


def call(body, **options):
    return pl.pallas_call(
        body,
        compiler_params=pltpu.CompilerParams(vmem_limit_bytes=VMEM_LIMIT),
        cost_estimate=pl.CostEstimate(flops=1, bytes_accessed=1, transcendentals=0),
        **options,
    )


def unread(arrays):
    return [pl.BlockSpec(memory_space=pl.ANY)] * len(arrays)


def whole_vmem(count):
    return [pl.BlockSpec(memory_space=pltpu.VMEM)] * count


def shape_of(depth, across, along, dtype):
    return jax.ShapeDtypeStruct((depth, across, along, LANES), dtype)


def turned(field, scratch):
    rows, along = field.shape
    scratch[:rows, :along] = field
    return jnp.transpose(scratch[...])


def lane(values, n):
    return jnp.broadcast_to(values[:, n : n + 1], (values.shape[0], LANES))


def store_edges(x, span, news, even, even_ref, odd_ref):
    for j in range(RADIUS):
        low = news[j].astype(BF16)
        high = news[len(news) - RADIUS + j].astype(BF16)
        even_ref[j, x, span] = jnp.where(even, high, low)
        odd_ref[j, x, span] = jnp.where(even, low, high)


def store_beside(span, rows, core, u_ref, edge_ref):
    depth, across, _, _ = u_ref.shape
    first = (across - RADIUS) * (1 - core)
    for z in range(depth):
        for j in range(RADIUS):
            edge_ref[z, j, span] = u_ref[z, first + j, rows].astype(BF16)


def slab_is_even():
    return lax.rem(lax.axis_index("slab"), 2) == 0


def clear_pads(u_ref):
    depth, across, padded, _ = u_ref.shape

    def plane(z, _):
        blank = jnp.zeros((across, EDGE, LANES), F32)
        u_ref[z, :, pl.ds(0, EDGE)] = blank
        u_ref[z, :, pl.ds(padded - EDGE, EDGE)] = blank
        return 0

    lax.fori_loop(0, depth, plane, 0)


def tiles(along, body):
    def one(t, _):
        body(pl.multiple_of(t * TILE, TILE))
        return 0

    lax.fori_loop(0, along // TILE, one, 0)


def first_body(chunk, after, p_ref, s_ref, *refs):
    u_ref, odd_ref, even_ref, edge_ref, square, turned_s = refs[after:]
    depth, across, padded, _ = u_ref.shape
    along = padded - 2 * EDGE
    core = lax.axis_index("sub")
    even = slab_is_even()
    turned_s[...] = turned(s_ref[0], square)
    clear_pads(u_ref)

    def tile(start):
        span = pl.ds(start, TILE)
        rows = pl.ds(start + EDGE, TILE)
        source = turned_s[span]
        for x in range(across):
            news = []
            for z in range(depth):
                p = p_ref[z, x, span, chunk * LANES : (chunk + 1) * LANES].astype(F32)
                new = lane(source, z * across + x) * p
                u_ref[z, x, rows] = new
                news.append(new)
            store_edges(x, span, news, even, even_ref, odd_ref)
        store_beside(span, rows, core, u_ref, edge_ref)

    tiles(along, tile)


def square_scratch():
    return [pltpu.VMEM((LANES, LANES), F32)] * 2


def first_field(probes, chunk, source, after=()):
    depth, across, along, _ = probes.shape
    return call(
        functools.partial(first_body, chunk, len(after)),
        in_specs=whole_vmem(2) + unread(after),
        out_specs=whole_vmem(4),
        out_shape=[
            shape_of(depth, across, along + 2 * EDGE, F32),
            shape_of(RADIUS, across, along, BF16),
            shape_of(RADIUS, across, along, BF16),
            shape_of(depth, RADIUS, along, BF16),
        ],
        scratch_shapes=square_scratch(),
    )(probes, source, *after)


def local_body(chunk, moment, has_previous, *refs):
    refs = list(refs)
    u_ref, beside_ref, p_ref, c_ref, s_ref = refs[:5]
    prev_ref = refs[5] if has_previous else None
    base_ref, square, turned_c, turned_s = refs[-4:]
    depth, across, along, _ = base_ref.shape
    core = lax.axis_index("sub")
    left_on = (core == 1).astype(F32)
    right_on = (core == 0).astype(F32)
    turned_c[...] = turned(c_ref[...], square)
    turned_s[...] = turned(s_ref[moment], square)

    def tile(start):
        span = pl.ds(start, TILE)
        rows = start + EDGE
        courant = turned_c[span]
        source = turned_s[span]
        for z in range(depth):
            beside = [beside_ref[z, j, span].astype(F32) for j in range(RADIUS)]
            row = [v * left_on for v in beside]
            row += [u_ref[z, x, pl.ds(rows, TILE)] for x in range(across)]
            row += [v * right_on for v in beside]
            for x in range(across):
                here = row[RADIUS + x]
                total = (3.0 * COEFFICIENTS[0]) * here
                for r in range(1, RADIUS + 1):
                    near = row[RADIUS + x + r] + row[RADIUS + x - r]
                    near = near + (
                        u_ref[z, x, pl.ds(rows + r, TILE)] + u_ref[z, x, pl.ds(rows - r, TILE)]
                    )
                    if z + r < depth:
                        near = near + u_ref[z + r, x, pl.ds(rows, TILE)]
                    if z - r >= 0:
                        near = near + u_ref[z - r, x, pl.ds(rows, TILE)]
                    total = total + COEFFICIENTS[r] * near
                cell = z * across + x
                p = p_ref[z, x, span, chunk * LANES : (chunk + 1) * LANES].astype(F32)
                new = 2.0 * here
                if has_previous:
                    new = new - prev_ref[z, x, pl.ds(rows, TILE)]
                new = new + lane(courant, cell) * total + lane(source, cell) * p
                base_ref[z, x, span] = new

    tiles(along, tile)


def local_step(u, beside, probes, chunk, courant, source, moment, previous):
    depth, across, along, _ = probes.shape
    operands = [u, beside, probes, courant, source]
    if previous is not None:
        operands.append(previous)
    return call(
        functools.partial(local_body, chunk, moment, previous is not None),
        in_specs=whole_vmem(len(operands)),
        out_specs=whole_vmem(1)[0],
        out_shape=shape_of(depth, across, along, F32),
        scratch_shapes=square_scratch() + square_scratch()[:1],
    )(*operands)


def rim_body(kind, after, *refs):
    base_ref, odd_ref, even_ref, c_ref = refs[:4]
    outs, (square, turned_c) = refs[4 + after : -2], refs[-2:]
    depth, across, along, _ = base_ref.shape
    core = lax.axis_index("sub")
    even = slab_is_even()
    lower = lax.axis_index("probe") == 0
    turned_c[...] = turned(c_ref[...], square)
    if kind == "middle":
        clear_pads(outs[0])

    def tile(start):
        span = pl.ds(start, TILE)
        rows = pl.ds(start + EDGE, TILE)
        courant = turned_c[span]
        for x in range(across):
            below, above = [], []
            for j in range(RADIUS):
                one, two = even_ref[j, x, span], odd_ref[j, x, span]
                below.append(jnp.where(even, two, one).astype(F32))
                above.append(jnp.where(even, one, two).astype(F32))
            news = []
            for z in range(depth):
                added = None
                for r in range(1, RADIUS + 1):
                    if z - r < 0:
                        term = COEFFICIENTS[r] * below[RADIUS + z - r]
                        added = term if added is None else added + term
                    if z + r >= depth:
                        term = COEFFICIENTS[r] * above[z + r - depth]
                        added = term if added is None else added + term
                new = base_ref[z, x, span]
                if added is not None:
                    new = new + lane(courant, z * across + x) * added
                news.append(new)
            if kind == "middle":
                for z, new in enumerate(news):
                    outs[0][z, x, rows] = new
                store_edges(x, span, news, even, outs[2], outs[1])
            elif kind == "half":
                for z in range(depth // 2):
                    one, two = news[z].astype(BF16), news[z + depth // 2].astype(BF16)
                    outs[0][z, x, span] = jnp.where(lower, one, two)
                    outs[1][z, x, span] = jnp.where(lower, two, one)
            else:
                for z, new in enumerate(news):
                    outs[0][z, x, span] = new.astype(BF16)
        if kind == "middle":
            store_beside(span, rows, core, outs[0], outs[3])

    tiles(along, tile)


def rim_step(base, odds, evens, courant, kind, after=()):
    depth, across, along, _ = base.shape
    if kind == "middle":
        out_shape = [
            shape_of(depth, across, along + 2 * EDGE, F32),
            shape_of(RADIUS, across, along, BF16),
            shape_of(RADIUS, across, along, BF16),
            shape_of(depth, RADIUS, along, BF16),
        ]
    elif kind == "half":
        out_shape = [shape_of(depth // 2, across, along, BF16)] * 2
    else:
        out_shape = [shape_of(depth, across, along, BF16)]
    return call(
        functools.partial(rim_body, kind, len(after)),
        in_specs=whole_vmem(4) + unread(after),
        out_specs=whole_vmem(len(out_shape)),
        out_shape=out_shape,
        scratch_shapes=square_scratch(),
    )(base, odds, evens, courant, *after)


def swap(x, axis, pairs):
    return lax.ppermute(x, axis, [p for a, b in pairs for p in ((a, b), (b, a))])


def even_swap(x):
    return swap(x, "slab", [(i, i + 1) for i in range(0, lax.axis_size("slab") - 1, 2)])


def odd_swap(x):
    return swap(x, "slab", [(i, i + 1) for i in range(1, lax.axis_size("slab") - 1, 2)])


def core_swap(x):
    return swap(x, "sub", [(0, 1)])


def chip_swap(x):
    return swap(x, "probe", [(0, 1)])


def half_rows(square, field, half, chip):
    square[...] = turned(field, square)
    rows = square[pl.ds(pl.multiple_of(chip * half, 8), half)]
    return jnp.concatenate([rows, rows], axis=0)


def own_half(window, half, chip):
    return jnp.where(chip == 0, window[:half], window[window.shape[0] - half :])


def window_body(p_ref, window_ref):
    depth, _, rows, _ = window_ref.shape
    skip = p_ref.shape[2] - rows
    start = pl.multiple_of((1 - lax.axis_index("probe")) * skip, TILE)

    def plane(z, _):
        window_ref[z] = p_ref[z, :, pl.ds(start, rows), LANES : 2 * LANES]
        return 0

    lax.fori_loop(0, depth, plane, 0)


def window_of(probes):
    depth, across, along, _ = probes.shape
    return call(
        window_body,
        in_specs=whole_vmem(1),
        out_specs=whole_vmem(1)[0],
        out_shape=shape_of(depth, across, along // 2 + EDGE, BF16),
    )(probes)


def store_sides(core, chip, u_ref, edge_ref, rows_ref):
    depth, across, padded, _ = u_ref.shape
    segment = padded // 2
    half = segment - 2 * EDGE
    first = (across - RADIUS) * (1 - core)
    near = pl.multiple_of(jnp.where(chip == 0, half, EDGE), 8)

    def plane(z, _):
        for j in range(RADIUS):
            parts = [
                u_ref[z, first + j, g * segment + EDGE : g * segment + EDGE + half]
                for g in range(2)
            ]
            edge_ref[z, j] = jnp.concatenate(parts, axis=0).astype(BF16)
        if rows_ref is not None:
            for x in range(across):
                parts = [u_ref[z, x, pl.ds(near + g * segment, EDGE)] for g in range(2)]
                rows_ref[z, x] = jnp.concatenate(parts, axis=0).astype(BF16)
        return 0

    lax.fori_loop(0, depth, plane, 0)


def shared_first_body(
    p_ref, got_ref, s_ref, u_ref, odd_ref, even_ref, edge_ref, both_ref, square
):
    depth, across, rows, _ = got_ref.shape
    half = rows - EDGE
    segment = half + 2 * EDGE
    along = 2 * half
    chip = lax.axis_index("probe")
    core = lax.axis_index("sub")
    even = slab_is_even()
    lanes = slice(LANES, 2 * LANES)
    square[...] = turned(s_ref[0], square)
    start = pl.multiple_of(chip * (along - rows), TILE)
    source = square[pl.ds(start, rows)]
    blank = jnp.zeros((EDGE, LANES), F32)
    for x in range(across):
        news = []
        for z in range(depth):
            mine = p_ref[z, x, pl.ds(start, rows), lanes].astype(F32)
            got = got_ref[z, x].astype(F32)
            scale = lane(source, z * across + x)
            windows = [jnp.where(chip == 0, mine, got), jnp.where(chip == 0, got, mine)]
            for g, window in enumerate(windows):
                at = pl.multiple_of(g * segment + EDGE * (1 - chip), 8)
                u_ref[z, x, pl.ds(at, rows)] = scale * window
                out = pl.multiple_of(g * segment + chip * (half + EDGE), 8)
                u_ref[z, x, pl.ds(out, EDGE)] = blank
            both = [own_half(window, half, chip) for window in windows]
            both_ref[z, x] = jnp.concatenate(both, axis=0).astype(BF16)
            u = [own_half(scale * window, half, chip) for window in windows]
            news.append(jnp.concatenate(u, axis=0))
        store_edges(x, pl.ds(0, along), news, even, even_ref, odd_ref)
    store_sides(core, chip, u_ref, edge_ref, None)


def shared_first(probes, got, source):
    depth, across, along, _ = probes.shape
    edge = shape_of(RADIUS, across, along, BF16)
    return call(
        shared_first_body,
        in_specs=whole_vmem(3),
        out_specs=whole_vmem(5),
        out_shape=[
            shape_of(depth, across, along + 4 * EDGE, F32),
            edge,
            edge,
            shape_of(depth, RADIUS, along, BF16),
            shape_of(depth, across, along, BF16),
        ],
        scratch_shapes=square_scratch()[:1],
    )(probes, got, source)


def shared_local_body(moment, has_previous, *refs):
    refs = list(refs)
    u_ref, beside_ref, p_ref, c_ref, s_ref = refs[:5]
    prev_ref = refs[5] if has_previous else None
    base_ref, square, turned_c, turned_s = refs[-4:]
    depth, across, along, _ = base_ref.shape
    half = along // 2
    core = lax.axis_index("sub")
    chip = lax.axis_index("probe")
    left_on = (core == 1).astype(F32)
    right_on = (core == 0).astype(F32)
    turned_c[:along] = half_rows(square, c_ref[...], half, chip)
    turned_s[:along] = half_rows(square, s_ref[moment], half, chip)

    def tile(start):
        span = pl.ds(start, TILE)
        courant = turned_c[span]
        source = turned_s[span]
        firsts = []
        for k in range(TILE // 8):
            row = start + 8 * k
            firsts.append(pl.multiple_of(row + EDGE + jnp.where(row >= half, 2 * EDGE, 0), 8))

        def load(ref, z, x, shift=0):
            parts = [ref[z, x, pl.ds(first + shift, 8)] for first in firsts]
            return jnp.concatenate(parts, axis=0)

        for z in range(depth):
            beside = [beside_ref[z, j, span].astype(F32) for j in range(RADIUS)]
            row = [v * left_on for v in beside]
            row += [load(u_ref, z, x) for x in range(across)]
            row += [v * right_on for v in beside]
            for x in range(across):
                here = row[RADIUS + x]
                total = (3.0 * COEFFICIENTS[0]) * here
                for r in range(1, RADIUS + 1):
                    near = row[RADIUS + x + r] + row[RADIUS + x - r]
                    near = near + (load(u_ref, z, x, r) + load(u_ref, z, x, -r))
                    if z + r < depth:
                        near = near + load(u_ref, z + r, x)
                    if z - r >= 0:
                        near = near + load(u_ref, z - r, x)
                    total = total + COEFFICIENTS[r] * near
                cell = z * across + x
                new = 2.0 * here
                if has_previous:
                    new = new - load(prev_ref, z, x)
                p = p_ref[z, x, span].astype(F32)
                base_ref[z, x, span] = new + lane(courant, cell) * total + lane(source, cell) * p

    tiles(along, tile)


def shared_local(u, beside, both, courant, source, moment, previous):
    depth, across, along, _ = both.shape
    operands = [u, beside, both, courant, source]
    if previous is not None:
        operands.append(previous)
    return call(
        functools.partial(shared_local_body, moment, previous is not None),
        in_specs=whole_vmem(len(operands)),
        out_specs=whole_vmem(1)[0],
        out_shape=shape_of(depth, across, along, F32),
        scratch_shapes=square_scratch() + square_scratch()[:1],
    )(*operands)


def wide_rim_body(kind, has_rows, after, *refs):
    base_ref, c_ref, odd_ref, even_ref = refs[:4]
    rows_ref = refs[4] if has_rows else None
    outs = refs[4 + has_rows + after : -2]
    square, shifted = refs[-2:]
    depth, across, along, _ = base_ref.shape
    half = along // 2
    segment = half + 2 * EDGE
    core = lax.axis_index("sub")
    chip = lax.axis_index("probe")
    even = slab_is_even()
    blank = jnp.zeros((EDGE, LANES), F32)
    if kind == "own":
        courant = turned(c_ref[...], square)[:along]
    else:
        courant = half_rows(square, c_ref[...], half, chip)

    if has_rows:

        def place(z, _):
            for x in range(across):
                got = rows_ref[z, x].astype(F32)
                for g in range(2):
                    shifted[z, x, g, :EDGE] = blank
                    shifted[z, x, g, EDGE : 2 * EDGE] = got[g * EDGE : (g + 1) * EDGE]
                    shifted[z, x, g, 2 * EDGE :] = blank
            return 0

        lax.fori_loop(0, depth, place, 0)

    def rows_beyond(z, x):
        parts = []
        for g in range(2):
            total = None
            for r in range(1, RADIUS + 1):
                after = shifted[z, x, g, r : r + EDGE]
                before = shifted[z, x, g, 2 * EDGE - r : 3 * EDGE - r]
                term = COEFFICIENTS[r] * jnp.where(chip == 0, after, before)
                total = term if total is None else total + term
            first = jnp.where(chip == 0, blank, total)
            last = jnp.where(chip == 0, total, blank)
            parts += [first] + [blank] * (half // EDGE - 2) + [last]
        return jnp.concatenate(parts, axis=0)

    def values(x):
        ones = [even_ref[j, x].astype(F32) for j in range(RADIUS)]
        twos = [odd_ref[j, x].astype(F32) for j in range(RADIUS)]
        below = [jnp.where(even, two, one) for one, two in zip(ones, twos)]
        above = [jnp.where(even, one, two) for one, two in zip(ones, twos)]
        news = []
        for z in range(depth):
            added = rows_beyond(z, x) if has_rows else None
            for r in range(1, RADIUS + 1):
                if z - r < 0:
                    term = COEFFICIENTS[r] * below[RADIUS + z - r]
                    added = term if added is None else added + term
                if z + r >= depth:
                    term = COEFFICIENTS[r] * above[z + r - depth]
                    added = term if added is None else added + term
            new = base_ref[z, x]
            if added is not None:
                new = new + lane(courant, z * across + x) * added
            news.append(new)
        return news

    if kind == "middle":
        u_ref, odd_out, even_out, edge_ref, rows_out = outs
        for x in range(across):
            news = values(x)
            for z, new in enumerate(news):
                for g in range(2):
                    at = g * segment + EDGE
                    u_ref[z, x, at - EDGE : at] = blank
                    u_ref[z, x, at : at + half] = new[g * half : (g + 1) * half]
                    u_ref[z, x, at + half : at + half + EDGE] = blank
            store_edges(x, pl.ds(0, along), news, even, even_out, odd_out)
        store_sides(core, chip, u_ref, edge_ref, rows_out)
        return
    for i in range(across // 2):
        for z, (one, two) in enumerate(zip(values(2 * i), values(2 * i + 1))):
            first = jnp.concatenate([one[:half], two[:half]], axis=0).astype(BF16)
            second = jnp.concatenate([one[half:], two[half:]], axis=0).astype(BF16)
            if kind == "own":
                first, second = (
                    jnp.where(chip == 0, first, second),
                    jnp.where(chip == 0, second, first),
                )
            outs[0][z, i] = first
            outs[1][z, i] = second


def wide_rim(base, courant, odd, even, kind, rows=None, after=()):
    depth, across, along, _ = base.shape
    if kind == "middle":
        edge = shape_of(RADIUS, across, along, BF16)
        out_shape = [
            shape_of(depth, across, along + 4 * EDGE, F32),
            edge,
            edge,
            shape_of(depth, RADIUS, along, BF16),
            shape_of(depth, across, 2 * EDGE, BF16),
        ]
    else:
        out_shape = [shape_of(depth, across // 2, along, BF16)] * 2
    operands = [base, courant, odd, even]
    if rows is not None:
        operands.append(rows)
    return call(
        functools.partial(wide_rim_body, kind, rows is not None, len(after)),
        in_specs=whole_vmem(len(operands)) + unread(after),
        out_specs=whole_vmem(len(out_shape)),
        out_shape=out_shape,
        scratch_shapes=square_scratch()[:1]
        + [pltpu.VMEM((depth, across, 2, 3 * EDGE, LANES), F32)],
    )(*operands, *after)


def gram_body(kept_ref, got_ref, one_ref, two_ref, keep_ref, send_ref, panel):
    chip = lax.axis_index("probe")
    core = lax.axis_index("sub")
    cells, size = panel.shape
    places = (2 * chip, 2 * (1 - chip), 1, 3)
    for place, ref in zip(places, (kept_ref, got_ref, one_ref, two_ref)):
        at = place * LANES if isinstance(place, int) else pl.multiple_of(place * LANES, LANES)
        panel[:, pl.ds(at, LANES)] = ref[...].reshape(cells, LANES)
    everything = panel[...]

    def columns(which):
        one = panel[:, pl.ds(pl.multiple_of(which * LANES, LANES), LANES)]
        two = panel[:, pl.ds(pl.multiple_of((2 + which) * LANES, LANES), LANES)]
        return lax.dot_general(
            everything,
            jnp.concatenate([one, two], axis=1),
            (((0,), (0,)), ((), ())),
            preferred_element_type=F32,
        )

    keep_ref[:size] = columns(core)
    send_ref[:size] = columns(1 - core)
    rows = lax.broadcasted_iota(jnp.int32, (LANES, LANES), 0)
    cols = lax.broadcasted_iota(jnp.int32, (LANES, LANES), 1)
    eye = rows == cols

    def diagonal(which):
        block = slice(which * LANES, (which + 1) * LANES)
        lanes = slice(which // 2 * LANES, (which // 2 + 1) * LANES)
        block = jnp.where(core == which % 2, keep_ref[block, lanes], send_ref[block, lanes])
        return jnp.sum(jnp.where(eye, block, 0.0), axis=0, keepdims=True)

    diag = [diagonal(n) for n in range(4)]
    row0 = jnp.concatenate(diag[:2], axis=1)
    row1 = jnp.concatenate(diag[2:], axis=1)
    tail = jnp.concatenate([row0, row1, jnp.zeros((6, 2 * LANES), F32)], axis=0)
    keep_ref[size:] = tail
    send_ref[size:] = tail


def gram(fields):
    cells = math.prod(fields[0].shape[:3])
    size = 4 * LANES
    shape = jax.ShapeDtypeStruct((size + 8, 2 * LANES), F32)
    return call(
        gram_body,
        in_specs=whole_vmem(4),
        out_specs=whole_vmem(2),
        out_shape=[shape, shape],
        scratch_shapes=[pltpu.VMEM((cells, size), BF16)],
    )(*fields)


def rounded(ref, block, tail):
    count = block.shape[0]
    high = tail.astype(BF16)
    low = tail - high.astype(F32)
    ref[:count] = block.astype(BF16)
    ref[count:] = jnp.concatenate([high.astype(F32), low], axis=0).astype(BF16)


def opened(ref):
    count = ref.shape[0] - 16
    tail = ref[count:].astype(F32)
    return ref[:count].astype(F32), tail[:8] + tail[8:]


def rows_body(slabs, count, keep_ref, got_ref, own_ref, *outs):
    slab = lax.axis_index("slab")
    size = slabs * count
    tail = keep_ref[pl.ds(size, 8)] + got_ref[pl.ds(size, 8)]
    for d in range(slabs):
        owner = slab ^ d
        span = pl.ds(pl.multiple_of(owner * count, count), count)
        block = keep_ref[span] + got_ref[span]
        if d == 0:
            own_ref[:count] = block
            own_ref[count:] = tail
        else:
            rounded(outs[d - 1], block, tail)


def split_rows(keep, got, slabs):
    count = (keep.shape[0] - 8) // slabs
    own = jax.ShapeDtypeStruct((count + 8, keep.shape[1]), F32)
    sent = jax.ShapeDtypeStruct((count + 16, keep.shape[1]), BF16)
    return call(
        functools.partial(rows_body, slabs, count),
        in_specs=whole_vmem(2),
        out_specs=whole_vmem(slabs),
        out_shape=[own] + [sent] * (slabs - 1),
    )(keep, got)


def sum_body(own_ref, *refs):
    count = own_ref.shape[0] - 8
    block, tail = own_ref[:count], own_ref[count:]
    for ref in refs[:-1]:
        more, more_tail = opened(ref)
        block, tail = block + more, tail + more_tail
    rounded(refs[-1], block, tail)


def sum_all(own, others):
    return call(
        sum_body,
        in_specs=whole_vmem(1 + len(others)),
        out_specs=whole_vmem(1)[0],
        out_shape=jax.ShapeDtypeStruct(others[0].shape, BF16),
    )(own, *others)


def normalise_body(cell_count, mine_ref, other_ref, out_ref, norms_ref):
    slab = lax.axis_index("slab")
    core = lax.axis_index("sub")
    one, one_tail = opened(mine_ref)
    two, two_tail = opened(other_ref)
    total = one + two
    norms = jnp.sqrt((one_tail + two_tail)[:2] / cell_count + EPSILON)
    blocks = [norms[n // 2 : n // 2 + 1, (n % 2) * LANES : (n % 2 + 1) * LANES] for n in range(4)]
    own = blocks[0]
    for n in range(1, 4):
        own = jnp.where(slab == n, blocks[n], own)
    norms_ref[...] = own
    rows = lax.broadcasted_iota(jnp.int32, (LANES, LANES), 0)
    cols = lax.broadcasted_iota(jnp.int32, (LANES, LANES), 1)
    eye = rows == cols
    own_column = jnp.sum(
        jnp.where(eye, jnp.broadcast_to(own, (LANES, LANES)), 0.0), axis=1, keepdims=True
    )
    for side in range(2):
        columns = slice(side * LANES, (side + 1) * LANES)
        others = jnp.where(core == 0, blocks[2 * side], blocks[2 * side + 1])
        value = total[:, columns] / math.sqrt(cell_count) / (own_column * others)
        out_ref[:, columns] = jnp.where(eye & (2 * side + core == slab), 0.0, value)


def normalise(mine, other, cell_count):
    count = mine.shape[0] - 16
    return call(
        functools.partial(normalise_body, cell_count),
        in_specs=whole_vmem(2),
        out_specs=whole_vmem(2),
        out_shape=[
            jax.ShapeDtypeStruct((count, 2 * LANES), F32),
            jax.ShapeDtypeStruct((1, LANES), F32),
        ],
    )(mine, other)


def assemble_body(near_ref, far_ref, out_ref):
    core = lax.axis_index("sub")
    for side in range(2):
        columns = slice(side * LANES, (side + 1) * LANES)
        for ref, which in ((near_ref, core), (far_ref, 1 - core)):
            start = pl.multiple_of((2 * side + which) * LANES, LANES)
            out_ref[:, pl.ds(start, LANES)] = ref[:, columns]


def assemble(near, far):
    return call(
        assemble_body,
        in_specs=whole_vmem(2),
        out_specs=whole_vmem(1)[0],
        out_shape=jax.ShapeDtypeStruct((near.shape[0], 4 * LANES), F32),
    )(near, far)


def coupled(fields, cell_count):
    slabs = 4
    keep, send = gram(fields)
    own, *blocks = split_rows(keep, core_swap(send), slabs)
    arrived = [
        lax.ppermute(blocks[d - 1], "slab", [(i, i ^ d) for i in range(slabs)])
        for d in (2, 3, 1)
    ]
    mine = sum_all(own, arrived)
    near, norms = normalise(mine, chip_swap(mine), cell_count)
    return assemble(near, core_swap(near)), norms.reshape(-1)


def coupled_general(fields, cell_count):
    chips = lax.axis_size("probe")
    sketch = jnp.concatenate(fields, axis=-1)
    sketch = sketch.reshape(-1, sketch.shape[-1])
    if chips > 1:
        sketch = lax.all_to_all(sketch, "probe", split_axis=0, concat_axis=1, tiled=True)
    partial_gram = lax.dot_general(
        sketch, sketch, (((0,), (0,)), ((), ())), preferred_element_type=F32
    )
    rows = lax.psum_scatter(partial_gram, "slab", scatter_dimension=0, tiled=True)
    rows = lax.psum(rows, ("probe", "sub"))
    count = rows.shape[0]
    start = lax.axis_index("slab") * count
    own = jnp.diagonal(lax.dynamic_slice_in_dim(rows, start, count, 1))
    own_norms = jnp.sqrt(own / cell_count + EPSILON)
    norms = lax.all_gather(own_norms, "slab", axis=0, tiled=True)
    coupling = rows / math.sqrt(cell_count) / (own_norms[:, None] * norms[None, :])
    row_ids = start + lax.broadcasted_iota(jnp.int32, coupling.shape, 0)
    col_ids = lax.broadcasted_iota(jnp.int32, coupling.shape, 1)
    return jnp.where(row_ids == col_ids, 0.0, coupling), own_norms


def shards(probes, courant, source):
    depth, across, along, count = probes.shape
    chunks = count // LANES
    slabs, chips = lax.axis_size("slab"), lax.axis_size("probe")
    cell_count = depth * across * along * slabs * lax.axis_size("sub")
    half = along // 2
    paired = chips == 2 and slabs == 4 and chunks == 2 and depth == 2 * RADIUS
    paired = paired and half % 8 == 0 and (half - EDGE) % TILE == 0 and along % TILE == 0
    steps = source.shape[0]
    courant = courant.reshape(depth * across, along)
    source = source.reshape(steps, depth * across, along)
    exchange = lambda odd, even, edge: (odd_swap(odd), even_swap(even), core_swap(edge))
    if paired and across % 2 == 0:
        return shared_shards(probes, courant, source, exchange, cell_count)

    now, previous, halos = [], [None] * chunks, []
    for c in range(chunks):
        u, *edges = first_field(probes, c, source[:1])
        now.append(u)
        halos.append(exchange(*edges))
    fields = []
    for n in range(1, steps):
        for c in range(chunks):
            odd, even, beside = halos[c]
            base = local_step(now[c], beside, probes, c, courant, source, n, previous[c])
            if n == steps - 1:
                fields += rim_step(base, odd, even, courant, "all")
            else:
                u, *edges = rim_step(base, odd, even, courant, "middle")
                previous[c], now[c] = now[c], u
                halos[c] = exchange(*edges)
    return coupled_general(fields, cell_count)


def shared_shards(probes, courant, source, exchange, cell_count):
    steps = source.shape[0]
    first_source = source[:1]
    window = window_of(probes)
    got = chip_swap(window)
    u, *edges = first_field(probes, 0, first_source, (window,))
    odd, even, beside = exchange(*edges)
    shared_u, *edges, both = shared_first(probes, got, first_source)
    shared_odd, shared_even, shared_beside = exchange(*edges)

    previous = shared_previous = rows = None
    before = (both,)
    for n in range(1, steps):
        last = n == steps - 1
        base = local_step(u, beside, probes, 0, courant, source, n, previous)
        if last:
            kept, sent = wide_rim(base, courant, odd, even, "own", after=before)
            fields = [kept, chip_swap(sent)]
            before = (kept,)
        else:
            previous = u
            u, *edges = rim_step(base, odd, even, courant, "middle", before)
            odd, even, beside = exchange(*edges)
            before = (edges[-1],)
        base = shared_local(
            shared_u, shared_beside, both, courant, source, n, shared_previous
        )
        if last:
            fields += wide_rim(base, courant, shared_odd, shared_even, "both", rows, before)
        else:
            shared_previous = shared_u
            shared_u, *edges, rows = wide_rim(
                base, courant, shared_odd, shared_even, "middle", rows, before
            )
            before = (edges[-1],)
            shared_odd, shared_even, shared_beside = exchange(*edges)
            rows = chip_swap(rows)
    return coupled(fields, cell_count)


def solution(mesh):
    placed = (
        P(("groups", "slab"), "sub", None, "probe"),
        P("slab", "sub", None),
        P(None, ("groups", "slab"), "sub", None),
    )
    return jax.shard_map(
        shards,
        mesh=mesh,
        in_specs=placed,
        out_specs=(P(("groups", "slab"), None), P(("groups", "slab"))),
        check_vma=False,
    )
```

```python
import functools
import math

import jax
import jax.numpy as jnp
from jax import lax
from jax.experimental import pallas as pl
from jax.experimental.pallas import tpu as pltpu
from jax.sharding import PartitionSpec as P

COEFFICIENTS = (-205.0 / 72.0, 8.0 / 5.0, -1.0 / 5.0, 8.0 / 315.0, -1.0 / 560.0)
EPSILON = 1e-06
LANES = 128
RADIUS = 4
EDGE = 8
TILE = 16
F32 = jnp.float32
BF16 = jnp.bfloat16
VMEM_LIMIT = 32 * 1024 * 1024


def call(body, **options):
    return pl.pallas_call(
        body,
        compiler_params=pltpu.CompilerParams(vmem_limit_bytes=VMEM_LIMIT),
        cost_estimate=pl.CostEstimate(flops=1, bytes_accessed=1, transcendentals=0),
        **options,
    )


def unread(arrays):
    return [pl.BlockSpec(memory_space=pl.ANY)] * len(arrays)


def whole_vmem(count):
    return [pl.BlockSpec(memory_space=pltpu.VMEM)] * count


def shape_of(depth, across, along, dtype):
    return jax.ShapeDtypeStruct((depth, across, along, LANES), dtype)


def turned(field, scratch):
    rows, along = field.shape
    scratch[:rows, :along] = field
    return jnp.transpose(scratch[...])


def lane(values, n):
    return jnp.broadcast_to(values[:, n : n + 1], (values.shape[0], LANES))


def store_edges(x, span, news, even, even_ref, odd_ref):
    for j in range(RADIUS):
        low = news[j].astype(BF16)
        high = news[len(news) - RADIUS + j].astype(BF16)
        even_ref[j, x, span] = jnp.where(even, high, low)
        odd_ref[j, x, span] = jnp.where(even, low, high)


def store_beside(span, rows, core, u_ref, edge_ref):
    depth, across, _, _ = u_ref.shape
    first = (across - RADIUS) * (1 - core)
    for z in range(depth):
        for j in range(RADIUS):
            edge_ref[z, j, span] = u_ref[z, first + j, rows].astype(BF16)


def slab_is_even():
    return lax.rem(lax.axis_index("slab"), 2) == 0


def clear_pads(u_ref):
    depth, across, padded, _ = u_ref.shape

    def plane(z, _):
        blank = jnp.zeros((across, EDGE, LANES), F32)
        u_ref[z, :, pl.ds(0, EDGE)] = blank
        u_ref[z, :, pl.ds(padded - EDGE, EDGE)] = blank
        return 0

    lax.fori_loop(0, depth, plane, 0)


def tiles(along, body):
    def one(t, _):
        body(pl.multiple_of(t * TILE, TILE))
        return 0

    lax.fori_loop(0, along // TILE, one, 0)


def first_body(chunk, after, p_ref, s_ref, *refs):
    u_ref, odd_ref, even_ref, edge_ref, square, turned_s = refs[after:]
    depth, across, padded, _ = u_ref.shape
    along = padded - 2 * EDGE
    core = lax.axis_index("sub")
    even = slab_is_even()
    turned_s[...] = turned(s_ref[0], square)
    clear_pads(u_ref)

    def tile(start):
        span = pl.ds(start, TILE)
        rows = pl.ds(start + EDGE, TILE)
        source = turned_s[span]
        for x in range(across):
            news = []
            for z in range(depth):
                p = p_ref[z, x, span, chunk * LANES : (chunk + 1) * LANES].astype(F32)
                new = lane(source, z * across + x) * p
                u_ref[z, x, rows] = new
                news.append(new)
            store_edges(x, span, news, even, even_ref, odd_ref)
        store_beside(span, rows, core, u_ref, edge_ref)

    tiles(along, tile)


def square_scratch():
    return [pltpu.VMEM((LANES, LANES), F32)] * 2


def first_field(probes, chunk, source, after=()):
    depth, across, along, _ = probes.shape
    return call(
        functools.partial(first_body, chunk, len(after)),
        in_specs=whole_vmem(2) + unread(after),
        out_specs=whole_vmem(4),
        out_shape=[
            shape_of(depth, across, along + 2 * EDGE, F32),
            shape_of(RADIUS, across, along, BF16),
            shape_of(RADIUS, across, along, BF16),
            shape_of(depth, RADIUS, along, BF16),
        ],
        scratch_shapes=square_scratch(),
    )(probes, source, *after)


def local_body(chunk, moment, has_previous, *refs):
    refs = list(refs)
    u_ref, beside_ref, p_ref, c_ref, s_ref = refs[:5]
    prev_ref = refs[5] if has_previous else None
    base_ref, square, turned_c, turned_s = refs[-4:]
    depth, across, along, _ = base_ref.shape
    core = lax.axis_index("sub")
    left_on = (core == 1).astype(F32)
    right_on = (core == 0).astype(F32)
    turned_c[...] = turned(c_ref[...], square)
    turned_s[...] = turned(s_ref[moment], square)

    def tile(start):
        span = pl.ds(start, TILE)
        rows = start + EDGE
        courant = turned_c[span]
        source = turned_s[span]
        for z in range(depth):
            beside = [beside_ref[z, j, span].astype(F32) for j in range(RADIUS)]
            row = [v * left_on for v in beside]
            row += [u_ref[z, x, pl.ds(rows, TILE)] for x in range(across)]
            row += [v * right_on for v in beside]
            for x in range(across):
                here = row[RADIUS + x]
                total = (3.0 * COEFFICIENTS[0]) * here
                for r in range(1, RADIUS + 1):
                    near = row[RADIUS + x + r] + row[RADIUS + x - r]
                    near = near + (
                        u_ref[z, x, pl.ds(rows + r, TILE)] + u_ref[z, x, pl.ds(rows - r, TILE)]
                    )
                    if z + r < depth:
                        near = near + u_ref[z + r, x, pl.ds(rows, TILE)]
                    if z - r >= 0:
                        near = near + u_ref[z - r, x, pl.ds(rows, TILE)]
                    total = total + COEFFICIENTS[r] * near
                cell = z * across + x
                p = p_ref[z, x, span, chunk * LANES : (chunk + 1) * LANES].astype(F32)
                new = 2.0 * here
                if has_previous:
                    new = new - prev_ref[z, x, pl.ds(rows, TILE)]
                new = new + lane(courant, cell) * total + lane(source, cell) * p
                base_ref[z, x, span] = new

    tiles(along, tile)


def local_step(u, beside, probes, chunk, courant, source, moment, previous):
    depth, across, along, _ = probes.shape
    operands = [u, beside, probes, courant, source]
    if previous is not None:
        operands.append(previous)
    return call(
        functools.partial(local_body, chunk, moment, previous is not None),
        in_specs=whole_vmem(len(operands)),
        out_specs=whole_vmem(1)[0],
        out_shape=shape_of(depth, across, along, F32),
        scratch_shapes=square_scratch() + square_scratch()[:1],
    )(*operands)


def rim_body(kind, after, *refs):
    base_ref, odd_ref, even_ref, c_ref = refs[:4]
    outs, (square, turned_c) = refs[4 + after : -2], refs[-2:]
    depth, across, along, _ = base_ref.shape
    core = lax.axis_index("sub")
    even = slab_is_even()
    lower = lax.axis_index("probe") == 0
    turned_c[...] = turned(c_ref[...], square)
    if kind == "middle":
        clear_pads(outs[0])

    def tile(start):
        span = pl.ds(start, TILE)
        rows = pl.ds(start + EDGE, TILE)
        courant = turned_c[span]
        for x in range(across):
            below, above = [], []
            for j in range(RADIUS):
                one, two = even_ref[j, x, span], odd_ref[j, x, span]
                below.append(jnp.where(even, two, one).astype(F32))
                above.append(jnp.where(even, one, two).astype(F32))
            news = []
            for z in range(depth):
                added = None
                for r in range(1, RADIUS + 1):
                    if z - r < 0:
                        term = COEFFICIENTS[r] * below[RADIUS + z - r]
                        added = term if added is None else added + term
                    if z + r >= depth:
                        term = COEFFICIENTS[r] * above[z + r - depth]
                        added = term if added is None else added + term
                new = base_ref[z, x, span]
                if added is not None:
                    new = new + lane(courant, z * across + x) * added
                news.append(new)
            if kind == "middle":
                for z, new in enumerate(news):
                    outs[0][z, x, rows] = new
                store_edges(x, span, news, even, outs[2], outs[1])
            elif kind == "half":
                for z in range(depth // 2):
                    one, two = news[z].astype(BF16), news[z + depth // 2].astype(BF16)
                    outs[0][z, x, span] = jnp.where(lower, one, two)
                    outs[1][z, x, span] = jnp.where(lower, two, one)
            else:
                for z, new in enumerate(news):
                    outs[0][z, x, span] = new.astype(BF16)
        if kind == "middle":
            store_beside(span, rows, core, outs[0], outs[3])

    tiles(along, tile)


def rim_step(base, odds, evens, courant, kind, after=()):
    depth, across, along, _ = base.shape
    if kind == "middle":
        out_shape = [
            shape_of(depth, across, along + 2 * EDGE, F32),
            shape_of(RADIUS, across, along, BF16),
            shape_of(RADIUS, across, along, BF16),
            shape_of(depth, RADIUS, along, BF16),
        ]
    elif kind == "half":
        out_shape = [shape_of(depth // 2, across, along, BF16)] * 2
    else:
        out_shape = [shape_of(depth, across, along, BF16)]
    return call(
        functools.partial(rim_body, kind, len(after)),
        in_specs=whole_vmem(4) + unread(after),
        out_specs=whole_vmem(len(out_shape)),
        out_shape=out_shape,
        scratch_shapes=square_scratch(),
    )(base, odds, evens, courant, *after)


def swap(x, axis, pairs):
    return lax.ppermute(x, axis, [p for a, b in pairs for p in ((a, b), (b, a))])


def even_swap(x):
    return swap(x, "slab", [(i, i + 1) for i in range(0, lax.axis_size("slab") - 1, 2)])


def odd_swap(x):
    return swap(x, "slab", [(i, i + 1) for i in range(1, lax.axis_size("slab") - 1, 2)])


def core_swap(x):
    return swap(x, "sub", [(0, 1)])


def chip_swap(x):
    return swap(x, "probe", [(0, 1)])


def half_rows(square, field, half, chip):
    square[...] = turned(field, square)
    rows = square[pl.ds(pl.multiple_of(chip * half, 8), half)]
    return jnp.concatenate([rows, rows], axis=0)


def own_half(window, half, chip):
    return jnp.where(chip == 0, window[:half], window[window.shape[0] - half :])


def window_body(p_ref, window_ref):
    depth, _, rows, _ = window_ref.shape
    skip = p_ref.shape[2] - rows
    start = pl.multiple_of((1 - lax.axis_index("probe")) * skip, TILE)

    def plane(z, _):
        window_ref[z] = p_ref[z, :, pl.ds(start, rows), LANES : 2 * LANES]
        return 0

    lax.fori_loop(0, depth, plane, 0)


def window_of(probes):
    depth, across, along, _ = probes.shape
    return call(
        window_body,
        in_specs=whole_vmem(1),
        out_specs=whole_vmem(1)[0],
        out_shape=shape_of(depth, across, along // 2 + EDGE, BF16),
    )(probes)


def store_sides(core, chip, u_ref, edge_ref, rows_ref):
    depth, across, padded, _ = u_ref.shape
    segment = padded // 2
    half = segment - 2 * EDGE
    first = (across - RADIUS) * (1 - core)
    near = pl.multiple_of(jnp.where(chip == 0, half, EDGE), 8)

    def plane(z, _):
        for j in range(RADIUS):
            parts = [
                u_ref[z, first + j, g * segment + EDGE : g * segment + EDGE + half]
                for g in range(2)
            ]
            edge_ref[z, j] = jnp.concatenate(parts, axis=0).astype(BF16)
        if rows_ref is not None:
            for x in range(across):
                parts = [u_ref[z, x, pl.ds(near + g * segment, EDGE)] for g in range(2)]
                rows_ref[z, x] = jnp.concatenate(parts, axis=0).astype(BF16)
        return 0

    lax.fori_loop(0, depth, plane, 0)


def shared_first_body(
    p_ref, got_ref, s_ref, _, u_ref, odd_ref, even_ref, edge_ref, both_ref, square
):
    depth, across, rows, _ = got_ref.shape
    half = rows - EDGE
    segment = half + 2 * EDGE
    along = 2 * half
    chip = lax.axis_index("probe")
    core = lax.axis_index("sub")
    even = slab_is_even()
    lanes = slice(LANES, 2 * LANES)
    square[...] = turned(s_ref[0], square)
    start = pl.multiple_of(chip * (along - rows), TILE)
    source = square[pl.ds(start, rows)]
    blank = jnp.zeros((EDGE, LANES), F32)
    for x in range(across):
        news = []
        for z in range(depth):
            mine = p_ref[z, x, pl.ds(start, rows), lanes].astype(F32)
            got = got_ref[z, x].astype(F32)
            scale = lane(source, z * across + x)
            windows = [jnp.where(chip == 0, mine, got), jnp.where(chip == 0, got, mine)]
            for g, window in enumerate(windows):
                at = pl.multiple_of(g * segment + EDGE * (1 - chip), 8)
                u_ref[z, x, pl.ds(at, rows)] = scale * window
                out = pl.multiple_of(g * segment + chip * (half + EDGE), 8)
                u_ref[z, x, pl.ds(out, EDGE)] = blank
            both = [own_half(window, half, chip) for window in windows]
            both_ref[z, x] = jnp.concatenate(both, axis=0).astype(BF16)
            u = [own_half(scale * window, half, chip) for window in windows]
            news.append(jnp.concatenate(u, axis=0))
        store_edges(x, pl.ds(0, along), news, even, even_ref, odd_ref)
    store_sides(core, chip, u_ref, edge_ref, None)


def shared_first(probes, got, source, after):
    depth, across, along, _ = probes.shape
    edge = shape_of(RADIUS, across, along, BF16)
    return call(
        shared_first_body,
        in_specs=whole_vmem(3) + unread([after]),
        out_specs=whole_vmem(5),
        out_shape=[
            shape_of(depth, across, along + 4 * EDGE, F32),
            edge,
            edge,
            shape_of(depth, RADIUS, along, BF16),
            shape_of(depth, across, along, BF16),
        ],
        scratch_shapes=square_scratch()[:1],
    )(probes, got, source, after)


def shared_local_body(moment, has_previous, *refs):
    refs = list(refs)
    u_ref, beside_ref, p_ref, c_ref, s_ref = refs[:5]
    prev_ref = refs[5] if has_previous else None
    base_ref, square, turned_c, turned_s = refs[-4:]
    depth, across, along, _ = base_ref.shape
    half = along // 2
    core = lax.axis_index("sub")
    chip = lax.axis_index("probe")
    left_on = (core == 1).astype(F32)
    right_on = (core == 0).astype(F32)
    turned_c[:along] = half_rows(square, c_ref[...], half, chip)
    turned_s[:along] = half_rows(square, s_ref[moment], half, chip)

    def tile(start):
        span = pl.ds(start, TILE)
        courant = turned_c[span]
        source = turned_s[span]
        firsts = []
        for k in range(TILE // 8):
            row = start + 8 * k
            firsts.append(pl.multiple_of(row + EDGE + jnp.where(row >= half, 2 * EDGE, 0), 8))

        def load(ref, z, x, shift=0):
            parts = [ref[z, x, pl.ds(first + shift, 8)] for first in firsts]
            return jnp.concatenate(parts, axis=0)

        for z in range(depth):
            beside = [beside_ref[z, j, span].astype(F32) for j in range(RADIUS)]
            row = [v * left_on for v in beside]
            row += [load(u_ref, z, x) for x in range(across)]
            row += [v * right_on for v in beside]
            for x in range(across):
                here = row[RADIUS + x]
                total = (3.0 * COEFFICIENTS[0]) * here
                for r in range(1, RADIUS + 1):
                    near = row[RADIUS + x + r] + row[RADIUS + x - r]
                    near = near + (load(u_ref, z, x, r) + load(u_ref, z, x, -r))
                    if z + r < depth:
                        near = near + load(u_ref, z + r, x)
                    if z - r >= 0:
                        near = near + load(u_ref, z - r, x)
                    total = total + COEFFICIENTS[r] * near
                cell = z * across + x
                new = 2.0 * here
                if has_previous:
                    new = new - load(prev_ref, z, x)
                p = p_ref[z, x, span].astype(F32)
                base_ref[z, x, span] = new + lane(courant, cell) * total + lane(source, cell) * p

    tiles(along, tile)


def shared_local(u, beside, both, courant, source, moment, previous):
    depth, across, along, _ = both.shape
    operands = [u, beside, both, courant, source]
    if previous is not None:
        operands.append(previous)
    return call(
        functools.partial(shared_local_body, moment, previous is not None),
        in_specs=whole_vmem(len(operands)),
        out_specs=whole_vmem(1)[0],
        out_shape=shape_of(depth, across, along, F32),
        scratch_shapes=square_scratch() + square_scratch()[:1],
    )(*operands)


def wide_rim_body(kind, has_rows, after, *refs):
    base_ref, c_ref, odd_ref, even_ref = refs[:4]
    rows_ref = refs[4] if has_rows else None
    outs = refs[4 + has_rows + after : -2]
    square, shifted = refs[-2:]
    depth, across, along, _ = base_ref.shape
    half = along // 2
    segment = half + 2 * EDGE
    core = lax.axis_index("sub")
    chip = lax.axis_index("probe")
    even = slab_is_even()
    blank = jnp.zeros((EDGE, LANES), F32)
    if kind == "own":
        courant = turned(c_ref[...], square)[:along]
    else:
        courant = half_rows(square, c_ref[...], half, chip)

    if has_rows:

        def place(z, _):
            for x in range(across):
                got = rows_ref[z, x].astype(F32)
                for g in range(2):
                    shifted[z, x, g, :EDGE] = blank
                    shifted[z, x, g, EDGE : 2 * EDGE] = got[g * EDGE : (g + 1) * EDGE]
                    shifted[z, x, g, 2 * EDGE :] = blank
            return 0

        lax.fori_loop(0, depth, place, 0)

    def rows_beyond(z, x):
        parts = []
        for g in range(2):
            total = None
            for r in range(1, RADIUS + 1):
                after = shifted[z, x, g, r : r + EDGE]
                before = shifted[z, x, g, 2 * EDGE - r : 3 * EDGE - r]
                term = COEFFICIENTS[r] * jnp.where(chip == 0, after, before)
                total = term if total is None else total + term
            first = jnp.where(chip == 0, blank, total)
            last = jnp.where(chip == 0, total, blank)
            parts += [first] + [blank] * (half // EDGE - 2) + [last]
        return jnp.concatenate(parts, axis=0)

    def values(x):
        ones = [even_ref[j, x].astype(F32) for j in range(RADIUS)]
        twos = [odd_ref[j, x].astype(F32) for j in range(RADIUS)]
        below = [jnp.where(even, two, one) for one, two in zip(ones, twos)]
        above = [jnp.where(even, one, two) for one, two in zip(ones, twos)]
        news = []
        for z in range(depth):
            added = rows_beyond(z, x) if has_rows else None
            for r in range(1, RADIUS + 1):
                if z - r < 0:
                    term = COEFFICIENTS[r] * below[RADIUS + z - r]
                    added = term if added is None else added + term
                if z + r >= depth:
                    term = COEFFICIENTS[r] * above[z + r - depth]
                    added = term if added is None else added + term
            new = base_ref[z, x]
            if added is not None:
                new = new + lane(courant, z * across + x) * added
            news.append(new)
        return news

    if kind == "middle":
        u_ref, odd_out, even_out, edge_ref, rows_out = outs
        for x in range(across):
            news = values(x)
            for z, new in enumerate(news):
                for g in range(2):
                    at = g * segment + EDGE
                    u_ref[z, x, at - EDGE : at] = blank
                    u_ref[z, x, at : at + half] = new[g * half : (g + 1) * half]
                    u_ref[z, x, at + half : at + half + EDGE] = blank
            store_edges(x, pl.ds(0, along), news, even, even_out, odd_out)
        store_sides(core, chip, u_ref, edge_ref, rows_out)
        return
    for i in range(across // 2):
        for z, (one, two) in enumerate(zip(values(2 * i), values(2 * i + 1))):
            first = jnp.concatenate([one[:half], two[:half]], axis=0).astype(BF16)
            second = jnp.concatenate([one[half:], two[half:]], axis=0).astype(BF16)
            if kind == "own":
                first, second = (
                    jnp.where(chip == 0, first, second),
                    jnp.where(chip == 0, second, first),
                )
            outs[0][z, i] = first
            outs[1][z, i] = second


def wide_rim(base, courant, odd, even, kind, rows=None, after=()):
    depth, across, along, _ = base.shape
    if kind == "middle":
        edge = shape_of(RADIUS, across, along, BF16)
        out_shape = [
            shape_of(depth, across, along + 4 * EDGE, F32),
            edge,
            edge,
            shape_of(depth, RADIUS, along, BF16),
            shape_of(depth, across, 2 * EDGE, BF16),
        ]
    else:
        out_shape = [shape_of(depth, across // 2, along, BF16)] * 2
    operands = [base, courant, odd, even]
    if rows is not None:
        operands.append(rows)
    return call(
        functools.partial(wide_rim_body, kind, rows is not None, len(after)),
        in_specs=whole_vmem(len(operands)) + unread(after),
        out_specs=whole_vmem(len(out_shape)),
        out_shape=out_shape,
        scratch_shapes=square_scratch()[:1]
        + [pltpu.VMEM((depth, across, 2, 3 * EDGE, LANES), F32)],
    )(*operands, *after)


def gram_body(kept_ref, got_ref, one_ref, two_ref, keep_ref, send_ref, panel):
    chip = lax.axis_index("probe")
    core = lax.axis_index("sub")
    cells, size = panel.shape
    places = (2 * chip, 2 * (1 - chip), 1, 3)
    for place, ref in zip(places, (kept_ref, got_ref, one_ref, two_ref)):
        at = place * LANES if isinstance(place, int) else pl.multiple_of(place * LANES, LANES)
        panel[:, pl.ds(at, LANES)] = ref[...].reshape(cells, LANES)
    everything = panel[...]

    def columns(which):
        one = panel[:, pl.ds(pl.multiple_of(which * LANES, LANES), LANES)]
        two = panel[:, pl.ds(pl.multiple_of((2 + which) * LANES, LANES), LANES)]
        return lax.dot_general(
            everything,
            jnp.concatenate([one, two], axis=1),
            (((0,), (0,)), ((), ())),
            preferred_element_type=F32,
        )

    keep_ref[:size] = columns(core)
    send_ref[:size] = columns(1 - core)
    rows = lax.broadcasted_iota(jnp.int32, (LANES, LANES), 0)
    cols = lax.broadcasted_iota(jnp.int32, (LANES, LANES), 1)
    eye = rows == cols

    def diagonal(which):
        block = slice(which * LANES, (which + 1) * LANES)
        lanes = slice(which // 2 * LANES, (which // 2 + 1) * LANES)
        block = jnp.where(core == which % 2, keep_ref[block, lanes], send_ref[block, lanes])
        return jnp.sum(jnp.where(eye, block, 0.0), axis=0, keepdims=True)

    diag = [diagonal(n) for n in range(4)]
    row0 = jnp.concatenate(diag[:2], axis=1)
    row1 = jnp.concatenate(diag[2:], axis=1)
    tail = jnp.concatenate([row0, row1, jnp.zeros((6, 2 * LANES), F32)], axis=0)
    keep_ref[size:] = tail
    send_ref[size:] = tail


def gram(fields):
    cells = math.prod(fields[0].shape[:3])
    size = 4 * LANES
    shape = jax.ShapeDtypeStruct((size + 8, 2 * LANES), F32)
    return call(
        gram_body,
        in_specs=whole_vmem(4),
        out_specs=whole_vmem(2),
        out_shape=[shape, shape],
        scratch_shapes=[pltpu.VMEM((cells, size), BF16)],
    )(*fields)


def rounded(ref, block, tail):
    count = block.shape[0]
    high = tail.astype(BF16)
    low = tail - high.astype(F32)
    ref[:count] = block.astype(BF16)
    ref[count:] = jnp.concatenate([high.astype(F32), low], axis=0).astype(BF16)


def opened(ref):
    count = ref.shape[0] - 16
    tail = ref[count:].astype(F32)
    return ref[:count].astype(F32), tail[:8] + tail[8:]


def rows_body(slabs, count, keep_ref, got_ref, own_ref, *outs):
    slab = lax.axis_index("slab")
    size = slabs * count
    tail = keep_ref[pl.ds(size, 8)] + got_ref[pl.ds(size, 8)]
    for d in range(slabs):
        owner = slab ^ d
        span = pl.ds(pl.multiple_of(owner * count, count), count)
        block = keep_ref[span] + got_ref[span]
        if d == 0:
            own_ref[:count] = block
            own_ref[count:] = tail
        else:
            rounded(outs[d - 1], block, tail)


def split_rows(keep, got, slabs):
    count = (keep.shape[0] - 8) // slabs
    own = jax.ShapeDtypeStruct((count + 8, keep.shape[1]), F32)
    sent = jax.ShapeDtypeStruct((count + 16, keep.shape[1]), BF16)
    return call(
        functools.partial(rows_body, slabs, count),
        in_specs=whole_vmem(2),
        out_specs=whole_vmem(slabs),
        out_shape=[own] + [sent] * (slabs - 1),
    )(keep, got)


def sum_body(own_ref, *refs):
    count = own_ref.shape[0] - 8
    block, tail = own_ref[:count], own_ref[count:]
    for ref in refs[:-1]:
        more, more_tail = opened(ref)
        block, tail = block + more, tail + more_tail
    rounded(refs[-1], block, tail)


def sum_all(own, others):
    return call(
        sum_body,
        in_specs=whole_vmem(1 + len(others)),
        out_specs=whole_vmem(1)[0],
        out_shape=jax.ShapeDtypeStruct(others[0].shape, BF16),
    )(own, *others)


def normalise_body(cell_count, mine_ref, other_ref, out_ref, norms_ref):
    slab = lax.axis_index("slab")
    core = lax.axis_index("sub")
    one, one_tail = opened(mine_ref)
    two, two_tail = opened(other_ref)
    total = one + two
    norms = jnp.sqrt((one_tail + two_tail)[:2] / cell_count + EPSILON)
    blocks = [norms[n // 2 : n // 2 + 1, (n % 2) * LANES : (n % 2 + 1) * LANES] for n in range(4)]
    own = blocks[0]
    for n in range(1, 4):
        own = jnp.where(slab == n, blocks[n], own)
    norms_ref[...] = own
    rows = lax.broadcasted_iota(jnp.int32, (LANES, LANES), 0)
    cols = lax.broadcasted_iota(jnp.int32, (LANES, LANES), 1)
    eye = rows == cols
    own_column = jnp.sum(
        jnp.where(eye, jnp.broadcast_to(own, (LANES, LANES)), 0.0), axis=1, keepdims=True
    )
    for side in range(2):
        columns = slice(side * LANES, (side + 1) * LANES)
        others = jnp.where(core == 0, blocks[2 * side], blocks[2 * side + 1])
        value = total[:, columns] / math.sqrt(cell_count) / (own_column * others)
        out_ref[:, columns] = jnp.where(eye & (2 * side + core == slab), 0.0, value)


def normalise(mine, other, cell_count):
    count = mine.shape[0] - 16
    return call(
        functools.partial(normalise_body, cell_count),
        in_specs=whole_vmem(2),
        out_specs=whole_vmem(2),
        out_shape=[
            jax.ShapeDtypeStruct((count, 2 * LANES), F32),
            jax.ShapeDtypeStruct((1, LANES), F32),
        ],
    )(mine, other)


def assemble_body(near_ref, far_ref, out_ref):
    core = lax.axis_index("sub")
    for side in range(2):
        columns = slice(side * LANES, (side + 1) * LANES)
        for ref, which in ((near_ref, core), (far_ref, 1 - core)):
            start = pl.multiple_of((2 * side + which) * LANES, LANES)
            out_ref[:, pl.ds(start, LANES)] = ref[:, columns]


def assemble(near, far):
    return call(
        assemble_body,
        in_specs=whole_vmem(2),
        out_specs=whole_vmem(1)[0],
        out_shape=jax.ShapeDtypeStruct((near.shape[0], 4 * LANES), F32),
    )(near, far)


def coupled(fields, cell_count):
    slabs = 4
    keep, send = gram(fields)
    own, *blocks = split_rows(keep, core_swap(send), slabs)
    arrived = [
        lax.ppermute(blocks[d - 1], "slab", [(i, i ^ d) for i in range(slabs)])
        for d in (2, 3, 1)
    ]
    mine = sum_all(own, arrived)
    near, norms = normalise(mine, chip_swap(mine), cell_count)
    return assemble(near, core_swap(near)), norms.reshape(-1)


def coupled_general(fields, cell_count):
    chips = lax.axis_size("probe")
    sketch = jnp.concatenate(fields, axis=-1)
    sketch = sketch.reshape(-1, sketch.shape[-1])
    if chips > 1:
        sketch = lax.all_to_all(sketch, "probe", split_axis=0, concat_axis=1, tiled=True)
    partial_gram = lax.dot_general(
        sketch, sketch, (((0,), (0,)), ((), ())), preferred_element_type=F32
    )
    rows = lax.psum_scatter(partial_gram, "slab", scatter_dimension=0, tiled=True)
    rows = lax.psum(rows, ("probe", "sub"))
    count = rows.shape[0]
    start = lax.axis_index("slab") * count
    own = jnp.diagonal(lax.dynamic_slice_in_dim(rows, start, count, 1))
    own_norms = jnp.sqrt(own / cell_count + EPSILON)
    norms = lax.all_gather(own_norms, "slab", axis=0, tiled=True)
    coupling = rows / math.sqrt(cell_count) / (own_norms[:, None] * norms[None, :])
    row_ids = start + lax.broadcasted_iota(jnp.int32, coupling.shape, 0)
    col_ids = lax.broadcasted_iota(jnp.int32, coupling.shape, 1)
    return jnp.where(row_ids == col_ids, 0.0, coupling), own_norms


def shards(probes, courant, source):
    depth, across, along, count = probes.shape
    chunks = count // LANES
    slabs, chips = lax.axis_size("slab"), lax.axis_size("probe")
    cell_count = depth * across * along * slabs * lax.axis_size("sub")
    half = along // 2
    paired = chips == 2 and slabs == 4 and chunks == 2 and depth == 2 * RADIUS
    paired = paired and half % 8 == 0 and (half - EDGE) % TILE == 0 and along % TILE == 0
    steps = source.shape[0]
    courant = courant.reshape(depth * across, along)
    source = source.reshape(steps, depth * across, along)
    exchange = lambda odd, even, edge: (odd_swap(odd), even_swap(even), core_swap(edge))
    if paired and across % 2 == 0:
        return shared_shards(probes, courant, source, exchange, cell_count)

    now, previous, halos = [], [None] * chunks, []
    for c in range(chunks):
        u, *edges = first_field(probes, c, source[:1])
        now.append(u)
        halos.append(exchange(*edges))
    fields = []
    for n in range(1, steps):
        for c in range(chunks):
            odd, even, beside = halos[c]
            base = local_step(now[c], beside, probes, c, courant, source, n, previous[c])
            if n == steps - 1:
                fields += rim_step(base, odd, even, courant, "all")
            else:
                u, *edges = rim_step(base, odd, even, courant, "middle")
                previous[c], now[c] = now[c], u
                halos[c] = exchange(*edges)
    return coupled_general(fields, cell_count)


def shared_shards(probes, courant, source, exchange, cell_count):
    steps = source.shape[0]
    first_source = source[:1]
    window = window_of(probes)
    got = chip_swap(window)
    u, *edges = first_field(probes, 0, first_source, (window,))
    odd, even, beside = exchange(*edges)
    base = local_step(u, beside, probes, 0, courant, source, 1, None)
    shared_u, *edges, both = shared_first(probes, got, first_source, base)
    shared_odd, shared_even, shared_beside = exchange(*edges)

    previous = shared_previous = rows = None
    before = both
    for n in range(1, steps):
        last = n == steps - 1
        if last:
            kept, sent = wide_rim(base, courant, odd, even, "own", after=(before,))
            fields = [kept, chip_swap(sent)]
            before = kept
        else:
            previous, (u, *edges) = u, rim_step(base, odd, even, courant, "middle", (before,))
            odd, even, beside = exchange(*edges)
            base = local_step(u, beside, probes, 0, courant, source, n + 1, previous)
            before = base
        shared_base = shared_local(
            shared_u, shared_beside, both, courant, source, n, shared_previous
        )
        shared = (shared_base, courant, shared_odd, shared_even)
        if last:
            fields += wide_rim(*shared, "both", rows, (before,))
        else:
            shared_previous = shared_u
            shared_u, *edges, rows = wide_rim(*shared, "middle", rows, (before,))
            rows = chip_swap(rows)
            before = rows if n == steps - 2 else edges[-1]
            shared_odd, shared_even, shared_beside = exchange(*edges)
    return coupled(fields, cell_count)


def solution(mesh):
    placed = (
        P(("groups", "slab"), "sub", None, "probe"),
        P("slab", "sub", None),
        P(None, ("groups", "slab"), "sub", None),
    )
    return jax.shard_map(
        shards,
        mesh=mesh,
        in_specs=placed,
        out_specs=(P(("groups", "slab"), None), P(("groups", "slab"))),
        check_vma=False,
    )
```

```python
import functools
import math

import jax
import jax.numpy as jnp
from jax import lax
from jax.experimental import pallas as pl
from jax.experimental.pallas import tpu as pltpu
from jax.sharding import PartitionSpec as P

COEFFICIENTS = (-205.0 / 72.0, 8.0 / 5.0, -1.0 / 5.0, 8.0 / 315.0, -1.0 / 560.0)
EPSILON = 1e-06
LANES = 128
RADIUS = 4
EDGE = 8
TILE = 16
F32 = jnp.float32
BF16 = jnp.bfloat16
VMEM_LIMIT = 32 * 1024 * 1024


def call(body, **options):
    return pl.pallas_call(
        body,
        compiler_params=pltpu.CompilerParams(vmem_limit_bytes=VMEM_LIMIT),
        cost_estimate=pl.CostEstimate(flops=1, bytes_accessed=1, transcendentals=0),
        **options,
    )


def unread(arrays):
    return [pl.BlockSpec(memory_space=pl.ANY)] * len(arrays)


def whole_vmem(count):
    return [pl.BlockSpec(memory_space=pltpu.VMEM)] * count


def shape_of(depth, across, along, dtype):
    return jax.ShapeDtypeStruct((depth, across, along, LANES), dtype)


def turned(field, scratch):
    rows, along = field.shape
    scratch[:rows, :along] = field
    return jnp.transpose(scratch[...])


def lane(values, n):
    return jnp.broadcast_to(values[:, n : n + 1], (values.shape[0], LANES))


def store_edges(x, span, news, even, even_ref, odd_ref):
    for j in range(RADIUS):
        low = news[j].astype(BF16)
        high = news[len(news) - RADIUS + j].astype(BF16)
        even_ref[j, x, span] = jnp.where(even, high, low)
        odd_ref[j, x, span] = jnp.where(even, low, high)


def store_beside(span, rows, core, u_ref, edge_ref):
    depth, across, _, _ = u_ref.shape
    first = (across - RADIUS) * (1 - core)
    for z in range(depth):
        for j in range(RADIUS):
            edge_ref[z, j, span] = u_ref[z, first + j, rows].astype(BF16)


def slab_is_even():
    return lax.rem(lax.axis_index("slab"), 2) == 0


def clear_pads(u_ref):
    depth, across, padded, _ = u_ref.shape

    def plane(z, _):
        blank = jnp.zeros((across, EDGE, LANES), F32)
        u_ref[z, :, pl.ds(0, EDGE)] = blank
        u_ref[z, :, pl.ds(padded - EDGE, EDGE)] = blank
        return 0

    lax.fori_loop(0, depth, plane, 0)


def tiles(along, body):
    def one(t, _):
        body(pl.multiple_of(t * TILE, TILE))
        return 0

    lax.fori_loop(0, along // TILE, one, 0)


def first_body(chunk, after, p_ref, s_ref, *refs):
    u_ref, odd_ref, even_ref, edge_ref, square, turned_s = refs[after:]
    depth, across, padded, _ = u_ref.shape
    along = padded - 2 * EDGE
    core = lax.axis_index("sub")
    even = slab_is_even()
    turned_s[...] = turned(s_ref[0], square)
    clear_pads(u_ref)

    def tile(start):
        span = pl.ds(start, TILE)
        rows = pl.ds(start + EDGE, TILE)
        source = turned_s[span]
        for x in range(across):
            news = []
            for z in range(depth):
                p = p_ref[z, x, span, chunk * LANES : (chunk + 1) * LANES].astype(F32)
                new = lane(source, z * across + x) * p
                u_ref[z, x, rows] = new
                news.append(new)
            store_edges(x, span, news, even, even_ref, odd_ref)
        store_beside(span, rows, core, u_ref, edge_ref)

    tiles(along, tile)


def square_scratch():
    return [pltpu.VMEM((LANES, LANES), F32)] * 2


def first_field(probes, chunk, source, after=()):
    depth, across, along, _ = probes.shape
    return call(
        functools.partial(first_body, chunk, len(after)),
        in_specs=whole_vmem(2) + unread(after),
        out_specs=whole_vmem(4),
        out_shape=[
            shape_of(depth, across, along + 2 * EDGE, F32),
            shape_of(RADIUS, across, along, BF16),
            shape_of(RADIUS, across, along, BF16),
            shape_of(depth, RADIUS, along, BF16),
        ],
        scratch_shapes=square_scratch(),
    )(probes, source, *after)


def local_body(chunk, moment, has_previous, *refs):
    refs = list(refs)
    u_ref, beside_ref, p_ref, c_ref, s_ref = refs[:5]
    prev_ref = refs[5] if has_previous else None
    base_ref, square, turned_c, turned_s = refs[-4:]
    depth, across, along, _ = base_ref.shape
    core = lax.axis_index("sub")
    left_on = (core == 1).astype(F32)
    right_on = (core == 0).astype(F32)
    turned_c[...] = turned(c_ref[...], square)
    turned_s[...] = turned(s_ref[moment], square)

    def tile(start):
        span = pl.ds(start, TILE)
        rows = start + EDGE
        courant = turned_c[span]
        source = turned_s[span]
        for z in range(depth):
            beside = [beside_ref[z, j, span].astype(F32) for j in range(RADIUS)]
            row = [v * left_on for v in beside]
            row += [u_ref[z, x, pl.ds(rows, TILE)] for x in range(across)]
            row += [v * right_on for v in beside]
            for x in range(across):
                here = row[RADIUS + x]
                total = (3.0 * COEFFICIENTS[0]) * here
                for r in range(1, RADIUS + 1):
                    near = row[RADIUS + x + r] + row[RADIUS + x - r]
                    near = near + (
                        u_ref[z, x, pl.ds(rows + r, TILE)] + u_ref[z, x, pl.ds(rows - r, TILE)]
                    )
                    if z + r < depth:
                        near = near + u_ref[z + r, x, pl.ds(rows, TILE)]
                    if z - r >= 0:
                        near = near + u_ref[z - r, x, pl.ds(rows, TILE)]
                    total = total + COEFFICIENTS[r] * near
                cell = z * across + x
                p = p_ref[z, x, span, chunk * LANES : (chunk + 1) * LANES].astype(F32)
                new = 2.0 * here
                if has_previous:
                    new = new - prev_ref[z, x, pl.ds(rows, TILE)]
                new = new + lane(courant, cell) * total + lane(source, cell) * p
                base_ref[z, x, span] = new

    tiles(along, tile)


def local_step(u, beside, probes, chunk, courant, source, moment, previous):
    depth, across, along, _ = probes.shape
    operands = [u, beside, probes, courant, source]
    if previous is not None:
        operands.append(previous)
    return call(
        functools.partial(local_body, chunk, moment, previous is not None),
        in_specs=whole_vmem(len(operands)),
        out_specs=whole_vmem(1)[0],
        out_shape=shape_of(depth, across, along, F32),
        scratch_shapes=square_scratch() + square_scratch()[:1],
    )(*operands)


def rim_body(kind, after, *refs):
    base_ref, odd_ref, even_ref, c_ref = refs[:4]
    outs, (square, turned_c) = refs[4 + after : -2], refs[-2:]
    depth, across, along, _ = base_ref.shape
    core = lax.axis_index("sub")
    even = slab_is_even()
    lower = lax.axis_index("probe") == 0
    turned_c[...] = turned(c_ref[...], square)
    if kind == "middle":
        clear_pads(outs[0])

    def tile(start):
        span = pl.ds(start, TILE)
        rows = pl.ds(start + EDGE, TILE)
        courant = turned_c[span]
        for x in range(across):
            below, above = [], []
            for j in range(RADIUS):
                one, two = even_ref[j, x, span], odd_ref[j, x, span]
                below.append(jnp.where(even, two, one).astype(F32))
                above.append(jnp.where(even, one, two).astype(F32))
            news = []
            for z in range(depth):
                added = None
                for r in range(1, RADIUS + 1):
                    if z - r < 0:
                        term = COEFFICIENTS[r] * below[RADIUS + z - r]
                        added = term if added is None else added + term
                    if z + r >= depth:
                        term = COEFFICIENTS[r] * above[z + r - depth]
                        added = term if added is None else added + term
                new = base_ref[z, x, span]
                if added is not None:
                    new = new + lane(courant, z * across + x) * added
                news.append(new)
            if kind == "middle":
                for z, new in enumerate(news):
                    outs[0][z, x, rows] = new
                store_edges(x, span, news, even, outs[2], outs[1])
            elif kind == "half":
                for z in range(depth // 2):
                    one, two = news[z].astype(BF16), news[z + depth // 2].astype(BF16)
                    outs[0][z, x, span] = jnp.where(lower, one, two)
                    outs[1][z, x, span] = jnp.where(lower, two, one)
            else:
                for z, new in enumerate(news):
                    outs[0][z, x, span] = new.astype(BF16)
        if kind == "middle":
            store_beside(span, rows, core, outs[0], outs[3])

    tiles(along, tile)


def rim_step(base, odds, evens, courant, kind, after=()):
    depth, across, along, _ = base.shape
    if kind == "middle":
        out_shape = [
            shape_of(depth, across, along + 2 * EDGE, F32),
            shape_of(RADIUS, across, along, BF16),
            shape_of(RADIUS, across, along, BF16),
            shape_of(depth, RADIUS, along, BF16),
        ]
    elif kind == "half":
        out_shape = [shape_of(depth // 2, across, along, BF16)] * 2
    else:
        out_shape = [shape_of(depth, across, along, BF16)]
    return call(
        functools.partial(rim_body, kind, len(after)),
        in_specs=whole_vmem(4) + unread(after),
        out_specs=whole_vmem(len(out_shape)),
        out_shape=out_shape,
        scratch_shapes=square_scratch(),
    )(base, odds, evens, courant, *after)


def swap(x, axis, pairs):
    return lax.ppermute(x, axis, [p for a, b in pairs for p in ((a, b), (b, a))])


def even_swap(x):
    return swap(x, "slab", [(i, i + 1) for i in range(0, lax.axis_size("slab") - 1, 2)])


def odd_swap(x):
    return swap(x, "slab", [(i, i + 1) for i in range(1, lax.axis_size("slab") - 1, 2)])


def core_swap(x):
    return swap(x, "sub", [(0, 1)])


def chip_swap(x):
    return swap(x, "probe", [(0, 1)])


def half_rows(square, field, half, chip):
    square[...] = turned(field, square)
    rows = square[pl.ds(pl.multiple_of(chip * half, 8), half)]
    return jnp.concatenate([rows, rows], axis=0)


def own_half(window, half, chip):
    return jnp.where(chip == 0, window[:half], window[window.shape[0] - half :])


def window_body(p_ref, window_ref):
    depth, _, rows, _ = window_ref.shape
    skip = p_ref.shape[2] - rows
    start = pl.multiple_of((1 - lax.axis_index("probe")) * skip, TILE)

    def plane(z, _):
        window_ref[z] = p_ref[z, :, pl.ds(start, rows), LANES : 2 * LANES]
        return 0

    lax.fori_loop(0, depth, plane, 0)


def window_of(probes):
    depth, across, along, _ = probes.shape
    return call(
        window_body,
        in_specs=whole_vmem(1),
        out_specs=whole_vmem(1)[0],
        out_shape=shape_of(depth, across, along // 2 + EDGE, BF16),
    )(probes)


def store_sides(core, u_ref, edge_ref):
    depth, across, padded, _ = u_ref.shape
    segment = padded // 2
    half = segment - 2 * EDGE
    first = (across - RADIUS) * (1 - core)

    def plane(z, _):
        for j in range(RADIUS):
            parts = [
                u_ref[z, first + j, g * segment + EDGE : g * segment + EDGE + half]
                for g in range(2)
            ]
            edge_ref[z, j] = jnp.concatenate(parts, axis=0).astype(BF16)
        return 0

    lax.fori_loop(0, depth, plane, 0)


def rows_body(u_ref, _, rows_ref):
    depth, across, padded, _ = u_ref.shape
    segment = padded // 2
    half = segment - 2 * EDGE
    near = pl.multiple_of(jnp.where(lax.axis_index("probe") == 0, half, EDGE), 8)

    def plane(z, _):
        for x in range(across):
            parts = [u_ref[z, x, pl.ds(near + g * segment, EDGE)] for g in range(2)]
            rows_ref[z, x] = jnp.concatenate(parts, axis=0).astype(BF16)
        return 0

    lax.fori_loop(0, depth, plane, 0)


def rows_of(u, after):
    depth, across, _, _ = u.shape
    return call(
        rows_body,
        in_specs=whole_vmem(1) + unread([after]),
        out_specs=whole_vmem(1)[0],
        out_shape=shape_of(depth, across, 2 * EDGE, BF16),
    )(u, after)


def shared_first_body(
    p_ref, got_ref, s_ref, u_ref, odd_ref, even_ref, edge_ref, both_ref, square
):
    depth, across, rows, _ = got_ref.shape
    half = rows - EDGE
    segment = half + 2 * EDGE
    along = 2 * half
    chip = lax.axis_index("probe")
    core = lax.axis_index("sub")
    even = slab_is_even()
    lanes = slice(LANES, 2 * LANES)
    square[...] = turned(s_ref[0], square)
    start = pl.multiple_of(chip * (along - rows), TILE)
    source = square[pl.ds(start, rows)]
    blank = jnp.zeros((EDGE, LANES), F32)
    for x in range(across):
        news = []
        for z in range(depth):
            mine = p_ref[z, x, pl.ds(start, rows), lanes].astype(F32)
            got = got_ref[z, x].astype(F32)
            scale = lane(source, z * across + x)
            windows = [jnp.where(chip == 0, mine, got), jnp.where(chip == 0, got, mine)]
            for g, window in enumerate(windows):
                at = pl.multiple_of(g * segment + EDGE * (1 - chip), 8)
                u_ref[z, x, pl.ds(at, rows)] = scale * window
                out = pl.multiple_of(g * segment + chip * (half + EDGE), 8)
                u_ref[z, x, pl.ds(out, EDGE)] = blank
            both = [own_half(window, half, chip) for window in windows]
            both_ref[z, x] = jnp.concatenate(both, axis=0).astype(BF16)
            u = [own_half(scale * window, half, chip) for window in windows]
            news.append(jnp.concatenate(u, axis=0))
        store_edges(x, pl.ds(0, along), news, even, even_ref, odd_ref)
    store_sides(core, u_ref, edge_ref)


def shared_first(probes, got, source):
    depth, across, along, _ = probes.shape
    edge = shape_of(RADIUS, across, along, BF16)
    return call(
        shared_first_body,
        in_specs=whole_vmem(3),
        out_specs=whole_vmem(5),
        out_shape=[
            shape_of(depth, across, along + 4 * EDGE, F32),
            edge,
            edge,
            shape_of(depth, RADIUS, along, BF16),
            shape_of(depth, across, along, BF16),
        ],
        scratch_shapes=square_scratch()[:1],
    )(probes, got, source)


def shared_local_body(moment, has_previous, *refs):
    refs = list(refs)
    u_ref, beside_ref, p_ref, c_ref, s_ref = refs[:5]
    prev_ref = refs[5] if has_previous else None
    base_ref, square, turned_c, turned_s = refs[-4:]
    depth, across, along, _ = base_ref.shape
    half = along // 2
    core = lax.axis_index("sub")
    chip = lax.axis_index("probe")
    left_on = (core == 1).astype(F32)
    right_on = (core == 0).astype(F32)
    turned_c[:along] = half_rows(square, c_ref[...], half, chip)
    turned_s[:along] = half_rows(square, s_ref[moment], half, chip)

    def tile(start):
        span = pl.ds(start, TILE)
        courant = turned_c[span]
        source = turned_s[span]
        firsts = []
        for k in range(TILE // 8):
            row = start + 8 * k
            firsts.append(pl.multiple_of(row + EDGE + jnp.where(row >= half, 2 * EDGE, 0), 8))

        def load(ref, z, x, shift=0):
            parts = [ref[z, x, pl.ds(first + shift, 8)] for first in firsts]
            return jnp.concatenate(parts, axis=0)

        for z in range(depth):
            beside = [beside_ref[z, j, span].astype(F32) for j in range(RADIUS)]
            row = [v * left_on for v in beside]
            row += [load(u_ref, z, x) for x in range(across)]
            row += [v * right_on for v in beside]
            for x in range(across):
                here = row[RADIUS + x]
                total = (3.0 * COEFFICIENTS[0]) * here
                for r in range(1, RADIUS + 1):
                    near = row[RADIUS + x + r] + row[RADIUS + x - r]
                    near = near + (load(u_ref, z, x, r) + load(u_ref, z, x, -r))
                    if z + r < depth:
                        near = near + load(u_ref, z + r, x)
                    if z - r >= 0:
                        near = near + load(u_ref, z - r, x)
                    total = total + COEFFICIENTS[r] * near
                cell = z * across + x
                new = 2.0 * here
                if has_previous:
                    new = new - load(prev_ref, z, x)
                p = p_ref[z, x, span].astype(F32)
                base_ref[z, x, span] = new + lane(courant, cell) * total + lane(source, cell) * p

    tiles(along, tile)


def shared_local(u, beside, both, courant, source, moment, previous):
    depth, across, along, _ = both.shape
    operands = [u, beside, both, courant, source]
    if previous is not None:
        operands.append(previous)
    return call(
        functools.partial(shared_local_body, moment, previous is not None),
        in_specs=whole_vmem(len(operands)),
        out_specs=whole_vmem(1)[0],
        out_shape=shape_of(depth, across, along, F32),
        scratch_shapes=square_scratch() + square_scratch()[:1],
    )(*operands)


def wide_rim_body(kind, has_rows, after, *refs):
    base_ref, c_ref, odd_ref, even_ref = refs[:4]
    rows_ref = refs[4] if has_rows else None
    outs = refs[4 + has_rows + after : -2]
    square, shifted = refs[-2:]
    depth, across, along, _ = base_ref.shape
    half = along // 2
    segment = half + 2 * EDGE
    core = lax.axis_index("sub")
    chip = lax.axis_index("probe")
    even = slab_is_even()
    blank = jnp.zeros((EDGE, LANES), F32)
    if kind == "own":
        courant = turned(c_ref[...], square)[:along]
    else:
        courant = half_rows(square, c_ref[...], half, chip)

    if has_rows:

        def place(z, _):
            for x in range(across):
                got = rows_ref[z, x].astype(F32)
                for g in range(2):
                    shifted[z, x, g, :EDGE] = blank
                    shifted[z, x, g, EDGE : 2 * EDGE] = got[g * EDGE : (g + 1) * EDGE]
                    shifted[z, x, g, 2 * EDGE :] = blank
            return 0

        lax.fori_loop(0, depth, place, 0)

    def rows_beyond(z, x):
        parts = []
        for g in range(2):
            total = None
            for r in range(1, RADIUS + 1):
                after = shifted[z, x, g, r : r + EDGE]
                before = shifted[z, x, g, 2 * EDGE - r : 3 * EDGE - r]
                term = COEFFICIENTS[r] * jnp.where(chip == 0, after, before)
                total = term if total is None else total + term
            first = jnp.where(chip == 0, blank, total)
            last = jnp.where(chip == 0, total, blank)
            parts += [first] + [blank] * (half // EDGE - 2) + [last]
        return jnp.concatenate(parts, axis=0)

    def values(x):
        ones = [even_ref[j, x].astype(F32) for j in range(RADIUS)]
        twos = [odd_ref[j, x].astype(F32) for j in range(RADIUS)]
        below = [jnp.where(even, two, one) for one, two in zip(ones, twos)]
        above = [jnp.where(even, one, two) for one, two in zip(ones, twos)]
        news = []
        for z in range(depth):
            added = rows_beyond(z, x) if has_rows else None
            for r in range(1, RADIUS + 1):
                if z - r < 0:
                    term = COEFFICIENTS[r] * below[RADIUS + z - r]
                    added = term if added is None else added + term
                if z + r >= depth:
                    term = COEFFICIENTS[r] * above[z + r - depth]
                    added = term if added is None else added + term
            new = base_ref[z, x]
            if added is not None:
                new = new + lane(courant, z * across + x) * added
            news.append(new)
        return news

    if kind == "middle":
        u_ref, odd_out, even_out, edge_ref = outs
        for x in range(across):
            news = values(x)
            for z, new in enumerate(news):
                for g in range(2):
                    at = g * segment + EDGE
                    u_ref[z, x, at - EDGE : at] = blank
                    u_ref[z, x, at : at + half] = new[g * half : (g + 1) * half]
                    u_ref[z, x, at + half : at + half + EDGE] = blank
            store_edges(x, pl.ds(0, along), news, even, even_out, odd_out)
        store_sides(core, u_ref, edge_ref)
        return
    for i in range(across // 2):
        for z, (one, two) in enumerate(zip(values(2 * i), values(2 * i + 1))):
            first = jnp.concatenate([one[:half], two[:half]], axis=0).astype(BF16)
            second = jnp.concatenate([one[half:], two[half:]], axis=0).astype(BF16)
            if kind == "own":
                first, second = (
                    jnp.where(chip == 0, first, second),
                    jnp.where(chip == 0, second, first),
                )
            outs[0][z, i] = first
            outs[1][z, i] = second


def wide_rim(base, courant, odd, even, kind, rows=None, after=()):
    depth, across, along, _ = base.shape
    if kind == "middle":
        edge = shape_of(RADIUS, across, along, BF16)
        out_shape = [
            shape_of(depth, across, along + 4 * EDGE, F32),
            edge,
            edge,
            shape_of(depth, RADIUS, along, BF16),
        ]
    else:
        out_shape = [shape_of(depth, across // 2, along, BF16)] * 2
    operands = [base, courant, odd, even]
    if rows is not None:
        operands.append(rows)
    return call(
        functools.partial(wide_rim_body, kind, rows is not None, len(after)),
        in_specs=whole_vmem(len(operands)) + unread(after),
        out_specs=whole_vmem(len(out_shape)),
        out_shape=out_shape,
        scratch_shapes=square_scratch()[:1]
        + [pltpu.VMEM((depth, across, 2, 3 * EDGE, LANES), F32)],
    )(*operands, *after)


def gram_body(kept_ref, got_ref, one_ref, two_ref, keep_ref, send_ref, panel):
    chip = lax.axis_index("probe")
    core = lax.axis_index("sub")
    cells, size = panel.shape
    places = (2 * chip, 2 * (1 - chip), 1, 3)
    for place, ref in zip(places, (kept_ref, got_ref, one_ref, two_ref)):
        at = place * LANES if isinstance(place, int) else pl.multiple_of(place * LANES, LANES)
        panel[:, pl.ds(at, LANES)] = ref[...].reshape(cells, LANES)
    everything = panel[...]

    def columns(which):
        one = panel[:, pl.ds(pl.multiple_of(which * LANES, LANES), LANES)]
        two = panel[:, pl.ds(pl.multiple_of((2 + which) * LANES, LANES), LANES)]
        return lax.dot_general(
            everything,
            jnp.concatenate([one, two], axis=1),
            (((0,), (0,)), ((), ())),
            preferred_element_type=F32,
        )

    keep_ref[:size] = columns(core)
    send_ref[:size] = columns(1 - core)
    rows = lax.broadcasted_iota(jnp.int32, (LANES, LANES), 0)
    cols = lax.broadcasted_iota(jnp.int32, (LANES, LANES), 1)
    eye = rows == cols

    def diagonal(which):
        block = slice(which * LANES, (which + 1) * LANES)
        lanes = slice(which // 2 * LANES, (which // 2 + 1) * LANES)
        block = jnp.where(core == which % 2, keep_ref[block, lanes], send_ref[block, lanes])
        return jnp.sum(jnp.where(eye, block, 0.0), axis=0, keepdims=True)

    diag = [diagonal(n) for n in range(4)]
    row0 = jnp.concatenate(diag[:2], axis=1)
    row1 = jnp.concatenate(diag[2:], axis=1)
    tail = jnp.concatenate([row0, row1, jnp.zeros((6, 2 * LANES), F32)], axis=0)
    keep_ref[size:] = tail
    send_ref[size:] = tail


def gram(fields):
    cells = math.prod(fields[0].shape[:3])
    size = 4 * LANES
    shape = jax.ShapeDtypeStruct((size + 8, 2 * LANES), F32)
    return call(
        gram_body,
        in_specs=whole_vmem(4),
        out_specs=whole_vmem(2),
        out_shape=[shape, shape],
        scratch_shapes=[pltpu.VMEM((cells, size), BF16)],
    )(*fields)


def rounded(ref, block, tail):
    count = block.shape[0]
    high = tail.astype(BF16)
    low = tail - high.astype(F32)
    ref[:count] = block.astype(BF16)
    ref[count:] = jnp.concatenate([high.astype(F32), low], axis=0).astype(BF16)


def opened(ref):
    count = ref.shape[0] - 16
    tail = ref[count:].astype(F32)
    return ref[:count].astype(F32), tail[:8] + tail[8:]


def split_rows_body(slabs, count, keep_ref, got_ref, own_ref, *outs):
    slab = lax.axis_index("slab")
    size = slabs * count
    tail = keep_ref[pl.ds(size, 8)] + got_ref[pl.ds(size, 8)]
    for d in range(slabs):
        owner = slab ^ d
        span = pl.ds(pl.multiple_of(owner * count, count), count)
        block = keep_ref[span] + got_ref[span]
        if d == 0:
            own_ref[:count] = block
            own_ref[count:] = tail
        else:
            rounded(outs[d - 1], block, tail)


def split_rows(keep, got, slabs):
    count = (keep.shape[0] - 8) // slabs
    own = jax.ShapeDtypeStruct((count + 8, keep.shape[1]), F32)
    sent = jax.ShapeDtypeStruct((count + 16, keep.shape[1]), BF16)
    return call(
        functools.partial(split_rows_body, slabs, count),
        in_specs=whole_vmem(2),
        out_specs=whole_vmem(slabs),
        out_shape=[own] + [sent] * (slabs - 1),
    )(keep, got)


def sum_body(own_ref, *refs):
    count = own_ref.shape[0] - 8
    block, tail = own_ref[:count], own_ref[count:]
    for ref in refs[:-1]:
        more, more_tail = opened(ref)
        block, tail = block + more, tail + more_tail
    rounded(refs[-1], block, tail)


def sum_all(own, others):
    return call(
        sum_body,
        in_specs=whole_vmem(1 + len(others)),
        out_specs=whole_vmem(1)[0],
        out_shape=jax.ShapeDtypeStruct(others[0].shape, BF16),
    )(own, *others)


def normalise_body(cell_count, mine_ref, other_ref, out_ref, norms_ref):
    slab = lax.axis_index("slab")
    core = lax.axis_index("sub")
    one, one_tail = opened(mine_ref)
    two, two_tail = opened(other_ref)
    total = one + two
    norms = jnp.sqrt((one_tail + two_tail)[:2] / cell_count + EPSILON)
    blocks = [norms[n // 2 : n // 2 + 1, (n % 2) * LANES : (n % 2 + 1) * LANES] for n in range(4)]
    own = blocks[0]
    for n in range(1, 4):
        own = jnp.where(slab == n, blocks[n], own)
    norms_ref[...] = own
    rows = lax.broadcasted_iota(jnp.int32, (LANES, LANES), 0)
    cols = lax.broadcasted_iota(jnp.int32, (LANES, LANES), 1)
    eye = rows == cols
    own_column = jnp.sum(
        jnp.where(eye, jnp.broadcast_to(own, (LANES, LANES)), 0.0), axis=1, keepdims=True
    )
    for side in range(2):
        columns = slice(side * LANES, (side + 1) * LANES)
        others = jnp.where(core == 0, blocks[2 * side], blocks[2 * side + 1])
        value = total[:, columns] / math.sqrt(cell_count) / (own_column * others)
        out_ref[:, columns] = jnp.where(eye & (2 * side + core == slab), 0.0, value)


def normalise(mine, other, cell_count):
    count = mine.shape[0] - 16
    return call(
        functools.partial(normalise_body, cell_count),
        in_specs=whole_vmem(2),
        out_specs=whole_vmem(2),
        out_shape=[
            jax.ShapeDtypeStruct((count, 2 * LANES), F32),
            jax.ShapeDtypeStruct((1, LANES), F32),
        ],
    )(mine, other)


def assemble_body(near_ref, far_ref, out_ref):
    core = lax.axis_index("sub")
    for side in range(2):
        columns = slice(side * LANES, (side + 1) * LANES)
        for ref, which in ((near_ref, core), (far_ref, 1 - core)):
            start = pl.multiple_of((2 * side + which) * LANES, LANES)
            out_ref[:, pl.ds(start, LANES)] = ref[:, columns]


def assemble(near, far):
    return call(
        assemble_body,
        in_specs=whole_vmem(2),
        out_specs=whole_vmem(1)[0],
        out_shape=jax.ShapeDtypeStruct((near.shape[0], 4 * LANES), F32),
    )(near, far)


def coupled(fields, cell_count):
    slabs = 4
    keep, send = gram(fields)
    own, *blocks = split_rows(keep, core_swap(send), slabs)
    arrived = [
        lax.ppermute(blocks[d - 1], "slab", [(i, i ^ d) for i in range(slabs)])
        for d in (2, 3, 1)
    ]
    mine = sum_all(own, arrived)
    near, norms = normalise(mine, chip_swap(mine), cell_count)
    return assemble(near, core_swap(near)), norms.reshape(-1)


def coupled_general(fields, cell_count):
    chips = lax.axis_size("probe")
    sketch = jnp.concatenate(fields, axis=-1)
    sketch = sketch.reshape(-1, sketch.shape[-1])
    if chips > 1:
        sketch = lax.all_to_all(sketch, "probe", split_axis=0, concat_axis=1, tiled=True)
    partial_gram = lax.dot_general(
        sketch, sketch, (((0,), (0,)), ((), ())), preferred_element_type=F32
    )
    rows = lax.psum_scatter(partial_gram, "slab", scatter_dimension=0, tiled=True)
    rows = lax.psum(rows, ("probe", "sub"))
    count = rows.shape[0]
    start = lax.axis_index("slab") * count
    own = jnp.diagonal(lax.dynamic_slice_in_dim(rows, start, count, 1))
    own_norms = jnp.sqrt(own / cell_count + EPSILON)
    norms = lax.all_gather(own_norms, "slab", axis=0, tiled=True)
    coupling = rows / math.sqrt(cell_count) / (own_norms[:, None] * norms[None, :])
    row_ids = start + lax.broadcasted_iota(jnp.int32, coupling.shape, 0)
    col_ids = lax.broadcasted_iota(jnp.int32, coupling.shape, 1)
    return jnp.where(row_ids == col_ids, 0.0, coupling), own_norms


def shards(probes, courant, source):
    depth, across, along, count = probes.shape
    chunks = count // LANES
    slabs, chips = lax.axis_size("slab"), lax.axis_size("probe")
    cell_count = depth * across * along * slabs * lax.axis_size("sub")
    half = along // 2
    paired = chips == 2 and slabs == 4 and chunks == 2 and depth == 2 * RADIUS
    paired = paired and half % 8 == 0 and (half - EDGE) % TILE == 0 and along % TILE == 0
    steps = source.shape[0]
    courant = courant.reshape(depth * across, along)
    source = source.reshape(steps, depth * across, along)
    exchange = lambda odd, even, edge: (odd_swap(odd), even_swap(even), core_swap(edge))
    if paired and across % 2 == 0:
        return shared_shards(probes, courant, source, exchange, cell_count)

    now, previous, halos = [], [None] * chunks, []
    for c in range(chunks):
        u, *edges = first_field(probes, c, source[:1])
        now.append(u)
        halos.append(exchange(*edges))
    fields = []
    for n in range(1, steps):
        for c in range(chunks):
            odd, even, beside = halos[c]
            base = local_step(now[c], beside, probes, c, courant, source, n, previous[c])
            if n == steps - 1:
                fields += rim_step(base, odd, even, courant, "all")
            else:
                u, *edges = rim_step(base, odd, even, courant, "middle")
                previous[c], now[c] = now[c], u
                halos[c] = exchange(*edges)
    return coupled_general(fields, cell_count)


def shared_shards(probes, courant, source, exchange, cell_count):
    steps = source.shape[0]
    first_source = source[:1]
    window = window_of(probes)
    got = chip_swap(window)
    u, *edges = first_field(probes, 0, first_source, (window,))
    odd, even, beside = exchange(*edges)
    shared_u, *edges, both = shared_first(probes, got, first_source)
    shared_odd, shared_even, shared_beside = exchange(*edges)

    previous = shared_previous = rows = None
    before = both
    base = local_step(u, beside, probes, 0, courant, source, 1, None)
    for n in range(1, steps):
        last = n == steps - 1
        if last:
            kept, sent = wide_rim(base, courant, odd, even, "own", after=(before,))
            fields = [kept, chip_swap(sent)]
            before = kept
        else:
            previous, (u, *edges) = u, rim_step(base, odd, even, courant, "middle", (before,))
            odd, even, beside = exchange(*edges)
            before = edges[-1]
            base = local_step(u, beside, probes, 0, courant, source, n + 1, previous)
        shared_base = shared_local(
            shared_u, shared_beside, both, courant, source, n, shared_previous
        )
        shared = (shared_base, courant, shared_odd, shared_even)
        if last:
            fields += wide_rim(*shared, "both", rows, (before,))
        else:
            shared_previous = shared_u
            shared_u, *edges = wide_rim(*shared, "middle", rows, (before,))
            shared_odd, shared_even, shared_beside = exchange(*edges)
            before = rows_of(shared_u, base)
            rows = chip_swap(before)
    return coupled(fields, cell_count)


def solution(mesh):
    placed = (
        P(("groups", "slab"), "sub", None, "probe"),
        P("slab", "sub", None),
        P(None, ("groups", "slab"), "sub", None),
    )
    return jax.shard_map(
        shards,
        mesh=mesh,
        in_specs=placed,
        out_specs=(P(("groups", "slab"), None), P(("groups", "slab"))),
        check_vma=False,
    )
```

```python
import functools
import math

import jax
import jax.numpy as jnp
from jax import lax
from jax.experimental import pallas as pl
from jax.experimental.pallas import tpu as pltpu
from jax.sharding import PartitionSpec as P

COEFFICIENTS = (-205.0 / 72.0, 8.0 / 5.0, -1.0 / 5.0, 8.0 / 315.0, -1.0 / 560.0)
EPSILON = 1e-06
LANES = 128
RADIUS = 4
EDGE = 8
TILE = 16
F32 = jnp.float32
BF16 = jnp.bfloat16
VMEM_LIMIT = 32 * 1024 * 1024


def call(body, **options):
    return pl.pallas_call(
        body,
        compiler_params=pltpu.CompilerParams(vmem_limit_bytes=VMEM_LIMIT),
        cost_estimate=pl.CostEstimate(flops=1, bytes_accessed=1, transcendentals=0),
        **options,
    )


def whole_vmem(count):
    return [pl.BlockSpec(memory_space=pltpu.VMEM)] * count


def shape_of(depth, across, along, dtype):
    return jax.ShapeDtypeStruct((depth, across, along, LANES), dtype)


def turned(field, scratch):
    rows, along = field.shape
    scratch[:rows, :along] = field
    return jnp.transpose(scratch[...])


def lane(values, n):
    return jnp.broadcast_to(values[:, n : n + 1], (values.shape[0], LANES))


def store_edges(x, span, news, even, even_ref, odd_ref):
    for j in range(RADIUS):
        low = news[j].astype(BF16)
        high = news[len(news) - RADIUS + j].astype(BF16)
        even_ref[j, x, span] = jnp.where(even, high, low)
        odd_ref[j, x, span] = jnp.where(even, low, high)


def store_beside(span, rows, core, u_ref, edge_ref):
    depth, across, _, _ = u_ref.shape
    first = (across - RADIUS) * (1 - core)
    for z in range(depth):
        for j in range(RADIUS):
            edge_ref[z, j, span] = u_ref[z, first + j, rows].astype(BF16)


def slab_is_even():
    return lax.rem(lax.axis_index("slab"), 2) == 0


def clear_pads(u_ref):
    depth, across, padded, _ = u_ref.shape

    def plane(z, _):
        blank = jnp.zeros((across, EDGE, LANES), F32)
        u_ref[z, :, pl.ds(0, EDGE)] = blank
        u_ref[z, :, pl.ds(padded - EDGE, EDGE)] = blank
        return 0

    lax.fori_loop(0, depth, plane, 0)


def tiles(along, body):
    def one(t, _):
        body(pl.multiple_of(t * TILE, TILE))
        return 0

    lax.fori_loop(0, along // TILE, one, 0)


def first_body(chunk, p_ref, s_ref, u_ref, odd_ref, even_ref, edge_ref, square, turned_s):
    depth, across, padded, _ = u_ref.shape
    along = padded - 2 * EDGE
    core = lax.axis_index("sub")
    even = slab_is_even()
    turned_s[...] = turned(s_ref[0], square)
    clear_pads(u_ref)

    def tile(start):
        span = pl.ds(start, TILE)
        rows = pl.ds(start + EDGE, TILE)
        source = turned_s[span]
        for x in range(across):
            news = []
            for z in range(depth):
                p = p_ref[z, x, span, chunk * LANES : (chunk + 1) * LANES].astype(F32)
                new = lane(source, z * across + x) * p
                u_ref[z, x, rows] = new
                news.append(new)
            store_edges(x, span, news, even, even_ref, odd_ref)
        store_beside(span, rows, core, u_ref, edge_ref)

    tiles(along, tile)


def square_scratch():
    return [pltpu.VMEM((LANES, LANES), F32)] * 2


def first_field(probes, chunk, source):
    depth, across, along, _ = probes.shape
    return call(
        functools.partial(first_body, chunk),
        in_specs=whole_vmem(2),
        out_specs=whole_vmem(4),
        out_shape=[
            shape_of(depth, across, along + 2 * EDGE, F32),
            shape_of(RADIUS, across, along, BF16),
            shape_of(RADIUS, across, along, BF16),
            shape_of(depth, RADIUS, along, BF16),
        ],
        scratch_shapes=square_scratch(),
    )(probes, source)


def local_body(chunk, moment, has_previous, *refs):
    refs = list(refs)
    u_ref, beside_ref, p_ref, c_ref, s_ref = refs[:5]
    prev_ref = refs[5] if has_previous else None
    base_ref, square, turned_c, turned_s = refs[-4:]
    depth, across, along, _ = base_ref.shape
    core = lax.axis_index("sub")
    left_on = (core == 1).astype(F32)
    right_on = (core == 0).astype(F32)
    turned_c[...] = turned(c_ref[...], square)
    turned_s[...] = turned(s_ref[moment], square)

    def tile(start):
        span = pl.ds(start, TILE)
        rows = start + EDGE
        courant = turned_c[span]
        source = turned_s[span]
        for z in range(depth):
            beside = [beside_ref[z, j, span].astype(F32) for j in range(RADIUS)]
            row = [v * left_on for v in beside]
            row += [u_ref[z, x, pl.ds(rows, TILE)] for x in range(across)]
            row += [v * right_on for v in beside]
            for x in range(across):
                here = row[RADIUS + x]
                total = (3.0 * COEFFICIENTS[0]) * here
                for r in range(1, RADIUS + 1):
                    near = row[RADIUS + x + r] + row[RADIUS + x - r]
                    near = near + (
                        u_ref[z, x, pl.ds(rows + r, TILE)] + u_ref[z, x, pl.ds(rows - r, TILE)]
                    )
                    if z + r < depth:
                        near = near + u_ref[z + r, x, pl.ds(rows, TILE)]
                    if z - r >= 0:
                        near = near + u_ref[z - r, x, pl.ds(rows, TILE)]
                    total = total + COEFFICIENTS[r] * near
                cell = z * across + x
                p = p_ref[z, x, span, chunk * LANES : (chunk + 1) * LANES].astype(F32)
                new = 2.0 * here
                if has_previous:
                    new = new - prev_ref[z, x, pl.ds(rows, TILE)]
                new = new + lane(courant, cell) * total + lane(source, cell) * p
                base_ref[z, x, span] = new

    tiles(along, tile)


def local_step(u, beside, probes, chunk, courant, source, moment, previous):
    depth, across, along, _ = probes.shape
    operands = [u, beside, probes, courant, source]
    if previous is not None:
        operands.append(previous)
    return call(
        functools.partial(local_body, chunk, moment, previous is not None),
        in_specs=whole_vmem(len(operands)),
        out_specs=whole_vmem(1)[0],
        out_shape=shape_of(depth, across, along, F32),
        scratch_shapes=square_scratch() + square_scratch()[:1],
    )(*operands)


def part_body(sent, base_ref, odd_ref, even_ref, c_ref, out_ref, square, turned_c):
    depth, across, along, _ = base_ref.shape
    even = slab_is_even()
    turned_c[...] = turned(c_ref[...], square)

    def planes(low):
        def tile(start):
            span = pl.ds(start, TILE)
            courant = turned_c[span]
            for x in range(across):
                near = []
                for j in range(RADIUS):
                    one, two = even_ref[j, x, span], odd_ref[j, x, span]
                    pair = (two, one) if low else (one, two)
                    near.append(jnp.where(even, *pair).astype(F32))
                for m in range(RADIUS):
                    z = m if low else depth - RADIUS + m
                    added = None
                    for r in range(1, RADIUS + 1):
                        at = RADIUS + m - r if low else m + r - RADIUS
                        if 0 <= at < RADIUS:
                            term = COEFFICIENTS[r] * near[at]
                            added = term if added is None else added + term
                    new = base_ref[z, x, span] + lane(courant, z * across + x) * added
                    out_ref[m, x, span] = new.astype(BF16)

        tiles(along, tile)

    low = lax.axis_index("probe") == (1 if sent else 0)
    pl.when(low)(lambda: planes(True))
    pl.when(jnp.logical_not(low))(lambda: planes(False))


def part_step(base, odds, evens, courant, sent):
    _, across, along, _ = base.shape
    return call(
        functools.partial(part_body, sent),
        in_specs=whole_vmem(4),
        out_specs=whole_vmem(1)[0],
        out_shape=shape_of(RADIUS, across, along, BF16),
        scratch_shapes=square_scratch(),
    )(base, odds, evens, courant)


def rim_body(kind, *refs):
    base_ref, odd_ref, even_ref, c_ref = refs[:4]
    outs, (square, turned_c) = refs[4:-2], refs[-2:]
    depth, across, along, _ = base_ref.shape
    core = lax.axis_index("sub")
    even = slab_is_even()
    lower = lax.axis_index("probe") == 0
    turned_c[...] = turned(c_ref[...], square)
    if kind == "middle":
        clear_pads(outs[0])

    def tile(start):
        span = pl.ds(start, TILE)
        rows = pl.ds(start + EDGE, TILE)
        courant = turned_c[span]
        for x in range(across):
            below, above = [], []
            for j in range(RADIUS):
                one, two = even_ref[j, x, span], odd_ref[j, x, span]
                below.append(jnp.where(even, two, one).astype(F32))
                above.append(jnp.where(even, one, two).astype(F32))
            news = []
            for z in range(depth):
                added = None
                for r in range(1, RADIUS + 1):
                    if z - r < 0:
                        term = COEFFICIENTS[r] * below[RADIUS + z - r]
                        added = term if added is None else added + term
                    if z + r >= depth:
                        term = COEFFICIENTS[r] * above[z + r - depth]
                        added = term if added is None else added + term
                new = base_ref[z, x, span]
                if added is not None:
                    new = new + lane(courant, z * across + x) * added
                news.append(new)
            if kind == "middle":
                for z, new in enumerate(news):
                    outs[0][z, x, rows] = new
                store_edges(x, span, news, even, outs[2], outs[1])
            elif kind == "half":
                for z in range(depth // 2):
                    one, two = news[z].astype(BF16), news[z + depth // 2].astype(BF16)
                    outs[0][z, x, span] = jnp.where(lower, one, two)
                    outs[1][z, x, span] = jnp.where(lower, two, one)
            else:
                for z, new in enumerate(news):
                    outs[0][z, x, span] = new.astype(BF16)
        if kind == "middle":
            store_beside(span, rows, core, outs[0], outs[3])

    tiles(along, tile)


def rim_step(base, odds, evens, courant, kind):
    depth, across, along, _ = base.shape
    if kind == "middle":
        out_shape = [
            shape_of(depth, across, along + 2 * EDGE, F32),
            shape_of(RADIUS, across, along, BF16),
            shape_of(RADIUS, across, along, BF16),
            shape_of(depth, RADIUS, along, BF16),
        ]
    elif kind == "half":
        out_shape = [shape_of(depth // 2, across, along, BF16)] * 2
    else:
        out_shape = [shape_of(depth, across, along, BF16)]
    return call(
        functools.partial(rim_body, kind),
        in_specs=whole_vmem(4),
        out_specs=whole_vmem(len(out_shape)),
        out_shape=out_shape,
        scratch_shapes=square_scratch(),
    )(base, odds, evens, courant)


def swap(x, axis, pairs):
    return lax.ppermute(x, axis, [p for a, b in pairs for p in ((a, b), (b, a))])


def even_swap(x):
    return swap(x, "slab", [(i, i + 1) for i in range(0, lax.axis_size("slab") - 1, 2)])


def odd_swap(x):
    return swap(x, "slab", [(i, i + 1) for i in range(1, lax.axis_size("slab") - 1, 2)])


def core_swap(x):
    return swap(x, "sub", [(0, 1)])


def chip_swap(x):
    return swap(x, "probe", [(0, 1)])


def product(a, b):
    return lax.dot_general(a, b, (((0,), (0,)), ((), ())), preferred_element_type=F32)


def block_of(array, i, j):
    return array[i * LANES : (i + 1) * LANES, j * LANES : (j + 1) * LANES]


def eye():
    rows = lax.broadcasted_iota(jnp.int32, (LANES, LANES), 0)
    cols = lax.broadcasted_iota(jnp.int32, (LANES, LANES), 1)
    return rows == cols


def inner_body(kept0, sent0, kept1, sent1, keep_ref, send_ref, panel):
    half = panel.shape[0] // 2
    for n, (kept, sent) in enumerate(((kept0, sent0), (kept1, sent1))):
        columns = slice(n * LANES, (n + 1) * LANES)
        panel[:half, columns] = kept[...].reshape(half, LANES)
        panel[half:, columns] = sent[...].reshape(half, LANES)
    core = lax.axis_index("sub")
    whole = product(panel[...], panel[...])
    first, second = whole[:, :LANES], whole[:, LANES:]
    size = 2 * LANES
    keep_ref[:size] = jnp.where(core == 0, first, second)
    send_ref[:size] = jnp.where(core == 0, second, first)
    diag = [
        jnp.sum(jnp.where(eye(), block_of(whole, n, n), 0.0), axis=0, keepdims=True)
        for n in range(2)
    ]
    none = jnp.zeros_like(diag[0])
    chip = lax.axis_index("probe")
    rows = [jnp.where(chip == n // 2, diag[n % 2], none) for n in range(4)]
    tail = jnp.concatenate(rows + [none] * 4, axis=0)
    keep_ref[size:] = tail
    send_ref[size:] = tail


def inner_gram(fields):
    size = 2 * LANES
    cells = 2 * math.prod(fields[0].shape[:3])
    half = jax.ShapeDtypeStruct((size + 8, LANES), F32)
    return call(
        inner_body,
        in_specs=whole_vmem(4),
        out_specs=whole_vmem(2),
        out_shape=[half, half],
        scratch_shapes=[pltpu.VMEM((cells, size), BF16)],
    )(*fields)


def inner_sum_body(keep_ref, got_ref, tail_ref, own_ref, sent_ref):
    size = 2 * LANES
    row = pl.multiple_of(lax.rem(lax.axis_index("slab"), 2) * LANES, LANES)
    own, other = pl.ds(row, LANES), pl.ds(LANES - row, LANES)
    own_ref[...] = keep_ref[own] + got_ref[own]
    sent_ref[...] = (keep_ref[other] + got_ref[other]).astype(BF16)
    tail_ref[...] = keep_ref[size:] + got_ref[size:]


def inner_sum(keep, got):
    return call(
        inner_sum_body,
        in_specs=whole_vmem(2),
        out_specs=whole_vmem(3),
        out_shape=[
            jax.ShapeDtypeStruct((8, LANES), F32),
            jax.ShapeDtypeStruct((LANES, LANES), F32),
            jax.ShapeDtypeStruct((LANES, LANES), BF16),
        ],
    )(keep, got)


def cross_body(kept0, got0, kept1, got1, _, keep_ref, send_ref, panel):
    chip = lax.axis_index("probe")
    core = lax.axis_index("sub")
    cells = panel.shape[0]
    for n, (kept, got) in enumerate(((kept0, got0), (kept1, got1))):
        mine = pl.multiple_of((chip * 2 + n) * LANES, LANES)
        other = pl.multiple_of(((1 - chip) * 2 + n) * LANES, LANES)
        panel[:, pl.ds(mine, LANES)] = kept[...].reshape(cells, LANES)
        panel[:, pl.ds(other, LANES)] = got[...].reshape(cells, LANES)
    whole = product(panel[:, : 2 * LANES], panel[:, 2 * LANES :])
    for ref, which in ((keep_ref, core), (send_ref, 1 - core)):
        here = which == 0
        ref[:LANES] = jnp.where(here, block_of(whole, 0, 0), block_of(whole, 0, 1))
        ref[LANES : 2 * LANES] = jnp.where(here, block_of(whole, 1, 0), block_of(whole, 1, 1))
        mixed = jnp.where(here, block_of(whole, 0, 1), block_of(whole, 1, 0))
        ref[2 * LANES :] = mixed


def cross_gram(fields, after):
    cells = math.prod(fields[0].shape[:3])
    three = jax.ShapeDtypeStruct((3 * LANES, LANES), F32)
    return call(
        cross_body,
        in_specs=whole_vmem(4) + [pl.BlockSpec(memory_space=pl.ANY)],
        out_specs=whole_vmem(2),
        out_shape=[three, three],
        scratch_shapes=[pltpu.VMEM((cells, 4 * LANES), BF16)],
    )(*fields, after)


def rounded(ref, block, tail):
    count = block.shape[0]
    high = tail.astype(BF16)
    low = tail - high.astype(F32)
    ref[:count] = block.astype(BF16)
    ref[count : count + 16] = jnp.concatenate([high.astype(F32), low], axis=0).astype(BF16)


def opened(ref, count):
    tail = ref[count : count + 16].astype(F32)
    return ref[:count].astype(F32), tail[:8] + tail[8:]


def cross_rows_body(keep_ref, got_ref, tail_ref, inner_ref, inner_got_ref, own_ref, *outs):
    slab = lax.axis_index("slab")
    core = lax.axis_index("sub")
    tail = tail_ref[...]
    inner = inner_ref[...] + inner_got_ref[...].astype(F32)
    for d in range(len(outs) + 1):
        owner = slab ^ d
        late = jnp.where(core == 0, jnp.where(owner == 2, 0, 2), jnp.where(owner == 2, 2, 1))
        at = jnp.where(owner < 2, owner, late)
        span = pl.ds(pl.multiple_of(at * LANES, LANES), LANES)
        block = keep_ref[span] + got_ref[span]
        if d == 0:
            own_ref[:LANES] = block
            own_ref[LANES : LANES + 8] = tail
            own_ref[LANES + 8 :] = inner
        else:
            rounded(outs[d - 1], block, tail)
            if d == 2:
                outs[1][LANES + 16 :] = inner.astype(BF16)


def cross_rows(keep, got, tail, inner, inner_got, slabs):
    own = jax.ShapeDtypeStruct((2 * LANES + 8, LANES), F32)
    long = jax.ShapeDtypeStruct((2 * LANES + 16, LANES), BF16)
    short = jax.ShapeDtypeStruct((LANES + 16, LANES), BF16)
    return call(
        cross_rows_body,
        in_specs=whole_vmem(5),
        out_specs=whole_vmem(slabs),
        out_shape=[own, short, long, short],
    )(keep, got, tail, inner, inner_got)


def sum_body(own_ref, *refs):
    block, tail = own_ref[:LANES], own_ref[LANES : LANES + 8]
    *others, out_ref = refs
    for ref in others:
        more, more_tail = opened(ref, LANES)
        block, tail = block + more, tail + more_tail
    inner = own_ref[LANES + 8 :] + others[0][LANES + 16 :].astype(F32)
    rounded(out_ref, block, tail)
    out_ref[LANES + 16 :] = inner.astype(BF16)


def sum_all(own, others):
    return call(
        sum_body,
        in_specs=whole_vmem(1 + len(others)),
        out_specs=whole_vmem(1)[0],
        out_shape=jax.ShapeDtypeStruct(others[0].shape, BF16),
    )(own, *others)


def normalise_body(cell_count, mine_ref, other_ref, out_ref, norms_ref):
    slab = lax.axis_index("slab")
    core = lax.axis_index("sub")
    chip = lax.axis_index("probe")
    one, one_tail = opened(mine_ref, LANES)
    two, two_tail = opened(other_ref, LANES)
    cross = one + two
    inner_span = pl.ds(LANES + 16, LANES)
    inner = jnp.where(slab // 2 == chip, mine_ref[inner_span], other_ref[inner_span]).astype(F32)
    upper = slab < 2
    values = [jnp.where(upper, inner, cross.T), jnp.where(upper, cross, inner)]
    norms = jnp.sqrt((one_tail + two_tail) / cell_count + EPSILON)
    blocks = [norms[n : n + 1] for n in range(4)]
    own = blocks[0]
    for n in range(1, 4):
        own = jnp.where(slab == n, blocks[n], own)
    norms_ref[...] = own
    own_column = jnp.sum(
        jnp.where(eye(), jnp.broadcast_to(own, (LANES, LANES)), 0.0), axis=1, keepdims=True
    )
    for side in range(2):
        others = jnp.where(core == 0, blocks[2 * side], blocks[2 * side + 1])
        value = values[side] / math.sqrt(cell_count) / (own_column * others)
        value = jnp.where(eye() & (2 * side + core == slab), 0.0, value)
        out_ref[:, side * LANES : (side + 1) * LANES] = value


def normalise(mine, other, cell_count):
    return call(
        functools.partial(normalise_body, cell_count),
        in_specs=whole_vmem(2),
        out_specs=whole_vmem(2),
        out_shape=[
            jax.ShapeDtypeStruct((LANES, 2 * LANES), F32),
            jax.ShapeDtypeStruct((1, LANES), F32),
        ],
    )(mine, other)


def assemble_body(near_ref, far_ref, out_ref):
    core = lax.axis_index("sub")
    for side in range(2):
        columns = slice(side * LANES, (side + 1) * LANES)
        for ref, which in ((near_ref, core), (far_ref, 1 - core)):
            start = pl.multiple_of((2 * side + which) * LANES, LANES)
            out_ref[:, pl.ds(start, LANES)] = ref[:, columns]


def assemble(near, far):
    return call(
        assemble_body,
        in_specs=whole_vmem(2),
        out_specs=whole_vmem(1)[0],
        out_shape=jax.ShapeDtypeStruct((near.shape[0], 4 * LANES), F32),
    )(near, far)


def coupled(finals, cell_count):
    slabs = 4
    own = [field for kept, sent, _ in finals for field in (kept, sent)]
    keep, send = inner_gram(own)
    tail, inner, sent = inner_sum(keep, core_swap(send))
    inner_got = lax.ppermute(sent, "slab", [(i, i ^ 1) for i in range(slabs)])
    pairs = [field for kept, _, got in finals for field in (kept, got)]
    keep, send = cross_gram(pairs, inner_got)
    mine, *blocks = cross_rows(keep, core_swap(send), tail, inner, inner_got, slabs)
    arrived = [
        lax.ppermute(blocks[d - 1], "slab", [(i, i ^ d) for i in range(slabs)])
        for d in (2, 3, 1)
    ]
    total = sum_all(mine, arrived)
    near, norms = normalise(total, chip_swap(total), cell_count)
    return assemble(near, core_swap(near)), norms.reshape(-1)


def coupled_general(fields, cell_count):
    chips = lax.axis_size("probe")
    sketch = jnp.concatenate(fields, axis=-1)
    sketch = sketch.reshape(-1, sketch.shape[-1])
    if chips > 1:
        sketch = lax.all_to_all(sketch, "probe", split_axis=0, concat_axis=1, tiled=True)
    partial_gram = lax.dot_general(
        sketch, sketch, (((0,), (0,)), ((), ())), preferred_element_type=F32
    )
    rows = lax.psum_scatter(partial_gram, "slab", scatter_dimension=0, tiled=True)
    rows = lax.psum(rows, ("probe", "sub"))
    count = rows.shape[0]
    start = lax.axis_index("slab") * count
    own = jnp.diagonal(lax.dynamic_slice_in_dim(rows, start, count, 1))
    own_norms = jnp.sqrt(own / cell_count + EPSILON)
    norms = lax.all_gather(own_norms, "slab", axis=0, tiled=True)
    coupling = rows / math.sqrt(cell_count) / (own_norms[:, None] * norms[None, :])
    row_ids = start + lax.broadcasted_iota(jnp.int32, coupling.shape, 0)
    col_ids = lax.broadcasted_iota(jnp.int32, coupling.shape, 1)
    return jnp.where(row_ids == col_ids, 0.0, coupling), own_norms


def shards(probes, courant, source):
    depth, across, along, count = probes.shape
    chunks = count // LANES
    slabs, chips = lax.axis_size("slab"), lax.axis_size("probe")
    cell_count = depth * across * along * slabs * lax.axis_size("sub")
    paired = chips == 2 and slabs == 4 and chunks == 2 and depth == 2 * RADIUS
    steps = source.shape[0]
    courant = courant.reshape(depth * across, along)
    source = source.reshape(steps, depth * across, along)

    exchange = lambda odd, even, edge: (odd_swap(odd), even_swap(even), core_swap(edge))
    now, previous, halos = [], [None] * chunks, []
    for c in range(chunks):
        u, *edges = first_field(probes, c, source[:1])
        now.append(u)
        halos.append(exchange(*edges))
    finals = []
    for n in range(1, steps):
        for c in range(chunks):
            odd, even, beside = halos[c]
            base = local_step(now[c], beside, probes, c, courant, source, n, previous[c])
            if n < steps - 1:
                u, *edges = rim_step(base, odd, even, courant, "middle")
                previous[c], now[c] = now[c], u
                halos[c] = exchange(*edges)
            elif paired:
                if c < chunks - 1:
                    kept, sent = rim_step(base, odd, even, courant, "half")
                else:
                    sent = part_step(base, odd, even, courant, True)
                    kept = part_step(base, odd, even, courant, False)
                finals.append((kept, sent, chip_swap(sent)))
            else:
                finals += rim_step(base, odd, even, courant, "all")
    return (coupled if paired else coupled_general)(finals, cell_count)


def solution(mesh):
    placed = (
        P(("groups", "slab"), "sub", None, "probe"),
        P("slab", "sub", None),
        P(None, ("groups", "slab"), "sub", None),
    )
    return jax.shard_map(
        shards,
        mesh=mesh,
        in_specs=placed,
        out_specs=(P(("groups", "slab"), None), P(("groups", "slab"))),
        check_vma=False,
    )
```

```python
import functools
import math

import jax
import jax.numpy as jnp
from jax import lax
from jax.experimental import pallas as pl
from jax.experimental.pallas import tpu as pltpu
from jax.sharding import PartitionSpec as P

COEFFICIENTS = (-205.0 / 72.0, 8.0 / 5.0, -1.0 / 5.0, 8.0 / 315.0, -1.0 / 560.0)
EPSILON = 1e-06
LANES = 128
RADIUS = 4
EDGE = 8
TILE = 16
F32 = jnp.float32
BF16 = jnp.bfloat16
VMEM_LIMIT = 32 * 1024 * 1024


def call(body, **options):
    return pl.pallas_call(
        body,
        compiler_params=pltpu.CompilerParams(vmem_limit_bytes=VMEM_LIMIT),
        cost_estimate=pl.CostEstimate(flops=1, bytes_accessed=1, transcendentals=0),
        **options,
    )


def whole_vmem(count):
    return [pl.BlockSpec(memory_space=pltpu.VMEM)] * count


def shape_of(depth, across, along, dtype):
    return jax.ShapeDtypeStruct((depth, across, along, LANES), dtype)


def turned(field, scratch):
    rows, along = field.shape
    scratch[:rows, :along] = field
    return jnp.transpose(scratch[...])


def lane(values, n):
    return jnp.broadcast_to(values[:, n : n + 1], (values.shape[0], LANES))


def store_edges(x, span, news, even, even_ref, odd_ref):
    for j in range(RADIUS):
        low = news[j].astype(BF16)
        high = news[len(news) - RADIUS + j].astype(BF16)
        even_ref[j, x, span] = jnp.where(even, high, low)
        odd_ref[j, x, span] = jnp.where(even, low, high)


def store_beside(span, rows, core, u_ref, edge_ref):
    depth, across, _, _ = u_ref.shape
    first = (across - RADIUS) * (1 - core)
    for z in range(depth):
        for j in range(RADIUS):
            edge_ref[z, j, span] = u_ref[z, first + j, rows].astype(BF16)


def slab_is_even():
    return lax.rem(lax.axis_index("slab"), 2) == 0


def clear_pads(u_ref):
    depth, across, padded, _ = u_ref.shape

    def plane(z, _):
        blank = jnp.zeros((across, EDGE, LANES), F32)
        u_ref[z, :, pl.ds(0, EDGE)] = blank
        u_ref[z, :, pl.ds(padded - EDGE, EDGE)] = blank
        return 0

    lax.fori_loop(0, depth, plane, 0)


def tiles(along, body):
    def one(t, _):
        body(pl.multiple_of(t * TILE, TILE))
        return 0

    lax.fori_loop(0, along // TILE, one, 0)


def first_body(chunk, p_ref, s_ref, u_ref, odd_ref, even_ref, edge_ref, square, turned_s):
    depth, across, padded, _ = u_ref.shape
    along = padded - 2 * EDGE
    core = lax.axis_index("sub")
    even = slab_is_even()
    turned_s[...] = turned(s_ref[0], square)
    clear_pads(u_ref)

    def tile(start):
        span = pl.ds(start, TILE)
        rows = pl.ds(start + EDGE, TILE)
        source = turned_s[span]
        for x in range(across):
            news = []
            for z in range(depth):
                p = p_ref[z, x, span, chunk * LANES : (chunk + 1) * LANES].astype(F32)
                new = lane(source, z * across + x) * p
                u_ref[z, x, rows] = new
                news.append(new)
            store_edges(x, span, news, even, even_ref, odd_ref)
        store_beside(span, rows, core, u_ref, edge_ref)

    tiles(along, tile)


def square_scratch():
    return [pltpu.VMEM((LANES, LANES), F32)] * 2


def first_field(probes, chunk, source):
    depth, across, along, _ = probes.shape
    return call(
        functools.partial(first_body, chunk),
        in_specs=whole_vmem(2),
        out_specs=whole_vmem(4),
        out_shape=[
            shape_of(depth, across, along + 2 * EDGE, F32),
            shape_of(RADIUS, across, along, BF16),
            shape_of(RADIUS, across, along, BF16),
            shape_of(depth, RADIUS, along, BF16),
        ],
        scratch_shapes=square_scratch(),
    )(probes, source)


def local_body(chunk, moment, has_previous, *refs):
    refs = list(refs)
    u_ref, beside_ref, p_ref, c_ref, s_ref = refs[:5]
    prev_ref = refs[5] if has_previous else None
    base_ref, square, turned_c, turned_s = refs[-4:]
    depth, across, along, _ = base_ref.shape
    core = lax.axis_index("sub")
    left_on = (core == 1).astype(F32)
    right_on = (core == 0).astype(F32)
    turned_c[...] = turned(c_ref[...], square)
    turned_s[...] = turned(s_ref[moment], square)

    def tile(start):
        span = pl.ds(start, TILE)
        rows = start + EDGE
        courant = turned_c[span]
        source = turned_s[span]
        for z in range(depth):
            beside = [beside_ref[z, j, span].astype(F32) for j in range(RADIUS)]
            row = [v * left_on for v in beside]
            row += [u_ref[z, x, pl.ds(rows, TILE)] for x in range(across)]
            row += [v * right_on for v in beside]
            for x in range(across):
                here = row[RADIUS + x]
                total = (3.0 * COEFFICIENTS[0]) * here
                for r in range(1, RADIUS + 1):
                    near = row[RADIUS + x + r] + row[RADIUS + x - r]
                    near = near + (
                        u_ref[z, x, pl.ds(rows + r, TILE)] + u_ref[z, x, pl.ds(rows - r, TILE)]
                    )
                    if z + r < depth:
                        near = near + u_ref[z + r, x, pl.ds(rows, TILE)]
                    if z - r >= 0:
                        near = near + u_ref[z - r, x, pl.ds(rows, TILE)]
                    total = total + COEFFICIENTS[r] * near
                cell = z * across + x
                p = p_ref[z, x, span, chunk * LANES : (chunk + 1) * LANES].astype(F32)
                new = 2.0 * here
                if has_previous:
                    new = new - prev_ref[z, x, pl.ds(rows, TILE)]
                new = new + lane(courant, cell) * total + lane(source, cell) * p
                base_ref[z, x, span] = new

    tiles(along, tile)


def local_step(u, beside, probes, chunk, courant, source, moment, previous):
    depth, across, along, _ = probes.shape
    operands = [u, beside, probes, courant, source]
    if previous is not None:
        operands.append(previous)
    return call(
        functools.partial(local_body, chunk, moment, previous is not None),
        in_specs=whole_vmem(len(operands)),
        out_specs=whole_vmem(1)[0],
        out_shape=shape_of(depth, across, along, F32),
        scratch_shapes=square_scratch() + square_scratch()[:1],
    )(*operands)


def part_body(sent, begin, base_ref, odd_ref, even_ref, c_ref, out_ref, square, turned_c):
    depth, across, along, _ = base_ref.shape
    even = slab_is_even()
    turned_c[...] = turned(c_ref[...], square)

    def planes(low):
        def tile(start):
            span = pl.ds(start, TILE)
            courant = turned_c[span]
            for x in range(across):
                near = []
                for j in range(RADIUS):
                    one, two = even_ref[j, x, span], odd_ref[j, x, span]
                    pair = (two, one) if low else (one, two)
                    near.append(jnp.where(even, *pair).astype(F32))
                for m in range(begin, begin + out_ref.shape[0]):
                    z = m if low else depth - RADIUS + m
                    added = None
                    for r in range(1, RADIUS + 1):
                        at = RADIUS + m - r if low else m + r - RADIUS
                        if 0 <= at < RADIUS:
                            term = COEFFICIENTS[r] * near[at]
                            added = term if added is None else added + term
                    new = base_ref[z, x, span] + lane(courant, z * across + x) * added
                    out_ref[m - begin, x, span] = new.astype(BF16)

        tiles(along, tile)

    low = lax.axis_index("probe") == (1 if sent else 0)
    pl.when(low)(lambda: planes(True))
    pl.when(jnp.logical_not(low))(lambda: planes(False))


def part_step(base, odds, evens, courant, sent, begin=0, count=RADIUS):
    _, across, along, _ = base.shape
    return call(
        functools.partial(part_body, sent, begin),
        in_specs=whole_vmem(4),
        out_specs=whole_vmem(1)[0],
        out_shape=shape_of(count, across, along, BF16),
        scratch_shapes=square_scratch(),
    )(base, odds, evens, courant)


def rim_body(kind, *refs):
    base_ref, odd_ref, even_ref, c_ref = refs[:4]
    outs, (square, turned_c) = refs[4:-2], refs[-2:]
    depth, across, along, _ = base_ref.shape
    core = lax.axis_index("sub")
    even = slab_is_even()
    lower = lax.axis_index("probe") == 0
    turned_c[...] = turned(c_ref[...], square)
    if kind == "middle":
        clear_pads(outs[0])

    def tile(start):
        span = pl.ds(start, TILE)
        rows = pl.ds(start + EDGE, TILE)
        courant = turned_c[span]
        for x in range(across):
            below, above = [], []
            for j in range(RADIUS):
                one, two = even_ref[j, x, span], odd_ref[j, x, span]
                below.append(jnp.where(even, two, one).astype(F32))
                above.append(jnp.where(even, one, two).astype(F32))
            news = []
            for z in range(depth):
                added = None
                for r in range(1, RADIUS + 1):
                    if z - r < 0:
                        term = COEFFICIENTS[r] * below[RADIUS + z - r]
                        added = term if added is None else added + term
                    if z + r >= depth:
                        term = COEFFICIENTS[r] * above[z + r - depth]
                        added = term if added is None else added + term
                new = base_ref[z, x, span]
                if added is not None:
                    new = new + lane(courant, z * across + x) * added
                news.append(new)
            if kind == "middle":
                for z, new in enumerate(news):
                    outs[0][z, x, rows] = new
                store_edges(x, span, news, even, outs[2], outs[1])
            elif kind == "half":
                for z in range(depth // 2):
                    one, two = news[z].astype(BF16), news[z + depth // 2].astype(BF16)
                    outs[0][z, x, span] = jnp.where(lower, one, two)
                    outs[1][z, x, span] = jnp.where(lower, two, one)
            else:
                for z, new in enumerate(news):
                    outs[0][z, x, span] = new.astype(BF16)
        if kind == "middle":
            store_beside(span, rows, core, outs[0], outs[3])

    tiles(along, tile)


def rim_step(base, odds, evens, courant, kind):
    depth, across, along, _ = base.shape
    if kind == "middle":
        out_shape = [
            shape_of(depth, across, along + 2 * EDGE, F32),
            shape_of(RADIUS, across, along, BF16),
            shape_of(RADIUS, across, along, BF16),
            shape_of(depth, RADIUS, along, BF16),
        ]
    elif kind == "half":
        out_shape = [shape_of(depth // 2, across, along, BF16)] * 2
    else:
        out_shape = [shape_of(depth, across, along, BF16)]
    return call(
        functools.partial(rim_body, kind),
        in_specs=whole_vmem(4),
        out_specs=whole_vmem(len(out_shape)),
        out_shape=out_shape,
        scratch_shapes=square_scratch(),
    )(base, odds, evens, courant)


def swap(x, axis, pairs):
    return lax.ppermute(x, axis, [p for a, b in pairs for p in ((a, b), (b, a))])


def even_swap(x):
    return swap(x, "slab", [(i, i + 1) for i in range(0, lax.axis_size("slab") - 1, 2)])


def odd_swap(x):
    return swap(x, "slab", [(i, i + 1) for i in range(1, lax.axis_size("slab") - 1, 2)])


def core_swap(x):
    return swap(x, "sub", [(0, 1)])


def chip_swap(x):
    return swap(x, "probe", [(0, 1)])


def product(a, b):
    return lax.dot_general(a, b, (((0,), (0,)), ((), ())), preferred_element_type=F32)


def block_of(array, i, j):
    return array[i * LANES : (i + 1) * LANES, j * LANES : (j + 1) * LANES]


def eye():
    rows = lax.broadcasted_iota(jnp.int32, (LANES, LANES), 0)
    cols = lax.broadcasted_iota(jnp.int32, (LANES, LANES), 1)
    return rows == cols


def lay(panel, columns, refs):
    row = 0
    for ref in refs:
        cells = math.prod(ref.shape[:3])
        panel[row : row + cells, columns] = ref[...].reshape(cells, LANES)
        row += cells


def flat(groups):
    return [field for group in groups for field in group]


def regroup(sizes, refs):
    groups, refs = [], list(refs)
    for size in sizes:
        groups.append(refs[:size])
        refs = refs[size:]
    return groups, refs


def inner_body(sizes, *refs):
    groups, (keep_ref, send_ref, panel) = regroup(sizes, refs)
    for n, group in enumerate(groups):
        lay(panel, slice(n * LANES, (n + 1) * LANES), group)
    core = lax.axis_index("sub")
    whole = product(panel[...], panel[...])
    first, second = whole[:, :LANES], whole[:, LANES:]
    size = 2 * LANES
    keep_ref[:size] = jnp.where(core == 0, first, second)
    send_ref[:size] = jnp.where(core == 0, second, first)
    diag = [
        jnp.sum(jnp.where(eye(), block_of(whole, n, n), 0.0), axis=0, keepdims=True)
        for n in range(2)
    ]
    none = jnp.zeros_like(diag[0])
    chip = lax.axis_index("probe")
    rows = [jnp.where(chip == n // 2, diag[n % 2], none) for n in range(4)]
    tail = jnp.concatenate(rows + [none] * 4, axis=0)
    keep_ref[size:] = tail
    send_ref[size:] = tail


def inner_gram(groups):
    size = 2 * LANES
    cells = sum(math.prod(field.shape[:3]) for field in groups[0])
    half = jax.ShapeDtypeStruct((size + 8, LANES), F32)
    return call(
        functools.partial(inner_body, [len(group) for group in groups]),
        in_specs=whole_vmem(len(flat(groups))),
        out_specs=whole_vmem(2),
        out_shape=[half, half],
        scratch_shapes=[pltpu.VMEM((cells, size), BF16)],
    )(*flat(groups))


def inner_sum_body(keep_ref, got_ref, tail_ref, own_ref, sent_ref):
    size = 2 * LANES
    row = pl.multiple_of(lax.rem(lax.axis_index("slab"), 2) * LANES, LANES)
    own, other = pl.ds(row, LANES), pl.ds(LANES - row, LANES)
    own_ref[...] = keep_ref[own] + got_ref[own]
    sent_ref[...] = (keep_ref[other] + got_ref[other]).astype(BF16)
    tail_ref[...] = keep_ref[size:] + got_ref[size:]


def inner_sum(keep, got):
    return call(
        inner_sum_body,
        in_specs=whole_vmem(2),
        out_specs=whole_vmem(3),
        out_shape=[
            jax.ShapeDtypeStruct((8, LANES), F32),
            jax.ShapeDtypeStruct((LANES, LANES), F32),
            jax.ShapeDtypeStruct((LANES, LANES), BF16),
        ],
    )(keep, got)


def cross_body(sizes, *refs):
    groups, (_, keep_ref, send_ref, panel) = regroup(sizes, refs)
    chip = lax.axis_index("probe")
    core = lax.axis_index("sub")
    for n in range(2):
        mine = pl.multiple_of((chip * 2 + n) * LANES, LANES)
        other = pl.multiple_of(((1 - chip) * 2 + n) * LANES, LANES)
        lay(panel, pl.ds(mine, LANES), groups[2 * n])
        lay(panel, pl.ds(other, LANES), groups[2 * n + 1])
    whole = product(panel[:, : 2 * LANES], panel[:, 2 * LANES :])
    for ref, which in ((keep_ref, core), (send_ref, 1 - core)):
        here = which == 0
        ref[:LANES] = jnp.where(here, block_of(whole, 0, 0), block_of(whole, 0, 1))
        ref[LANES : 2 * LANES] = jnp.where(here, block_of(whole, 1, 0), block_of(whole, 1, 1))
        mixed = jnp.where(here, block_of(whole, 0, 1), block_of(whole, 1, 0))
        ref[2 * LANES :] = mixed


def cross_gram(groups, after):
    cells = sum(math.prod(field.shape[:3]) for field in groups[0])
    three = jax.ShapeDtypeStruct((3 * LANES, LANES), F32)
    return call(
        functools.partial(cross_body, [len(group) for group in groups]),
        in_specs=whole_vmem(len(flat(groups))) + [pl.BlockSpec(memory_space=pl.ANY)],
        out_specs=whole_vmem(2),
        out_shape=[three, three],
        scratch_shapes=[pltpu.VMEM((cells, 4 * LANES), BF16)],
    )(*flat(groups), after)


def rounded(ref, block, tail):
    count = block.shape[0]
    high = tail.astype(BF16)
    low = tail - high.astype(F32)
    ref[:count] = block.astype(BF16)
    ref[count : count + 16] = jnp.concatenate([high.astype(F32), low], axis=0).astype(BF16)


def opened(ref, count):
    tail = ref[count : count + 16].astype(F32)
    return ref[:count].astype(F32), tail[:8] + tail[8:]


def cross_rows_body(keep_ref, got_ref, tail_ref, inner_ref, inner_got_ref, own_ref, *outs):
    slab = lax.axis_index("slab")
    core = lax.axis_index("sub")
    tail = tail_ref[...]
    inner = inner_ref[...] + inner_got_ref[...].astype(F32)
    for d in range(len(outs) + 1):
        owner = slab ^ d
        late = jnp.where(core == 0, jnp.where(owner == 2, 0, 2), jnp.where(owner == 2, 2, 1))
        at = jnp.where(owner < 2, owner, late)
        span = pl.ds(pl.multiple_of(at * LANES, LANES), LANES)
        block = keep_ref[span] + got_ref[span]
        if d == 0:
            own_ref[:LANES] = block
            own_ref[LANES : LANES + 8] = tail
            own_ref[LANES + 8 :] = inner
        else:
            rounded(outs[d - 1], block, tail)
            if d == 2:
                outs[1][LANES + 16 :] = inner.astype(BF16)


def cross_rows(keep, got, tail, inner, inner_got, slabs):
    own = jax.ShapeDtypeStruct((2 * LANES + 8, LANES), F32)
    long = jax.ShapeDtypeStruct((2 * LANES + 16, LANES), BF16)
    short = jax.ShapeDtypeStruct((LANES + 16, LANES), BF16)
    return call(
        cross_rows_body,
        in_specs=whole_vmem(5),
        out_specs=whole_vmem(slabs),
        out_shape=[own, short, long, short],
    )(keep, got, tail, inner, inner_got)


def sum_body(own_ref, *refs):
    block, tail = own_ref[:LANES], own_ref[LANES : LANES + 8]
    *others, out_ref = refs
    for ref in others:
        more, more_tail = opened(ref, LANES)
        block, tail = block + more, tail + more_tail
    inner = own_ref[LANES + 8 :] + others[0][LANES + 16 :].astype(F32)
    rounded(out_ref, block, tail)
    out_ref[LANES + 16 :] = inner.astype(BF16)


def sum_all(own, others):
    return call(
        sum_body,
        in_specs=whole_vmem(1 + len(others)),
        out_specs=whole_vmem(1)[0],
        out_shape=jax.ShapeDtypeStruct(others[0].shape, BF16),
    )(own, *others)


def normalise_body(cell_count, mine_ref, other_ref, out_ref, norms_ref):
    slab = lax.axis_index("slab")
    core = lax.axis_index("sub")
    chip = lax.axis_index("probe")
    one, one_tail = opened(mine_ref, LANES)
    two, two_tail = opened(other_ref, LANES)
    cross = one + two
    inner_span = pl.ds(LANES + 16, LANES)
    inner = jnp.where(slab // 2 == chip, mine_ref[inner_span], other_ref[inner_span]).astype(F32)
    upper = slab < 2
    values = [jnp.where(upper, inner, cross.T), jnp.where(upper, cross, inner)]
    norms = jnp.sqrt((one_tail + two_tail) / cell_count + EPSILON)
    blocks = [norms[n : n + 1] for n in range(4)]
    own = blocks[0]
    for n in range(1, 4):
        own = jnp.where(slab == n, blocks[n], own)
    norms_ref[...] = own
    own_column = jnp.sum(
        jnp.where(eye(), jnp.broadcast_to(own, (LANES, LANES)), 0.0), axis=1, keepdims=True
    )
    for side in range(2):
        others = jnp.where(core == 0, blocks[2 * side], blocks[2 * side + 1])
        value = values[side] / math.sqrt(cell_count) / (own_column * others)
        value = jnp.where(eye() & (2 * side + core == slab), 0.0, value)
        out_ref[:, side * LANES : (side + 1) * LANES] = value


def normalise(mine, other, cell_count):
    return call(
        functools.partial(normalise_body, cell_count),
        in_specs=whole_vmem(2),
        out_specs=whole_vmem(2),
        out_shape=[
            jax.ShapeDtypeStruct((LANES, 2 * LANES), F32),
            jax.ShapeDtypeStruct((1, LANES), F32),
        ],
    )(mine, other)


def assemble_body(near_ref, far_ref, out_ref):
    core = lax.axis_index("sub")
    for side in range(2):
        columns = slice(side * LANES, (side + 1) * LANES)
        for ref, which in ((near_ref, core), (far_ref, 1 - core)):
            start = pl.multiple_of((2 * side + which) * LANES, LANES)
            out_ref[:, pl.ds(start, LANES)] = ref[:, columns]


def assemble(near, far):
    return call(
        assemble_body,
        in_specs=whole_vmem(2),
        out_specs=whole_vmem(1)[0],
        out_shape=jax.ShapeDtypeStruct((near.shape[0], 4 * LANES), F32),
    )(near, far)


def coupled(finals, cell_count):
    slabs = 4
    keep, send = inner_gram([kept + sent for kept, sent, _ in finals])
    tail, inner, sent = inner_sum(keep, core_swap(send))
    inner_got = lax.ppermute(sent, "slab", [(i, i ^ 1) for i in range(slabs)])
    keep, send = cross_gram([g for kept, _, got in finals for g in (kept, got)], inner_got)
    mine, *blocks = cross_rows(keep, core_swap(send), tail, inner, inner_got, slabs)
    arrived = [
        lax.ppermute(blocks[d - 1], "slab", [(i, i ^ d) for i in range(slabs)])
        for d in (2, 3, 1)
    ]
    total = sum_all(mine, arrived)
    near, norms = normalise(total, chip_swap(total), cell_count)
    return assemble(near, core_swap(near)), norms.reshape(-1)


def coupled_general(fields, cell_count):
    chips = lax.axis_size("probe")
    sketch = jnp.concatenate(fields, axis=-1)
    sketch = sketch.reshape(-1, sketch.shape[-1])
    if chips > 1:
        sketch = lax.all_to_all(sketch, "probe", split_axis=0, concat_axis=1, tiled=True)
    partial_gram = lax.dot_general(
        sketch, sketch, (((0,), (0,)), ((), ())), preferred_element_type=F32
    )
    rows = lax.psum_scatter(partial_gram, "slab", scatter_dimension=0, tiled=True)
    rows = lax.psum(rows, ("probe", "sub"))
    count = rows.shape[0]
    start = lax.axis_index("slab") * count
    own = jnp.diagonal(lax.dynamic_slice_in_dim(rows, start, count, 1))
    own_norms = jnp.sqrt(own / cell_count + EPSILON)
    norms = lax.all_gather(own_norms, "slab", axis=0, tiled=True)
    coupling = rows / math.sqrt(cell_count) / (own_norms[:, None] * norms[None, :])
    row_ids = start + lax.broadcasted_iota(jnp.int32, coupling.shape, 0)
    col_ids = lax.broadcasted_iota(jnp.int32, coupling.shape, 1)
    return jnp.where(row_ids == col_ids, 0.0, coupling), own_norms


def shards(probes, courant, source):
    depth, across, along, count = probes.shape
    chunks = count // LANES
    slabs, chips = lax.axis_size("slab"), lax.axis_size("probe")
    cell_count = depth * across * along * slabs * lax.axis_size("sub")
    paired = chips == 2 and slabs == 4 and chunks == 2 and depth == 2 * RADIUS
    steps = source.shape[0]
    courant = courant.reshape(depth * across, along)
    source = source.reshape(steps, depth * across, along)

    exchange = lambda odd, even, edge: (odd_swap(odd), even_swap(even), core_swap(edge))
    now, previous, halos = [], [None] * chunks, []
    for c in range(chunks):
        u, *edges = first_field(probes, c, source[:1])
        now.append(u)
        halos.append(exchange(*edges))
    finals = []
    for n in range(1, steps):
        for c in range(chunks):
            odd, even, beside = halos[c]
            base = local_step(now[c], beside, probes, c, courant, source, n, previous[c])
            if n < steps - 1:
                u, *edges = rim_step(base, odd, even, courant, "middle")
                previous[c], now[c] = now[c], u
                halos[c] = exchange(*edges)
            elif paired:
                if c > 0:
                    kept, *sent = rim_step(base, odd, even, courant, "half")
                else:
                    sent = [
                        part_step(base, odd, even, courant, True, begin, RADIUS // 2)
                        for begin in (0, RADIUS // 2)
                    ]
                    kept = part_step(base, odd, even, courant, False)
                finals.append(([kept], sent, [chip_swap(a) for a in sent]))
            else:
                finals += rim_step(base, odd, even, courant, "all")
    return (coupled if paired else coupled_general)(finals, cell_count)


def solution(mesh):
    placed = (
        P(("groups", "slab"), "sub", None, "probe"),
        P("slab", "sub", None),
        P(None, ("groups", "slab"), "sub", None),
    )
    return jax.shard_map(
        shards,
        mesh=mesh,
        in_specs=placed,
        out_specs=(P(("groups", "slab"), None), P(("groups", "slab"))),
        check_vma=False,
    )
```

```python
import functools
import math

import jax
import jax.numpy as jnp
from jax import lax
from jax.experimental import pallas as pl
from jax.experimental.pallas import tpu as pltpu
from jax.sharding import PartitionSpec as P

COEFFICIENTS = (-205.0 / 72.0, 8.0 / 5.0, -1.0 / 5.0, 8.0 / 315.0, -1.0 / 560.0)
EPSILON = 1e-06
LANES = 128
RADIUS = 4
EDGE = 8
TILE = 16
F32 = jnp.float32
BF16 = jnp.bfloat16
VMEM_LIMIT = 32 * 1024 * 1024


def call(body, **options):
    return pl.pallas_call(
        body,
        compiler_params=pltpu.CompilerParams(vmem_limit_bytes=VMEM_LIMIT),
        cost_estimate=pl.CostEstimate(flops=1, bytes_accessed=1, transcendentals=0),
        **options,
    )


def whole_vmem(count):
    return [pl.BlockSpec(memory_space=pltpu.VMEM)] * count


def shape_of(depth, across, along, dtype):
    return jax.ShapeDtypeStruct((depth, across, along, LANES), dtype)


def turned(field, scratch):
    rows, along = field.shape
    scratch[:rows, :along] = field
    return jnp.transpose(scratch[...])


def lane(values, n):
    return jnp.broadcast_to(values[:, n : n + 1], (values.shape[0], LANES))


def store_edges(x, span, news, even, even_ref, odd_ref):
    for j in range(RADIUS):
        low = news[j].astype(BF16)
        high = news[len(news) - RADIUS + j].astype(BF16)
        even_ref[j, x, span] = jnp.where(even, high, low)
        odd_ref[j, x, span] = jnp.where(even, low, high)


def store_beside(span, rows, core, u_ref, edge_ref):
    depth, across, _, _ = u_ref.shape
    first = (across - RADIUS) * (1 - core)
    for z in range(depth):
        for j in range(RADIUS):
            edge_ref[z, j, span] = u_ref[z, first + j, rows].astype(BF16)


def slab_is_even():
    return lax.rem(lax.axis_index("slab"), 2) == 0


def clear_pads(u_ref):
    depth, across, padded, _ = u_ref.shape

    def plane(z, _):
        blank = jnp.zeros((across, EDGE, LANES), F32)
        u_ref[z, :, pl.ds(0, EDGE)] = blank
        u_ref[z, :, pl.ds(padded - EDGE, EDGE)] = blank
        return 0

    lax.fori_loop(0, depth, plane, 0)


def tiles(along, body):
    def one(t, _):
        body(pl.multiple_of(t * TILE, TILE))
        return 0

    lax.fori_loop(0, along // TILE, one, 0)


def first_body(chunk, p_ref, s_ref, u_ref, odd_ref, even_ref, edge_ref, square, turned_s):
    depth, across, padded, _ = u_ref.shape
    along = padded - 2 * EDGE
    core = lax.axis_index("sub")
    even = slab_is_even()
    turned_s[...] = turned(s_ref[0], square)
    clear_pads(u_ref)

    def tile(start):
        span = pl.ds(start, TILE)
        rows = pl.ds(start + EDGE, TILE)
        source = turned_s[span]
        for x in range(across):
            news = []
            for z in range(depth):
                p = p_ref[z, x, span, chunk * LANES : (chunk + 1) * LANES].astype(F32)
                new = lane(source, z * across + x) * p
                u_ref[z, x, rows] = new
                news.append(new)
            store_edges(x, span, news, even, even_ref, odd_ref)
        store_beside(span, rows, core, u_ref, edge_ref)

    tiles(along, tile)


def square_scratch():
    return [pltpu.VMEM((LANES, LANES), F32)] * 2


def first_field(probes, chunk, source):
    depth, across, along, _ = probes.shape
    return call(
        functools.partial(first_body, chunk),
        in_specs=whole_vmem(2),
        out_specs=whole_vmem(4),
        out_shape=[
            shape_of(depth, across, along + 2 * EDGE, F32),
            shape_of(RADIUS, across, along, BF16),
            shape_of(RADIUS, across, along, BF16),
            shape_of(depth, RADIUS, along, BF16),
        ],
        scratch_shapes=square_scratch(),
    )(probes, source)


def local_body(chunk, moment, has_previous, *refs):
    refs = list(refs)
    u_ref, beside_ref, p_ref, c_ref, s_ref = refs[:5]
    prev_ref = refs[5] if has_previous else None
    base_ref, square, turned_c, turned_s = refs[-4:]
    depth, across, along, _ = base_ref.shape
    core = lax.axis_index("sub")
    left_on = (core == 1).astype(F32)
    right_on = (core == 0).astype(F32)
    turned_c[...] = turned(c_ref[...], square)
    turned_s[...] = turned(s_ref[moment], square)

    def tile(start):
        span = pl.ds(start, TILE)
        rows = start + EDGE
        courant = turned_c[span]
        source = turned_s[span]
        for z in range(depth):
            beside = [beside_ref[z, j, span].astype(F32) for j in range(RADIUS)]
            row = [v * left_on for v in beside]
            row += [u_ref[z, x, pl.ds(rows, TILE)] for x in range(across)]
            row += [v * right_on for v in beside]
            for x in range(across):
                here = row[RADIUS + x]
                total = (3.0 * COEFFICIENTS[0]) * here
                for r in range(1, RADIUS + 1):
                    near = row[RADIUS + x + r] + row[RADIUS + x - r]
                    near = near + (
                        u_ref[z, x, pl.ds(rows + r, TILE)] + u_ref[z, x, pl.ds(rows - r, TILE)]
                    )
                    if z + r < depth:
                        near = near + u_ref[z + r, x, pl.ds(rows, TILE)]
                    if z - r >= 0:
                        near = near + u_ref[z - r, x, pl.ds(rows, TILE)]
                    total = total + COEFFICIENTS[r] * near
                cell = z * across + x
                p = p_ref[z, x, span, chunk * LANES : (chunk + 1) * LANES].astype(F32)
                new = 2.0 * here
                if has_previous:
                    new = new - prev_ref[z, x, pl.ds(rows, TILE)]
                new = new + lane(courant, cell) * total + lane(source, cell) * p
                base_ref[z, x, span] = new

    tiles(along, tile)


def local_step(u, beside, probes, chunk, courant, source, moment, previous):
    depth, across, along, _ = probes.shape
    operands = [u, beside, probes, courant, source]
    if previous is not None:
        operands.append(previous)
    return call(
        functools.partial(local_body, chunk, moment, previous is not None),
        in_specs=whole_vmem(len(operands)),
        out_specs=whole_vmem(1)[0],
        out_shape=shape_of(depth, across, along, F32),
        scratch_shapes=square_scratch() + square_scratch()[:1],
    )(*operands)


def part_body(sent, begin, base_ref, odd_ref, even_ref, c_ref, out_ref, square, turned_c):
    depth, across, along, _ = base_ref.shape
    even = slab_is_even()
    turned_c[...] = turned(c_ref[...], square)

    def planes(low):
        def tile(start):
            span = pl.ds(start, TILE)
            courant = turned_c[span]
            for x in range(across):
                near = []
                for j in range(RADIUS):
                    one, two = even_ref[j, x, span], odd_ref[j, x, span]
                    pair = (two, one) if low else (one, two)
                    near.append(jnp.where(even, *pair).astype(F32))
                for m in range(begin, begin + out_ref.shape[0]):
                    z = m if low else depth - RADIUS + m
                    added = None
                    for r in range(1, RADIUS + 1):
                        at = RADIUS + m - r if low else m + r - RADIUS
                        if 0 <= at < RADIUS:
                            term = COEFFICIENTS[r] * near[at]
                            added = term if added is None else added + term
                    new = base_ref[z, x, span] + lane(courant, z * across + x) * added
                    out_ref[m - begin, x, span] = new.astype(BF16)

        tiles(along, tile)

    low = lax.axis_index("probe") == (1 if sent else 0)
    pl.when(low)(lambda: planes(True))
    pl.when(jnp.logical_not(low))(lambda: planes(False))


def part_step(base, odds, evens, courant, sent, begin=0, count=RADIUS):
    _, across, along, _ = base.shape
    return call(
        functools.partial(part_body, sent, begin),
        in_specs=whole_vmem(4),
        out_specs=whole_vmem(1)[0],
        out_shape=shape_of(count, across, along, BF16),
        scratch_shapes=square_scratch(),
    )(base, odds, evens, courant)


def rim_body(kind, *refs):
    base_ref, odd_ref, even_ref, c_ref = refs[:4]
    outs, (square, turned_c) = refs[4:-2], refs[-2:]
    depth, across, along, _ = base_ref.shape
    core = lax.axis_index("sub")
    even = slab_is_even()
    lower = lax.axis_index("probe") == 0
    turned_c[...] = turned(c_ref[...], square)
    if kind == "middle":
        clear_pads(outs[0])

    def tile(start):
        span = pl.ds(start, TILE)
        rows = pl.ds(start + EDGE, TILE)
        courant = turned_c[span]
        for x in range(across):
            below, above = [], []
            for j in range(RADIUS):
                one, two = even_ref[j, x, span], odd_ref[j, x, span]
                below.append(jnp.where(even, two, one).astype(F32))
                above.append(jnp.where(even, one, two).astype(F32))
            news = []
            for z in range(depth):
                added = None
                for r in range(1, RADIUS + 1):
                    if z - r < 0:
                        term = COEFFICIENTS[r] * below[RADIUS + z - r]
                        added = term if added is None else added + term
                    if z + r >= depth:
                        term = COEFFICIENTS[r] * above[z + r - depth]
                        added = term if added is None else added + term
                new = base_ref[z, x, span]
                if added is not None:
                    new = new + lane(courant, z * across + x) * added
                news.append(new)
            if kind == "middle":
                for z, new in enumerate(news):
                    outs[0][z, x, rows] = new
                store_edges(x, span, news, even, outs[2], outs[1])
            elif kind == "half":
                for z in range(depth // 2):
                    one, two = news[z].astype(BF16), news[z + depth // 2].astype(BF16)
                    outs[0][z, x, span] = jnp.where(lower, one, two)
                    outs[1][z, x, span] = jnp.where(lower, two, one)
            else:
                for z, new in enumerate(news):
                    outs[0][z, x, span] = new.astype(BF16)
        if kind == "middle":
            store_beside(span, rows, core, outs[0], outs[3])

    tiles(along, tile)


def rim_step(base, odds, evens, courant, kind):
    depth, across, along, _ = base.shape
    if kind == "middle":
        out_shape = [
            shape_of(depth, across, along + 2 * EDGE, F32),
            shape_of(RADIUS, across, along, BF16),
            shape_of(RADIUS, across, along, BF16),
            shape_of(depth, RADIUS, along, BF16),
        ]
    elif kind == "half":
        out_shape = [shape_of(depth // 2, across, along, BF16)] * 2
    else:
        out_shape = [shape_of(depth, across, along, BF16)]
    return call(
        functools.partial(rim_body, kind),
        in_specs=whole_vmem(4),
        out_specs=whole_vmem(len(out_shape)),
        out_shape=out_shape,
        scratch_shapes=square_scratch(),
    )(base, odds, evens, courant)


def swap(x, axis, pairs):
    return lax.ppermute(x, axis, [p for a, b in pairs for p in ((a, b), (b, a))])


def even_swap(x):
    return swap(x, "slab", [(i, i + 1) for i in range(0, lax.axis_size("slab") - 1, 2)])


def odd_swap(x):
    return swap(x, "slab", [(i, i + 1) for i in range(1, lax.axis_size("slab") - 1, 2)])


def core_swap(x):
    return swap(x, "sub", [(0, 1)])


def chip_swap(x):
    return swap(x, "probe", [(0, 1)])


def product(a, b):
    return lax.dot_general(a, b, (((0,), (0,)), ((), ())), preferred_element_type=F32)


def block_of(array, i, j):
    return array[i * LANES : (i + 1) * LANES, j * LANES : (j + 1) * LANES]


def eye():
    rows = lax.broadcasted_iota(jnp.int32, (LANES, LANES), 0)
    cols = lax.broadcasted_iota(jnp.int32, (LANES, LANES), 1)
    return rows == cols


def lay(panel, columns, refs):
    row = 0
    for ref in refs:
        cells = math.prod(ref.shape[:3])
        panel[row : row + cells, columns] = ref[...].reshape(cells, LANES)
        row += cells


def flat(groups):
    return [field for group in groups for field in group]


def regroup(sizes, refs):
    groups, refs = [], list(refs)
    for size in sizes:
        groups.append(refs[:size])
        refs = refs[size:]
    return groups, refs


def inner_body(sizes, *refs):
    groups, (keep_ref, send_ref, panel) = regroup(sizes, refs)
    for n, group in enumerate(groups):
        lay(panel, slice(n * LANES, (n + 1) * LANES), group)
    core = lax.axis_index("sub")
    whole = product(panel[...], panel[...])
    first, second = whole[:, :LANES], whole[:, LANES:]
    size = 2 * LANES
    keep_ref[:size] = jnp.where(core == 0, first, second)
    send_ref[:size] = jnp.where(core == 0, second, first)
    diag = [
        jnp.sum(jnp.where(eye(), block_of(whole, n, n), 0.0), axis=0, keepdims=True)
        for n in range(2)
    ]
    none = jnp.zeros_like(diag[0])
    chip = lax.axis_index("probe")
    rows = [jnp.where(chip == n // 2, diag[n % 2], none) for n in range(4)]
    tail = jnp.concatenate(rows + [none] * 4, axis=0)
    keep_ref[size:] = tail
    send_ref[size:] = tail


def inner_gram(groups):
    size = 2 * LANES
    cells = sum(math.prod(field.shape[:3]) for field in groups[0])
    half = jax.ShapeDtypeStruct((size + 8, LANES), F32)
    return call(
        functools.partial(inner_body, [len(group) for group in groups]),
        in_specs=whole_vmem(len(flat(groups))),
        out_specs=whole_vmem(2),
        out_shape=[half, half],
        scratch_shapes=[pltpu.VMEM((cells, size), BF16)],
    )(*flat(groups))


def inner_rows_body(keep_ref, got_ref, tail_ref, *outs):
    slab = lax.axis_index("slab")
    chip = lax.axis_index("probe")
    tail_ref[...] = keep_ref[2 * LANES :] + got_ref[2 * LANES :]
    for d, out in enumerate(outs):
        row = jnp.clip((slab ^ d) - 2 * chip, 0, 1)
        span = pl.ds(pl.multiple_of(row * LANES, LANES), LANES)
        out[...] = (keep_ref[span] + got_ref[span]).astype(out.dtype)


def inner_rows(keep, got, slabs):
    own = jax.ShapeDtypeStruct((LANES, LANES), F32)
    sent = jax.ShapeDtypeStruct((LANES, LANES), BF16)
    return call(
        inner_rows_body,
        in_specs=whole_vmem(2),
        out_specs=whole_vmem(1 + slabs),
        out_shape=[jax.ShapeDtypeStruct((8, LANES), F32), own] + [sent] * (slabs - 1),
    )(keep, got)


def inner_total_body(own_ref, *refs):
    total = own_ref[...]
    for ref in refs[:-1]:
        total = total + ref[...].astype(F32)
    refs[-1][...] = total.astype(BF16)


def inner_total(own, others):
    return call(
        inner_total_body,
        in_specs=whole_vmem(1 + len(others)),
        out_specs=whole_vmem(1)[0],
        out_shape=jax.ShapeDtypeStruct(own.shape, BF16),
    )(own, *others)


def cross_body(sizes, *refs):
    groups, (*_, keep_ref, send_ref, panel) = regroup(sizes, refs)
    chip = lax.axis_index("probe")
    core = lax.axis_index("sub")
    for n in range(2):
        mine = pl.multiple_of((chip * 2 + n) * LANES, LANES)
        other = pl.multiple_of(((1 - chip) * 2 + n) * LANES, LANES)
        lay(panel, pl.ds(mine, LANES), groups[2 * n])
        lay(panel, pl.ds(other, LANES), groups[2 * n + 1])
    whole = product(panel[:, : 2 * LANES], panel[:, 2 * LANES :])
    for ref, which in ((keep_ref, core), (send_ref, 1 - core)):
        here = which == 0
        ref[:LANES] = jnp.where(here, block_of(whole, 0, 0), block_of(whole, 0, 1))
        ref[LANES : 2 * LANES] = jnp.where(here, block_of(whole, 1, 0), block_of(whole, 1, 1))
        mixed = jnp.where(here, block_of(whole, 0, 1), block_of(whole, 1, 0))
        ref[2 * LANES :] = mixed


def cross_gram(groups, after):
    cells = sum(math.prod(field.shape[:3]) for field in groups[0])
    three = jax.ShapeDtypeStruct((3 * LANES, LANES), F32)
    return call(
        functools.partial(cross_body, [len(group) for group in groups]),
        in_specs=whole_vmem(len(flat(groups))) + [pl.BlockSpec(memory_space=pl.ANY)] * len(after),
        out_specs=whole_vmem(2),
        out_shape=[three, three],
        scratch_shapes=[pltpu.VMEM((cells, 4 * LANES), BF16)],
    )(*flat(groups), *after)


def rounded(ref, block, tail):
    count = block.shape[0]
    high = tail.astype(BF16)
    low = tail - high.astype(F32)
    ref[:count] = block.astype(BF16)
    ref[count : count + 16] = jnp.concatenate([high.astype(F32), low], axis=0).astype(BF16)


def opened(ref, count):
    tail = ref[count : count + 16].astype(F32)
    return ref[:count].astype(F32), tail[:8] + tail[8:]


def cross_rows_body(keep_ref, got_ref, tail_ref, own_ref, *outs):
    slab = lax.axis_index("slab")
    core = lax.axis_index("sub")
    tail = tail_ref[...]
    for d in range(len(outs) + 1):
        owner = slab ^ d
        late = jnp.where(core == 0, jnp.where(owner == 2, 0, 2), jnp.where(owner == 2, 2, 1))
        at = jnp.where(owner < 2, owner, late)
        span = pl.ds(pl.multiple_of(at * LANES, LANES), LANES)
        block = keep_ref[span] + got_ref[span]
        if d == 0:
            own_ref[:LANES] = block
            own_ref[LANES:] = tail
        else:
            rounded(outs[d - 1], block, tail)


def cross_rows(keep, got, tail, slabs):
    own = jax.ShapeDtypeStruct((LANES + 8, LANES), F32)
    sent = jax.ShapeDtypeStruct((LANES + 16, LANES), BF16)
    return call(
        cross_rows_body,
        in_specs=whole_vmem(3),
        out_specs=whole_vmem(slabs),
        out_shape=[own] + [sent] * (slabs - 1),
    )(keep, got, tail)


def sum_body(own_ref, *refs):
    block, tail = own_ref[:LANES], own_ref[LANES:]
    *others, out_ref = refs
    for ref in others:
        more, more_tail = opened(ref, LANES)
        block, tail = block + more, tail + more_tail
    rounded(out_ref, block, tail)


def sum_all(own, others):
    return call(
        sum_body,
        in_specs=whole_vmem(1 + len(others)),
        out_specs=whole_vmem(1)[0],
        out_shape=jax.ShapeDtypeStruct(others[0].shape, BF16),
    )(own, *others)


def normalise_body(cell_count, mine_ref, other_ref, inner_ref, other_inner_ref, out_ref, norms_ref):
    slab = lax.axis_index("slab")
    core = lax.axis_index("sub")
    chip = lax.axis_index("probe")
    one, one_tail = opened(mine_ref, LANES)
    two, two_tail = opened(other_ref, LANES)
    cross = one + two
    inner = jnp.where(slab // 2 == chip, inner_ref[...], other_inner_ref[...]).astype(F32)
    upper = slab < 2
    values = [jnp.where(upper, inner, cross.T), jnp.where(upper, cross, inner)]
    norms = jnp.sqrt((one_tail + two_tail) / cell_count + EPSILON)
    blocks = [norms[n : n + 1] for n in range(4)]
    own = blocks[0]
    for n in range(1, 4):
        own = jnp.where(slab == n, blocks[n], own)
    norms_ref[...] = own
    own_column = jnp.sum(
        jnp.where(eye(), jnp.broadcast_to(own, (LANES, LANES)), 0.0), axis=1, keepdims=True
    )
    for side in range(2):
        others = jnp.where(core == 0, blocks[2 * side], blocks[2 * side + 1])
        value = values[side] / math.sqrt(cell_count) / (own_column * others)
        value = jnp.where(eye() & (2 * side + core == slab), 0.0, value)
        out_ref[:, side * LANES : (side + 1) * LANES] = value


def normalise(mine, other, inner, other_inner, cell_count):
    return call(
        functools.partial(normalise_body, cell_count),
        in_specs=whole_vmem(4),
        out_specs=whole_vmem(2),
        out_shape=[
            jax.ShapeDtypeStruct((LANES, 2 * LANES), F32),
            jax.ShapeDtypeStruct((1, LANES), F32),
        ],
    )(mine, other, inner, other_inner)


def assemble_body(near_ref, far_ref, out_ref):
    core = lax.axis_index("sub")
    for side in range(2):
        columns = slice(side * LANES, (side + 1) * LANES)
        for ref, which in ((near_ref, core), (far_ref, 1 - core)):
            start = pl.multiple_of((2 * side + which) * LANES, LANES)
            out_ref[:, pl.ds(start, LANES)] = ref[:, columns]


def assemble(near, far):
    return call(
        assemble_body,
        in_specs=whole_vmem(2),
        out_specs=whole_vmem(1)[0],
        out_shape=jax.ShapeDtypeStruct((near.shape[0], 4 * LANES), F32),
    )(near, far)


def coupled(finals, cell_count):
    slabs = 4
    keep, send = inner_gram([kept + sent for kept, sent, _ in finals])
    tail, own, *sent = inner_rows(keep, core_swap(send), slabs)
    inner_arrived = []
    for d in (2, 3, 1):
        pairs = [
            (2 * (k ^ d) + chip, 2 * k + chip)
            for chip in range(2)
            for k in (2 * chip, 2 * chip + 1)
        ]
        inner_arrived.append(lax.ppermute(sent[d - 1], ("slab", "probe"), pairs))
    inner = inner_total(own, inner_arrived)

    groups = [group for kept, _, got in finals for group in (kept, got)]
    keep, send = cross_gram(groups, inner_arrived)
    mine, *blocks = cross_rows(keep, core_swap(send), tail, slabs)
    arrived = [
        lax.ppermute(blocks[d - 1], "slab", [(i, i ^ d) for i in range(slabs)])
        for d in (2, 3, 1)
    ]
    total = sum_all(mine, arrived)
    near, norms = normalise(total, chip_swap(total), inner, chip_swap(inner), cell_count)
    return assemble(near, core_swap(near)), norms.reshape(-1)


def coupled_general(fields, cell_count):
    chips = lax.axis_size("probe")
    sketch = jnp.concatenate(fields, axis=-1)
    sketch = sketch.reshape(-1, sketch.shape[-1])
    if chips > 1:
        sketch = lax.all_to_all(sketch, "probe", split_axis=0, concat_axis=1, tiled=True)
    partial_gram = lax.dot_general(
        sketch, sketch, (((0,), (0,)), ((), ())), preferred_element_type=F32
    )
    rows = lax.psum_scatter(partial_gram, "slab", scatter_dimension=0, tiled=True)
    rows = lax.psum(rows, ("probe", "sub"))
    count = rows.shape[0]
    start = lax.axis_index("slab") * count
    own = jnp.diagonal(lax.dynamic_slice_in_dim(rows, start, count, 1))
    own_norms = jnp.sqrt(own / cell_count + EPSILON)
    norms = lax.all_gather(own_norms, "slab", axis=0, tiled=True)
    coupling = rows / math.sqrt(cell_count) / (own_norms[:, None] * norms[None, :])
    row_ids = start + lax.broadcasted_iota(jnp.int32, coupling.shape, 0)
    col_ids = lax.broadcasted_iota(jnp.int32, coupling.shape, 1)
    return jnp.where(row_ids == col_ids, 0.0, coupling), own_norms


def shards(probes, courant, source):
    depth, across, along, count = probes.shape
    chunks = count // LANES
    slabs, chips = lax.axis_size("slab"), lax.axis_size("probe")
    cell_count = depth * across * along * slabs * lax.axis_size("sub")
    paired = chips == 2 and slabs == 4 and chunks == 2 and depth == 2 * RADIUS
    steps = source.shape[0]
    courant = courant.reshape(depth * across, along)
    source = source.reshape(steps, depth * across, along)

    exchange = lambda odd, even, edge: (odd_swap(odd), even_swap(even), core_swap(edge))
    now, previous, halos = [], [None] * chunks, []
    for c in range(chunks):
        u, *edges = first_field(probes, c, source[:1])
        now.append(u)
        halos.append(exchange(*edges))
    finals = []
    for n in range(1, steps):
        for c in range(chunks):
            odd, even, beside = halos[c]
            base = local_step(now[c], beside, probes, c, courant, source, n, previous[c])
            if n < steps - 1:
                u, *edges = rim_step(base, odd, even, courant, "middle")
                previous[c], now[c] = now[c], u
                halos[c] = exchange(*edges)
            elif paired:
                if c > 0:
                    kept, *sent = rim_step(base, odd, even, courant, "half")
                else:
                    sent = [
                        part_step(base, odd, even, courant, True, begin, RADIUS // 2)
                        for begin in (0, RADIUS // 2)
                    ]
                    kept = part_step(base, odd, even, courant, False)
                finals.append(([kept], sent, [chip_swap(a) for a in sent]))
            else:
                finals += rim_step(base, odd, even, courant, "all")
    return (coupled if paired else coupled_general)(finals, cell_count)


def solution(mesh):
    placed = (
        P(("groups", "slab"), "sub", None, "probe"),
        P("slab", "sub", None),
        P(None, ("groups", "slab"), "sub", None),
    )
    return jax.shard_map(
        shards,
        mesh=mesh,
        in_specs=placed,
        out_specs=(P(("groups", "slab"), None), P(("groups", "slab"))),
        check_vma=False,
    )
```

```python
import functools
import math

import jax
import jax.numpy as jnp
from jax import lax
from jax.experimental import pallas as pl
from jax.experimental.pallas import tpu as pltpu
from jax.sharding import PartitionSpec as P

COEFFICIENTS = (-205.0 / 72.0, 8.0 / 5.0, -1.0 / 5.0, 8.0 / 315.0, -1.0 / 560.0)
EPSILON = 1e-06
LANES = 128
RADIUS = 4
EDGE = 8
TILE = 16
F32 = jnp.float32
BF16 = jnp.bfloat16
VMEM_LIMIT = 32 * 1024 * 1024


def call(body, **options):
    return pl.pallas_call(
        body,
        compiler_params=pltpu.CompilerParams(vmem_limit_bytes=VMEM_LIMIT),
        cost_estimate=pl.CostEstimate(flops=1, bytes_accessed=1, transcendentals=0),
        **options,
    )


def whole_vmem(count):
    return [pl.BlockSpec(memory_space=pltpu.VMEM)] * count


def shape_of(depth, across, along, dtype):
    return jax.ShapeDtypeStruct((depth, across, along, LANES), dtype)


def turned(field, scratch):
    rows, along = field.shape
    scratch[:rows, :along] = field
    return jnp.transpose(scratch[...])


def lane(values, n):
    return jnp.broadcast_to(values[:, n : n + 1], (values.shape[0], LANES))


def store_edges(x, span, news, even, even_ref, odd_ref):
    for j in range(RADIUS):
        low = news[j].astype(BF16)
        high = news[len(news) - RADIUS + j].astype(BF16)
        even_ref[j, x, span] = jnp.where(even, high, low)
        odd_ref[j, x, span] = jnp.where(even, low, high)


def store_beside(span, rows, core, u_ref, edge_ref):
    depth, across, _, _ = u_ref.shape
    first = (across - RADIUS) * (1 - core)
    for z in range(depth):
        for j in range(RADIUS):
            edge_ref[z, j, span] = u_ref[z, first + j, rows].astype(BF16)


def slab_is_even():
    return lax.rem(lax.axis_index("slab"), 2) == 0


def clear_pads(u_ref):
    depth, across, padded, _ = u_ref.shape

    def plane(z, _):
        blank = jnp.zeros((across, EDGE, LANES), F32)
        u_ref[z, :, pl.ds(0, EDGE)] = blank
        u_ref[z, :, pl.ds(padded - EDGE, EDGE)] = blank
        return 0

    lax.fori_loop(0, depth, plane, 0)


def tiles(along, body):
    def one(t, _):
        body(pl.multiple_of(t * TILE, TILE))
        return 0

    lax.fori_loop(0, along // TILE, one, 0)


def first_body(chunk, p_ref, s_ref, u_ref, odd_ref, even_ref, edge_ref, square, turned_s):
    depth, across, padded, _ = u_ref.shape
    along = padded - 2 * EDGE
    core = lax.axis_index("sub")
    even = slab_is_even()
    turned_s[...] = turned(s_ref[0], square)
    clear_pads(u_ref)

    def tile(start):
        span = pl.ds(start, TILE)
        rows = pl.ds(start + EDGE, TILE)
        source = turned_s[span]
        for x in range(across):
            news = []
            for z in range(depth):
                p = p_ref[z, x, span, chunk * LANES : (chunk + 1) * LANES].astype(F32)
                new = lane(source, z * across + x) * p
                u_ref[z, x, rows] = new
                news.append(new)
            store_edges(x, span, news, even, even_ref, odd_ref)
        store_beside(span, rows, core, u_ref, edge_ref)

    tiles(along, tile)


def square_scratch():
    return [pltpu.VMEM((LANES, LANES), F32)] * 2


def first_field(probes, chunk, source):
    depth, across, along, _ = probes.shape
    return call(
        functools.partial(first_body, chunk),
        in_specs=whole_vmem(2),
        out_specs=whole_vmem(4),
        out_shape=[
            shape_of(depth, across, along + 2 * EDGE, F32),
            shape_of(RADIUS, across, along, BF16),
            shape_of(RADIUS, across, along, BF16),
            shape_of(depth, RADIUS, along, BF16),
        ],
        scratch_shapes=square_scratch(),
    )(probes, source)


def local_body(chunk, moment, has_previous, *refs):
    refs = list(refs)
    u_ref, beside_ref, p_ref, c_ref, s_ref = refs[:5]
    prev_ref = refs[5] if has_previous else None
    base_ref, square, turned_c, turned_s = refs[-4:]
    depth, across, along, _ = base_ref.shape
    core = lax.axis_index("sub")
    left_on = (core == 1).astype(F32)
    right_on = (core == 0).astype(F32)
    turned_c[...] = turned(c_ref[...], square)
    turned_s[...] = turned(s_ref[moment], square)

    def tile(start):
        span = pl.ds(start, TILE)
        rows = start + EDGE
        courant = turned_c[span]
        source = turned_s[span]
        for z in range(depth):
            beside = [beside_ref[z, j, span].astype(F32) for j in range(RADIUS)]
            row = [v * left_on for v in beside]
            row += [u_ref[z, x, pl.ds(rows, TILE)] for x in range(across)]
            row += [v * right_on for v in beside]
            for x in range(across):
                here = row[RADIUS + x]
                total = (3.0 * COEFFICIENTS[0]) * here
                for r in range(1, RADIUS + 1):
                    near = row[RADIUS + x + r] + row[RADIUS + x - r]
                    near = near + (
                        u_ref[z, x, pl.ds(rows + r, TILE)] + u_ref[z, x, pl.ds(rows - r, TILE)]
                    )
                    if z + r < depth:
                        near = near + u_ref[z + r, x, pl.ds(rows, TILE)]
                    if z - r >= 0:
                        near = near + u_ref[z - r, x, pl.ds(rows, TILE)]
                    total = total + COEFFICIENTS[r] * near
                cell = z * across + x
                p = p_ref[z, x, span, chunk * LANES : (chunk + 1) * LANES].astype(F32)
                new = 2.0 * here
                if has_previous:
                    new = new - prev_ref[z, x, pl.ds(rows, TILE)]
                new = new + lane(courant, cell) * total + lane(source, cell) * p
                base_ref[z, x, span] = new

    tiles(along, tile)


def local_step(u, beside, probes, chunk, courant, source, moment, previous):
    depth, across, along, _ = probes.shape
    operands = [u, beside, probes, courant, source]
    if previous is not None:
        operands.append(previous)
    return call(
        functools.partial(local_body, chunk, moment, previous is not None),
        in_specs=whole_vmem(len(operands)),
        out_specs=whole_vmem(1)[0],
        out_shape=shape_of(depth, across, along, F32),
        scratch_shapes=square_scratch() + square_scratch()[:1],
    )(*operands)


def part_body(sent, begin, base_ref, odd_ref, even_ref, c_ref, out_ref, square, turned_c):
    depth, across, along, _ = base_ref.shape
    even = slab_is_even()
    turned_c[...] = turned(c_ref[...], square)

    def planes(low):
        def tile(start):
            span = pl.ds(start, TILE)
            courant = turned_c[span]
            for x in range(across):
                near = []
                for j in range(RADIUS):
                    one, two = even_ref[j, x, span], odd_ref[j, x, span]
                    pair = (two, one) if low else (one, two)
                    near.append(jnp.where(even, *pair).astype(F32))
                for m in range(begin, begin + out_ref.shape[0]):
                    z = m if low else depth - RADIUS + m
                    added = None
                    for r in range(1, RADIUS + 1):
                        at = RADIUS + m - r if low else m + r - RADIUS
                        if 0 <= at < RADIUS:
                            term = COEFFICIENTS[r] * near[at]
                            added = term if added is None else added + term
                    new = base_ref[z, x, span] + lane(courant, z * across + x) * added
                    out_ref[m - begin, x, span] = new.astype(BF16)

        tiles(along, tile)

    low = lax.axis_index("probe") == (1 if sent else 0)
    pl.when(low)(lambda: planes(True))
    pl.when(jnp.logical_not(low))(lambda: planes(False))


def part_step(base, odds, evens, courant, sent, begin=0, count=RADIUS):
    _, across, along, _ = base.shape
    return call(
        functools.partial(part_body, sent, begin),
        in_specs=whole_vmem(4),
        out_specs=whole_vmem(1)[0],
        out_shape=shape_of(count, across, along, BF16),
        scratch_shapes=square_scratch(),
    )(base, odds, evens, courant)


def rim_body(kind, *refs):
    base_ref, odd_ref, even_ref, c_ref = refs[:4]
    outs, (square, turned_c) = refs[4:-2], refs[-2:]
    depth, across, along, _ = base_ref.shape
    core = lax.axis_index("sub")
    even = slab_is_even()
    lower = lax.axis_index("probe") == 0
    turned_c[...] = turned(c_ref[...], square)
    if kind == "middle":
        clear_pads(outs[0])

    def tile(start):
        span = pl.ds(start, TILE)
        rows = pl.ds(start + EDGE, TILE)
        courant = turned_c[span]
        for x in range(across):
            below, above = [], []
            for j in range(RADIUS):
                one, two = even_ref[j, x, span], odd_ref[j, x, span]
                below.append(jnp.where(even, two, one).astype(F32))
                above.append(jnp.where(even, one, two).astype(F32))
            news = []
            for z in range(depth):
                added = None
                for r in range(1, RADIUS + 1):
                    if z - r < 0:
                        term = COEFFICIENTS[r] * below[RADIUS + z - r]
                        added = term if added is None else added + term
                    if z + r >= depth:
                        term = COEFFICIENTS[r] * above[z + r - depth]
                        added = term if added is None else added + term
                new = base_ref[z, x, span]
                if added is not None:
                    new = new + lane(courant, z * across + x) * added
                news.append(new)
            if kind == "middle":
                for z, new in enumerate(news):
                    outs[0][z, x, rows] = new
                store_edges(x, span, news, even, outs[2], outs[1])
            elif kind == "half":
                for z in range(depth // 2):
                    one, two = news[z].astype(BF16), news[z + depth // 2].astype(BF16)
                    outs[0][z, x, span] = jnp.where(lower, one, two)
                    outs[1][z, x, span] = jnp.where(lower, two, one)
            else:
                for z, new in enumerate(news):
                    outs[0][z, x, span] = new.astype(BF16)
        if kind == "middle":
            store_beside(span, rows, core, outs[0], outs[3])

    tiles(along, tile)


def rim_step(base, odds, evens, courant, kind):
    depth, across, along, _ = base.shape
    if kind == "middle":
        out_shape = [
            shape_of(depth, across, along + 2 * EDGE, F32),
            shape_of(RADIUS, across, along, BF16),
            shape_of(RADIUS, across, along, BF16),
            shape_of(depth, RADIUS, along, BF16),
        ]
    elif kind == "half":
        out_shape = [shape_of(depth // 2, across, along, BF16)] * 2
    else:
        out_shape = [shape_of(depth, across, along, BF16)]
    return call(
        functools.partial(rim_body, kind),
        in_specs=whole_vmem(4),
        out_specs=whole_vmem(len(out_shape)),
        out_shape=out_shape,
        scratch_shapes=square_scratch(),
    )(base, odds, evens, courant)


def swap(x, axis, pairs):
    return lax.ppermute(x, axis, [p for a, b in pairs for p in ((a, b), (b, a))])


def even_swap(x):
    return swap(x, "slab", [(i, i + 1) for i in range(0, lax.axis_size("slab") - 1, 2)])


def odd_swap(x):
    return swap(x, "slab", [(i, i + 1) for i in range(1, lax.axis_size("slab") - 1, 2)])


def core_swap(x):
    return swap(x, "sub", [(0, 1)])


def chip_swap(x):
    return swap(x, "probe", [(0, 1)])


def product(a, b):
    return lax.dot_general(a, b, (((0,), (0,)), ((), ())), preferred_element_type=F32)


def block_of(array, i, j):
    return array[i * LANES : (i + 1) * LANES, j * LANES : (j + 1) * LANES]


def eye():
    rows = lax.broadcasted_iota(jnp.int32, (LANES, LANES), 0)
    cols = lax.broadcasted_iota(jnp.int32, (LANES, LANES), 1)
    return rows == cols


def lay(panel, columns, refs):
    row = 0
    for ref in refs:
        cells = math.prod(ref.shape[:3])
        panel[row : row + cells, columns] = ref[...].reshape(cells, LANES)
        row += cells


def flat(groups):
    return [field for group in groups for field in group]


def regroup(sizes, refs):
    groups, refs = [], list(refs)
    for size in sizes:
        groups.append(refs[:size])
        refs = refs[size:]
    return groups, refs


def inner_body(sizes, *refs):
    groups, (keep_ref, send_ref, panel) = regroup(sizes, refs)
    for n, group in enumerate(groups):
        lay(panel, slice(n * LANES, (n + 1) * LANES), group)
    core = lax.axis_index("sub")
    whole = product(panel[...], panel[...])
    first, second = whole[:, :LANES], whole[:, LANES:]
    size = 2 * LANES
    keep_ref[:size] = jnp.where(core == 0, first, second)
    send_ref[:size] = jnp.where(core == 0, second, first)
    diag = [
        jnp.sum(jnp.where(eye(), block_of(whole, n, n), 0.0), axis=0, keepdims=True)
        for n in range(2)
    ]
    none = jnp.zeros_like(diag[0])
    chip = lax.axis_index("probe")
    rows = [jnp.where(chip == n // 2, diag[n % 2], none) for n in range(4)]
    tail = jnp.concatenate(rows + [none] * 4, axis=0)
    keep_ref[size:] = tail
    send_ref[size:] = tail


def inner_gram(groups):
    size = 2 * LANES
    cells = sum(math.prod(field.shape[:3]) for field in groups[0])
    half = jax.ShapeDtypeStruct((size + 8, LANES), F32)
    return call(
        functools.partial(inner_body, [len(group) for group in groups]),
        in_specs=whole_vmem(len(flat(groups))),
        out_specs=whole_vmem(2),
        out_shape=[half, half],
        scratch_shapes=[pltpu.VMEM((cells, size), BF16)],
    )(*flat(groups))


def inner_sum_body(keep_ref, got_ref, tail_ref, own_ref, sent_ref):
    size = 2 * LANES
    row = pl.multiple_of(lax.rem(lax.axis_index("slab"), 2) * LANES, LANES)
    own, other = pl.ds(row, LANES), pl.ds(LANES - row, LANES)
    own_ref[...] = keep_ref[own] + got_ref[own]
    sent_ref[...] = (keep_ref[other] + got_ref[other]).astype(BF16)
    tail_ref[...] = keep_ref[size:] + got_ref[size:]


def inner_sum(keep, got):
    return call(
        inner_sum_body,
        in_specs=whole_vmem(2),
        out_specs=whole_vmem(3),
        out_shape=[
            jax.ShapeDtypeStruct((8, LANES), F32),
            jax.ShapeDtypeStruct((LANES, LANES), F32),
            jax.ShapeDtypeStruct((LANES, LANES), BF16),
        ],
    )(keep, got)


def pair_blocks(got_refs, panel, chip):
    got = [ref[...].reshape(-1, LANES) for ref in got_refs]
    both = product(got[0] if len(got) == 1 else jnp.concatenate(got, axis=0), panel[...])
    blocks = [both[:, n * LANES : (n + 1) * LANES] for n in range(2)]
    return [jnp.where(chip == 0, block.T, block) for block in blocks]


def first_cross_body(sizes, *refs):
    (got, *kept), (panel, out_ref) = regroup(sizes, refs)
    chip = lax.axis_index("probe")
    for n, group in enumerate(kept):
        lay(panel, slice(n * LANES, (n + 1) * LANES), group)
    one, two = pair_blocks(got, panel, chip)
    out_ref[:LANES] = one
    out_ref[LANES:] = two


def first_cross(got, kept):
    groups = [got] + kept
    cells = sum(math.prod(field.shape[:3]) for field in got)
    return call(
        functools.partial(first_cross_body, [len(group) for group in groups]),
        in_specs=whole_vmem(len(flat(groups))),
        out_specs=whole_vmem(2),
        out_shape=[
            jax.ShapeDtypeStruct((cells, 2 * LANES), BF16),
            jax.ShapeDtypeStruct((2 * LANES, LANES), F32),
        ],
    )(*flat(groups))


def cross_body(count, *refs):
    got, (panel, first_ref, _, keep_ref, send_ref) = refs[:count], refs[count:]
    chip = lax.axis_index("probe")
    core = lax.axis_index("sub")
    zero, one = pair_blocks(got, panel, chip)
    mixed = first_ref[:LANES]
    corner = first_ref[LANES:]
    upper = jnp.where(chip == 0, mixed, one)
    lower = jnp.where(chip == 0, one, mixed)
    for ref, which in ((keep_ref, core), (send_ref, 1 - core)):
        here = which == 0
        ref[:LANES] = jnp.where(here, zero, upper)
        ref[LANES : 2 * LANES] = jnp.where(here, lower, corner)
        ref[2 * LANES :] = jnp.where(here, upper, lower)


def cross_gram(got, panel, first, after):
    three = jax.ShapeDtypeStruct((3 * LANES, LANES), F32)
    return call(
        functools.partial(cross_body, len(got)),
        in_specs=whole_vmem(len(got) + 2) + [pl.BlockSpec(memory_space=pl.ANY)],
        out_specs=whole_vmem(2),
        out_shape=[three, three],
    )(*got, panel, first, after)


def rounded(ref, block, tail):
    count = block.shape[0]
    high = tail.astype(BF16)
    low = tail - high.astype(F32)
    ref[:count] = block.astype(BF16)
    ref[count : count + 16] = jnp.concatenate([high.astype(F32), low], axis=0).astype(BF16)


def opened(ref, count):
    tail = ref[count : count + 16].astype(F32)
    return ref[:count].astype(F32), tail[:8] + tail[8:]


def cross_rows_body(keep_ref, got_ref, tail_ref, inner_ref, inner_got_ref, own_ref, *outs):
    slab = lax.axis_index("slab")
    core = lax.axis_index("sub")
    tail = tail_ref[...]
    inner = inner_ref[...] + inner_got_ref[...].astype(F32)
    for d in range(len(outs) + 1):
        owner = slab ^ d
        late = jnp.where(core == 0, jnp.where(owner == 2, 0, 2), jnp.where(owner == 2, 2, 1))
        at = jnp.where(owner < 2, owner, late)
        span = pl.ds(pl.multiple_of(at * LANES, LANES), LANES)
        block = keep_ref[span] + got_ref[span]
        if d == 0:
            own_ref[:LANES] = block
            own_ref[LANES : LANES + 8] = tail
            own_ref[LANES + 8 :] = inner
        else:
            rounded(outs[d - 1], block, tail)
            if d == 2:
                outs[1][LANES + 16 :] = inner.astype(BF16)


def cross_rows(keep, got, tail, inner, inner_got, slabs):
    own = jax.ShapeDtypeStruct((2 * LANES + 8, LANES), F32)
    long = jax.ShapeDtypeStruct((2 * LANES + 16, LANES), BF16)
    short = jax.ShapeDtypeStruct((LANES + 16, LANES), BF16)
    return call(
        cross_rows_body,
        in_specs=whole_vmem(5),
        out_specs=whole_vmem(slabs),
        out_shape=[own, short, long, short],
    )(keep, got, tail, inner, inner_got)


def sum_body(own_ref, *refs):
    block, tail = own_ref[:LANES], own_ref[LANES : LANES + 8]
    *others, out_ref = refs
    for ref in others:
        more, more_tail = opened(ref, LANES)
        block, tail = block + more, tail + more_tail
    inner = own_ref[LANES + 8 :] + others[0][LANES + 16 :].astype(F32)
    rounded(out_ref, block, tail)
    out_ref[LANES + 16 :] = inner.astype(BF16)


def sum_all(own, others):
    return call(
        sum_body,
        in_specs=whole_vmem(1 + len(others)),
        out_specs=whole_vmem(1)[0],
        out_shape=jax.ShapeDtypeStruct(others[0].shape, BF16),
    )(own, *others)


def normalise_body(cell_count, mine_ref, other_ref, out_ref, norms_ref):
    slab = lax.axis_index("slab")
    core = lax.axis_index("sub")
    chip = lax.axis_index("probe")
    one, one_tail = opened(mine_ref, LANES)
    two, two_tail = opened(other_ref, LANES)
    cross = one + two
    inner_span = pl.ds(LANES + 16, LANES)
    inner = jnp.where(slab // 2 == chip, mine_ref[inner_span], other_ref[inner_span]).astype(F32)
    upper = slab < 2
    values = [jnp.where(upper, inner, cross.T), jnp.where(upper, cross, inner)]
    norms = jnp.sqrt((one_tail + two_tail) / cell_count + EPSILON)
    blocks = [norms[n : n + 1] for n in range(4)]
    own = blocks[0]
    for n in range(1, 4):
        own = jnp.where(slab == n, blocks[n], own)
    norms_ref[...] = own
    own_column = jnp.sum(
        jnp.where(eye(), jnp.broadcast_to(own, (LANES, LANES)), 0.0), axis=1, keepdims=True
    )
    for side in range(2):
        others = jnp.where(core == 0, blocks[2 * side], blocks[2 * side + 1])
        value = values[side] / math.sqrt(cell_count) / (own_column * others)
        value = jnp.where(eye() & (2 * side + core == slab), 0.0, value)
        out_ref[:, side * LANES : (side + 1) * LANES] = value


def normalise(mine, other, cell_count):
    return call(
        functools.partial(normalise_body, cell_count),
        in_specs=whole_vmem(2),
        out_specs=whole_vmem(2),
        out_shape=[
            jax.ShapeDtypeStruct((LANES, 2 * LANES), F32),
            jax.ShapeDtypeStruct((1, LANES), F32),
        ],
    )(mine, other)


def assemble_body(near_ref, far_ref, out_ref):
    core = lax.axis_index("sub")
    for side in range(2):
        columns = slice(side * LANES, (side + 1) * LANES)
        for ref, which in ((near_ref, core), (far_ref, 1 - core)):
            start = pl.multiple_of((2 * side + which) * LANES, LANES)
            out_ref[:, pl.ds(start, LANES)] = ref[:, columns]


def assemble(near, far):
    return call(
        assemble_body,
        in_specs=whole_vmem(2),
        out_specs=whole_vmem(1)[0],
        out_shape=jax.ShapeDtypeStruct((near.shape[0], 4 * LANES), F32),
    )(near, far)


def coupled(finals, cell_count):
    slabs = 4
    keep, send = inner_gram([kept + sent for kept, sent, _ in finals])
    tail, inner, sent = inner_sum(keep, core_swap(send))
    inner_got = lax.ppermute(sent, "slab", [(i, i ^ 1) for i in range(slabs)])
    panel, first = first_cross(finals[1][2], [kept for kept, _, _ in finals])
    keep, send = cross_gram(finals[0][2], panel, first, inner_got)
    mine, *blocks = cross_rows(keep, core_swap(send), tail, inner, inner_got, slabs)
    arrived = [
        lax.ppermute(blocks[d - 1], "slab", [(i, i ^ d) for i in range(slabs)])
        for d in (2, 3, 1)
    ]
    total = sum_all(mine, arrived)
    near, norms = normalise(total, chip_swap(total), cell_count)
    return assemble(near, core_swap(near)), norms.reshape(-1)


def coupled_general(fields, cell_count):
    chips = lax.axis_size("probe")
    sketch = jnp.concatenate(fields, axis=-1)
    sketch = sketch.reshape(-1, sketch.shape[-1])
    if chips > 1:
        sketch = lax.all_to_all(sketch, "probe", split_axis=0, concat_axis=1, tiled=True)
    partial_gram = lax.dot_general(
        sketch, sketch, (((0,), (0,)), ((), ())), preferred_element_type=F32
    )
    rows = lax.psum_scatter(partial_gram, "slab", scatter_dimension=0, tiled=True)
    rows = lax.psum(rows, ("probe", "sub"))
    count = rows.shape[0]
    start = lax.axis_index("slab") * count
    own = jnp.diagonal(lax.dynamic_slice_in_dim(rows, start, count, 1))
    own_norms = jnp.sqrt(own / cell_count + EPSILON)
    norms = lax.all_gather(own_norms, "slab", axis=0, tiled=True)
    coupling = rows / math.sqrt(cell_count) / (own_norms[:, None] * norms[None, :])
    row_ids = start + lax.broadcasted_iota(jnp.int32, coupling.shape, 0)
    col_ids = lax.broadcasted_iota(jnp.int32, coupling.shape, 1)
    return jnp.where(row_ids == col_ids, 0.0, coupling), own_norms


def shards(probes, courant, source):
    depth, across, along, count = probes.shape
    chunks = count // LANES
    slabs, chips = lax.axis_size("slab"), lax.axis_size("probe")
    cell_count = depth * across * along * slabs * lax.axis_size("sub")
    paired = chips == 2 and slabs == 4 and chunks == 2 and depth == 2 * RADIUS
    steps = source.shape[0]
    courant = courant.reshape(depth * across, along)
    source = source.reshape(steps, depth * across, along)

    exchange = lambda odd, even, edge: (odd_swap(odd), even_swap(even), core_swap(edge))
    now, previous, halos = [], [None] * chunks, []
    for c in range(chunks):
        u, *edges = first_field(probes, c, source[:1])
        now.append(u)
        halos.append(exchange(*edges))
    finals = []
    for n in range(1, steps):
        for c in range(chunks):
            odd, even, beside = halos[c]
            base = local_step(now[c], beside, probes, c, courant, source, n, previous[c])
            if n < steps - 1:
                u, *edges = rim_step(base, odd, even, courant, "middle")
                previous[c], now[c] = now[c], u
                halos[c] = exchange(*edges)
            elif paired:
                if c > 0:
                    kept, *sent = rim_step(base, odd, even, courant, "half")
                else:
                    sent = [
                        part_step(base, odd, even, courant, True, begin, RADIUS // 2)
                        for begin in (0, RADIUS // 2)
                    ]
                    kept = part_step(base, odd, even, courant, False)
                finals.append(([kept], sent, [chip_swap(a) for a in sent]))
            else:
                finals += rim_step(base, odd, even, courant, "all")
    return (coupled if paired else coupled_general)(finals, cell_count)


def solution(mesh):
    placed = (
        P(("groups", "slab"), "sub", None, "probe"),
        P("slab", "sub", None),
        P(None, ("groups", "slab"), "sub", None),
    )
    return jax.shard_map(
        shards,
        mesh=mesh,
        in_specs=placed,
        out_specs=(P(("groups", "slab"), None), P(("groups", "slab"))),
        check_vma=False,
    )
```

```python
import functools
import math

import jax
import jax.numpy as jnp
from jax import lax
from jax.experimental import pallas as pl
from jax.experimental.pallas import tpu as pltpu
from jax.sharding import PartitionSpec as P

COEFFICIENTS = (-205.0 / 72.0, 8.0 / 5.0, -1.0 / 5.0, 8.0 / 315.0, -1.0 / 560.0)
EPSILON = 1e-06
LANES = 128
RADIUS = 4
EDGE = 8
TILE = 16
F32 = jnp.float32
BF16 = jnp.bfloat16
VMEM_LIMIT = 32 * 1024 * 1024


def call(body, **options):
    return pl.pallas_call(
        body,
        compiler_params=pltpu.CompilerParams(vmem_limit_bytes=VMEM_LIMIT),
        cost_estimate=pl.CostEstimate(flops=1, bytes_accessed=1, transcendentals=0),
        **options,
    )


def whole_vmem(count):
    return [pl.BlockSpec(memory_space=pltpu.VMEM)] * count


def shape_of(depth, across, along, dtype):
    return jax.ShapeDtypeStruct((depth, across, along, LANES), dtype)


def turned(field, scratch):
    rows, along = field.shape
    scratch[:rows, :along] = field
    return jnp.transpose(scratch[...])


def lane(values, n):
    return jnp.broadcast_to(values[:, n : n + 1], (values.shape[0], LANES))


def store_edges(x, span, news, even, even_ref, odd_ref):
    for j in range(RADIUS):
        low = news[j].astype(BF16)
        high = news[len(news) - RADIUS + j].astype(BF16)
        even_ref[j, x, span] = jnp.where(even, high, low)
        odd_ref[j, x, span] = jnp.where(even, low, high)


def store_beside(span, rows, core, u_ref, edge_ref):
    depth, across, _, _ = u_ref.shape
    first = (across - RADIUS) * (1 - core)
    for z in range(depth):
        for j in range(RADIUS):
            edge_ref[z, j, span] = u_ref[z, first + j, rows].astype(BF16)


def slab_is_even():
    return lax.rem(lax.axis_index("slab"), 2) == 0


def clear_pads(u_ref):
    depth, across, padded, _ = u_ref.shape

    def plane(z, _):
        blank = jnp.zeros((across, EDGE, LANES), F32)
        u_ref[z, :, pl.ds(0, EDGE)] = blank
        u_ref[z, :, pl.ds(padded - EDGE, EDGE)] = blank
        return 0

    lax.fori_loop(0, depth, plane, 0)


def tiles(along, body):
    def one(t, _):
        body(pl.multiple_of(t * TILE, TILE))
        return 0

    lax.fori_loop(0, along // TILE, one, 0)


def first_body(chunk, p_ref, s_ref, u_ref, odd_ref, even_ref, edge_ref, square, turned_s):
    depth, across, padded, _ = u_ref.shape
    along = padded - 2 * EDGE
    core = lax.axis_index("sub")
    even = slab_is_even()
    turned_s[...] = turned(s_ref[0], square)
    clear_pads(u_ref)

    def tile(start):
        span = pl.ds(start, TILE)
        rows = pl.ds(start + EDGE, TILE)
        source = turned_s[span]
        for x in range(across):
            news = []
            for z in range(depth):
                p = p_ref[z, x, span, chunk * LANES : (chunk + 1) * LANES].astype(F32)
                new = lane(source, z * across + x) * p
                u_ref[z, x, rows] = new
                news.append(new)
            store_edges(x, span, news, even, even_ref, odd_ref)
        store_beside(span, rows, core, u_ref, edge_ref)

    tiles(along, tile)


def square_scratch():
    return [pltpu.VMEM((LANES, LANES), F32)] * 2


def first_field(probes, chunk, source):
    depth, across, along, _ = probes.shape
    return call(
        functools.partial(first_body, chunk),
        in_specs=whole_vmem(2),
        out_specs=whole_vmem(4),
        out_shape=[
            shape_of(depth, across, along + 2 * EDGE, F32),
            shape_of(RADIUS, across, along, BF16),
            shape_of(RADIUS, across, along, BF16),
            shape_of(depth, RADIUS, along, BF16),
        ],
        scratch_shapes=square_scratch(),
    )(probes, source)


def turn_body(c_ref, s_ref, _, c_out, s_out, square):
    c_out[...] = turned(c_ref[...], square)
    for n in range(s_ref.shape[0]):
        s_out[n] = turned(s_ref[n], square)


def turn(courant, source, after):
    return call(
        turn_body,
        in_specs=whole_vmem(2) + [pl.BlockSpec(memory_space=pl.ANY)],
        out_specs=whole_vmem(2),
        out_shape=[
            jax.ShapeDtypeStruct((LANES, LANES), F32),
            jax.ShapeDtypeStruct((source.shape[0], LANES, LANES), F32),
        ],
        scratch_shapes=square_scratch()[:1],
    )(courant, source, after)


def local_body(chunk, moment, has_previous, *refs):
    refs = list(refs)
    u_ref, beside_ref, p_ref, c_ref, s_ref = refs[:5]
    prev_ref = refs[5] if has_previous else None
    base_ref = refs[-1]
    depth, across, along, _ = base_ref.shape
    core = lax.axis_index("sub")
    left_on = (core == 1).astype(F32)
    right_on = (core == 0).astype(F32)

    def tile(start):
        span = pl.ds(start, TILE)
        rows = start + EDGE
        courant = c_ref[span]
        source = s_ref[moment, span]
        for z in range(depth):
            beside = [beside_ref[z, j, span].astype(F32) for j in range(RADIUS)]
            row = [v * left_on for v in beside]
            row += [u_ref[z, x, pl.ds(rows, TILE)] for x in range(across)]
            row += [v * right_on for v in beside]
            for x in range(across):
                here = row[RADIUS + x]
                total = (3.0 * COEFFICIENTS[0]) * here
                for r in range(1, RADIUS + 1):
                    near = row[RADIUS + x + r] + row[RADIUS + x - r]
                    near = near + (
                        u_ref[z, x, pl.ds(rows + r, TILE)] + u_ref[z, x, pl.ds(rows - r, TILE)]
                    )
                    if z + r < depth:
                        near = near + u_ref[z + r, x, pl.ds(rows, TILE)]
                    if z - r >= 0:
                        near = near + u_ref[z - r, x, pl.ds(rows, TILE)]
                    total = total + COEFFICIENTS[r] * near
                cell = z * across + x
                p = p_ref[z, x, span, chunk * LANES : (chunk + 1) * LANES].astype(F32)
                new = 2.0 * here
                if has_previous:
                    new = new - prev_ref[z, x, pl.ds(rows, TILE)]
                new = new + lane(courant, cell) * total + lane(source, cell) * p
                base_ref[z, x, span] = new

    tiles(along, tile)


def local_step(u, beside, probes, chunk, courant, source, moment, previous):
    depth, across, along, _ = probes.shape
    operands = [u, beside, probes, courant, source]
    if previous is not None:
        operands.append(previous)
    return call(
        functools.partial(local_body, chunk, moment, previous is not None),
        in_specs=whole_vmem(len(operands)),
        out_specs=whole_vmem(1)[0],
        out_shape=shape_of(depth, across, along, F32),
    )(*operands)


def part_body(sent, begin, base_ref, odd_ref, even_ref, c_ref, out_ref):
    depth, across, along, _ = base_ref.shape
    even = slab_is_even()

    def planes(low):
        def tile(start):
            span = pl.ds(start, TILE)
            courant = c_ref[span]
            for x in range(across):
                near = []
                for j in range(RADIUS):
                    one, two = even_ref[j, x, span], odd_ref[j, x, span]
                    pair = (two, one) if low else (one, two)
                    near.append(jnp.where(even, *pair).astype(F32))
                for m in range(begin, begin + out_ref.shape[0]):
                    z = m if low else depth - RADIUS + m
                    added = None
                    for r in range(1, RADIUS + 1):
                        at = RADIUS + m - r if low else m + r - RADIUS
                        if 0 <= at < RADIUS:
                            term = COEFFICIENTS[r] * near[at]
                            added = term if added is None else added + term
                    new = base_ref[z, x, span] + lane(courant, z * across + x) * added
                    out_ref[m - begin, x, span] = new.astype(BF16)

        tiles(along, tile)

    low = lax.axis_index("probe") == (1 if sent else 0)
    pl.when(low)(lambda: planes(True))
    pl.when(jnp.logical_not(low))(lambda: planes(False))


def part_step(base, odds, evens, courant, sent, begin=0, count=RADIUS):
    _, across, along, _ = base.shape
    return call(
        functools.partial(part_body, sent, begin),
        in_specs=whole_vmem(4),
        out_specs=whole_vmem(1)[0],
        out_shape=shape_of(count, across, along, BF16),
    )(base, odds, evens, courant)


def rim_body(kind, *refs):
    base_ref, odd_ref, even_ref, c_ref = refs[:4]
    outs = refs[4:]
    depth, across, along, _ = base_ref.shape
    core = lax.axis_index("sub")
    even = slab_is_even()
    lower = lax.axis_index("probe") == 0
    if kind == "middle":
        clear_pads(outs[0])

    def tile(start):
        span = pl.ds(start, TILE)
        rows = pl.ds(start + EDGE, TILE)
        courant = c_ref[span]
        for x in range(across):
            below, above = [], []
            for j in range(RADIUS):
                one, two = even_ref[j, x, span], odd_ref[j, x, span]
                below.append(jnp.where(even, two, one).astype(F32))
                above.append(jnp.where(even, one, two).astype(F32))
            news = []
            for z in range(depth):
                added = None
                for r in range(1, RADIUS + 1):
                    if z - r < 0:
                        term = COEFFICIENTS[r] * below[RADIUS + z - r]
                        added = term if added is None else added + term
                    if z + r >= depth:
                        term = COEFFICIENTS[r] * above[z + r - depth]
                        added = term if added is None else added + term
                new = base_ref[z, x, span]
                if added is not None:
                    new = new + lane(courant, z * across + x) * added
                news.append(new)
            if kind == "middle":
                for z, new in enumerate(news):
                    outs[0][z, x, rows] = new
                store_edges(x, span, news, even, outs[2], outs[1])
            elif kind == "half":
                for z in range(depth // 2):
                    one, two = news[z].astype(BF16), news[z + depth // 2].astype(BF16)
                    outs[0][z, x, span] = jnp.where(lower, one, two)
                    outs[1][z, x, span] = jnp.where(lower, two, one)
            else:
                for z, new in enumerate(news):
                    outs[0][z, x, span] = new.astype(BF16)
        if kind == "middle":
            store_beside(span, rows, core, outs[0], outs[3])

    tiles(along, tile)


def rim_step(base, odds, evens, courant, kind):
    depth, across, along, _ = base.shape
    if kind == "middle":
        out_shape = [
            shape_of(depth, across, along + 2 * EDGE, F32),
            shape_of(RADIUS, across, along, BF16),
            shape_of(RADIUS, across, along, BF16),
            shape_of(depth, RADIUS, along, BF16),
        ]
    elif kind == "half":
        out_shape = [shape_of(depth // 2, across, along, BF16)] * 2
    else:
        out_shape = [shape_of(depth, across, along, BF16)]
    return call(
        functools.partial(rim_body, kind),
        in_specs=whole_vmem(4),
        out_specs=whole_vmem(len(out_shape)),
        out_shape=out_shape,
    )(base, odds, evens, courant)


def swap(x, axis, pairs):
    return lax.ppermute(x, axis, [p for a, b in pairs for p in ((a, b), (b, a))])


def even_swap(x):
    return swap(x, "slab", [(i, i + 1) for i in range(0, lax.axis_size("slab") - 1, 2)])


def odd_swap(x):
    return swap(x, "slab", [(i, i + 1) for i in range(1, lax.axis_size("slab") - 1, 2)])


def core_swap(x):
    return swap(x, "sub", [(0, 1)])


def chip_swap(x):
    return swap(x, "probe", [(0, 1)])


def product(a, b):
    return lax.dot_general(a, b, (((0,), (0,)), ((), ())), preferred_element_type=F32)


def block_of(array, i, j):
    return array[i * LANES : (i + 1) * LANES, j * LANES : (j + 1) * LANES]


def eye():
    rows = lax.broadcasted_iota(jnp.int32, (LANES, LANES), 0)
    cols = lax.broadcasted_iota(jnp.int32, (LANES, LANES), 1)
    return rows == cols


def lay(panel, columns, refs):
    row = 0
    for ref in refs:
        cells = math.prod(ref.shape[:3])
        panel[row : row + cells, columns] = ref[...].reshape(cells, LANES)
        row += cells


def flat(groups):
    return [field for group in groups for field in group]


def regroup(sizes, refs):
    groups, refs = [], list(refs)
    for size in sizes:
        groups.append(refs[:size])
        refs = refs[size:]
    return groups, refs


def inner_body(sizes, *refs):
    groups, (keep_ref, send_ref, panel) = regroup(sizes, refs)
    for n, group in enumerate(groups):
        lay(panel, slice(n * LANES, (n + 1) * LANES), group)
    core = lax.axis_index("sub")
    whole = product(panel[...], panel[...])
    first, second = whole[:, :LANES], whole[:, LANES:]
    size = 2 * LANES
    keep_ref[:size] = jnp.where(core == 0, first, second)
    send_ref[:size] = jnp.where(core == 0, second, first)
    diag = [
        jnp.sum(jnp.where(eye(), block_of(whole, n, n), 0.0), axis=0, keepdims=True)
        for n in range(2)
    ]
    none = jnp.zeros_like(diag[0])
    chip = lax.axis_index("probe")
    rows = [jnp.where(chip == n // 2, diag[n % 2], none) for n in range(4)]
    tail = jnp.concatenate(rows + [none] * 4, axis=0)
    keep_ref[size:] = tail
    send_ref[size:] = tail


def inner_gram(groups):
    size = 2 * LANES
    cells = sum(math.prod(field.shape[:3]) for field in groups[0])
    half = jax.ShapeDtypeStruct((size + 8, LANES), F32)
    return call(
        functools.partial(inner_body, [len(group) for group in groups]),
        in_specs=whole_vmem(len(flat(groups))),
        out_specs=whole_vmem(2),
        out_shape=[half, half],
        scratch_shapes=[pltpu.VMEM((cells, size), BF16)],
    )(*flat(groups))


def inner_sum_body(keep_ref, got_ref, tail_ref, own_ref, sent_ref):
    size = 2 * LANES
    row = pl.multiple_of(lax.rem(lax.axis_index("slab"), 2) * LANES, LANES)
    own, other = pl.ds(row, LANES), pl.ds(LANES - row, LANES)
    own_ref[...] = keep_ref[own] + got_ref[own]
    sent_ref[...] = (keep_ref[other] + got_ref[other]).astype(BF16)
    tail_ref[...] = keep_ref[size:] + got_ref[size:]


def inner_sum(keep, got):
    return call(
        inner_sum_body,
        in_specs=whole_vmem(2),
        out_specs=whole_vmem(3),
        out_shape=[
            jax.ShapeDtypeStruct((8, LANES), F32),
            jax.ShapeDtypeStruct((LANES, LANES), F32),
            jax.ShapeDtypeStruct((LANES, LANES), BF16),
        ],
    )(keep, got)


def pair_blocks(got_refs, panel, chip):
    got = [ref[...].reshape(-1, LANES) for ref in got_refs]
    both = product(got[0] if len(got) == 1 else jnp.concatenate(got, axis=0), panel[...])
    blocks = [both[:, n * LANES : (n + 1) * LANES] for n in range(2)]
    return [jnp.where(chip == 0, block.T, block) for block in blocks]


def first_cross_body(sizes, *refs):
    (got, *kept), (panel, out_ref) = regroup(sizes, refs)
    chip = lax.axis_index("probe")
    for n, group in enumerate(kept):
        lay(panel, slice(n * LANES, (n + 1) * LANES), group)
    one, two = pair_blocks(got, panel, chip)
    out_ref[:LANES] = one
    out_ref[LANES:] = two


def first_cross(got, kept):
    groups = [got] + kept
    cells = sum(math.prod(field.shape[:3]) for field in got)
    return call(
        functools.partial(first_cross_body, [len(group) for group in groups]),
        in_specs=whole_vmem(len(flat(groups))),
        out_specs=whole_vmem(2),
        out_shape=[
            jax.ShapeDtypeStruct((cells, 2 * LANES), BF16),
            jax.ShapeDtypeStruct((2 * LANES, LANES), F32),
        ],
    )(*flat(groups))


def cross_body(count, *refs):
    got, (panel, first_ref, _, keep_ref, send_ref) = refs[:count], refs[count:]
    chip = lax.axis_index("probe")
    core = lax.axis_index("sub")
    zero, one = pair_blocks(got, panel, chip)
    mixed = first_ref[:LANES]
    corner = first_ref[LANES:]
    upper = jnp.where(chip == 0, mixed, one)
    lower = jnp.where(chip == 0, one, mixed)
    for ref, which in ((keep_ref, core), (send_ref, 1 - core)):
        here = which == 0
        ref[:LANES] = jnp.where(here, zero, upper)
        ref[LANES : 2 * LANES] = jnp.where(here, lower, corner)
        ref[2 * LANES :] = jnp.where(here, upper, lower)


def cross_gram(got, panel, first, after):
    three = jax.ShapeDtypeStruct((3 * LANES, LANES), F32)
    return call(
        functools.partial(cross_body, len(got)),
        in_specs=whole_vmem(len(got) + 2) + [pl.BlockSpec(memory_space=pl.ANY)],
        out_specs=whole_vmem(2),
        out_shape=[three, three],
    )(*got, panel, first, after)


def rounded(ref, block, tail):
    count = block.shape[0]
    high = tail.astype(BF16)
    low = tail - high.astype(F32)
    ref[:count] = block.astype(BF16)
    ref[count : count + 16] = jnp.concatenate([high.astype(F32), low], axis=0).astype(BF16)


def opened(ref, count):
    tail = ref[count : count + 16].astype(F32)
    return ref[:count].astype(F32), tail[:8] + tail[8:]


def cross_rows_body(keep_ref, got_ref, tail_ref, inner_ref, inner_got_ref, own_ref, *outs):
    slab = lax.axis_index("slab")
    core = lax.axis_index("sub")
    tail = tail_ref[...]
    inner = inner_ref[...] + inner_got_ref[...].astype(F32)
    for d in range(len(outs) + 1):
        owner = slab ^ d
        late = jnp.where(core == 0, jnp.where(owner == 2, 0, 2), jnp.where(owner == 2, 2, 1))
        at = jnp.where(owner < 2, owner, late)
        span = pl.ds(pl.multiple_of(at * LANES, LANES), LANES)
        block = keep_ref[span] + got_ref[span]
        if d == 0:
            own_ref[:LANES] = block
            own_ref[LANES : LANES + 8] = tail
            own_ref[LANES + 8 :] = inner
        else:
            rounded(outs[d - 1], block, tail)
            if d == 2:
                outs[1][LANES + 16 :] = inner.astype(BF16)


def cross_rows(keep, got, tail, inner, inner_got, slabs):
    own = jax.ShapeDtypeStruct((2 * LANES + 8, LANES), F32)
    long = jax.ShapeDtypeStruct((2 * LANES + 16, LANES), BF16)
    short = jax.ShapeDtypeStruct((LANES + 16, LANES), BF16)
    return call(
        cross_rows_body,
        in_specs=whole_vmem(5),
        out_specs=whole_vmem(slabs),
        out_shape=[own, short, long, short],
    )(keep, got, tail, inner, inner_got)


def sum_body(own_ref, *refs):
    block, tail = own_ref[:LANES], own_ref[LANES : LANES + 8]
    *others, out_ref = refs
    for ref in others:
        more, more_tail = opened(ref, LANES)
        block, tail = block + more, tail + more_tail
    inner = own_ref[LANES + 8 :] + others[0][LANES + 16 :].astype(F32)
    rounded(out_ref, block, tail)
    out_ref[LANES + 16 :] = inner.astype(BF16)


def sum_all(own, others):
    return call(
        sum_body,
        in_specs=whole_vmem(1 + len(others)),
        out_specs=whole_vmem(1)[0],
        out_shape=jax.ShapeDtypeStruct(others[0].shape, BF16),
    )(own, *others)


def normalise_body(cell_count, mine_ref, other_ref, out_ref, norms_ref):
    slab = lax.axis_index("slab")
    core = lax.axis_index("sub")
    chip = lax.axis_index("probe")
    one, one_tail = opened(mine_ref, LANES)
    two, two_tail = opened(other_ref, LANES)
    cross = one + two
    inner_span = pl.ds(LANES + 16, LANES)
    inner = jnp.where(slab // 2 == chip, mine_ref[inner_span], other_ref[inner_span]).astype(F32)
    upper = slab < 2
    values = [jnp.where(upper, inner, cross.T), jnp.where(upper, cross, inner)]
    norms = jnp.sqrt((one_tail + two_tail) / cell_count + EPSILON)
    blocks = [norms[n : n + 1] for n in range(4)]
    own = blocks[0]
    for n in range(1, 4):
        own = jnp.where(slab == n, blocks[n], own)
    norms_ref[...] = own
    own_column = jnp.sum(
        jnp.where(eye(), jnp.broadcast_to(own, (LANES, LANES)), 0.0), axis=1, keepdims=True
    )
    for side in range(2):
        others = jnp.where(core == 0, blocks[2 * side], blocks[2 * side + 1])
        value = values[side] / math.sqrt(cell_count) / (own_column * others)
        value = jnp.where(eye() & (2 * side + core == slab), 0.0, value)
        out_ref[:, side * LANES : (side + 1) * LANES] = value


def normalise(mine, other, cell_count):
    return call(
        functools.partial(normalise_body, cell_count),
        in_specs=whole_vmem(2),
        out_specs=whole_vmem(2),
        out_shape=[
            jax.ShapeDtypeStruct((LANES, 2 * LANES), F32),
            jax.ShapeDtypeStruct((1, LANES), F32),
        ],
    )(mine, other)


def assemble_body(near_ref, far_ref, out_ref):
    core = lax.axis_index("sub")
    for side in range(2):
        columns = slice(side * LANES, (side + 1) * LANES)
        for ref, which in ((near_ref, core), (far_ref, 1 - core)):
            start = pl.multiple_of((2 * side + which) * LANES, LANES)
            out_ref[:, pl.ds(start, LANES)] = ref[:, columns]


def assemble(near, far):
    return call(
        assemble_body,
        in_specs=whole_vmem(2),
        out_specs=whole_vmem(1)[0],
        out_shape=jax.ShapeDtypeStruct((near.shape[0], 4 * LANES), F32),
    )(near, far)


def coupled(finals, cell_count):
    slabs = 4
    keep, send = inner_gram([kept + sent for kept, sent, _ in finals])
    tail, inner, sent = inner_sum(keep, core_swap(send))
    inner_got = lax.ppermute(sent, "slab", [(i, i ^ 1) for i in range(slabs)])
    panel, first = first_cross(finals[1][2], [kept for kept, _, _ in finals])
    keep, send = cross_gram(finals[0][2], panel, first, inner_got)
    mine, *blocks = cross_rows(keep, core_swap(send), tail, inner, inner_got, slabs)
    arrived = [
        lax.ppermute(blocks[d - 1], "slab", [(i, i ^ d) for i in range(slabs)])
        for d in (2, 3, 1)
    ]
    total = sum_all(mine, arrived)
    near, norms = normalise(total, chip_swap(total), cell_count)
    return assemble(near, core_swap(near)), norms.reshape(-1)


def coupled_general(fields, cell_count):
    chips = lax.axis_size("probe")
    sketch = jnp.concatenate(fields, axis=-1)
    sketch = sketch.reshape(-1, sketch.shape[-1])
    if chips > 1:
        sketch = lax.all_to_all(sketch, "probe", split_axis=0, concat_axis=1, tiled=True)
    partial_gram = lax.dot_general(
        sketch, sketch, (((0,), (0,)), ((), ())), preferred_element_type=F32
    )
    rows = lax.psum_scatter(partial_gram, "slab", scatter_dimension=0, tiled=True)
    rows = lax.psum(rows, ("probe", "sub"))
    count = rows.shape[0]
    start = lax.axis_index("slab") * count
    own = jnp.diagonal(lax.dynamic_slice_in_dim(rows, start, count, 1))
    own_norms = jnp.sqrt(own / cell_count + EPSILON)
    norms = lax.all_gather(own_norms, "slab", axis=0, tiled=True)
    coupling = rows / math.sqrt(cell_count) / (own_norms[:, None] * norms[None, :])
    row_ids = start + lax.broadcasted_iota(jnp.int32, coupling.shape, 0)
    col_ids = lax.broadcasted_iota(jnp.int32, coupling.shape, 1)
    return jnp.where(row_ids == col_ids, 0.0, coupling), own_norms


def shards(probes, courant, source):
    depth, across, along, count = probes.shape
    chunks = count // LANES
    slabs, chips = lax.axis_size("slab"), lax.axis_size("probe")
    cell_count = depth * across * along * slabs * lax.axis_size("sub")
    paired = chips == 2 and slabs == 4 and chunks == 2 and depth == 2 * RADIUS
    steps = source.shape[0]
    courant = courant.reshape(depth * across, along)
    source = source.reshape(steps, depth * across, along)

    exchange = lambda odd, even, edge: (odd_swap(odd), even_swap(even), core_swap(edge))
    now, previous, halos = [], [None] * chunks, []
    for c in range(chunks):
        u, *edges = first_field(probes, c, source[:1])
        now.append(u)
        halos.append(exchange(*edges))
    courant, source = turn(courant, source, now[-1])
    finals = []
    for n in range(1, steps):
        for c in range(chunks):
            odd, even, beside = halos[c]
            base = local_step(now[c], beside, probes, c, courant, source, n, previous[c])
            if n < steps - 1:
                u, *edges = rim_step(base, odd, even, courant, "middle")
                previous[c], now[c] = now[c], u
                halos[c] = exchange(*edges)
            elif paired:
                if c > 0:
                    kept, *sent = rim_step(base, odd, even, courant, "half")
                else:
                    sent = [
                        part_step(base, odd, even, courant, True, begin, RADIUS // 2)
                        for begin in (0, RADIUS // 2)
                    ]
                    kept = part_step(base, odd, even, courant, False)
                finals.append(([kept], sent, [chip_swap(a) for a in sent]))
            else:
                finals += rim_step(base, odd, even, courant, "all")
    return (coupled if paired else coupled_general)(finals, cell_count)


def solution(mesh):
    placed = (
        P(("groups", "slab"), "sub", None, "probe"),
        P("slab", "sub", None),
        P(None, ("groups", "slab"), "sub", None),
    )
    return jax.shard_map(
        shards,
        mesh=mesh,
        in_specs=placed,
        out_specs=(P(("groups", "slab"), None), P(("groups", "slab"))),
        check_vma=False,
    )
```

```python
import functools
import math

import jax
import jax.numpy as jnp
from jax import lax
from jax.experimental import pallas as pl
from jax.experimental.pallas import tpu as pltpu
from jax.sharding import PartitionSpec as P

COEFFICIENTS = (-205.0 / 72.0, 8.0 / 5.0, -1.0 / 5.0, 8.0 / 315.0, -1.0 / 560.0)
EPSILON = 1e-06
LANES = 128
RADIUS = 4
EDGE = 8
TILE = 16
F32 = jnp.float32
BF16 = jnp.bfloat16
VMEM_LIMIT = 32 * 1024 * 1024


def call(body, **options):
    return pl.pallas_call(
        body,
        compiler_params=pltpu.CompilerParams(vmem_limit_bytes=VMEM_LIMIT),
        cost_estimate=pl.CostEstimate(flops=1, bytes_accessed=1, transcendentals=0),
        **options,
    )


def whole_vmem(count):
    return [pl.BlockSpec(memory_space=pltpu.VMEM)] * count


def shape_of(depth, across, along, dtype):
    return jax.ShapeDtypeStruct((depth, across, along, LANES), dtype)


def turned(field, scratch):
    rows, along = field.shape
    scratch[:rows, :along] = field
    return jnp.transpose(scratch[...])


def lane(values, n):
    return jnp.broadcast_to(values[:, n : n + 1], (values.shape[0], LANES))


def store_edges(x, span, news, even, even_ref, odd_ref):
    for j in range(RADIUS):
        low = news[j].astype(BF16)
        high = news[len(news) - RADIUS + j].astype(BF16)
        even_ref[j, x, span] = jnp.where(even, high, low)
        odd_ref[j, x, span] = jnp.where(even, low, high)


def store_beside(span, rows, core, u_ref, edge_ref):
    depth, across, _, _ = u_ref.shape
    first = (across - RADIUS) * (1 - core)
    for z in range(depth):
        for j in range(RADIUS):
            edge_ref[z, j, span] = u_ref[z, first + j, rows].astype(BF16)


def slab_is_even():
    return lax.rem(lax.axis_index("slab"), 2) == 0


def clear_pads(u_ref):
    depth, across, padded, _ = u_ref.shape

    def plane(z, _):
        blank = jnp.zeros((across, EDGE, LANES), F32)
        u_ref[z, :, pl.ds(0, EDGE)] = blank
        u_ref[z, :, pl.ds(padded - EDGE, EDGE)] = blank
        return 0

    lax.fori_loop(0, depth, plane, 0)


def tiles(along, body):
    def one(t, _):
        body(pl.multiple_of(t * TILE, TILE))
        return 0

    lax.fori_loop(0, along // TILE, one, 0)


def first_body(chunk, p_ref, s_ref, u_ref, odd_ref, even_ref, edge_ref, square, turned_s):
    depth, across, padded, _ = u_ref.shape
    along = padded - 2 * EDGE
    core = lax.axis_index("sub")
    even = slab_is_even()
    turned_s[...] = turned(s_ref[0], square)
    clear_pads(u_ref)

    def tile(start):
        span = pl.ds(start, TILE)
        rows = pl.ds(start + EDGE, TILE)
        source = turned_s[span]
        for x in range(across):
            news = []
            for z in range(depth):
                p = p_ref[z, x, span, chunk * LANES : (chunk + 1) * LANES].astype(F32)
                new = lane(source, z * across + x) * p
                u_ref[z, x, rows] = new
                news.append(new)
            store_edges(x, span, news, even, even_ref, odd_ref)
        store_beside(span, rows, core, u_ref, edge_ref)

    tiles(along, tile)


def square_scratch():
    return [pltpu.VMEM((LANES, LANES), F32)] * 2


def first_field(probes, chunk, source):
    depth, across, along, _ = probes.shape
    return call(
        functools.partial(first_body, chunk),
        grid=(1,),
        in_specs=whole_vmem(1) + [pl.BlockSpec((1,) + source.shape[1:], lambda i: (0, 0, 0))],
        out_specs=whole_vmem(4),
        out_shape=[
            shape_of(depth, across, along + 2 * EDGE, F32),
            shape_of(RADIUS, across, along, BF16),
            shape_of(RADIUS, across, along, BF16),
            shape_of(depth, RADIUS, along, BF16),
        ],
        scratch_shapes=square_scratch(),
    )(probes, source)


def turn_body(c_ref, s_ref, _, c_out, s_out, square):
    c_out[...] = turned(c_ref[...], square)
    for n in range(s_ref.shape[0]):
        s_out[n] = turned(s_ref[n], square)


def turn(courant, source, after):
    return call(
        turn_body,
        in_specs=whole_vmem(2) + [pl.BlockSpec(memory_space=pl.ANY)],
        out_specs=whole_vmem(2),
        out_shape=[
            jax.ShapeDtypeStruct((LANES, LANES), F32),
            jax.ShapeDtypeStruct((source.shape[0], LANES, LANES), F32),
        ],
        scratch_shapes=square_scratch()[:1],
    )(courant, source, after)


def local_body(chunk, moment, has_previous, *refs):
    refs = list(refs)
    u_ref, beside_ref, p_ref, c_ref, s_ref = refs[:5]
    prev_ref = refs[5] if has_previous else None
    base_ref = refs[-1]
    depth, across, along, _ = base_ref.shape
    core = lax.axis_index("sub")
    left_on = (core == 1).astype(F32)
    right_on = (core == 0).astype(F32)

    def tile(start):
        span = pl.ds(start, TILE)
        rows = start + EDGE
        courant = c_ref[span]
        source = s_ref[moment, span]
        for z in range(depth):
            beside = [beside_ref[z, j, span].astype(F32) for j in range(RADIUS)]
            row = [v * left_on for v in beside]
            row += [u_ref[z, x, pl.ds(rows, TILE)] for x in range(across)]
            row += [v * right_on for v in beside]
            for x in range(across):
                here = row[RADIUS + x]
                total = (3.0 * COEFFICIENTS[0]) * here
                for r in range(1, RADIUS + 1):
                    near = row[RADIUS + x + r] + row[RADIUS + x - r]
                    near = near + (
                        u_ref[z, x, pl.ds(rows + r, TILE)] + u_ref[z, x, pl.ds(rows - r, TILE)]
                    )
                    if z + r < depth:
                        near = near + u_ref[z + r, x, pl.ds(rows, TILE)]
                    if z - r >= 0:
                        near = near + u_ref[z - r, x, pl.ds(rows, TILE)]
                    total = total + COEFFICIENTS[r] * near
                cell = z * across + x
                p = p_ref[z, x, span, chunk * LANES : (chunk + 1) * LANES].astype(F32)
                new = 2.0 * here
                if has_previous:
                    new = new - prev_ref[z, x, pl.ds(rows, TILE)]
                new = new + lane(courant, cell) * total + lane(source, cell) * p
                base_ref[z, x, span] = new

    tiles(along, tile)


def local_step(u, beside, probes, chunk, courant, source, moment, previous):
    depth, across, along, _ = probes.shape
    operands = [u, beside, probes, courant, source]
    if previous is not None:
        operands.append(previous)
    return call(
        functools.partial(local_body, chunk, moment, previous is not None),
        in_specs=whole_vmem(len(operands)),
        out_specs=whole_vmem(1)[0],
        out_shape=shape_of(depth, across, along, F32),
    )(*operands)


def part_body(sent, begin, base_ref, odd_ref, even_ref, c_ref, out_ref):
    depth, across, along, _ = base_ref.shape
    even = slab_is_even()

    def planes(low):
        def tile(start):
            span = pl.ds(start, TILE)
            courant = c_ref[span]
            for x in range(across):
                near = []
                for j in range(RADIUS):
                    one, two = even_ref[j, x, span], odd_ref[j, x, span]
                    pair = (two, one) if low else (one, two)
                    near.append(jnp.where(even, *pair).astype(F32))
                for m in range(begin, begin + out_ref.shape[0]):
                    z = m if low else depth - RADIUS + m
                    added = None
                    for r in range(1, RADIUS + 1):
                        at = RADIUS + m - r if low else m + r - RADIUS
                        if 0 <= at < RADIUS:
                            term = COEFFICIENTS[r] * near[at]
                            added = term if added is None else added + term
                    new = base_ref[z, x, span] + lane(courant, z * across + x) * added
                    out_ref[m - begin, x, span] = new.astype(BF16)

        tiles(along, tile)

    low = lax.axis_index("probe") == (1 if sent else 0)
    pl.when(low)(lambda: planes(True))
    pl.when(jnp.logical_not(low))(lambda: planes(False))


def part_step(base, odds, evens, courant, sent, begin=0, count=RADIUS):
    _, across, along, _ = base.shape
    return call(
        functools.partial(part_body, sent, begin),
        in_specs=whole_vmem(4),
        out_specs=whole_vmem(1)[0],
        out_shape=shape_of(count, across, along, BF16),
    )(base, odds, evens, courant)


def rim_body(kind, *refs):
    base_ref, odd_ref, even_ref, c_ref = refs[:4]
    outs = refs[4:]
    depth, across, along, _ = base_ref.shape
    core = lax.axis_index("sub")
    even = slab_is_even()
    lower = lax.axis_index("probe") == 0
    if kind == "middle":
        clear_pads(outs[0])

    def tile(start):
        span = pl.ds(start, TILE)
        rows = pl.ds(start + EDGE, TILE)
        courant = c_ref[span]
        for x in range(across):
            below, above = [], []
            for j in range(RADIUS):
                one, two = even_ref[j, x, span], odd_ref[j, x, span]
                below.append(jnp.where(even, two, one).astype(F32))
                above.append(jnp.where(even, one, two).astype(F32))
            news = []
            for z in range(depth):
                added = None
                for r in range(1, RADIUS + 1):
                    if z - r < 0:
                        term = COEFFICIENTS[r] * below[RADIUS + z - r]
                        added = term if added is None else added + term
                    if z + r >= depth:
                        term = COEFFICIENTS[r] * above[z + r - depth]
                        added = term if added is None else added + term
                new = base_ref[z, x, span]
                if added is not None:
                    new = new + lane(courant, z * across + x) * added
                news.append(new)
            if kind == "middle":
                for z, new in enumerate(news):
                    outs[0][z, x, rows] = new
                store_edges(x, span, news, even, outs[2], outs[1])
            elif kind == "half":
                for z in range(depth // 2):
                    one, two = news[z].astype(BF16), news[z + depth // 2].astype(BF16)
                    outs[0][z, x, span] = jnp.where(lower, one, two)
                    outs[1][z, x, span] = jnp.where(lower, two, one)
            else:
                for z, new in enumerate(news):
                    outs[0][z, x, span] = new.astype(BF16)
        if kind == "middle":
            store_beside(span, rows, core, outs[0], outs[3])

    tiles(along, tile)


def rim_step(base, odds, evens, courant, kind):
    depth, across, along, _ = base.shape
    if kind == "middle":
        out_shape = [
            shape_of(depth, across, along + 2 * EDGE, F32),
            shape_of(RADIUS, across, along, BF16),
            shape_of(RADIUS, across, along, BF16),
            shape_of(depth, RADIUS, along, BF16),
        ]
    elif kind == "half":
        out_shape = [shape_of(depth // 2, across, along, BF16)] * 2
    else:
        out_shape = [shape_of(depth, across, along, BF16)]
    return call(
        functools.partial(rim_body, kind),
        in_specs=whole_vmem(4),
        out_specs=whole_vmem(len(out_shape)),
        out_shape=out_shape,
    )(base, odds, evens, courant)


def swap(x, axis, pairs):
    return lax.ppermute(x, axis, [p for a, b in pairs for p in ((a, b), (b, a))])


def even_swap(x):
    return swap(x, "slab", [(i, i + 1) for i in range(0, lax.axis_size("slab") - 1, 2)])


def odd_swap(x):
    return swap(x, "slab", [(i, i + 1) for i in range(1, lax.axis_size("slab") - 1, 2)])


def core_swap(x):
    return swap(x, "sub", [(0, 1)])


def chip_swap(x):
    return swap(x, "probe", [(0, 1)])


def product(a, b):
    return lax.dot_general(a, b, (((0,), (0,)), ((), ())), preferred_element_type=F32)


def block_of(array, i, j):
    return array[i * LANES : (i + 1) * LANES, j * LANES : (j + 1) * LANES]


def eye():
    rows = lax.broadcasted_iota(jnp.int32, (LANES, LANES), 0)
    cols = lax.broadcasted_iota(jnp.int32, (LANES, LANES), 1)
    return rows == cols


def lay(panel, columns, refs):
    row = 0
    for ref in refs:
        cells = math.prod(ref.shape[:3])
        panel[row : row + cells, columns] = ref[...].reshape(cells, LANES)
        row += cells


def flat(groups):
    return [field for group in groups for field in group]


def regroup(sizes, refs):
    groups, refs = [], list(refs)
    for size in sizes:
        groups.append(refs[:size])
        refs = refs[size:]
    return groups, refs


def inner_body(sizes, *refs):
    groups, (keep_ref, send_ref, panel) = regroup(sizes, refs)
    for n, group in enumerate(groups):
        lay(panel, slice(n * LANES, (n + 1) * LANES), group)
    core = lax.axis_index("sub")
    whole = product(panel[...], panel[...])
    first, second = whole[:, :LANES], whole[:, LANES:]
    size = 2 * LANES
    keep_ref[:size] = jnp.where(core == 0, first, second)
    send_ref[:size] = jnp.where(core == 0, second, first)
    diag = [
        jnp.sum(jnp.where(eye(), block_of(whole, n, n), 0.0), axis=0, keepdims=True)
        for n in range(2)
    ]
    none = jnp.zeros_like(diag[0])
    chip = lax.axis_index("probe")
    rows = [jnp.where(chip == n // 2, diag[n % 2], none) for n in range(4)]
    tail = jnp.concatenate(rows + [none] * 4, axis=0)
    keep_ref[size:] = tail
    send_ref[size:] = tail


def inner_gram(groups):
    size = 2 * LANES
    cells = sum(math.prod(field.shape[:3]) for field in groups[0])
    half = jax.ShapeDtypeStruct((size + 8, LANES), F32)
    return call(
        functools.partial(inner_body, [len(group) for group in groups]),
        in_specs=whole_vmem(len(flat(groups))),
        out_specs=whole_vmem(2),
        out_shape=[half, half],
        scratch_shapes=[pltpu.VMEM((cells, size), BF16)],
    )(*flat(groups))


def inner_sum_body(keep_ref, got_ref, tail_ref, own_ref, sent_ref):
    size = 2 * LANES
    row = pl.multiple_of(lax.rem(lax.axis_index("slab"), 2) * LANES, LANES)
    own, other = pl.ds(row, LANES), pl.ds(LANES - row, LANES)
    own_ref[...] = keep_ref[own] + got_ref[own]
    sent_ref[...] = (keep_ref[other] + got_ref[other]).astype(BF16)
    tail_ref[...] = keep_ref[size:] + got_ref[size:]


def inner_sum(keep, got):
    return call(
        inner_sum_body,
        in_specs=whole_vmem(2),
        out_specs=whole_vmem(3),
        out_shape=[
            jax.ShapeDtypeStruct((8, LANES), F32),
            jax.ShapeDtypeStruct((LANES, LANES), F32),
            jax.ShapeDtypeStruct((LANES, LANES), BF16),
        ],
    )(keep, got)


def pair_blocks(got_refs, panel, chip):
    got = [ref[...].reshape(-1, LANES) for ref in got_refs]
    both = product(got[0] if len(got) == 1 else jnp.concatenate(got, axis=0), panel[...])
    blocks = [both[:, n * LANES : (n + 1) * LANES] for n in range(2)]
    return [jnp.where(chip == 0, block.T, block) for block in blocks]


def first_cross_body(sizes, *refs):
    (got, *kept), (panel, out_ref) = regroup(sizes, refs)
    chip = lax.axis_index("probe")
    for n, group in enumerate(kept):
        lay(panel, slice(n * LANES, (n + 1) * LANES), group)
    one, two = pair_blocks(got, panel, chip)
    out_ref[:LANES] = one
    out_ref[LANES:] = two


def first_cross(got, kept):
    groups = [got] + kept
    cells = sum(math.prod(field.shape[:3]) for field in got)
    return call(
        functools.partial(first_cross_body, [len(group) for group in groups]),
        in_specs=whole_vmem(len(flat(groups))),
        out_specs=whole_vmem(2),
        out_shape=[
            jax.ShapeDtypeStruct((cells, 2 * LANES), BF16),
            jax.ShapeDtypeStruct((2 * LANES, LANES), F32),
        ],
    )(*flat(groups))


def cross_body(count, *refs):
    got, (panel, first_ref, _, keep_ref, send_ref) = refs[:count], refs[count:]
    chip = lax.axis_index("probe")
    core = lax.axis_index("sub")
    zero, one = pair_blocks(got, panel, chip)
    mixed = first_ref[:LANES]
    corner = first_ref[LANES:]
    upper = jnp.where(chip == 0, mixed, one)
    lower = jnp.where(chip == 0, one, mixed)
    for ref, which in ((keep_ref, core), (send_ref, 1 - core)):
        here = which == 0
        ref[:LANES] = jnp.where(here, zero, upper)
        ref[LANES : 2 * LANES] = jnp.where(here, lower, corner)
        ref[2 * LANES :] = jnp.where(here, upper, lower)


def cross_gram(got, panel, first, after):
    three = jax.ShapeDtypeStruct((3 * LANES, LANES), F32)
    return call(
        functools.partial(cross_body, len(got)),
        in_specs=whole_vmem(len(got) + 2) + [pl.BlockSpec(memory_space=pl.ANY)],
        out_specs=whole_vmem(2),
        out_shape=[three, three],
    )(*got, panel, first, after)


def rounded(ref, block, tail):
    count = block.shape[0]
    high = tail.astype(BF16)
    low = tail - high.astype(F32)
    ref[:count] = block.astype(BF16)
    ref[count : count + 16] = jnp.concatenate([high.astype(F32), low], axis=0).astype(BF16)


def opened(ref, count):
    tail = ref[count : count + 16].astype(F32)
    return ref[:count].astype(F32), tail[:8] + tail[8:]


def cross_rows_body(keep_ref, got_ref, tail_ref, inner_ref, inner_got_ref, own_ref, *outs):
    slab = lax.axis_index("slab")
    core = lax.axis_index("sub")
    tail = tail_ref[...]
    inner = inner_ref[...] + inner_got_ref[...].astype(F32)
    for d in range(len(outs) + 1):
        owner = slab ^ d
        late = jnp.where(core == 0, jnp.where(owner == 2, 0, 2), jnp.where(owner == 2, 2, 1))
        at = jnp.where(owner < 2, owner, late)
        span = pl.ds(pl.multiple_of(at * LANES, LANES), LANES)
        block = keep_ref[span] + got_ref[span]
        if d == 0:
            own_ref[:LANES] = block
            own_ref[LANES : LANES + 8] = tail
            own_ref[LANES + 8 :] = inner
        else:
            rounded(outs[d - 1], block, tail)
            if d == 2:
                outs[1][LANES + 16 :] = inner.astype(BF16)


def cross_rows(keep, got, tail, inner, inner_got, slabs):
    own = jax.ShapeDtypeStruct((2 * LANES + 8, LANES), F32)
    long = jax.ShapeDtypeStruct((2 * LANES + 16, LANES), BF16)
    short = jax.ShapeDtypeStruct((LANES + 16, LANES), BF16)
    return call(
        cross_rows_body,
        in_specs=whole_vmem(5),
        out_specs=whole_vmem(slabs),
        out_shape=[own, short, long, short],
    )(keep, got, tail, inner, inner_got)


def sum_body(own_ref, *refs):
    block, tail = own_ref[:LANES], own_ref[LANES : LANES + 8]
    *others, out_ref = refs
    for ref in others:
        more, more_tail = opened(ref, LANES)
        block, tail = block + more, tail + more_tail
    inner = own_ref[LANES + 8 :] + others[0][LANES + 16 :].astype(F32)
    rounded(out_ref, block, tail)
    out_ref[LANES + 16 :] = inner.astype(BF16)


def sum_all(own, others):
    return call(
        sum_body,
        in_specs=whole_vmem(1 + len(others)),
        out_specs=whole_vmem(1)[0],
        out_shape=jax.ShapeDtypeStruct(others[0].shape, BF16),
    )(own, *others)


def normalise_body(cell_count, mine_ref, other_ref, out_ref, norms_ref):
    slab = lax.axis_index("slab")
    core = lax.axis_index("sub")
    chip = lax.axis_index("probe")
    one, one_tail = opened(mine_ref, LANES)
    two, two_tail = opened(other_ref, LANES)
    cross = one + two
    inner_span = pl.ds(LANES + 16, LANES)
    inner = jnp.where(slab // 2 == chip, mine_ref[inner_span], other_ref[inner_span]).astype(F32)
    upper = slab < 2
    values = [jnp.where(upper, inner, cross.T), jnp.where(upper, cross, inner)]
    norms = jnp.sqrt((one_tail + two_tail) / cell_count + EPSILON)
    blocks = [norms[n : n + 1] for n in range(4)]
    own = blocks[0]
    for n in range(1, 4):
        own = jnp.where(slab == n, blocks[n], own)
    norms_ref[...] = own
    own_column = jnp.sum(
        jnp.where(eye(), jnp.broadcast_to(own, (LANES, LANES)), 0.0), axis=1, keepdims=True
    )
    for side in range(2):
        others = jnp.where(core == 0, blocks[2 * side], blocks[2 * side + 1])
        value = values[side] / math.sqrt(cell_count) / (own_column * others)
        value = jnp.where(eye() & (2 * side + core == slab), 0.0, value)
        out_ref[:, side * LANES : (side + 1) * LANES] = value


def normalise(mine, other, cell_count):
    return call(
        functools.partial(normalise_body, cell_count),
        in_specs=whole_vmem(2),
        out_specs=whole_vmem(2),
        out_shape=[
            jax.ShapeDtypeStruct((LANES, 2 * LANES), F32),
            jax.ShapeDtypeStruct((1, LANES), F32),
        ],
    )(mine, other)


def assemble_body(near_ref, far_ref, out_ref):
    core = lax.axis_index("sub")
    for side in range(2):
        columns = slice(side * LANES, (side + 1) * LANES)
        for ref, which in ((near_ref, core), (far_ref, 1 - core)):
            start = pl.multiple_of((2 * side + which) * LANES, LANES)
            out_ref[:, pl.ds(start, LANES)] = ref[:, columns]


def assemble(near, far):
    return call(
        assemble_body,
        in_specs=whole_vmem(2),
        out_specs=whole_vmem(1)[0],
        out_shape=jax.ShapeDtypeStruct((near.shape[0], 4 * LANES), F32),
    )(near, far)


def coupled(finals, cell_count):
    slabs = 4
    keep, send = inner_gram([kept + sent for kept, sent, _ in finals])
    tail, inner, sent = inner_sum(keep, core_swap(send))
    inner_got = lax.ppermute(sent, "slab", [(i, i ^ 1) for i in range(slabs)])
    panel, first = first_cross(finals[1][2], [kept for kept, _, _ in finals])
    keep, send = cross_gram(finals[0][2], panel, first, inner_got)
    mine, *blocks = cross_rows(keep, core_swap(send), tail, inner, inner_got, slabs)
    arrived = [
        lax.ppermute(blocks[d - 1], "slab", [(i, i ^ d) for i in range(slabs)])
        for d in (2, 3, 1)
    ]
    total = sum_all(mine, arrived)
    near, norms = normalise(total, chip_swap(total), cell_count)
    return assemble(near, core_swap(near)), norms.reshape(-1)


def coupled_general(fields, cell_count):
    chips = lax.axis_size("probe")
    sketch = jnp.concatenate(fields, axis=-1)
    sketch = sketch.reshape(-1, sketch.shape[-1])
    if chips > 1:
        sketch = lax.all_to_all(sketch, "probe", split_axis=0, concat_axis=1, tiled=True)
    partial_gram = lax.dot_general(
        sketch, sketch, (((0,), (0,)), ((), ())), preferred_element_type=F32
    )
    rows = lax.psum_scatter(partial_gram, "slab", scatter_dimension=0, tiled=True)
    rows = lax.psum(rows, ("probe", "sub"))
    count = rows.shape[0]
    start = lax.axis_index("slab") * count
    own = jnp.diagonal(lax.dynamic_slice_in_dim(rows, start, count, 1))
    own_norms = jnp.sqrt(own / cell_count + EPSILON)
    norms = lax.all_gather(own_norms, "slab", axis=0, tiled=True)
    coupling = rows / math.sqrt(cell_count) / (own_norms[:, None] * norms[None, :])
    row_ids = start + lax.broadcasted_iota(jnp.int32, coupling.shape, 0)
    col_ids = lax.broadcasted_iota(jnp.int32, coupling.shape, 1)
    return jnp.where(row_ids == col_ids, 0.0, coupling), own_norms


def shards(probes, courant, source):
    depth, across, along, count = probes.shape
    chunks = count // LANES
    slabs, chips = lax.axis_size("slab"), lax.axis_size("probe")
    cell_count = depth * across * along * slabs * lax.axis_size("sub")
    paired = chips == 2 and slabs == 4 and chunks == 2 and depth == 2 * RADIUS
    steps = source.shape[0]
    courant = courant.reshape(depth * across, along)
    source = source.reshape(steps, depth * across, along)

    exchange = lambda odd, even, edge: (odd_swap(odd), even_swap(even), core_swap(edge))
    now, previous, halos = [], [None] * chunks, []
    for c in range(chunks):
        u, *edges = first_field(probes, c, source)
        now.append(u)
        halos.append(exchange(*edges))
    courant, source = turn(courant, source, now[-1])
    finals = []
    for n in range(1, steps):
        for c in range(chunks):
            odd, even, beside = halos[c]
            base = local_step(now[c], beside, probes, c, courant, source, n, previous[c])
            if n < steps - 1:
                u, *edges = rim_step(base, odd, even, courant, "middle")
                previous[c], now[c] = now[c], u
                halos[c] = exchange(*edges)
            elif paired:
                if c > 0:
                    kept, *sent = rim_step(base, odd, even, courant, "half")
                else:
                    sent = [
                        part_step(base, odd, even, courant, True, begin, RADIUS // 2)
                        for begin in (0, RADIUS // 2)
                    ]
                    kept = part_step(base, odd, even, courant, False)
                finals.append(([kept], sent, [chip_swap(a) for a in sent]))
            else:
                finals += rim_step(base, odd, even, courant, "all")
    return (coupled if paired else coupled_general)(finals, cell_count)


def solution(mesh):
    placed = (
        P(("groups", "slab"), "sub", None, "probe"),
        P("slab", "sub", None),
        P(None, ("groups", "slab"), "sub", None),
    )
    return jax.shard_map(
        shards,
        mesh=mesh,
        in_specs=placed,
        out_specs=(P(("groups", "slab"), None), P(("groups", "slab"))),
        check_vma=False,
    )
```

```python
import functools
import math

import jax
import jax.numpy as jnp
from jax import lax
from jax.experimental import pallas as pl
from jax.experimental.pallas import tpu as pltpu
from jax.sharding import PartitionSpec as P

COEFFICIENTS = (-205.0 / 72.0, 8.0 / 5.0, -1.0 / 5.0, 8.0 / 315.0, -1.0 / 560.0)
EPSILON = 1e-06
LANES = 128
RADIUS = 4
EDGE = 8
TILE = 16
F32 = jnp.float32
BF16 = jnp.bfloat16
VMEM_LIMIT = 32 * 1024 * 1024


def call(body, **options):
    return pl.pallas_call(
        body,
        compiler_params=pltpu.CompilerParams(vmem_limit_bytes=VMEM_LIMIT),
        cost_estimate=pl.CostEstimate(flops=1, bytes_accessed=1, transcendentals=0),
        **options,
    )


def whole_vmem(count):
    return [pl.BlockSpec(memory_space=pltpu.VMEM)] * count


def shape_of(depth, across, along, dtype):
    return jax.ShapeDtypeStruct((depth, across, along, LANES), dtype)


def turned(field, scratch):
    rows, along = field.shape
    scratch[:rows, :along] = field
    return jnp.transpose(scratch[...])


def lane(values, n):
    return jnp.broadcast_to(values[:, n : n + 1], (values.shape[0], LANES))


def store_edges(x, span, news, even, even_ref, odd_ref):
    for j in range(RADIUS):
        low = news[j].astype(BF16)
        high = news[len(news) - RADIUS + j].astype(BF16)
        even_ref[j, x, span] = jnp.where(even, high, low)
        odd_ref[j, x, span] = jnp.where(even, low, high)


def store_beside(span, rows, core, u_ref, edge_ref):
    depth, across, _, _ = u_ref.shape
    first = (across - RADIUS) * (1 - core)
    for z in range(depth):
        for j in range(RADIUS):
            edge_ref[z, j, span] = u_ref[z, first + j, rows].astype(BF16)


def slab_is_even():
    return lax.rem(lax.axis_index("slab"), 2) == 0


def clear_pads(u_ref):
    depth, across, padded, _ = u_ref.shape

    def plane(z, _):
        blank = jnp.zeros((across, EDGE, LANES), F32)
        u_ref[z, :, pl.ds(0, EDGE)] = blank
        u_ref[z, :, pl.ds(padded - EDGE, EDGE)] = blank
        return 0

    lax.fori_loop(0, depth, plane, 0)


def tiles(along, body):
    def one(t, _):
        body(pl.multiple_of(t * TILE, TILE))
        return 0

    lax.fori_loop(0, along // TILE, one, 0)


def first_body(chunk, p_ref, s_ref, u_ref, odd_ref, even_ref, edge_ref, square, turned_s):
    depth, across, padded, _ = u_ref.shape
    along = padded - 2 * EDGE
    core = lax.axis_index("sub")
    even = slab_is_even()
    turned_s[...] = turned(s_ref[0], square)
    clear_pads(u_ref)

    def tile(start):
        span = pl.ds(start, TILE)
        rows = pl.ds(start + EDGE, TILE)
        source = turned_s[span]
        for x in range(across):
            news = []
            for z in range(depth):
                p = p_ref[z, x, span, chunk * LANES : (chunk + 1) * LANES].astype(F32)
                new = lane(source, z * across + x) * p
                u_ref[z, x, rows] = new
                news.append(new)
            store_edges(x, span, news, even, even_ref, odd_ref)
        store_beside(span, rows, core, u_ref, edge_ref)

    tiles(along, tile)


def square_scratch():
    return [pltpu.VMEM((LANES, LANES), F32)] * 2


def first_field(probes, chunk, source):
    depth, across, along, _ = probes.shape
    return call(
        functools.partial(first_body, chunk),
        in_specs=whole_vmem(2),
        out_specs=whole_vmem(4),
        out_shape=[
            shape_of(depth, across, along + 2 * EDGE, F32),
            shape_of(RADIUS, across, along, BF16),
            shape_of(RADIUS, across, along, BF16),
            shape_of(depth, RADIUS, along, BF16),
        ],
        scratch_shapes=square_scratch(),
    )(probes, source)


def turn_body(c_ref, s_ref, _, c_out, s_out, square):
    c_out[...] = turned(c_ref[...], square)
    for n in range(s_ref.shape[0]):
        s_out[n] = turned(s_ref[n], square)


def turn(courant, source, after):
    return call(
        turn_body,
        in_specs=whole_vmem(2) + [pl.BlockSpec(memory_space=pl.ANY)],
        out_specs=whole_vmem(2),
        out_shape=[
            jax.ShapeDtypeStruct((LANES, LANES), F32),
            jax.ShapeDtypeStruct((source.shape[0], LANES, LANES), F32),
        ],
        scratch_shapes=square_scratch()[:1],
    )(courant, source, after)


def local_body(chunk, moment, has_previous, *refs):
    refs = list(refs)
    u_ref, beside_ref, p_ref, c_ref, s_ref = refs[:5]
    prev_ref = refs[5] if has_previous else None
    base_ref = refs[-1]
    depth, across, along, _ = base_ref.shape
    core = lax.axis_index("sub")
    left_on = (core == 1).astype(F32)
    right_on = (core == 0).astype(F32)

    def tile(start):
        span = pl.ds(start, TILE)
        rows = start + EDGE
        courant = c_ref[span]
        source = s_ref[moment, span]
        for z in range(depth):
            beside = [beside_ref[z, j, span].astype(F32) for j in range(RADIUS)]
            row = [v * left_on for v in beside]
            row += [u_ref[z, x, pl.ds(rows, TILE)] for x in range(across)]
            row += [v * right_on for v in beside]
            for x in range(across):
                here = row[RADIUS + x]
                total = (3.0 * COEFFICIENTS[0]) * here
                for r in range(1, RADIUS + 1):
                    near = row[RADIUS + x + r] + row[RADIUS + x - r]
                    near = near + (
                        u_ref[z, x, pl.ds(rows + r, TILE)] + u_ref[z, x, pl.ds(rows - r, TILE)]
                    )
                    if z + r < depth:
                        near = near + u_ref[z + r, x, pl.ds(rows, TILE)]
                    if z - r >= 0:
                        near = near + u_ref[z - r, x, pl.ds(rows, TILE)]
                    total = total + COEFFICIENTS[r] * near
                cell = z * across + x
                p = p_ref[z, x, span, chunk * LANES : (chunk + 1) * LANES].astype(F32)
                new = 2.0 * here
                if has_previous:
                    new = new - prev_ref[z, x, pl.ds(rows, TILE)]
                new = new + lane(courant, cell) * total + lane(source, cell) * p
                base_ref[z, x, span] = new

    tiles(along, tile)


def local_step(u, beside, probes, chunk, courant, source, moment, previous):
    depth, across, along, _ = probes.shape
    operands = [u, beside, probes, courant, source]
    if previous is not None:
        operands.append(previous)
    return call(
        functools.partial(local_body, chunk, moment, previous is not None),
        in_specs=whole_vmem(len(operands)),
        out_specs=whole_vmem(1)[0],
        out_shape=shape_of(depth, across, along, F32),
    )(*operands)


def part_body(sent, begin, base_ref, odd_ref, even_ref, c_ref, out_ref):
    depth, across, along, _ = base_ref.shape
    even = slab_is_even()

    def planes(low):
        def tile(start):
            span = pl.ds(start, TILE)
            courant = c_ref[span]
            for x in range(across):
                near = []
                for j in range(RADIUS):
                    one, two = even_ref[j, x, span], odd_ref[j, x, span]
                    pair = (two, one) if low else (one, two)
                    near.append(jnp.where(even, *pair).astype(F32))
                for m in range(begin, begin + out_ref.shape[0]):
                    z = m if low else depth - RADIUS + m
                    added = None
                    for r in range(1, RADIUS + 1):
                        at = RADIUS + m - r if low else m + r - RADIUS
                        if 0 <= at < RADIUS:
                            term = COEFFICIENTS[r] * near[at]
                            added = term if added is None else added + term
                    new = base_ref[z, x, span] + lane(courant, z * across + x) * added
                    out_ref[m - begin, x, span] = new.astype(BF16)

        tiles(along, tile)

    low = lax.axis_index("probe") == (1 if sent else 0)
    pl.when(low)(lambda: planes(True))
    pl.when(jnp.logical_not(low))(lambda: planes(False))


def part_step(base, odds, evens, courant, sent, begin=0, count=RADIUS):
    _, across, along, _ = base.shape
    return call(
        functools.partial(part_body, sent, begin),
        in_specs=whole_vmem(4),
        out_specs=whole_vmem(1)[0],
        out_shape=shape_of(count, across, along, BF16),
    )(base, odds, evens, courant)


def rim_body(kind, *refs):
    base_ref, odd_ref, even_ref, c_ref = refs[:4]
    outs = refs[4:]
    depth, across, along, _ = base_ref.shape
    core = lax.axis_index("sub")
    even = slab_is_even()
    lower = lax.axis_index("probe") == 0
    if kind == "middle":
        clear_pads(outs[0])

    def tile(start):
        span = pl.ds(start, TILE)
        rows = pl.ds(start + EDGE, TILE)
        courant = c_ref[span]
        for x in range(across):
            below, above = [], []
            for j in range(RADIUS):
                one, two = even_ref[j, x, span], odd_ref[j, x, span]
                below.append(jnp.where(even, two, one).astype(F32))
                above.append(jnp.where(even, one, two).astype(F32))
            news = []
            for z in range(depth):
                added = None
                for r in range(1, RADIUS + 1):
                    if z - r < 0:
                        term = COEFFICIENTS[r] * below[RADIUS + z - r]
                        added = term if added is None else added + term
                    if z + r >= depth:
                        term = COEFFICIENTS[r] * above[z + r - depth]
                        added = term if added is None else added + term
                new = base_ref[z, x, span]
                if added is not None:
                    new = new + lane(courant, z * across + x) * added
                news.append(new)
            if kind == "middle":
                for z, new in enumerate(news):
                    outs[0][z, x, rows] = new
                store_edges(x, span, news, even, outs[2], outs[1])
            elif kind == "half":
                for z in range(depth // 2):
                    one, two = news[z].astype(BF16), news[z + depth // 2].astype(BF16)
                    outs[0][z, x, span] = jnp.where(lower, one, two)
                    outs[1][z, x, span] = jnp.where(lower, two, one)
            else:
                for z, new in enumerate(news):
                    outs[0][z, x, span] = new.astype(BF16)
        if kind == "middle":
            store_beside(span, rows, core, outs[0], outs[3])

    tiles(along, tile)


def rim_step(base, odds, evens, courant, kind):
    depth, across, along, _ = base.shape
    if kind == "middle":
        out_shape = [
            shape_of(depth, across, along + 2 * EDGE, F32),
            shape_of(RADIUS, across, along, BF16),
            shape_of(RADIUS, across, along, BF16),
            shape_of(depth, RADIUS, along, BF16),
        ]
    elif kind == "half":
        out_shape = [shape_of(depth // 2, across, along, BF16)] * 2
    else:
        out_shape = [shape_of(depth, across, along, BF16)]
    return call(
        functools.partial(rim_body, kind),
        in_specs=whole_vmem(4),
        out_specs=whole_vmem(len(out_shape)),
        out_shape=out_shape,
    )(base, odds, evens, courant)


def swap(x, axis, pairs):
    return lax.ppermute(x, axis, [p for a, b in pairs for p in ((a, b), (b, a))])


def even_swap(x):
    return swap(x, "slab", [(i, i + 1) for i in range(0, lax.axis_size("slab") - 1, 2)])


def odd_swap(x):
    return swap(x, "slab", [(i, i + 1) for i in range(1, lax.axis_size("slab") - 1, 2)])


def core_swap(x):
    return swap(x, "sub", [(0, 1)])


def chip_swap(x):
    return swap(x, "probe", [(0, 1)])


def product(a, b):
    return lax.dot_general(a, b, (((0,), (0,)), ((), ())), preferred_element_type=F32)


def block_of(array, i, j):
    return array[i * LANES : (i + 1) * LANES, j * LANES : (j + 1) * LANES]


def eye():
    rows = lax.broadcasted_iota(jnp.int32, (LANES, LANES), 0)
    cols = lax.broadcasted_iota(jnp.int32, (LANES, LANES), 1)
    return rows == cols


def lay(panel, columns, refs):
    row = 0
    for ref in refs:
        cells = math.prod(ref.shape[:3])
        panel[row : row + cells, columns] = ref[...].reshape(cells, LANES)
        row += cells


def flat(groups):
    return [field for group in groups for field in group]


def regroup(sizes, refs):
    groups, refs = [], list(refs)
    for size in sizes:
        groups.append(refs[:size])
        refs = refs[size:]
    return groups, refs


def inner_body(sizes, *refs):
    groups, (keep_ref, send_ref, panel) = regroup(sizes, refs)
    for n, group in enumerate(groups):
        lay(panel, slice(n * LANES, (n + 1) * LANES), group)
    core = lax.axis_index("sub")
    whole = product(panel[...], panel[...])
    first, second = whole[:, :LANES], whole[:, LANES:]
    size = 2 * LANES
    keep_ref[:size] = jnp.where(core == 0, first, second)
    send_ref[:size] = jnp.where(core == 0, second, first)
    diag = [
        jnp.sum(jnp.where(eye(), block_of(whole, n, n), 0.0), axis=0, keepdims=True)
        for n in range(2)
    ]
    none = jnp.zeros_like(diag[0])
    chip = lax.axis_index("probe")
    rows = [jnp.where(chip == n // 2, diag[n % 2], none) for n in range(4)]
    tail = jnp.concatenate(rows + [none] * 4, axis=0)
    keep_ref[size:] = tail
    send_ref[size:] = tail


def inner_gram(groups):
    size = 2 * LANES
    cells = sum(math.prod(field.shape[:3]) for field in groups[0])
    half = jax.ShapeDtypeStruct((size + 8, LANES), F32)
    return call(
        functools.partial(inner_body, [len(group) for group in groups]),
        in_specs=whole_vmem(len(flat(groups))),
        out_specs=whole_vmem(2),
        out_shape=[half, half],
        scratch_shapes=[pltpu.VMEM((cells, size), BF16)],
    )(*flat(groups))


def inner_sum_body(keep_ref, got_ref, tail_ref, own_ref, sent_ref):
    size = 2 * LANES
    row = pl.multiple_of(lax.rem(lax.axis_index("slab"), 2) * LANES, LANES)
    own, other = pl.ds(row, LANES), pl.ds(LANES - row, LANES)
    own_ref[...] = keep_ref[own] + got_ref[own]
    sent_ref[...] = (keep_ref[other] + got_ref[other]).astype(BF16)
    tail_ref[...] = keep_ref[size:] + got_ref[size:]


def inner_sum(keep, got):
    return call(
        inner_sum_body,
        in_specs=whole_vmem(2),
        out_specs=whole_vmem(3),
        out_shape=[
            jax.ShapeDtypeStruct((8, LANES), F32),
            jax.ShapeDtypeStruct((LANES, LANES), F32),
            jax.ShapeDtypeStruct((LANES, LANES), BF16),
        ],
    )(keep, got)


def pair_blocks(got_refs, panel, chip):
    got = [ref[...].reshape(-1, LANES) for ref in got_refs]
    both = product(got[0] if len(got) == 1 else jnp.concatenate(got, axis=0), panel[...])
    blocks = [both[:, n * LANES : (n + 1) * LANES] for n in range(2)]
    return [jnp.where(chip == 0, block.T, block) for block in blocks]


def first_cross_body(sizes, *refs):
    (got, *kept), (panel, out_ref) = regroup(sizes, refs)
    chip = lax.axis_index("probe")
    for n, group in enumerate(kept):
        lay(panel, slice(n * LANES, (n + 1) * LANES), group)
    one, two = pair_blocks(got, panel, chip)
    out_ref[:LANES] = one
    out_ref[LANES:] = two


def first_cross(got, kept):
    groups = [got] + kept
    cells = sum(math.prod(field.shape[:3]) for field in got)
    return call(
        functools.partial(first_cross_body, [len(group) for group in groups]),
        in_specs=whole_vmem(len(flat(groups))),
        out_specs=whole_vmem(2),
        out_shape=[
            jax.ShapeDtypeStruct((cells, 2 * LANES), BF16),
            jax.ShapeDtypeStruct((2 * LANES, LANES), F32),
        ],
    )(*flat(groups))


def cross_body(count, *refs):
    got, (panel, first_ref, _, keep_ref, send_ref) = refs[:count], refs[count:]
    chip = lax.axis_index("probe")
    core = lax.axis_index("sub")
    zero, one = pair_blocks(got, panel, chip)
    mixed = first_ref[:LANES]
    corner = first_ref[LANES:]
    upper = jnp.where(chip == 0, mixed, one)
    lower = jnp.where(chip == 0, one, mixed)
    for ref, which in ((keep_ref, core), (send_ref, 1 - core)):
        here = which == 0
        ref[:LANES] = jnp.where(here, zero, upper)
        ref[LANES : 2 * LANES] = jnp.where(here, lower, corner)
        ref[2 * LANES :] = jnp.where(here, upper, lower)


def cross_gram(got, panel, first, after):
    three = jax.ShapeDtypeStruct((3 * LANES, LANES), F32)
    return call(
        functools.partial(cross_body, len(got)),
        in_specs=whole_vmem(len(got) + 2) + [pl.BlockSpec(memory_space=pl.ANY)],
        out_specs=whole_vmem(2),
        out_shape=[three, three],
    )(*got, panel, first, after)


def rounded(ref, block, tail):
    count = block.shape[0]
    high = tail.astype(BF16)
    low = tail - high.astype(F32)
    ref[:count] = block.astype(BF16)
    ref[count : count + 16] = jnp.concatenate([high.astype(F32), low], axis=0).astype(BF16)


def opened(ref, count):
    tail = ref[count : count + 16].astype(F32)
    return ref[:count].astype(F32), tail[:8] + tail[8:]


def cross_rows_body(keep_ref, got_ref, tail_ref, inner_ref, inner_got_ref, own_ref, *outs):
    slab = lax.axis_index("slab")
    core = lax.axis_index("sub")
    tail = tail_ref[...]
    inner = inner_ref[...] + inner_got_ref[...].astype(F32)
    for d in range(len(outs) + 1):
        owner = slab ^ d
        late = jnp.where(core == 0, jnp.where(owner == 2, 0, 2), jnp.where(owner == 2, 2, 1))
        at = jnp.where(owner < 2, owner, late)
        span = pl.ds(pl.multiple_of(at * LANES, LANES), LANES)
        block = keep_ref[span] + got_ref[span]
        if d == 0:
            own_ref[:LANES] = block
            own_ref[LANES : LANES + 8] = tail
            own_ref[LANES + 8 :] = inner
        else:
            rounded(outs[d - 1], block, tail)
            if d == 2:
                outs[1][LANES + 16 :] = inner.astype(BF16)


def cross_rows(keep, got, tail, inner, inner_got, slabs):
    own = jax.ShapeDtypeStruct((2 * LANES + 8, LANES), F32)
    long = jax.ShapeDtypeStruct((2 * LANES + 16, LANES), BF16)
    short = jax.ShapeDtypeStruct((LANES + 16, LANES), BF16)
    return call(
        cross_rows_body,
        in_specs=whole_vmem(5),
        out_specs=whole_vmem(slabs),
        out_shape=[own, short, long, short],
    )(keep, got, tail, inner, inner_got)


def sum_body(own_ref, *refs):
    block, tail = own_ref[:LANES], own_ref[LANES : LANES + 8]
    *others, out_ref = refs
    for ref in others:
        more, more_tail = opened(ref, LANES)
        block, tail = block + more, tail + more_tail
    inner = own_ref[LANES + 8 :] + others[0][LANES + 16 :].astype(F32)
    rounded(out_ref, block, tail)
    out_ref[LANES + 16 :] = inner.astype(BF16)


def sum_all(own, others):
    return call(
        sum_body,
        in_specs=whole_vmem(1 + len(others)),
        out_specs=whole_vmem(1)[0],
        out_shape=jax.ShapeDtypeStruct(others[0].shape, BF16),
    )(own, *others)


def normalise_body(cell_count, mine_ref, other_ref, out_ref, norms_ref):
    slab = lax.axis_index("slab")
    core = lax.axis_index("sub")
    chip = lax.axis_index("probe")
    one, one_tail = opened(mine_ref, LANES)
    two, two_tail = opened(other_ref, LANES)
    cross = one + two
    inner_span = pl.ds(LANES + 16, LANES)
    inner = jnp.where(slab // 2 == chip, mine_ref[inner_span], other_ref[inner_span]).astype(F32)
    upper = slab < 2
    values = [jnp.where(upper, inner, cross.T), jnp.where(upper, cross, inner)]
    norms = jnp.sqrt((one_tail + two_tail) / cell_count + EPSILON)
    blocks = [norms[n : n + 1] for n in range(4)]
    own = blocks[0]
    for n in range(1, 4):
        own = jnp.where(slab == n, blocks[n], own)
    norms_ref[...] = own
    own_column = jnp.sum(
        jnp.where(eye(), jnp.broadcast_to(own, (LANES, LANES)), 0.0), axis=1, keepdims=True
    )
    for side in range(2):
        others = jnp.where(core == 0, blocks[2 * side], blocks[2 * side + 1])
        value = values[side] / math.sqrt(cell_count) / (own_column * others)
        value = jnp.where(eye() & (2 * side + core == slab), 0.0, value)
        out_ref[:, side * LANES : (side + 1) * LANES] = value


def normalise(mine, other, cell_count):
    return call(
        functools.partial(normalise_body, cell_count),
        in_specs=whole_vmem(2),
        out_specs=whole_vmem(2),
        out_shape=[
            jax.ShapeDtypeStruct((LANES, 2 * LANES), F32),
            jax.ShapeDtypeStruct((1, LANES), F32),
        ],
    )(mine, other)


def assemble_body(near_ref, far_ref, out_ref):
    core = lax.axis_index("sub")
    for side in range(2):
        columns = slice(side * LANES, (side + 1) * LANES)
        for ref, which in ((near_ref, core), (far_ref, 1 - core)):
            start = pl.multiple_of((2 * side + which) * LANES, LANES)
            out_ref[:, pl.ds(start, LANES)] = ref[:, columns]


def assemble(near, far):
    return call(
        assemble_body,
        in_specs=whole_vmem(2),
        out_specs=whole_vmem(1)[0],
        out_shape=jax.ShapeDtypeStruct((near.shape[0], 4 * LANES), F32),
    )(near, far)


def coupled(finals, cell_count):
    slabs = 4
    keep, send = inner_gram([kept + sent for kept, sent, _ in finals])
    tail, inner, sent = inner_sum(keep, core_swap(send))
    inner_got = lax.ppermute(sent, "slab", [(i, i ^ 1) for i in range(slabs)])
    panel, first = first_cross(finals[1][2], [kept for kept, _, _ in finals])
    keep, send = cross_gram(finals[0][2], panel, first, inner_got)
    mine, *blocks = cross_rows(keep, core_swap(send), tail, inner, inner_got, slabs)
    arrived = [
        lax.ppermute(blocks[d - 1], "slab", [(i, i ^ d) for i in range(slabs)])
        for d in (2, 3, 1)
    ]
    total = sum_all(mine, arrived)
    near, norms = normalise(total, chip_swap(total), cell_count)
    return assemble(near, core_swap(near)), norms.reshape(-1)


def coupled_general(fields, cell_count):
    chips = lax.axis_size("probe")
    sketch = jnp.concatenate(fields, axis=-1)
    sketch = sketch.reshape(-1, sketch.shape[-1])
    if chips > 1:
        sketch = lax.all_to_all(sketch, "probe", split_axis=0, concat_axis=1, tiled=True)
    partial_gram = lax.dot_general(
        sketch, sketch, (((0,), (0,)), ((), ())), preferred_element_type=F32
    )
    rows = lax.psum_scatter(partial_gram, "slab", scatter_dimension=0, tiled=True)
    rows = lax.psum(rows, ("probe", "sub"))
    count = rows.shape[0]
    start = lax.axis_index("slab") * count
    own = jnp.diagonal(lax.dynamic_slice_in_dim(rows, start, count, 1))
    own_norms = jnp.sqrt(own / cell_count + EPSILON)
    norms = lax.all_gather(own_norms, "slab", axis=0, tiled=True)
    coupling = rows / math.sqrt(cell_count) / (own_norms[:, None] * norms[None, :])
    row_ids = start + lax.broadcasted_iota(jnp.int32, coupling.shape, 0)
    col_ids = lax.broadcasted_iota(jnp.int32, coupling.shape, 1)
    return jnp.where(row_ids == col_ids, 0.0, coupling), own_norms


def shards(probes, courant, source):
    depth, across, along, count = probes.shape
    chunks = count // LANES
    slabs, chips = lax.axis_size("slab"), lax.axis_size("probe")
    cell_count = depth * across * along * slabs * lax.axis_size("sub")
    paired = chips == 2 and slabs == 4 and chunks == 2 and depth == 2 * RADIUS
    steps = source.shape[0]
    courant = courant.reshape(depth * across, along)
    source = source.reshape(steps, depth * across, along)

    exchange = lambda odd, even, edge: (odd_swap(odd), even_swap(even), core_swap(edge))
    now, previous, halos = [], [None] * chunks, []
    for c in range(chunks):
        u, *edges = first_field(probes, c, source[:1])
        now.append(u)
        halos.append(exchange(*edges))
    courant, source = turn(courant, source, now[-1])
    finals = []
    for n in range(1, steps):
        for c in range(chunks):
            odd, even, beside = halos[c]
            base = local_step(now[c], beside, probes, c, courant, source, n, previous[c])
            if n < steps - 1:
                u, *edges = rim_step(base, odd, even, courant, "middle")
                previous[c], now[c] = now[c], u
                halos[c] = exchange(*edges)
            elif paired:
                count = RADIUS if c > 0 else RADIUS // 2
                sent = [
                    part_step(base, odd, even, courant, True, begin, count)
                    for begin in range(0, RADIUS, count)
                ]
                kept = part_step(base, odd, even, courant, False)
                finals.append(([kept], sent, [chip_swap(a) for a in sent]))
            else:
                finals += rim_step(base, odd, even, courant, "all")
    return (coupled if paired else coupled_general)(finals, cell_count)


def solution(mesh):
    placed = (
        P(("groups", "slab"), "sub", None, "probe"),
        P("slab", "sub", None),
        P(None, ("groups", "slab"), "sub", None),
    )
    return jax.shard_map(
        shards,
        mesh=mesh,
        in_specs=placed,
        out_specs=(P(("groups", "slab"), None), P(("groups", "slab"))),
        check_vma=False,
    )
```
